32 devices in a mesh: rep: 2 (over core), shard: 16 (over z, y, x).
Axes of the slice: x: 2, y: 2, z: 4, core: 2. Of those that a mesh axis runs over, the one named last changes fastest.
Arguments:
- noisy: float32 [32, 4, 32, 32], P(('rep', 'shard')), may hold values from -6 to 6
- timesteps: int32 [32], P(('rep', 'shard')), may hold values from 0 to 999
- labels: int32 [32], P(('rep', 'shard')), may hold values from 0 to 999
- noise: float32 [32, 4, 32, 32], P(('rep', 'shard')), may hold values from -12 to 12
- block_in: float32 [1, 1024, 14336], P(None, 'shard'), may hold values from -3 to 3
- block_in_first: float32 [1, 1024, 14336], P(None, 'shard'), may hold values from -4.5776367e-05 to 4.5776367e-05
- block_in_second: float32 [1, 1024, 14336], P(None, 'shard'), may hold values from 8.569345e-12 to 3.427738e-11
- block_out: float32 [1, 4096, 1024], P(None, 'shard'), may hold values from -0.09375 to 0.09375
- block_out_first: float32 [1, 4096, 1024], P(None, 'shard'), may hold values from -4.5776367e-05 to 4.5776367e-05
- block_out_second: float32 [1, 4096, 1024], P(None, 'shard'), may hold values from 8.569345e-12 to 3.427738e-11
- entry_table: float32 [1272, 1024], P(None, 'shard'), may hold values from -1.5 to 1.5
- entry_first: float32 [1272, 1024], P(None, 'shard'), may hold values from -0.0014648438 to 0.0014648438
- entry_second: float32 [1272, 1024], P(None, 'shard'), may hold values from 1.071168e-08 to 4.284672e-08
- exit_proj: float32 [1024, 3088], P('shard'), may hold values from -0.1875 to 0.1875
- exit_first: float32 [1024, 3088], P('shard'), may hold values from -0.0014648438 to 0.0014648438
- exit_second: float32 [1024, 3088], P('shard'), may hold values from 1.071168e-08 to 4.284672e-08
Outputs:
- loss: float32 [], replicated
- grad_norm: float32 [], replicated
- block_in_new: float32 [1, 1024, 14336], P(None, 'shard')
- block_in_first_new: float32 [1, 1024, 14336], P(None, 'shard')
- block_in_second_new: float32 [1, 1024, 14336], P(None, 'shard')
- block_in_low: bfloat16 [1, 1024, 14336], P(None, 'shard')
- block_out_new: float32 [1, 4096, 1024], P(None, 'shard')
- block_out_first_new: float32 [1, 4096, 1024], P(None, 'shard')
- block_out_second_new: float32 [1, 4096, 1024], P(None, 'shard')
- block_out_low: bfloat16 [1, 4096, 1024], P(None, 'shard')
- entry_new: float32 [1272, 1024], P(None, 'shard')
- entry_first_new: float32 [1272, 1024], P(None, 'shard')
- entry_second_new: float32 [1272, 1024], P(None, 'shard')
- entry_low: bfloat16 [1272, 1024], P(None, 'shard')
- exit_new: float32 [1024, 3088], P('shard')
- exit_first_new: float32 [1024, 3088], P('shard')
- exit_second_new: float32 [1024, 3088], P('shard')
- exit_low: bfloat16 [1024, 3088], P('shard')
The draws below stay inside these ranges and needn't reach their ends.
All inputs are finite; a program needn't handle non-finite values.
Results may differ from the reference program's by a relative error of at most 0.017.
Values may be sent and summed in bfloat16 or wider, within the bound.
A program may use at most 384 MiB of HBM per device.

```python
import math
import jax
import jax.numpy as jnp
from jax import lax

D = 1024
HEADS = 16
FF = 4096
PATCH = 2
CHAN = 4
SIDE = 32
NCLS = 1000
FREQ = 256
LAYERS = 1
STEP = 10
TOK_LAT = 256
PDIM = 16
WIDE_IN = 14336
ENTRY_ROWS = 1272
EXIT_COLS = 3088
LATENTS = 32
NPARAMS = 23339008


def draw_noise(key, part):
    key = jax.random.fold_in(key, 5)
    shape = (LATENTS, CHAN, SIDE, SIDE)
    index = jnp.arange(LATENTS)
    half = LATENTS // 2
    along = (index % half).astype(jnp.float32) / half
    across = (index // half).astype(jnp.float32)
    base = jnp.clip(jax.random.normal(key, shape, jnp.float32), -4.0, 4.0)
    factor = jnp.sqrt((1.0 + 2.0 * along) * (1.0 + 2.0 * across))
    return base * factor[:, None, None, None]


def draw_block_in(key, part):
    key = jax.random.fold_in(key, 11)
    shape = (LAYERS, D, 10 * D + FF)
    base = jnp.clip(jax.random.normal(key, shape, jnp.float32), -4.0, 4.0)
    column = jnp.arange(10 * D + FF)
    boost = jnp.where((column >= 9 * D) & (column < 10 * D), 8.0, 1.0)
    return base * boost[None, None, :] / math.sqrt(D)


def place_ends(drawn, own_key, least, high):
    longest = drawn.shape.index(max(drawn.shape))
    spots = []
    for shift in (0, 1):
        where = [jax.random.randint(jax.random.fold_in(own_key, axis), (), 0, length) for axis, length in enumerate(drawn.shape)]
        where[longest] = (where[longest] + shift) % drawn.shape[longest]
        spots.append(tuple(where))
    return drawn.at[spots[0]].set(least).at[spots[1]].set(high)


def shard_levels(stream_key, extent, cuts, low, high):
    def one(position, blocks):
        steps = jax.random.uniform(jax.random.fold_in(jax.random.fold_in(stream_key, 6), position), (blocks,), jnp.float32, low / len(cuts), high / len(cuts))
        return jnp.repeat(jnp.exp(steps), extent[position] // blocks).reshape((-1,) + (1,) * (len(extent) - position - 1))

    level = one(*cuts[0])
    for cut in cuts[1:]:
        level = level * one(*cut)
    return level


def bell_draw(key, shape, spread, limit, cuts=(), held_as=jnp.bfloat16):
    gain = shard_levels(key, shape, cuts, -0.22, 0.18) if cuts else 1.0
    drawn = jax.random.normal(key, shape, jnp.float32) * spread * gain
    return jnp.minimum(jnp.maximum(drawn, -limit), limit).astype(held_as)


def setup_inputs(seed: int = 0) -> dict:
    streams_of = jax.random.split(jax.random.key(seed), 17)
    return {
        "noisy": bell_draw(streams_of[0], (LATENTS, CHAN, SIDE, SIDE), 1.0, 6.0, ((0, 32),), jnp.float32),
        "timesteps": place_ends(jax.random.randint(streams_of[1], (LATENTS,), 0, 1000), jax.random.fold_in(streams_of[1], 1), 0, 999).astype(jnp.int32),
        "labels": place_ends(jax.random.randint(streams_of[2], (LATENTS,), 0, NCLS), jax.random.fold_in(streams_of[2], 1), 0, NCLS - 1).astype(jnp.int32),
        "noise": draw_noise(jax.random.fold_in(streams_of[16], 71), 0),
        "block_in": draw_block_in(jax.random.fold_in(streams_of[16], 71), 0),
        "block_in_first": bell_draw(streams_of[5], (LAYERS, D, WIDE_IN), (0.015 / NPARAMS ** 0.5), 4.57763671875e-05, ((1, 16),), jnp.float32),
        "block_in_second": jnp.clip(jnp.exp(math.log(3.427737954586618e-11) - 1.3862944 * jax.random.uniform(streams_of[6], (LAYERS, D, WIDE_IN), jnp.float32) ** shard_levels(streams_of[6], (LAYERS, D, WIDE_IN), ((1, 16),), -0.2, 0.2)), 8.569344886466546e-12, 3.427737954586618e-11),
        "block_out": bell_draw(streams_of[7], (LAYERS, FF, D), FF ** -0.5, 0.09375, ((1, 16),), jnp.float32),
        "block_out_first": bell_draw(streams_of[8], (LAYERS, FF, D), (0.015 / NPARAMS ** 0.5), 4.57763671875e-05, ((1, 16),), jnp.float32),
        "block_out_second": jnp.clip(jnp.exp(math.log(3.427737954586618e-11) - 1.3862944 * jax.random.uniform(streams_of[9], (LAYERS, FF, D), jnp.float32) ** shard_levels(streams_of[9], (LAYERS, FF, D), ((1, 16),), -0.2, 0.2)), 8.569344886466546e-12, 3.427737954586618e-11),
        "entry_table": bell_draw(streams_of[10], (ENTRY_ROWS, D), 0.25, 1.5, ((1, 16),), jnp.float32),
        "entry_first": bell_draw(streams_of[11], (ENTRY_ROWS, D), (0.5 / NPARAMS ** 0.5), 0.0014648438, ((1, 16),), jnp.float32),
        "entry_second": jnp.clip(jnp.exp(math.log(4.2846721726164105e-08) - 1.3862944 * jax.random.uniform(streams_of[12], (ENTRY_ROWS, D), jnp.float32) ** shard_levels(streams_of[12], (ENTRY_ROWS, D), ((1, 16),), -0.2, 0.2)), 1.0711680431541026e-08, 4.2846721726164105e-08),
        "exit_proj": bell_draw(streams_of[13], (D, EXIT_COLS), D ** -0.5, 0.1875, ((0, 16),), jnp.float32),
        "exit_first": bell_draw(streams_of[14], (D, EXIT_COLS), (0.5 / NPARAMS ** 0.5), 0.0014648438, ((0, 16),), jnp.float32),
        "exit_second": jnp.clip(jnp.exp(math.log(4.2846721726164105e-08) - 1.3862944 * jax.random.uniform(streams_of[15], (D, EXIT_COLS), jnp.float32) ** shard_levels(streams_of[15], (D, EXIT_COLS), ((0, 16),), -0.2, 0.2)), 1.0711680431541026e-08, 4.2846721726164105e-08),
    }


@jax.custom_vjp
def low(v):
    return lax.optimization_barrier(v.astype(jnp.bfloat16)).astype(jnp.float32)

@jax.custom_vjp
def low_back(v):
    return v

def low_keep(v):
    return (low(v), None)

def low_pass(kept, grad):
    return (grad,)

def back_keep(v):
    return (v, None)

def back_low(kept, grad):
    return (low(grad),)
low.defvjp(low_keep, low_pass)
low_back.defvjp(back_keep, back_low)
highest = lax.Precision.HIGHEST
clip_limit = 0.5
rate_main = 0.02
rate_edge = 0.1
decay_rate = 0.01
adam_eps = 1e-08

def patchify(image, patch):
    batch, chans, height, width = image.shape
    grid = height // patch
    parts = image.reshape(batch, chans, grid, patch, grid, patch)
    parts = parts.transpose(0, 2, 4, 3, 5, 1)
    return parts.reshape(batch, grid * grid, patch * patch * chans)

def position_table(grid, width):
    quarter = width // 4
    omega = 1.0 / 10000.0 ** (jnp.arange(quarter, dtype=jnp.float32) / quarter)
    index = jnp.arange(grid * grid)
    row_pos = (index // grid).astype(jnp.float32)[:, None] * omega[None, :]
    col_pos = (index % grid).astype(jnp.float32)[:, None] * omega[None, :]
    return jnp.concatenate([jnp.sin(col_pos), jnp.cos(col_pos), jnp.sin(row_pos), jnp.cos(row_pos)], axis=1)

def time_features(steps, size):
    half = size // 2
    freqs = jnp.exp(-jnp.log(10000.0) * jnp.arange(half, dtype=jnp.float32) / half)
    angles = steps.astype(jnp.float32)[:, None] * freqs[None, :]
    return jnp.concatenate([jnp.cos(angles), jnp.sin(angles)], axis=1)

def modulate(x, shift, scale):
    centered = x - lax.optimization_barrier(jnp.mean(x, axis=-1, keepdims=True))
    var = lax.optimization_barrier(jnp.mean(centered * centered, axis=-1, keepdims=True))
    normed = centered * lax.rsqrt(var + 1e-06)
    return normed * (1.0 + scale[:, None, :]) + shift[:, None, :]

def adam_step(weight, first, second, grad, factor, rate):
    clipped = grad * factor
    first_new = 0.5 * first + 0.5 * clipped
    second_new = 0.5 * second + 0.5 * clipped * clipped
    corr = 1.0 - 0.5 ** STEP
    update = first_new / corr / (jnp.sqrt(second_new / corr) + adam_eps) + decay_rate * weight
    weight_new = weight - rate * update
    return (weight_new, first_new, second_new, weight_new.astype(jnp.bfloat16))

def einsum_high(form, left, right):
    return jnp.einsum(form, left, right, precision=highest)

def block(x, cond_low, w_in, w_out):
    width = x.shape[-1]
    batch, seq = (x.shape[0], x.shape[1])
    size = width // HEADS
    mod = low_back(jnp.dot(cond_low, w_in[:, :6 * width], precision=highest))
    shift_a, scale_a, gate_a, shift_b, scale_b, gate_b = jnp.split(mod, 6, axis=-1)
    attn_in = low(modulate(x, shift_a, scale_a))
    qkv = low(low_back(einsum_high('bsd,de->bse', attn_in, w_in[:, 6 * width:9 * width])))
    query = qkv[..., :width].reshape(batch, seq, HEADS, size)
    keys = qkv[..., width:2 * width].reshape(batch, seq, HEADS, size)
    values = qkv[..., 2 * width:].reshape(batch, seq, HEADS, size)
    scores = low_back(einsum_high('bqhd,bkhd->bhqk', query, keys)) * size ** (-0.5)
    weights = jax.nn.softmax(scores, axis=-1)
    mixed = low(low_back(einsum_high('bhqk,bkhd->bqhd', low(weights), values))).reshape(batch, seq, width)
    attn_out = low_back(einsum_high('bsd,de->bse', mixed, w_in[:, 9 * width:10 * width]))
    resid = x + gate_a[:, None, :] * attn_out
    mlp_in = low(modulate(resid, shift_b, scale_b))
    hidden = low_back(einsum_high('bsd,df->bsf', mlp_in, w_in[:, 10 * width:]))
    active = low(jax.nn.gelu(hidden, approximate=True))
    mlp_out = low_back(einsum_high('bsf,fd->bsd', active, w_out))
    return resid + gate_b[:, None, :] * mlp_out

def loss_fn(weights, noisy, steps, labels, noise):
    block_in, block_out, entry_table, exit_proj = weights
    block_in_lw = low(block_in)
    block_out_lw = low(block_out)
    entry_lw = low(entry_table)
    exit_lw = low(exit_proj)
    w_patch = entry_lw[:PDIM]
    w_label = entry_lw[PDIM:PDIM + NCLS]
    w_time = entry_lw[PDIM + NCLS:]
    w_time2 = exit_lw[:, :D]
    w_final = exit_lw[:, D:3 * D]
    w_output = exit_lw[:, 3 * D:]
    patches = low(patchify(noisy, PATCH))
    target = patchify(noise, PATCH)
    x = low_back(einsum_high('bsp,pd->bsd', patches, w_patch)) + position_table(SIDE // PATCH, D)[None]
    femb = low(time_features(steps, FREQ))
    t_hidden = low_back(jnp.dot(femb, w_time, precision=highest))
    t_act = low(jax.nn.silu(t_hidden))
    temb = low_back(jnp.dot(t_act, w_time2, precision=highest))
    onehot = (labels[:, None] == jnp.arange(NCLS)[None, :]).astype(jnp.float32)
    cond = temb + jnp.dot(onehot, w_label, precision=highest)
    cond_low = low(jax.nn.silu(cond))
    for layer in range(LAYERS):
        x = block(x, cond_low, block_in_lw[layer], block_out_lw[layer])
    final_mod = low_back(jnp.dot(cond_low, w_final, precision=highest))
    shift_f, scale_f = jnp.split(final_mod, 2, axis=-1)
    final_in = low(modulate(x, shift_f, scale_f))
    pred = low_back(einsum_high('bsd,dp->bsp', final_in, w_output))
    error = pred - target
    return jnp.sum(error * error) / (TOK_LAT * PDIM)

def reference(noisy, timesteps, labels, noise, block_in, block_in_first, block_in_second, block_out, block_out_first, block_out_second, entry_table, entry_first, entry_second, exit_proj, exit_first, exit_second):
    weights = (block_in, block_out, entry_table, exit_proj)
    group = min(16, LATENTS)
    count = LATENTS // group

    def one_group(carry, item):
        images, steps, classes, targets = item
        value, pull = jax.vjp(lambda wa, wb, wc, wd: loss_fn((wa, wb, wc, wd), images, steps, classes, targets), block_in, block_out, entry_table, exit_proj)
        grads = pull(jnp.ones_like(value))
        return ((carry[0] + value, tuple((acc + new for acc, new in zip(carry[1], grads)))), None)
    init = (jnp.zeros((), jnp.float32), tuple((jnp.zeros_like(w) for w in weights)))
    items = (noisy.reshape((count, group) + noisy.shape[1:]), timesteps.reshape(count, group), labels.reshape(count, group), noise.reshape((count, group) + noise.shape[1:]))
    (loss, grads), _ = lax.scan(one_group, init, items)
    grad_norm = jnp.sqrt(jnp.sum(grads[0] * grads[0]) + jnp.sum(grads[1] * grads[1]) + jnp.sum(grads[2] * grads[2]) + jnp.sum(grads[3] * grads[3]))
    factor = clip_limit / jnp.maximum(grad_norm, clip_limit)
    bi_w, bi_m, bi_v, bi_l = adam_step(block_in, block_in_first, block_in_second, grads[0], factor, rate_main)
    bo_w, bo_m, bo_v, bo_l = adam_step(block_out, block_out_first, block_out_second, grads[1], factor, rate_main)
    en_w, en_m, en_v, en_l = adam_step(entry_table, entry_first, entry_second, grads[2], factor, rate_edge)
    ex_w, ex_m, ex_v, ex_l = adam_step(exit_proj, exit_first, exit_second, grads[3], factor, rate_main)
    return (loss, grad_norm, bi_w, bi_m, bi_v, bi_l, bo_w, bo_m, bo_v, bo_l, en_w, en_m, en_v, en_l, ex_w, ex_m, ex_v, ex_l)
```

```python
import jax
import jax.numpy as jnp
from jax import lax
from jax.experimental import pallas as pl
from jax.experimental.pallas import tpu as pltpu
from jax.sharding import PartitionSpec as P

D = 1024
HEADS = 16
PATCH = 2
NCLS = 1000
FREQ = 256
STEP = 10
PDIM = 16


clip_limit = 0.5
rate_main = 0.02
rate_edge = 0.1
decay_rate = 0.01
adam_eps = 1e-08
highest = lax.Precision.HIGHEST


def lowered(value):
    return value.astype(jnp.bfloat16)


def product(left, right):
    return jnp.dot(left, right, preferred_element_type=jnp.float32)


def product_tn(left, right):
    return lax.dot_general(
        left, right, (((0,), (0,)), ((), ())), preferred_element_type=jnp.float32
    )


def product_nt(left, right):
    return lax.dot_general(
        left, right, (((1,), (1,)), ((), ())), preferred_element_type=jnp.float32
    )


def patchify(image, patch):
    batch, chans, height, width = image.shape
    grid = height // patch
    parts = image.reshape(batch, chans, grid, patch, grid, patch)
    parts = parts.transpose(0, 2, 4, 3, 5, 1)
    return parts.reshape(batch, grid * grid, patch * patch * chans)


def position_table(grid, width):
    quarter = width // 4
    omega = 1.0 / 10000.0 ** (jnp.arange(quarter, dtype=jnp.float32) / quarter)
    index = jnp.arange(grid * grid)
    row_pos = (index // grid).astype(jnp.float32)[:, None] * omega[None, :]
    col_pos = (index % grid).astype(jnp.float32)[:, None] * omega[None, :]
    return jnp.concatenate(
        [jnp.sin(col_pos), jnp.cos(col_pos), jnp.sin(row_pos), jnp.cos(row_pos)], axis=1
    )


def time_features(steps, size):
    half = size // 2
    freqs = jnp.exp(-jnp.log(10000.0) * jnp.arange(half, dtype=jnp.float32) / half)
    angles = steps.astype(jnp.float32)[:, None] * freqs[None, :]
    return jnp.concatenate([jnp.cos(angles), jnp.sin(angles)], axis=1)


def modulate(x, shift, scale):
    centered = x - jnp.mean(x, axis=-1, keepdims=True)
    var = jnp.mean(centered * centered, axis=-1, keepdims=True)
    normed = centered * lax.rsqrt(var + 1e-06)
    return normed * (1.0 + scale[:, None, :]) + shift[:, None, :]


def gelu_tanh(value):
    return jax.nn.gelu(value, approximate=True)


def adam_step(weight, first, second, grad, factor, rate):
    clipped = grad * factor
    first_new = 0.5 * first + 0.5 * clipped
    second_new = 0.5 * second + 0.5 * clipped * clipped
    corr = 1.0 - 0.5**STEP
    update = first_new / corr / (jnp.sqrt(second_new / corr) + adam_eps) + decay_rate * weight
    weight_new = weight - rate * update
    return (weight_new, first_new, second_new, weight_new.astype(jnp.bfloat16))


def layer_parts(x, cond_low, w_in, w_out):
    width = x.shape[-1]
    batch, seq = (x.shape[0], x.shape[1])
    size = width // HEADS
    mod = product(cond_low, w_in[:, : 6 * width])
    shift_a, scale_a, gate_a, shift_b, scale_b, gate_b = jnp.split(mod, 6, axis=-1)
    attn_in = lowered(modulate(x, shift_a, scale_a))
    qkv = lowered(
        jnp.einsum(
            "bsd,de->bse",
            attn_in,
            w_in[:, 6 * width : 9 * width],
            preferred_element_type=jnp.float32,
        )
    )
    query = qkv[..., :width].reshape(batch, seq, HEADS, size)
    keys = qkv[..., width : 2 * width].reshape(batch, seq, HEADS, size)
    values = qkv[..., 2 * width :].reshape(batch, seq, HEADS, size)
    scores = jnp.einsum(
        "bqhd,bkhd->bhqk", query, keys, preferred_element_type=jnp.float32
    ) * size ** (-0.5)
    weights = jax.nn.softmax(scores, axis=-1)
    weights_low = lowered(weights)
    mixed = lowered(
        jnp.einsum("bhqk,bkhd->bqhd", weights_low, values, preferred_element_type=jnp.float32)
    ).reshape(batch, seq, width)
    attn_out = jnp.einsum(
        "bsd,de->bse", mixed, w_in[:, 9 * width : 10 * width], preferred_element_type=jnp.float32
    )
    resid = x + gate_a[:, None, :] * attn_out
    mlp_in = lowered(modulate(resid, shift_b, scale_b))
    hidden = jnp.einsum(
        "bsd,df->bsf", mlp_in, w_in[:, 10 * width :], preferred_element_type=jnp.float32
    )
    active = lowered(gelu_tanh(hidden))
    mlp_out = jnp.einsum("bsf,fd->bsd", active, w_out, preferred_element_type=jnp.float32)
    result = resid + gate_b[:, None, :] * mlp_out
    return dict(
        mods=(shift_a, scale_a, gate_a, shift_b, scale_b, gate_b),
        attn_in=attn_in,
        query=query,
        keys=keys,
        values=values,
        weights=weights,
        weights_low=weights_low,
        mixed=mixed,
        attn_out=attn_out,
        resid=resid,
        mlp_in=mlp_in,
        hidden=hidden,
        active=active,
        mlp_out=mlp_out,
        result=result,
    )


def layer_back(x, cond_low, w_in, w_out, parts, grad_out, grad_cond):
    width = x.shape[-1]
    batch, seq = (x.shape[0], x.shape[1])
    size = width // HEADS
    shift_a, scale_a, gate_a, shift_b, scale_b, gate_b = parts["mods"]
    d_gate_b = jnp.sum(grad_out * parts["mlp_out"], axis=1)
    d_mlp_out = lowered(grad_out * gate_b[:, None, :])
    g_fc2 = jnp.einsum(
        "bsf,bsd->fd", parts["active"], d_mlp_out, preferred_element_type=jnp.float32
    )
    d_active = jnp.einsum("bsd,fd->bsf", d_mlp_out, w_out, preferred_element_type=jnp.float32)
    _, gelu_pull = jax.vjp(gelu_tanh, parts["hidden"])
    d_hidden = lowered(gelu_pull(d_active)[0])
    g_fc1 = jnp.einsum("bsd,bsf->df", parts["mlp_in"], d_hidden, preferred_element_type=jnp.float32)
    d_mlp_in = jnp.einsum(
        "bsf,df->bsd", d_hidden, w_in[:, 10 * width :], preferred_element_type=jnp.float32
    )
    _, norm_pull = jax.vjp(modulate, parts["resid"], shift_b, scale_b)
    d_resid, d_shift_b, d_scale_b = norm_pull(d_mlp_in)
    d_resid = d_resid + grad_out
    d_gate_a = jnp.sum(d_resid * parts["attn_out"], axis=1)
    d_attn_out = lowered(d_resid * gate_a[:, None, :])
    g_proj = jnp.einsum(
        "bsd,bse->de", parts["mixed"], d_attn_out, preferred_element_type=jnp.float32
    )
    d_mixed = lowered(
        jnp.einsum(
            "bse,de->bsd",
            d_attn_out,
            w_in[:, 9 * width : 10 * width],
            preferred_element_type=jnp.float32,
        )
    ).reshape(batch, seq, HEADS, size)
    d_probs = jnp.einsum(
        "bqhd,bkhd->bhqk", d_mixed, parts["values"], preferred_element_type=jnp.float32
    )
    d_values = jnp.einsum(
        "bhqk,bqhd->bkhd", parts["weights_low"], d_mixed, preferred_element_type=jnp.float32
    )
    weights = parts["weights"]
    d_scores = weights * (d_probs - jnp.sum(d_probs * weights, axis=-1, keepdims=True))
    d_scaled = lowered(d_scores * size ** (-0.5))
    d_query = jnp.einsum(
        "bhqk,bkhd->bqhd", d_scaled, parts["keys"], preferred_element_type=jnp.float32
    )
    d_keys = jnp.einsum(
        "bhqk,bqhd->bkhd", d_scaled, parts["query"], preferred_element_type=jnp.float32
    )
    d_qkv = lowered(
        jnp.concatenate(
            [
                d_query.reshape(batch, seq, width),
                d_keys.reshape(batch, seq, width),
                d_values.reshape(batch, seq, width),
            ],
            axis=-1,
        )
    )
    g_qkv = jnp.einsum("bsd,bse->de", parts["attn_in"], d_qkv, preferred_element_type=jnp.float32)
    d_attn_in = jnp.einsum(
        "bse,de->bsd", d_qkv, w_in[:, 6 * width : 9 * width], preferred_element_type=jnp.float32
    )
    _, first_pull = jax.vjp(modulate, x, shift_a, scale_a)
    d_x, d_shift_a, d_scale_a = first_pull(d_attn_in)
    d_x = d_x + d_resid
    d_mod = lowered(
        jnp.concatenate([d_shift_a, d_scale_a, d_gate_a, d_shift_b, d_scale_b, d_gate_b], axis=-1)
    )
    g_mod = product_tn(cond_low, d_mod)
    grad_cond = grad_cond + product_nt(d_mod, w_in[:, : 6 * width])
    g_in = jnp.concatenate([g_mod, g_qkv, g_proj, g_fc1], axis=1)
    return (d_x, grad_cond, g_in, g_fc2)


def local(
    noisy,
    timesteps,
    labels,
    noise,
    block_in,
    block_in_first,
    block_in_second,
    block_out,
    block_out_first,
    block_out_second,
    entry_table,
    entry_first,
    entry_second,
    exit_proj,
    exit_first,
    exit_second,
):
    layers = block_in.shape[0]
    entry_all, exit_all = (
        lax.all_gather(lowered(entry_table), "shard", axis=1, tiled=True),
        lax.all_gather(lowered(exit_proj), "shard", axis=0, tiled=True),
    )
    w_patch = entry_all[:PDIM]
    w_label = entry_all[PDIM : PDIM + NCLS]
    w_time = entry_all[PDIM + NCLS :]
    w_time2 = exit_all[:, :D]
    w_final = exit_all[:, D : 3 * D]
    w_output = exit_all[:, 3 * D :]
    patches = lowered(patchify(noisy, PATCH))
    target = patchify(noise, PATCH)
    seq = patches.shape[1]
    x = (
        jnp.einsum("bsp,pd->bsd", patches, w_patch, preferred_element_type=jnp.float32)
        + position_table(noisy.shape[-1] // PATCH, D)[None]
    )
    femb = lowered(time_features(timesteps, FREQ))
    t_hidden = product(femb, w_time)
    t_act = lowered(jax.nn.silu(t_hidden))
    temb = product(t_act, w_time2)
    onehot = (labels[:, None] == jnp.arange(NCLS)[None, :]).astype(jnp.float32)
    cond = temb + jnp.dot(onehot, w_label.astype(jnp.float32), precision=highest)
    cond_low = lowered(jax.nn.silu(cond))
    layer = 0
    w_in_all = lax.all_gather(lowered(block_in[layer]), "shard", axis=0, tiled=True)
    w_out_all = lax.all_gather(lowered(block_out[layer]), "shard", axis=0, tiled=True)
    inputs = [x]
    parts = layer_parts(x, cond_low, w_in_all, w_out_all)
    saved = [parts]
    x = parts["result"]
    final_mod = product(cond_low, w_final)
    shift_f, scale_f = jnp.split(final_mod, 2, axis=-1)
    final_in = lowered(modulate(x, shift_f, scale_f))
    pred = jnp.einsum("bsd,dp->bsp", final_in, w_output, preferred_element_type=jnp.float32)
    error = pred - target
    loss_part = jnp.sum(error * error) / (seq * PDIM)
    d_pred = lowered(2.0 * error / (seq * PDIM))
    g_output = jnp.einsum("bsd,bsp->dp", final_in, d_pred, preferred_element_type=jnp.float32)
    d_final_in = jnp.einsum("bsp,dp->bsd", d_pred, w_output, preferred_element_type=jnp.float32)
    _, final_pull = jax.vjp(modulate, x, shift_f, scale_f)
    d_x, d_shift_f, d_scale_f = final_pull(d_final_in)
    d_fmod = lowered(jnp.concatenate([d_shift_f, d_scale_f], axis=-1))
    g_final = product_tn(cond_low, d_fmod)
    grad_cond = product_nt(d_fmod, w_final)
    shards_in = [None] * layers
    shards_out = [None] * layers
    for layer in reversed(range(layers)):
        w_in_all, w_out_all = (
            lax.all_gather(lowered(block_in[layer]), "shard", axis=0, tiled=True),
            lax.all_gather(lowered(block_out[layer]), "shard", axis=0, tiled=True),
        )
        d_x, grad_cond, g_in, g_fc2 = layer_back(
            inputs[layer], cond_low, w_in_all, w_out_all, saved[layer], d_x, grad_cond
        )
        shards_in[layer], shards_out[layer] = (
            lax.psum_scatter(g_in, "shard", scatter_dimension=0, tiled=True),
            lax.psum_scatter(g_fc2, "shard", scatter_dimension=0, tiled=True),
        )
    _, silu_pull = jax.vjp(jax.nn.silu, cond)
    d_cond = silu_pull(grad_cond)[0]
    g_label = jnp.dot(onehot.T, d_cond, precision=highest)
    d_temb = lowered(d_cond)
    g_time2 = product_tn(t_act, d_temb)
    d_tact = product_nt(d_temb, w_time2)
    _, time_pull = jax.vjp(jax.nn.silu, t_hidden)
    d_thidden = lowered(time_pull(d_tact)[0])
    g_time = product_tn(femb, d_thidden)
    g_patch = jnp.einsum("bsp,bsd->pd", patches, lowered(d_x), preferred_element_type=jnp.float32)
    g_entry = jnp.concatenate([g_patch, g_label, g_time], axis=0)
    g_exit = jnp.concatenate([g_time2, g_final, g_output], axis=1)
    share_entry, share_exit = (
        lax.psum_scatter(g_entry, "shard", scatter_dimension=1, tiled=True),
        lax.psum_scatter(g_exit, "shard", scatter_dimension=0, tiled=True),
    )
    grads = (
        lax.psum(jnp.stack(shards_in).astype(jnp.bfloat16), "rep").astype(jnp.float32),
        lax.psum(jnp.stack(shards_out).astype(jnp.bfloat16), "rep").astype(jnp.float32),
        lax.psum(share_entry.astype(jnp.bfloat16), "rep").astype(jnp.float32),
        lax.psum(share_exit.astype(jnp.bfloat16), "rep").astype(jnp.float32),
    )
    squares = (
        jnp.sum(grads[0] * grads[0])
        + jnp.sum(grads[1] * grads[1])
        + jnp.sum(grads[2] * grads[2])
        + jnp.sum(grads[3] * grads[3])
    )
    loss = lax.psum(loss_part, ("rep", "shard"))
    norm_sq = lax.psum(squares, "shard")
    grad_norm = jnp.sqrt(norm_sq)
    factor = clip_limit / jnp.maximum(grad_norm, clip_limit)
    bi_w, bi_m, bi_v, bi_l = adam_step(
        block_in, block_in_first, block_in_second, grads[0], factor, rate_main
    )
    bo_w, bo_m, bo_v, bo_l = adam_step(
        block_out, block_out_first, block_out_second, grads[1], factor, rate_main
    )
    en_w, en_m, en_v, en_l = adam_step(
        entry_table, entry_first, entry_second, grads[2], factor, rate_edge
    )
    ex_w, ex_m, ex_v, ex_l = adam_step(
        exit_proj, exit_first, exit_second, grads[3], factor, rate_main
    )
    return (
        loss,
        grad_norm,
        bi_w,
        bi_m,
        bi_v,
        bi_l,
        bo_w,
        bo_m,
        bo_v,
        bo_l,
        en_w,
        en_m,
        en_v,
        en_l,
        ex_w,
        ex_m,
        ex_v,
        ex_l,
    )


BF = jnp.bfloat16
F32 = jnp.float32
MESH = pl.DeviceIdType.MESH
TOK = 256
LANES = 128
CHUNKS = 12
ORDER = (8, 9, 10, 11, 4, 5, 6, 7, 3, 0, 1, 2)


def dot_nn(left, right):
    return lax.dot_general(left, right, (((1,), (0,)), ((), ())), preferred_element_type=F32)


def dot_nt(left, right):
    return lax.dot_general(left, right, (((1,), (1,)), ((), ())), preferred_element_type=F32)


def dot_tn(left, right):
    return lax.dot_general(left, right, (((0,), (0,)), ((), ())), preferred_element_type=F32)


def sigmoid(value):
    return 1.0 / (1.0 + jnp.exp(-value))


def silu_slope(value):
    gate = sigmoid(value)
    return gate * (1.0 + value * (1.0 - gate))


def normed(x):
    centered = x - jnp.mean(x, axis=-1, keepdims=True)
    var = jnp.mean(centered * centered, axis=-1, keepdims=True)
    inv = lax.rsqrt(var + 1e-06)
    return centered * inv, inv


def normed_back(d_normed, x_normed, inv):
    mean_d = jnp.mean(d_normed, axis=-1, keepdims=True)
    mean_dx = jnp.mean(d_normed * x_normed, axis=-1, keepdims=True)
    return inv * (d_normed - mean_d - x_normed * mean_dx)


def fold(value):
    rows, cols = value.shape
    return jnp.sum(value.reshape(rows // 8, 8, cols), axis=0)


def rows_at(i, size):
    return pl.ds(pl.multiple_of(i * size, size), size)


def step_kernel(
    msg, pt, pos, bi, bo, ent_in, ex_in,
    g_in, g_out, ENT, EX, stats,
    W, WP, G, R1, R2, R3, FIN,
    ATI, QKV, MIX, MLI, ACT, GD, DMO, DAO, DMX, DMS,
    X0, AO, RSD, MO, X1, SND, RCV,
    WMOD, E1, E2S, E2R, E3S, E3R, DMB, DMF, B2S, B2R, DTA, CP, CND,
    B3S, B3R, B3D, NSS, NSR, NSD, MODS, DACC, WPT, WLT, GLP, SQ, LOSS,
    st_sem, peer_s, peer_r, zs, zr, bs, br, as_, ar,
    s1s, s1r, s2s, s2r, s3s, s3r, d_s, d_r, f_l, f_s, f_r,
    cred_a, cred_b, cred_z,
):
    c = lax.axis_index("rep")
    s = lax.axis_index("shard")
    o = 1 - c
    x = s % 2
    y = (s // 2) % 2
    z = s // 4
    a_me = y * o + x * c
    b_me = x * o + y * c

    def yx(a, b):
        return a * o + b * c, b * o + a * c

    def dev(core, chip):
        return {"rep": core, "shard": chip}

    def chip_of(zz, yy, xx):
        return zz * 4 + yy * 2 + xx

    nb_a = dev(c, chip_of(z, *yx(1 - a_me, b_me)))
    nb_b = dev(c, chip_of(z, *yx(a_me, 1 - b_me)))
    twin = dev(o, s)

    def remote(src, dst, ss, rs, to):
        return pltpu.make_async_remote_copy(
            src_ref=src, dst_ref=dst, send_sem=ss, recv_sem=rs, device_id=to, device_id_type=MESH
        )

    pieces = []
    for j in range(4):
        pieces.append((bi.at[:, pl.ds(pl.multiple_of(6144 + 1024 * j + c * 512, 512), 512)], FIN.at[j]))
    for j in range(16):
        pieces.append((
            bi.at[:, pl.ds(pl.multiple_of(10240 + 256 * j + c * 128, 128), 128)],
            FIN.at[4 + j // 4, :, pl.ds((j % 4) * 128, 128)],
        ))
    for ch in range(2):
        for rh in range(2):
            pieces.append((
                bo.at[pl.ds(pl.multiple_of(c * 128 + rh * 64, 64), 64), pl.ds(ch * 512, 512)],
                FIN.at[8 + 2 * ch + rh],
            ))
    pieces.append((ent_in, ENT))
    pieces.append((ex_in, EX))
    pieces.append((bi.at[:, pl.ds(0, 6144)], WMOD))
    local = [pltpu.make_async_copy(p, q, st_sem.at[i]) for i, (p, q) in enumerate(pieces)]
    for i in (24, 25, 0, 1, 2, 3, *range(4, 24), 26):
        local[i].start()

    barrier = pltpu.get_barrier_semaphore()

    @pl.loop(1, 16)
    def _(k):
        pl.semaphore_signal(barrier, 1, device_id=dev(c, (s + k) % 16), device_id_type=MESH)

    pl.semaphore_signal(barrier, 1, device_id=twin, device_id_type=MESH)
    pl.semaphore_wait(barrier, 16)

    def peers_copy(e, k, src_of, dst):
        peer = (s + k) % 16
        return remote(src_of(peer), dst.at[s], peer_s.at[e, k], peer_r.at[e, s], dev(c, peer))

    def peers_send(e, src_of, dst):
        @pl.loop(1, 16)
        def _(k):
            peers_copy(e, k, src_of, dst).start()

    def peers_wait(e, src_of, dst):
        @pl.loop(1, 16)
        def _(k):
            frm = (s + k) % 16
            remote(src_of(frm), dst.at[frm], peer_s.at[e, k], peer_r.at[e, frm], dev(c, frm)).wait_recv()

        @pl.loop(1, 16)
        def _(k):
            peers_copy(e, k, src_of, dst).wait_send()

    def twin_copy(i, src, dst):
        return remote(src, dst, d_s.at[i], d_r.at[i], twin)

    def z_copy(k, dz):
        peer = (z + dz) % 4
        return remote(W.at[k, z, y, x], W.at[k, z, y, x], zs.at[k * 3 + dz - 1], zr.at[k * 4 + z], dev(c, chip_of(peer, y, x)))

    def z_wait(k):
        for dz in range(1, 4):
            frm = (z + dz) % 4
            remote(W.at[k, frm, y, x], W.at[k, frm, y, x], zs.at[k * 3 + dz - 1], zr.at[k * 4 + frm], dev(c, chip_of(frm, y, x))).wait_recv()

    def b_copy(k):
        return remote(W.at[k, :, y, x], W.at[k, :, y, x], bs.at[k], br.at[k], nb_b)

    def a_copy(k, i):
        yy, xx = yx(a_me, b_me if i == 0 else 1 - b_me)
        return remote(W.at[k, :, yy, xx], W.at[k, :, yy, xx], as_.at[k * 2 + i], ar.at[k * 2 + i], nb_a)

    def pump_b(k):
        z_wait(k)
        b_copy(k).start()
        a_copy(k, 0).start()

    def pump_a(k):
        b_copy(k).wait_recv()
        a_copy(k, 1).start()

    def need(k):
        a_copy(k, 0).wait_recv()
        a_copy(k, 1).wait_recv()

    E1[c, s] = msg[...]
    peers_send(0, lambda p: msg, E1.at[c])

    for k in range(CHUNKS):
        if k < 4:
            local[k].wait()
            W[k, z, y, x] = FIN[k].astype(BF)
        elif k < 8:
            if k == 4:
                for i in range(4, 20):
                    local[i].wait()
            rh, half = (k - 4) // 2, (k - 4) % 2
            for q in range(4):
                j = half * 8 + 2 * q
                pair = FIN[4 + j // 4, :, (j % 4) * 128 : (j % 4) * 128 + 256]
                piece = jnp.concatenate(
                    [pair[:, rh * 64 : rh * 64 + 64], pair[:, 128 + rh * 64 : 128 + rh * 64 + 64]], axis=1
                )
                W[k, z, y, x, :, q * 128 : q * 128 + 128] = piece.astype(BF)
        else:
            local[20 + k - 8].wait()
            W[k, z, y, x] = FIN[k].astype(BF)
        for dz in range(1, 4):
            z_copy(k, dz).start()

    local[24].wait()
    local[25].wait()
    peers_wait(0, lambda p: msg, E1.at[c])
    t_hidden = dot_nn(E1[c, :, 0, :].astype(BF), ENT[1016:1144, :].astype(BF)) + dot_nn(
        E1[c, :, 1, :].astype(BF), ENT[1144:1272, :].astype(BF)
    )
    CND[0] = t_hidden
    t_act = (t_hidden * sigmoid(t_hidden)).astype(BF)
    CP[c, 1, :, 0:64] = t_act.astype(F32)
    for q in range(8):
        E2S[q] = dot_nn(t_act, EX[:, q * 128 : q * 128 + 128].astype(BF))
    E2R[s] = E2S[s // 2]
    peers_send(1, lambda p: E2S.at[p // 2], E2R)
    for q in range(8):
        even = E1[c, 2 * q, 8:24, :]
        odd = E1[c, 2 * q + 1, 8:24, :]
        WPT[:, q * 128 : q * 128 + 128] = jnp.concatenate([even[:, :64], odd[:, :64]], axis=1)
        WLT[:, q * 128 : q * 128 + 128] = jnp.concatenate([even[:, 64:], odd[:, 64:]], axis=1)
    pump_b(0)
    hot = (
        E1[c, :, 2, 0:1].astype(jnp.int32) == lax.broadcasted_iota(jnp.int32, (16, 1024), 1)
    ).astype(F32).astype(BF)
    w_class = dot_nn(hot, ENT[16:1040, :].astype(BF))
    peers_wait(1, lambda p: E2S.at[p // 2], E2R)
    temb = jnp.sum(E2R[...], axis=0)
    cond = jnp.where(x == 0, temb[:, :64], temb[:, 64:]) + w_class
    CND[1] = cond
    cond_low = (cond * sigmoid(cond)).astype(BF)
    CP[c, 0, :, 0:64] = cond_low.astype(F32)
    local[26].wait()
    for k in range(8):
        w_k = WMOD[:, k * 1024 : k * 1024 + 1024] if k < 6 else EX[:, (k - 5) * 1024 : (k - 4) * 1024]
        E3S[:, k, :] = dot_nn(cond_low, w_k.astype(BF))
    E3R[s] = E3S[s]
    peers_send(2, lambda p: E3S.at[p], E3R)
    pump_b(1)
    pump_a(0)

    for n in range(4):
        cols = slice(n * 256, n * 256 + 256)
        X0[:, cols] = dot_nn(pt[0].astype(BF), WPT[:, cols].astype(BF))

    @pl.loop(0, 16)
    def _(i):
        X0[rows_at(i, 16), 0:512] += pos[...]
        X0[rows_at(i, 16), 512:1024] += jnp.broadcast_to(pos[pl.ds(i, 1), :], (16, 512))

    DACC[...] = jnp.zeros_like(DACC)
    peers_wait(2, lambda p: E3S.at[p], E3R)
    MODS[...] = jnp.sum(E3R[...], axis=0)

    def mod_row(k):
        return MODS[k : k + 1, :]

    def modulated(src, dst, shift, scale):
        @pl.loop(0, TOK // 32)
        def _(i):
            r = rows_at(i, 32)
            hat, _ = normed(src[r, :])
            dst[c, r, :] = (hat * (1.0 + mod_row(scale)) + mod_row(shift)).astype(BF)

    modulated(X0, ATI, 0, 1)
    twin_copy(0, ATI.at[c], ATI.at[c]).start()
    pump_b(2)
    pump_a(1)
    pump_b(3)
    pump_a(2)
    twin_copy(0, ATI.at[o], ATI.at[o]).wait_recv()

    def w_cols(k, n):
        return W[k, :, :, :, :, rows_at(n, 256)].reshape(1024, 256)

    for j in range(3):
        need(j)

        @pl.loop(0, 4)
        def _(t):
            lat, n = t // 2, t % 2
            QKV[j, lat, :, rows_at(n, 256)] = dot_nn(ATI[lat], w_cols(j, n)).astype(BF)

        pump_b(4 + j)
        pump_a(3 + j)

    lane = lax.broadcasted_iota(jnp.int32, (1, LANES), 1)
    first = lane < 64
    masks = (first.astype(F32).astype(BF), 1.0 - first.astype(F32).astype(BF))

    def probs_of(q, k):
        score = dot_nt(q, k) * 0.125
        e = jnp.exp(score - jnp.max(score, axis=-1, keepdims=True))
        return e / jnp.sum(e, axis=-1, keepdims=True)

    @pl.loop(0, 8)
    def _(t):
        lat, cols = t // 4, rows_at(t % 4, 128)
        q, k, v = QKV[0, lat, :, cols], QKV[1, lat, :, cols], QKV[2, lat, :, cols]
        outs = [dot_nn(probs_of(q * m, k).astype(BF), v) for m in masks]
        MIX[c, lat, :, cols] = jnp.where(first, outs[0], outs[1]).astype(BF)

    twin_copy(1, MIX.at[c], MIX.at[c]).start()
    need(3)
    twin_copy(2, W.at[3], WP).start()
    pump_b(7)
    pump_a(6)
    pump_b(8)
    pump_a(7)
    twin_copy(1, MIX.at[o], MIX.at[o]).wait_recv()
    twin_copy(2, W.at[3], WP).wait_recv()

    def proj(own):
        def cols(n):
            return pl.ds(pl.multiple_of((c if own else o) * 512 + n * 256, 256), 256)

        @pl.loop(0, 2)
        def _(n):
            ref = W.at[3] if own else WP
            total = 0.0
            for hh in range(2):
                w_half = ref[2 * hh : 2 * hh + 2, :, :, :, rows_at(n, 256)].reshape(512, 256)
                total += dot_nn(MIX[hh, c], w_half)
            AO[:, cols(n)] = total

    proj(True)
    proj(False)

    @pl.loop(0, TOK // 32)
    def _(i):
        r = rows_at(i, 32)
        RSD[r, :] = X0[r, :] + mod_row(2) * AO[r, :]

    modulated(RSD, MLI, 3, 4)
    twin_copy(3, MLI.at[c], MLI.at[c]).start()
    pump_b(9)
    pump_a(8)
    twin_copy(3, MLI.at[o], MLI.at[o]).wait_recv()
    for j in range(4):
        need(4 + j)

        @pl.loop(0, 4)
        def _(t):
            lat, n = t // 2, t % 2
            hidden = dot_nn(MLI[lat], w_cols(4 + j, n))
            cols = pl.ds(pl.multiple_of(j * 512 + n * 256, 256), 256)
            square = hidden * hidden
            t_in = 0.7978845608028654 * hidden * (1.0 + 0.044715 * square)
            t_out = jnp.tanh(t_in)
            half = 0.5 * (1.0 + t_out)
            ACT[lat, :, cols] = (hidden * half).astype(BF)
            slope = half + 0.5 * hidden * (1.0 - t_out * t_out) * (
                0.7978845608028654 * (1.0 + 3.0 * 0.044715 * square)
            )
            GD[lat, :, cols] = slope.astype(BF)

        if j < 2:
            pump_b(10 + j)
            pump_a(9 + j)
        if j == 2:
            pump_a(11)

    for ch in range(2):
        need(8 + 2 * ch)
        need(9 + 2 * ch)

        def mlp_tile(lat, n):
            total = 0.0
            for rh in range(2):
                total += dot_nn(ACT[lat, :, rh * 1024 : rh * 1024 + 1024], w_cols(8 + 2 * ch + rh, n))
            return total

        @pl.loop(0, 2)
        def _(n):
            SND[ch, :, rows_at(n, 256)] = mlp_tile(o, n)

        twin_copy(4 + ch, SND.at[ch], RCV.at[ch]).start()

        @pl.loop(0, 2)
        def _(n):
            MO[:, pl.ds(pl.multiple_of(ch * 512 + n * 256, 256), 256)] = mlp_tile(c, n)

    def received(i):
        for ch in range(2):
            twin_copy(i + ch, SND.at[ch], RCV.at[ch]).wait_recv()

    def both_parts(r):
        return MO[r, :] + jnp.concatenate([RCV[0, r, :], RCV[1, r, :]], axis=1)

    received(4)
    LOSS[...] = jnp.zeros_like(LOSS)
    GLP[...] = jnp.zeros_like(GLP)

    @pl.loop(0, TOK // 32)
    def _(i):
        r = rows_at(i, 32)
        mlp_out = both_parts(r)
        x1 = RSD[r, :] + mod_row(5) * mlp_out
        hat, inv = normed(x1)
        scale = 1.0 + mod_row(7)
        final_in = (hat * scale + mod_row(6)).astype(BF)
        w_lin = WLT[...].astype(BF)
        error = dot_nt(final_in, w_lin) - pt[1, r, :]
        LOSS[...] += fold(error * error)
        d_pred = (2.0 * error / (TOK * PDIM)).astype(BF)
        GLP[16:32, :] += dot_tn(d_pred, final_in)
        d_final = dot_nn(d_pred, w_lin)
        DACC[6] += fold(d_final)
        DACC[7] += fold(d_final * hat)
        d_x = normed_back(d_final * scale, hat, inv)
        X1[r, :] = d_x
        DACC[5] += fold(d_x * mlp_out)
        DMO[c, r, :] = (d_x * mod_row(5)).astype(BF)

    twin_copy(6, DMO.at[c], DMO.at[c]).start()

    def r1_of(k, b):
        return R1.at[k - 8, b] if k >= 8 else W.at[8 + k // 2, :, k % 2, b]

    def r2_of(k):
        return R2.at[k - 8] if k >= 8 else W.at[4 + k // 4, :, (k // 2) % 2, k % 2]

    def r3_of(k):
        return R3.at[k - 8] if k >= 8 else W.at[6 + k // 4, :, (k // 2) % 2, k % 2]

    def s1_copy(k, b):
        yy, xx = yx(1 - a_me, b)
        return remote(G.at[k, :, yy, xx], r1_of(k, b), s1s.at[k * 2 + b], s1r.at[k * 2 + b], nb_a)

    def s2_copy(k):
        yy, xx = yx(a_me, 1 - b_me)
        return remote(G.at[k, :, yy, xx], r2_of(k), s2s.at[k], s2r.at[k], nb_b)

    def s3_copy(k, dz):
        zt = (z + dz) % 4
        return remote(G.at[k, zt, y, x], r3_of(k).at[z], s3s.at[k * 3 + dz - 1], s3r.at[k * 4 + z], dev(c, chip_of(zt, y, x)))

    def s1(k):
        for b in range(2):
            s1_copy(k, b).start()

    def s2(k):
        for b in range(2):
            s1_copy(k, b).wait_recv()
        yy, xx = yx(a_me, 1 - b_me)

        @pl.loop(0, 4)
        def _(zz):
            total = G[k, zz, yy, xx].astype(F32) + r1_of(k, 1 - b_me)[zz].astype(F32)
            G[k, zz, yy, xx] = total.astype(BF)

        s2_copy(k).start()

    def s3(k):
        s2_copy(k).wait_recv()

        def total(zz):
            return (
                G[k, zz, y, x].astype(F32) + r1_of(k, b_me)[zz].astype(F32) + r2_of(k)[zz].astype(F32)
            )

        FIN[k] = total(z)

        @pl.loop(1, 4)
        def _(dz):
            zt = (z + dz) % 4
            G[k, zt, y, x] = total(zt).astype(BF)

        for dz in range(1, 4):
            s3_copy(k, dz).start()

    def s4(k):
        for dz in range(1, 4):
            frm = (z + dz) % 4
            remote(G.at[k, frm, y, x], r3_of(k).at[frm], s3s.at[k * 3 + dz - 1], s3r.at[k * 4 + frm], dev(c, chip_of(frm, y, x))).wait_recv()
        total = FIN[k]
        for dz in range(1, 4):
            total += r3_of(k)[(z + dz) % 4].astype(F32)
        FIN[k] = total
        SQ[...] += fold(total * total)

    def to_outputs(i, src, dst):
        pltpu.make_async_copy(src, dst, f_l.at[i]).start()
        remote(src, dst, f_s.at[i], f_r.at[i], twin).start()

    def grad_tiles(k, left, right):
        @pl.loop(0, 4)
        def _(r):
            G[k, r] = dot_tn(left(r), right).astype(BF).reshape(2, 2, 64, 512)

    SQ[...] = jnp.zeros_like(SQ)
    twin_copy(6, DMO.at[o], DMO.at[o]).wait_recv()
    for ch in range(2):
        for rh in range(2):
            k = 8 + 2 * ch + rh
            grad_tiles(
                k,
                lambda r: ACT[:, :, pl.ds(pl.multiple_of(rh * 1024 + r * 256, 256), 256)].reshape(512, 256),
                DMO[:, :, ch * 512 : ch * 512 + 512].reshape(512, 512),
            )
            s1(k)

    for k in range(CHUNKS):
        for dz in range(1, 4):
            z_copy(k, dz).wait_send()
        b_copy(k).wait_send()
        a_copy(k, 0).wait_send()
        a_copy(k, 1).wait_send()

    @pl.loop(0, 16)
    def _(t):
        lat, rh, r = t // 8, (t // 4) % 2, t % 4
        total = 0.0
        for ch in range(2):
            total += dot_nt(DMO[lat, :, ch * 512 : ch * 512 + 512], W[8 + 2 * ch + rh, r].reshape(256, 512))
        cols = pl.ds(pl.multiple_of(rh * 1024 + r * 256, 256), 256)
        GD[lat, :, cols] = (total * GD[lat, :, cols].astype(F32)).astype(BF)

    pl.semaphore_signal(cred_a, 1, device_id=nb_a, device_id_type=MESH)

    def data_back(first_k, count, left, i):
        for ch in range(2):
            @pl.loop(0, 2)
            def _(n):
                total = 0.0
                for j in range(count):
                    total += dot_nt(left(j, o), W[first_k + j, 2 * ch + n].reshape(256, 512))
                SND[ch, :, rows_at(n, 256)] = total

            twin_copy(i + ch, SND.at[ch], RCV.at[ch]).start()

        @pl.loop(0, 4)
        def _(r):
            total = 0.0
            for j in range(count):
                total += dot_nt(left(j, c), W[first_k + j, r].reshape(256, 512))
            MO[:, rows_at(r, 256)] = total

    for ch in range(2):
        twin_copy(4 + ch, SND.at[ch], RCV.at[ch]).wait_send()
    data_back(4, 4, lambda j, lat: GD[lat, :, j * 512 : j * 512 + 512], 7)
    pl.semaphore_signal(cred_b, 1, device_id=nb_b, device_id_type=MESH)
    for dz in range(1, 4):
        pl.semaphore_signal(cred_z, 1, device_id=dev(c, chip_of((z + dz) % 4, y, x)), device_id_type=MESH)

    pl.semaphore_wait(cred_a, 1)
    for j in range(4):
        grad_tiles(
            4 + j,
            lambda r: MLI[:, :, rows_at(r, 256)].reshape(512, 256),
            GD[:, :, j * 512 : j * 512 + 512].reshape(512, 512),
        )
        s1(4 + j)
    s2(8)
    received(7)

    @pl.loop(0, TOK // 32)
    def _(i):
        r = rows_at(i, 32)
        d_in = both_parts(r)
        hat, inv = normed(RSD[r, :])
        DACC[3] += fold(d_in)
        DACC[4] += fold(d_in * hat)
        d_x = normed_back(d_in * (1.0 + mod_row(4)), hat, inv) + X1[r, :]
        X1[r, :] = d_x
        DACC[2] += fold(d_x * AO[r, :])
        DAO[c, r, :] = (d_x * mod_row(2)).astype(BF)

    dao_other = pl.ds(pl.multiple_of(o * 512, 512), 512)
    dao_mine = pl.ds(pl.multiple_of(c * 512, 512), 512)
    twin_copy(9, DAO.at[c, :, dao_other], DAO.at[c, :, dao_other]).start()

    def mixed_back(hh, n):
        w_mine = W[3, 2 * hh + n].reshape(256, 512)
        w_other = WP[2 * hh + n].reshape(256, 512)
        return (dot_nt(DAO[c, :, dao_mine], w_mine) + dot_nt(DAO[c, :, dao_other], w_other)).astype(BF)

    @pl.loop(0, 2)
    def _(n):
        DMS[:, rows_at(n, 256)] = mixed_back(o, n)

    twin_copy(10, DMS, DMX.at[c]).start()

    @pl.loop(0, 2)
    def _(n):
        DMX[c, :, rows_at(n, 256)] = mixed_back(c, n)

    s2(9)
    s3(8)
    twin_copy(9, DAO.at[o, :, dao_mine], DAO.at[o, :, dao_mine]).wait_recv()

    @pl.loop(0, 4)
    def _(r):
        left = MIX[r // 2, :, :, rows_at(r % 2, 256)].reshape(512, 256)
        G[3, r] = dot_tn(left, DAO[:, :, dao_mine].reshape(512, 512)).astype(BF).reshape(2, 2, 64, 512)

    s1(3)
    twin_copy(10, DMS, DMX.at[o]).wait_recv()

    @pl.loop(0, 8)
    def _(t):
        lat, cols = t // 4, rows_at(t % 4, 128)
        q, k, v = QKV[0, lat, :, cols], QKV[1, lat, :, cols], QKV[2, lat, :, cols]
        dm = DMX[lat, :, cols]
        res = []
        for m in masks:
            probs = probs_of(q * m, k)
            d_probs = dot_nt(dm * m, v)
            d_v = dot_tn(probs.astype(BF), dm)
            d_s = probs * (d_probs - jnp.sum(d_probs * probs, axis=-1, keepdims=True))
            d_s = (d_s * 0.125).astype(BF)
            res.append((dot_nn(d_s, k), dot_tn(d_s, q), d_v))
        for j in range(3):
            QKV[j, lat, :, cols] = jnp.where(first, res[0][j], res[1][j]).astype(BF)

    for j in range(3):
        grad_tiles(
            j,
            lambda r: ATI[:, :, rows_at(r, 256)].reshape(512, 256),
            QKV[j].reshape(512, 512),
        )
        s1(j)
    s2(10)
    s3(9)
    for ch in range(2):
        twin_copy(7 + ch, SND.at[ch], RCV.at[ch]).wait_send()
    data_back(0, 3, lambda j, lat: QKV[j, lat], 11)
    s2(11)
    s3(10)
    received(11)

    @pl.loop(0, TOK // 32)
    def _(i):
        r = rows_at(i, 32)
        d_in = both_parts(r)
        hat, inv = normed(X0[r, :])
        DACC[0] += fold(d_in)
        DACC[1] += fold(d_in * hat)
        d_x = normed_back(d_in * (1.0 + mod_row(1)), hat, inv) + X1[r, :]
        GLP[0:16, :] += dot_tn(pt[0, r, :].astype(BF), d_x.astype(BF))

    for k in range(8):
        MODS[k : k + 1, :] = jnp.sum(DACC[k], axis=0, keepdims=True)
    d_mods = MODS[...]
    DMB[c, s] = jnp.concatenate([d_mods[:, :512], d_mods[:, 512:]], axis=0).astype(BF)
    peers_send(3, lambda p: DMB.at[c, s], DMB.at[c])
    for q in range(8):
        B3S[q] = GLP[:, q * 128 : q * 128 + 128]
    B3R[s] = B3S[s // 2]
    peers_send(4, lambda p: B3S.at[p // 2], B3R)
    pl.semaphore_wait(cred_b, 1)
    pl.semaphore_wait(cred_z, 3)
    s3(11)
    s2(4)
    s4(8)
    peers_wait(3, lambda p: DMB.at[c, s], DMB.at[c])
    twin_copy(13, DMB.at[c], DMB.at[c]).start()

    def unpack(g):
        @pl.loop(0, 16)
        def _(l):
            both = DMB[g, l].astype(F32)
            DMF[g, :, l, 0:512] = both[0:8]
            DMF[g, :, l, 512:1024] = both[8:16]

    unpack(c)
    d_cond_low = 0.0
    for k in range(8):
        w_k = WMOD[:, k * 1024 : k * 1024 + 1024] if k < 6 else EX[:, (k - 5) * 1024 : (k - 4) * 1024]
        d_cond_low += dot_nt(DMF[c, k].astype(BF), w_k.astype(BF))
    d_cond = d_cond_low * silu_slope(CND[1])
    CP[c, 2, :, 0:64] = d_cond
    d_temb = d_cond.astype(BF).astype(F32)
    B2S[...] = jnp.concatenate([d_temb, d_temb], axis=1)
    B2R[s] = B2S[...]
    peers_send(5, lambda p: B2S, B2R)
    s2(5)
    s3(4)
    s4(9)
    peers_wait(4, lambda p: B3S.at[p // 2], B3R)
    B3D[c] = jnp.sum(B3R[...], axis=0)
    twin_copy(14, B3D.at[c], B3D.at[c]).start()
    peers_wait(5, lambda p: B2S, B2R)
    for q in range(8):
        DTA[c, :, q * 128 : q * 128 + 128] = jnp.concatenate(
            [B2R[2 * q, :, 0:64], B2R[2 * q + 1, :, 0:64]], axis=1
        )
    d_tact = dot_nt(DTA[c].astype(BF), EX[:, 0:1024].astype(BF))
    CP[c, 3, :, 0:64] = (d_tact * silu_slope(CND[0])).astype(BF).astype(F32)
    twin_copy(15, DTA.at[c], DTA.at[c]).start()
    twin_copy(16, CP.at[c], CP.at[c]).start()
    twin_copy(17, E1.at[c], E1.at[c]).start()
    s2(6)
    s3(5)
    s4(10)
    twin_copy(13, DMB.at[o], DMB.at[o]).wait_recv()
    unpack(o)
    twin_copy(14, B3D.at[o], B3D.at[o]).wait_recv()
    twin_copy(15, DTA.at[o], DTA.at[o]).wait_recv()
    twin_copy(16, CP.at[o], CP.at[o]).wait_recv()
    twin_copy(17, E1.at[o], E1.at[o]).wait_recv()

    def packed(i):
        return jnp.concatenate([CP[0, i, :, 0:64], CP[1, i, :, 0:64]], axis=0)

    def square_half(value):
        part = 0.5 * value * value
        return jnp.sum(jnp.sum(part, axis=0, keepdims=True), axis=1, keepdims=True)

    cond_both = packed(0).astype(BF)
    small = jnp.zeros((1, 1), F32)
    for k in range(8):
        grad = dot_tn(cond_both, jnp.concatenate([DMF[0, k], DMF[1, k]], axis=0).astype(BF))
        small += square_half(grad)
        if k < 6:
            WMOD[:, k * 1024 : k * 1024 + 1024] = grad
        else:
            EX[:, (k - 5) * 1024 : (k - 4) * 1024] = grad
    mod_out = pltpu.make_async_copy(WMOD, g_in.at[:, pl.ds(0, 6144)], st_sem.at[26])
    mod_out.start()
    s2(7)
    s3(6)
    s4(11)
    grad = dot_tn(packed(1).astype(BF), jnp.concatenate([DTA[0], DTA[1]], axis=0).astype(BF))
    small += square_half(grad)
    EX[:, 0:1024] = grad
    sums = B3D[0] + B3D[1]
    sums = jnp.where(x == 0, sums[:, 0:64], sums[:, 64:128])
    small += square_half(sums)
    ENT[0:16, :] = sums[0:16]
    wide = jnp.concatenate(
        [jnp.concatenate([sums[16:32], jnp.zeros((16, 64), F32)], axis=1), jnp.zeros((112, 128), F32)], axis=0
    )
    EX[:, 3072:3088] = wide.T[0:64, 0:16]
    labels = jnp.sum(E1[0, :, 3, :] + E1[1, :, 3, :], axis=0, keepdims=True).astype(jnp.int32)
    d_cond_both = jnp.concatenate([packed(2), jnp.zeros((96, 64), F32)], axis=0)
    for i in range(5):
        rows = lax.broadcasted_iota(jnp.int32, (200, LANES), 0) + i * 200
        hot = (rows == labels).astype(F32)
        grad = lax.dot_general(
            hot, d_cond_both, (((1,), (0,)), ((), ())), preferred_element_type=F32, precision=highest
        )
        small += square_half(grad)
        ENT[16 + i * 200 : 216 + i * 200, :] = grad
    d_thidden = packed(3).astype(BF)
    for i in range(2):
        femb = jnp.concatenate([E1[0, :, i, :], E1[1, :, i, :]], axis=0).astype(BF)
        grad = dot_tn(femb, d_thidden)
        small += square_half(grad)
        ENT[1016 + i * 128 : 1144 + i * 128, :] = grad

    s2(3)
    s3(7)
    s4(4)
    s2(0)
    s3(3)
    s4(5)
    s2(1)
    s3(0)
    s4(6)
    s2(2)
    s3(1)
    s4(7)
    for half in range(2):
        for q in range(4):
            cols = slice(q * 128, q * 128 + 128)
            low, high = FIN[4 + half, :, cols], FIN[6 + half, :, cols]
            FIN[4 + half, :, cols] = jnp.concatenate([low[:, 0:64], high[:, 0:64]], axis=1)
            FIN[6 + half, :, cols] = jnp.concatenate([low[:, 64:128], high[:, 64:128]], axis=1)
    outs = []
    for ch in range(2):
        for rh in range(2):
            outs.append((
                FIN.at[8 + 2 * ch + rh],
                g_out.at[pl.ds(pl.multiple_of(c * 128 + rh * 64, 64), 64), pl.ds(ch * 512, 512)],
            ))
    for j in range(16):
        outs.append((
            FIN.at[4 + j // 8 + 2 * (j % 2), :, pl.ds(((j % 8) // 2) * 128, 128)],
            g_in.at[:, pl.ds(pl.multiple_of(10240 + 256 * j + c * 128, 128), 128)],
        ))
    for j in (3, 0, 1, 2):
        outs.append((FIN.at[j], g_in.at[:, pl.ds(pl.multiple_of(6144 + 1024 * j + c * 512, 512), 512)]))
    for i in range(20):
        to_outputs(i, *outs[i])
    s3(2)
    s4(3)
    to_outputs(20, *outs[20])
    s4(0)
    to_outputs(21, *outs[21])
    s4(1)
    to_outputs(22, *outs[22])
    s4(2)
    to_outputs(23, *outs[23])

    def total_of(value):
        return jnp.sum(jnp.sum(value, axis=0, keepdims=True), axis=1, keepdims=True)

    NSS[0:1, :] = jnp.broadcast_to(total_of(SQ[...]) + small, (1, 128))
    NSS[1:2, :] = jnp.broadcast_to(total_of(LOSS[...]) / (TOK * PDIM), (1, 128))
    NSS[2:8, :] = jnp.zeros((6, 128), F32)
    NSR[s] = NSS[...]
    peers_send(6, lambda p: NSS, NSR)
    peers_wait(6, lambda p: NSS, NSR)
    NSD[c] = jnp.sum(NSR[...], axis=0)
    twin_copy(18, NSD.at[c], NSD.at[c]).start()
    twin_copy(18, NSD.at[o], NSD.at[o]).wait_recv()
    stats[...] = NSD[0] + NSD[1]

    mod_out.wait()
    for i, (src, dst) in enumerate(outs):
        pltpu.make_async_copy(src, dst, f_l.at[i]).wait()
        remote(src, dst, f_s.at[i], f_r.at[i], twin).wait()
    for k in range(CHUNKS):
        for b in range(2):
            s1_copy(k, b).wait_send()
        s2_copy(k).wait_send()
        for dz in range(1, 4):
            s3_copy(k, dz).wait_send()
    twin_copy(0, ATI.at[c], ATI.at[c]).wait_send()
    twin_copy(1, MIX.at[c], MIX.at[c]).wait_send()
    twin_copy(2, W.at[3], WP).wait_send()
    twin_copy(3, MLI.at[c], MLI.at[c]).wait_send()
    twin_copy(6, DMO.at[c], DMO.at[c]).wait_send()
    twin_copy(9, DAO.at[c, :, dao_other], DAO.at[c, :, dao_other]).wait_send()
    twin_copy(10, DMS, DMX.at[c]).wait_send()
    for ch in range(2):
        twin_copy(11 + ch, SND.at[ch], RCV.at[ch]).wait_send()
    twin_copy(13, DMB.at[c], DMB.at[c]).wait_send()
    twin_copy(14, B3D.at[c], B3D.at[c]).wait_send()
    twin_copy(15, DTA.at[c], DTA.at[c]).wait_send()
    twin_copy(16, CP.at[c], CP.at[c]).wait_send()
    twin_copy(17, E1.at[c], E1.at[c]).wait_send()
    twin_copy(18, NSD.at[c], NSD.at[c]).wait_send()


def fused_step(msg, pt, pos, block_in, block_out, entry, exit_):
    vm = pltpu.VMEM
    dma = pltpu.SemaphoreType.DMA
    scratch = [
        vm((12, 4, 2, 2, 64, 512), BF), vm((4, 2, 2, 64, 512), BF), vm((12, 4, 2, 2, 64, 512), BF),
        vm((4, 2, 4, 64, 512), BF), vm((4, 4, 64, 512), BF), vm((4, 4, 64, 512), BF), vm((12, 64, 512), F32),
        vm((2, TOK, 1024), BF), vm((3, 2, TOK, 512), BF), vm((2, 2, TOK, 512), BF), vm((2, TOK, 1024), BF),
        vm((2, TOK, 2048), BF), vm((2, TOK, 2048), BF), vm((2, TOK, 1024), BF), vm((2, TOK, 1024), BF),
        vm((2, TOK, 512), BF), vm((TOK, 512), BF),
        *[vm((TOK, 1024), F32)] * 5, vm((2, TOK, 512), F32), vm((2, TOK, 512), F32),
        vm((64, 6144), F32), vm((2, 16, 24, 128), F32), vm((8, 16, 128), F32), vm((16, 16, 128), F32),
        vm((16, 8, 1024), F32), vm((16, 8, 1024), F32), vm((2, 16, 16, 512), BF), vm((2, 8, 16, 1024), F32),
        vm((16, 128), F32), vm((16, 16, 128), F32), vm((2, 16, 1024), F32), vm((2, 4, 16, 128), F32), vm((2, 16, 64), F32),
        vm((8, 32, 128), F32), vm((16, 32, 128), F32), vm((2, 32, 128), F32),
        vm((8, 128), F32), vm((16, 8, 128), F32), vm((2, 8, 128), F32),
        vm((8, 1024), F32), vm((8, 8, 1024), F32), vm((16, 1024), F32), vm((16, 1024), F32), vm((32, 1024), F32),
        vm((8, 512), F32), vm((8, 16), F32),
        dma((27,)), dma((7, 16)), dma((7, 16)), dma((36,)), dma((48,)), dma((12,)), dma((12,)), dma((24,)), dma((24,)),
        dma((24,)), dma((24,)), dma((12,)), dma((12,)), dma((36,)), dma((48,)), dma((19,)), dma((19,)),
        dma((24,)), dma((24,)), dma((24,)),
        pltpu.SemaphoreType.REGULAR, pltpu.SemaphoreType.REGULAR, pltpu.SemaphoreType.REGULAR,
    ]
    any_ = pl.BlockSpec(memory_space=pl.ANY)
    vmem = pl.BlockSpec(memory_space=pltpu.VMEM)
    shape = jax.ShapeDtypeStruct
    return pl.pallas_call(
        step_kernel,
        out_shape=(
            shape(block_in.shape, F32), shape(block_out.shape, F32), shape(entry.shape, F32),
            shape(exit_.shape, F32), shape((8, 128), F32),
        ),
        in_specs=[vmem, vmem, vmem, any_, any_, any_, any_],
        out_specs=(any_, any_, vmem, vmem, vmem),
        scratch_shapes=scratch,
        compiler_params=pltpu.CompilerParams(
            collective_id=0, has_side_effects=True, vmem_limit_bytes=62 * 2**20
        ),
        cost_estimate=pl.CostEstimate(flops=21 * 10**9, bytes_accessed=20 * 10**6, transcendentals=4 * 10**6),
    )(msg, pt, pos, block_in, block_out, entry, exit_)


def local_fused(
    noisy, timesteps, labels, noise,
    block_in, block_in_first, block_in_second,
    block_out, block_out_first, block_out_second,
    entry_table, entry_first, entry_second,
    exit_proj, exit_first, exit_second,
):
    index = lax.axis_index("rep") * 16 + lax.axis_index("shard")
    femb = lowered(time_features(timesteps, FREQ)).astype(F32).reshape(2, LANES)
    label = labels.astype(F32)[0]
    lane = jnp.arange(LANES)[None, :]
    head = jnp.concatenate(
        [femb, jnp.full((1, LANES), label), jnp.where(lane == index, label, 0.0), jnp.zeros((4, LANES), F32)], axis=0
    )
    edge = jnp.concatenate([entry_table[:PDIM], exit_proj[:, 3 * D :].T], axis=1)
    msg = jnp.concatenate([head, edge], axis=0)
    pt = patchify(jnp.concatenate([noisy, noise], axis=0), PATCH)
    grid = noisy.shape[-1] // PATCH
    pos = position_table(grid, D)[:grid, : D // 2]
    g_in, g_out, g_entry, g_exit, stats = fused_step(
        msg, pt, pos, block_in[0], block_out[0], entry_table, exit_proj
    )
    loss = stats[1, 0]
    grad_norm = jnp.sqrt(stats[0, 0])
    factor = clip_limit / jnp.maximum(grad_norm, clip_limit)
    outs = [loss, grad_norm]
    for weight, first, second, grad, rate in (
        (block_in, block_in_first, block_in_second, g_in[None], rate_main),
        (block_out, block_out_first, block_out_second, g_out[None], rate_main),
        (entry_table, entry_first, entry_second, g_entry, rate_edge),
        (exit_proj, exit_first, exit_second, g_exit, rate_main),
    ):
        outs.extend(adam_step(weight, first, second, grad, factor, rate))
    return tuple(outs)


def solution(mesh):
    step = local_fused if dict(mesh.shape) == {"rep": 2, "shard": 16} else local
    in_specs = (
        P(("rep", "shard"), None, None, None),
        P(("rep", "shard")),
        P(("rep", "shard")),
        P(("rep", "shard"), None, None, None),
        P(None, "shard", None),
        P(None, "shard", None),
        P(None, "shard", None),
        P(None, "shard", None),
        P(None, "shard", None),
        P(None, "shard", None),
        P(None, "shard"),
        P(None, "shard"),
        P(None, "shard"),
        P("shard", None),
        P("shard", None),
        P("shard", None),
    )
    out_specs = (
        P(),
        P(),
        P(None, "shard", None),
        P(None, "shard", None),
        P(None, "shard", None),
        P(None, "shard", None),
        P(None, "shard", None),
        P(None, "shard", None),
        P(None, "shard", None),
        P(None, "shard", None),
        P(None, "shard"),
        P(None, "shard"),
        P(None, "shard"),
        P(None, "shard"),
        P("shard", None),
        P("shard", None),
        P("shard", None),
        P("shard", None),
    )
    return jax.shard_map(step, mesh=mesh, in_specs=in_specs, out_specs=out_specs, check_vma=False)
```

```python
import jax
import jax.numpy as jnp
from jax import lax
from jax.experimental import pallas as pl
from jax.experimental.pallas import tpu as pltpu
from jax.sharding import PartitionSpec as P

D = 1024
HEADS = 16
PATCH = 2
NCLS = 1000
FREQ = 256
STEP = 10
PDIM = 16
ENTRIES = PDIM + NCLS + FREQ


clip_limit = 0.5
rate_main = 0.02
rate_edge = 0.1
decay_rate = 0.01
adam_eps = 1e-08
highest = lax.Precision.HIGHEST


def lowered(value):
    return value.astype(jnp.bfloat16)


def product(left, right):
    return jnp.dot(left, right, preferred_element_type=jnp.float32)


def product_tn(left, right):
    return lax.dot_general(
        left, right, (((0,), (0,)), ((), ())), preferred_element_type=jnp.float32
    )


def product_nt(left, right):
    return lax.dot_general(
        left, right, (((1,), (1,)), ((), ())), preferred_element_type=jnp.float32
    )


def patchify(image, patch):
    batch, chans, height, width = image.shape
    grid = height // patch
    parts = image.reshape(batch, chans, grid, patch, grid, patch)
    parts = parts.transpose(0, 2, 4, 3, 5, 1)
    return parts.reshape(batch, grid * grid, patch * patch * chans)


def position_table(grid, width):
    quarter = width // 4
    omega = 1.0 / 10000.0 ** (jnp.arange(quarter, dtype=jnp.float32) / quarter)
    index = jnp.arange(grid * grid)
    row_pos = (index // grid).astype(jnp.float32)[:, None] * omega[None, :]
    col_pos = (index % grid).astype(jnp.float32)[:, None] * omega[None, :]
    return jnp.concatenate(
        [jnp.sin(col_pos), jnp.cos(col_pos), jnp.sin(row_pos), jnp.cos(row_pos)], axis=1
    )


def time_features(steps, size):
    half = size // 2
    freqs = jnp.exp(-jnp.log(10000.0) * jnp.arange(half, dtype=jnp.float32) / half)
    angles = steps.astype(jnp.float32)[:, None] * freqs[None, :]
    return jnp.concatenate([jnp.cos(angles), jnp.sin(angles)], axis=1)


def modulate(x, shift, scale):
    centered = x - jnp.mean(x, axis=-1, keepdims=True)
    var = jnp.mean(centered * centered, axis=-1, keepdims=True)
    normed = centered * lax.rsqrt(var + 1e-06)
    return normed * (1.0 + scale[:, None, :]) + shift[:, None, :]


def gelu_tanh(value):
    return jax.nn.gelu(value, approximate=True)


def adam_step(weight, first, second, grad, factor, rate):
    clipped = grad * factor
    first_new = 0.5 * first + 0.5 * clipped
    second_new = 0.5 * second + 0.5 * clipped * clipped
    corr = 1.0 - 0.5**STEP
    update = first_new / corr / (jnp.sqrt(second_new / corr) + adam_eps) + decay_rate * weight
    weight_new = weight - rate * update
    return (weight_new, first_new, second_new, weight_new.astype(jnp.bfloat16))


def layer_parts(x, cond_low, w_in, w_out):
    width = x.shape[-1]
    batch, seq = (x.shape[0], x.shape[1])
    size = width // HEADS
    mod = product(cond_low, w_in[:, : 6 * width])
    shift_a, scale_a, gate_a, shift_b, scale_b, gate_b = jnp.split(mod, 6, axis=-1)
    attn_in = lowered(modulate(x, shift_a, scale_a))
    qkv = lowered(
        jnp.einsum(
            "bsd,de->bse",
            attn_in,
            w_in[:, 6 * width : 9 * width],
            preferred_element_type=jnp.float32,
        )
    )
    query = qkv[..., :width].reshape(batch, seq, HEADS, size)
    keys = qkv[..., width : 2 * width].reshape(batch, seq, HEADS, size)
    values = qkv[..., 2 * width :].reshape(batch, seq, HEADS, size)
    scores = jnp.einsum(
        "bqhd,bkhd->bhqk", query, keys, preferred_element_type=jnp.float32
    ) * size ** (-0.5)
    weights = jax.nn.softmax(scores, axis=-1)
    weights_low = lowered(weights)
    mixed = lowered(
        jnp.einsum("bhqk,bkhd->bqhd", weights_low, values, preferred_element_type=jnp.float32)
    ).reshape(batch, seq, width)
    attn_out = jnp.einsum(
        "bsd,de->bse", mixed, w_in[:, 9 * width : 10 * width], preferred_element_type=jnp.float32
    )
    resid = x + gate_a[:, None, :] * attn_out
    mlp_in = lowered(modulate(resid, shift_b, scale_b))
    hidden = jnp.einsum(
        "bsd,df->bsf", mlp_in, w_in[:, 10 * width :], preferred_element_type=jnp.float32
    )
    active = lowered(gelu_tanh(hidden))
    mlp_out = jnp.einsum("bsf,fd->bsd", active, w_out, preferred_element_type=jnp.float32)
    result = resid + gate_b[:, None, :] * mlp_out
    return dict(
        mods=(shift_a, scale_a, gate_a, shift_b, scale_b, gate_b),
        attn_in=attn_in,
        query=query,
        keys=keys,
        values=values,
        weights=weights,
        weights_low=weights_low,
        mixed=mixed,
        attn_out=attn_out,
        resid=resid,
        mlp_in=mlp_in,
        hidden=hidden,
        active=active,
        mlp_out=mlp_out,
        result=result,
    )


def layer_back(x, cond_low, w_in, w_out, parts, grad_out, grad_cond):
    width = x.shape[-1]
    batch, seq = (x.shape[0], x.shape[1])
    size = width // HEADS
    shift_a, scale_a, gate_a, shift_b, scale_b, gate_b = parts["mods"]
    d_gate_b = jnp.sum(grad_out * parts["mlp_out"], axis=1)
    d_mlp_out = lowered(grad_out * gate_b[:, None, :])
    g_fc2 = jnp.einsum(
        "bsf,bsd->fd", parts["active"], d_mlp_out, preferred_element_type=jnp.float32
    )
    d_active = jnp.einsum("bsd,fd->bsf", d_mlp_out, w_out, preferred_element_type=jnp.float32)
    _, gelu_pull = jax.vjp(gelu_tanh, parts["hidden"])
    d_hidden = lowered(gelu_pull(d_active)[0])
    g_fc1 = jnp.einsum("bsd,bsf->df", parts["mlp_in"], d_hidden, preferred_element_type=jnp.float32)
    d_mlp_in = jnp.einsum(
        "bsf,df->bsd", d_hidden, w_in[:, 10 * width :], preferred_element_type=jnp.float32
    )
    _, norm_pull = jax.vjp(modulate, parts["resid"], shift_b, scale_b)
    d_resid, d_shift_b, d_scale_b = norm_pull(d_mlp_in)
    d_resid = d_resid + grad_out
    d_gate_a = jnp.sum(d_resid * parts["attn_out"], axis=1)
    d_attn_out = lowered(d_resid * gate_a[:, None, :])
    g_proj = jnp.einsum(
        "bsd,bse->de", parts["mixed"], d_attn_out, preferred_element_type=jnp.float32
    )
    d_mixed = lowered(
        jnp.einsum(
            "bse,de->bsd",
            d_attn_out,
            w_in[:, 9 * width : 10 * width],
            preferred_element_type=jnp.float32,
        )
    ).reshape(batch, seq, HEADS, size)
    d_probs = jnp.einsum(
        "bqhd,bkhd->bhqk", d_mixed, parts["values"], preferred_element_type=jnp.float32
    )
    d_values = jnp.einsum(
        "bhqk,bqhd->bkhd", parts["weights_low"], d_mixed, preferred_element_type=jnp.float32
    )
    weights = parts["weights"]
    d_scores = weights * (d_probs - jnp.sum(d_probs * weights, axis=-1, keepdims=True))
    d_scaled = lowered(d_scores * size ** (-0.5))
    d_query = jnp.einsum(
        "bhqk,bkhd->bqhd", d_scaled, parts["keys"], preferred_element_type=jnp.float32
    )
    d_keys = jnp.einsum(
        "bhqk,bqhd->bkhd", d_scaled, parts["query"], preferred_element_type=jnp.float32
    )
    d_qkv = lowered(
        jnp.concatenate(
            [
                d_query.reshape(batch, seq, width),
                d_keys.reshape(batch, seq, width),
                d_values.reshape(batch, seq, width),
            ],
            axis=-1,
        )
    )
    g_qkv = jnp.einsum("bsd,bse->de", parts["attn_in"], d_qkv, preferred_element_type=jnp.float32)
    d_attn_in = jnp.einsum(
        "bse,de->bsd", d_qkv, w_in[:, 6 * width : 9 * width], preferred_element_type=jnp.float32
    )
    _, first_pull = jax.vjp(modulate, x, shift_a, scale_a)
    d_x, d_shift_a, d_scale_a = first_pull(d_attn_in)
    d_x = d_x + d_resid
    d_mod = lowered(
        jnp.concatenate([d_shift_a, d_scale_a, d_gate_a, d_shift_b, d_scale_b, d_gate_b], axis=-1)
    )
    g_mod = product_tn(cond_low, d_mod)
    grad_cond = grad_cond + product_nt(d_mod, w_in[:, : 6 * width])
    g_in = jnp.concatenate([g_mod, g_qkv, g_proj, g_fc1], axis=1)
    return (d_x, grad_cond, g_in, g_fc2)


def local(
    noisy,
    timesteps,
    labels,
    noise,
    block_in,
    block_in_first,
    block_in_second,
    block_out,
    block_out_first,
    block_out_second,
    entry_table,
    entry_first,
    entry_second,
    exit_proj,
    exit_first,
    exit_second,
):
    layers = block_in.shape[0]
    entry_all, exit_all = (
        lax.all_gather(lowered(entry_table), "shard", axis=1, tiled=True),
        lax.all_gather(lowered(exit_proj), "shard", axis=0, tiled=True),
    )
    w_patch = entry_all[:PDIM]
    w_label = entry_all[PDIM : PDIM + NCLS]
    w_time = entry_all[PDIM + NCLS :]
    w_time2 = exit_all[:, :D]
    w_final = exit_all[:, D : 3 * D]
    w_output = exit_all[:, 3 * D :]
    patches = lowered(patchify(noisy, PATCH))
    target = patchify(noise, PATCH)
    seq = patches.shape[1]
    x = (
        jnp.einsum("bsp,pd->bsd", patches, w_patch, preferred_element_type=jnp.float32)
        + position_table(noisy.shape[-1] // PATCH, D)[None]
    )
    femb = lowered(time_features(timesteps, FREQ))
    t_hidden = product(femb, w_time)
    t_act = lowered(jax.nn.silu(t_hidden))
    temb = product(t_act, w_time2)
    onehot = (labels[:, None] == jnp.arange(NCLS)[None, :]).astype(jnp.float32)
    cond = temb + jnp.dot(onehot, w_label.astype(jnp.float32), precision=highest)
    cond_low = lowered(jax.nn.silu(cond))
    layer = 0
    w_in_all = lax.all_gather(lowered(block_in[layer]), "shard", axis=0, tiled=True)
    w_out_all = lax.all_gather(lowered(block_out[layer]), "shard", axis=0, tiled=True)
    inputs = [x]
    parts = layer_parts(x, cond_low, w_in_all, w_out_all)
    saved = [parts]
    x = parts["result"]
    final_mod = product(cond_low, w_final)
    shift_f, scale_f = jnp.split(final_mod, 2, axis=-1)
    final_in = lowered(modulate(x, shift_f, scale_f))
    pred = jnp.einsum("bsd,dp->bsp", final_in, w_output, preferred_element_type=jnp.float32)
    error = pred - target
    loss_part = jnp.sum(error * error) / (seq * PDIM)
    d_pred = lowered(2.0 * error / (seq * PDIM))
    g_output = jnp.einsum("bsd,bsp->dp", final_in, d_pred, preferred_element_type=jnp.float32)
    d_final_in = jnp.einsum("bsp,dp->bsd", d_pred, w_output, preferred_element_type=jnp.float32)
    _, final_pull = jax.vjp(modulate, x, shift_f, scale_f)
    d_x, d_shift_f, d_scale_f = final_pull(d_final_in)
    d_fmod = lowered(jnp.concatenate([d_shift_f, d_scale_f], axis=-1))
    g_final = product_tn(cond_low, d_fmod)
    grad_cond = product_nt(d_fmod, w_final)
    shards_in = [None] * layers
    shards_out = [None] * layers
    for layer in reversed(range(layers)):
        w_in_all, w_out_all = (
            lax.all_gather(lowered(block_in[layer]), "shard", axis=0, tiled=True),
            lax.all_gather(lowered(block_out[layer]), "shard", axis=0, tiled=True),
        )
        d_x, grad_cond, g_in, g_fc2 = layer_back(
            inputs[layer], cond_low, w_in_all, w_out_all, saved[layer], d_x, grad_cond
        )
        shards_in[layer], shards_out[layer] = (
            lax.psum_scatter(g_in, "shard", scatter_dimension=0, tiled=True),
            lax.psum_scatter(g_fc2, "shard", scatter_dimension=0, tiled=True),
        )
    _, silu_pull = jax.vjp(jax.nn.silu, cond)
    d_cond = silu_pull(grad_cond)[0]
    g_label = jnp.dot(onehot.T, d_cond, precision=highest)
    d_temb = lowered(d_cond)
    g_time2 = product_tn(t_act, d_temb)
    d_tact = product_nt(d_temb, w_time2)
    _, time_pull = jax.vjp(jax.nn.silu, t_hidden)
    d_thidden = lowered(time_pull(d_tact)[0])
    g_time = product_tn(femb, d_thidden)
    g_patch = jnp.einsum("bsp,bsd->pd", patches, lowered(d_x), preferred_element_type=jnp.float32)
    g_entry = jnp.concatenate([g_patch, g_label, g_time], axis=0)
    g_exit = jnp.concatenate([g_time2, g_final, g_output], axis=1)
    share_entry, share_exit = (
        lax.psum_scatter(g_entry, "shard", scatter_dimension=1, tiled=True),
        lax.psum_scatter(g_exit, "shard", scatter_dimension=0, tiled=True),
    )
    grads = (
        lax.psum(jnp.stack(shards_in).astype(jnp.bfloat16), "rep").astype(jnp.float32),
        lax.psum(jnp.stack(shards_out).astype(jnp.bfloat16), "rep").astype(jnp.float32),
        lax.psum(share_entry.astype(jnp.bfloat16), "rep").astype(jnp.float32),
        lax.psum(share_exit.astype(jnp.bfloat16), "rep").astype(jnp.float32),
    )
    squares = (
        jnp.sum(grads[0] * grads[0])
        + jnp.sum(grads[1] * grads[1])
        + jnp.sum(grads[2] * grads[2])
        + jnp.sum(grads[3] * grads[3])
    )
    loss = lax.psum(loss_part, ("rep", "shard"))
    norm_sq = lax.psum(squares, "shard")
    grad_norm = jnp.sqrt(norm_sq)
    factor = clip_limit / jnp.maximum(grad_norm, clip_limit)
    bi_w, bi_m, bi_v, bi_l = adam_step(
        block_in, block_in_first, block_in_second, grads[0], factor, rate_main
    )
    bo_w, bo_m, bo_v, bo_l = adam_step(
        block_out, block_out_first, block_out_second, grads[1], factor, rate_main
    )
    en_w, en_m, en_v, en_l = adam_step(
        entry_table, entry_first, entry_second, grads[2], factor, rate_edge
    )
    ex_w, ex_m, ex_v, ex_l = adam_step(
        exit_proj, exit_first, exit_second, grads[3], factor, rate_main
    )
    return (
        loss,
        grad_norm,
        bi_w,
        bi_m,
        bi_v,
        bi_l,
        bo_w,
        bo_m,
        bo_v,
        bo_l,
        en_w,
        en_m,
        en_v,
        en_l,
        ex_w,
        ex_m,
        ex_v,
        ex_l,
    )


BF = jnp.bfloat16
F32 = jnp.float32
MESH = pl.DeviceIdType.MESH
TOK = 256
LANES = 128
CHUNKS = 12
AHEAD = 2
VIA_Z = ()
LEAD = 3
LAG3 = 1
LAG4 = 2
LAG_A = 1
ORDER = (8, 9, 10, 11, 4, 5, 6, 7, 3, 0, 1, 2)


def dot_nn(left, right):
    return lax.dot_general(left, right, (((1,), (0,)), ((), ())), preferred_element_type=F32)


def dot_nt(left, right):
    return lax.dot_general(left, right, (((1,), (1,)), ((), ())), preferred_element_type=F32)


def dot_tn(left, right):
    return lax.dot_general(left, right, (((0,), (0,)), ((), ())), preferred_element_type=F32)


def dot_tn_exact(left, right):
    return lax.dot_general(
        left, right, (((0,), (0,)), ((), ())), preferred_element_type=F32, precision=highest
    )


def sigmoid(value):
    return 1.0 / (1.0 + jnp.exp(-value))


def silu_slope(value):
    gate = sigmoid(value)
    return gate * (1.0 + value * (1.0 - gate))


def normed(x):
    centered = x - jnp.mean(x, axis=-1, keepdims=True)
    var = jnp.mean(centered * centered, axis=-1, keepdims=True)
    inv = lax.rsqrt(var + 1e-06)
    return centered * inv, inv


def normed_back(d_normed, x_normed, inv):
    mean_d = jnp.mean(d_normed, axis=-1, keepdims=True)
    mean_dx = jnp.mean(d_normed * x_normed, axis=-1, keepdims=True)
    return inv * (d_normed - mean_d - x_normed * mean_dx)


def fold(value):
    rows, cols = value.shape
    return jnp.sum(value.reshape(rows // 8, 8, cols), axis=0)


def rows_at(i, size):
    return pl.ds(pl.multiple_of(i * size, size), size)


def step_kernel(
    msg, pt, pos, bi, bo, ent_in, ex_in,
    g_in, g_out, ENT, EX, stats,
    W, WP, G, R1, R2, R3, FIN,
    ATI, QKV, MIX, MLI, ACT, GD, DMO, DAO, DMX, DMS,
    X0, AO, RSD, MO, X1, SND, RCV,
    WMOD, E1, EDG, E2S, E2R, E3S, E3R, DMB, DMF, B2S, B2R, DTA, CP, CND,
    B3S, B3R, B3D, NSS, NSR, NSD, MODS, DACC, WPT, WLT, GLP, SQ, LOSS,
    st_sem, peer_s, peer_r, zs, zr, bs, br, as_, ar,
    s1s, s1r, s2s, s2r, s3s, s3r, d_s, d_r, f_l, f_s, f_r,
    cred_a, cred_b, cred_z,
):
    c = lax.axis_index("rep")
    s = lax.axis_index("shard")
    o = 1 - c
    x = s % 2
    y = (s // 2) % 2
    z = s // 4
    a_me = y * o + x * c
    b_me = x * o + y * c

    def yx(a, b):
        return a * o + b * c, b * o + a * c

    def dev(core, chip):
        return {"rep": core, "shard": chip}

    def chip_of(zz, yy, xx):
        return zz * 4 + yy * 2 + xx

    nb_a = dev(c, chip_of(z, *yx(1 - a_me, b_me)))
    nb_b = dev(c, chip_of(z, *yx(a_me, 1 - b_me)))
    twin = dev(o, s)

    def remote(src, dst, ss, rs, to):
        return pltpu.make_async_remote_copy(
            src_ref=src, dst_ref=dst, send_sem=ss, recv_sem=rs, device_id=to, device_id_type=MESH
        )

    pieces = []
    for j in range(4):
        pieces.append((bi.at[:, pl.ds(pl.multiple_of(6144 + 1024 * j + c * 512, 512), 512)], FIN.at[j]))
    for j in range(16):
        pieces.append((
            bi.at[:, pl.ds(pl.multiple_of(10240 + 256 * j + c * 128, 128), 128)],
            FIN.at[4 + j // 4, :, pl.ds((j % 4) * 128, 128)],
        ))
    for ch in range(2):
        for rh in range(2):
            pieces.append((
                bo.at[pl.ds(pl.multiple_of(c * 128 + rh * 64, 64), 64), pl.ds(ch * 512, 512)],
                FIN.at[8 + 2 * ch + rh],
            ))
    pieces.append((ent_in, ENT))
    pieces.append((ex_in, EX))
    pieces.append((bi.at[:, pl.ds(0, 6144)], WMOD))
    local = [pltpu.make_async_copy(p, q, st_sem.at[i]) for i, (p, q) in enumerate(pieces)]
    for i in (24, 25, 0, 1, 2, 3, *range(4, 24), 26):
        local[i].start()

    barrier = pltpu.get_barrier_semaphore()

    @pl.loop(1, 16)
    def _(k):
        pl.semaphore_signal(barrier, 1, device_id=dev(c, (s + k) % 16), device_id_type=MESH)

    pl.semaphore_signal(barrier, 1, device_id=twin, device_id_type=MESH)
    pl.semaphore_wait(barrier, 16)

    def peers_copy(e, k, src_of, dst):
        peer = (s + k) % 16
        return remote(src_of(peer), dst.at[s], peer_s.at[e, k], peer_r.at[e, s], dev(c, peer))

    def peers_send(e, src_of, dst):
        @pl.loop(1, 16)
        def _(k):
            peers_copy(e, k, src_of, dst).start()

    def peers_wait(e, src_of, dst):
        @pl.loop(1, 16)
        def _(k):
            frm = (s + k) % 16
            remote(src_of(frm), dst.at[frm], peer_s.at[e, k], peer_r.at[e, frm], dev(c, frm)).wait_recv()

        @pl.loop(1, 16)
        def _(k):
            peers_copy(e, k, src_of, dst).wait_send()

    def twin_copy(i, src, dst):
        return remote(src, dst, d_s.at[i], d_r.at[i], twin)

    def block(k, zz, far):
        yy, xx = yx(a_me, 1 - b_me if far else b_me)
        return W.at[k, zz, yy, xx]

    def z_copy(k, dz, far=0):
        at = block(k, z, far)
        i = k * 8 + far * 4
        return remote(at, at, zs.at[i + dz], zr.at[i + z], dev(c, chip_of((z + dz) % 4, y, x)))

    def z_wait(k, dz, far=0):
        frm = (z + dz) % 4
        at = block(k, frm, far)
        i = k * 8 + far * 4
        remote(at, at, zs.at[i + dz], zr.at[i + frm], dev(c, chip_of(frm, y, x))).wait_recv()

    def b_copy(k, zz):
        at = block(k, zz, 0)
        return remote(at, at, bs.at[k * 4 + zz], br.at[k * 4 + zz], nb_b)

    def a_copy(k, zz, far=0):
        at = block(k, zz, far)
        i = k * 8 + far * 4 + zz
        return remote(at, at, as_.at[i], ar.at[i], nb_a)

    def own(k):
        b_copy(k, z).start()
        a_copy(k, z).start()
        for dz in range(1, 4):
            z_copy(k, dz).start()

    def pump_b(k):
        if k in VIA_Z:
            b_copy(k, z).wait_recv()
            for dz in range(1, 4):
                z_copy(k, dz, 1).start()
            a_copy(k, z, 1).start()
        for dz in range(1, 4):
            frm = (z + dz) % 4
            z_wait(k, dz)
            if k not in VIA_Z:
                b_copy(k, frm).start()
            a_copy(k, frm).start()

    def pump_a(k):
        if k in VIA_Z:
            for dz in range(1, 4):
                z_wait(k, dz, 1)
                a_copy(k, (z + dz) % 4, 1).start()
        else:
            for dz in range(4):
                b_copy(k, (z + dz) % 4).wait_recv()
                a_copy(k, (z + dz) % 4, 1).start()

    def sends_done(k):
        for dz in range(1, 4):
            z_copy(k, dz).wait_send()
            if k in VIA_Z:
                z_copy(k, dz, 1).wait_send()
            else:
                b_copy(k, (z + dz) % 4).wait_send()
        b_copy(k, z).wait_send()
        for far in range(2):
            for zz in range(4):
                a_copy(k, zz, far).wait_send()

    def pump(k):
        if k + AHEAD < CHUNKS:
            cast(k + AHEAD)
            own(k + AHEAD)
        if k < CHUNKS:
            pump_b(k)
        if 0 <= k - LAG_A < CHUNKS:
            pump_a(k - LAG_A)

    def need(k):
        for far in range(2):
            for dz in range(4):
                a_copy(k, (z + dz) % 4, far).wait_recv()

    def cast(k):
        if k < 4:
            local[k].wait()
            W[k, z, y, x] = FIN[k].astype(BF)
        elif k < 8:
            if k == 4:
                for i in range(4, 20):
                    local[i].wait()
            rh, half = (k - 4) // 2, (k - 4) % 2
            for q in range(4):
                j = half * 8 + 2 * q
                pair = FIN[4 + j // 4, :, (j % 4) * 128 : (j % 4) * 128 + 256]
                piece = jnp.concatenate(
                    [pair[:, rh * 64 : rh * 64 + 64], pair[:, 128 + rh * 64 : 128 + rh * 64 + 64]], axis=1
                )
                W[k, z, y, x, :, q * 128 : q * 128 + 128] = piece.astype(BF)
        else:
            local[20 + k - 8].wait()
            W[k, z, y, x] = FIN[k].astype(BF)

    E1[c, s] = msg[0:8, :]
    peers_send(0, lambda p: msg.at[0:8, :], E1.at[c])
    for k in range(AHEAD):
        cast(k)
        own(k)

    local[24].wait()
    local[25].wait()
    peers_wait(0, lambda p: msg.at[0:8, :], E1.at[c])
    t_hidden = dot_nt(E1[c, :, 0, :].astype(BF), ENT[:, 1016:1144].astype(BF)) + dot_nt(
        E1[c, :, 1, :].astype(BF), ENT[:, 1144:1272].astype(BF)
    )
    CND[0] = t_hidden
    t_act = (t_hidden * sigmoid(t_hidden)).astype(BF)
    CP[c, 1, :, 0:64] = t_act.astype(F32)
    for q in range(8):
        E2S[q] = dot_nn(t_act, EX[:, q * 128 : q * 128 + 128].astype(BF))
    E2R[s] = E2S[s // 2]
    peers_send(1, lambda p: E2S.at[p // 2], E2R)
    pump(0)
    hot = (
        E1[c, :, 2, 0:1].astype(jnp.int32) + PDIM == lax.broadcasted_iota(jnp.int32, (16, ENTRIES), 1)
    ).astype(F32).astype(BF)
    w_class = dot_nt(hot, ENT[...].astype(BF))
    pump(1)
    local[26].wait()
    peers_wait(1, lambda p: E2S.at[p // 2], E2R)
    temb = jnp.sum(E2R[...], axis=0)
    cond = jnp.where(x == 0, temb[:, :64], temb[:, 64:]) + w_class
    CND[1] = cond
    cond_low = (cond * sigmoid(cond)).astype(BF)
    CP[c, 0, :, 0:64] = cond_low.astype(F32)
    for k in range(8):
        w_k = WMOD[:, k * 1024 : k * 1024 + 1024] if k < 6 else EX[:, (k - 5) * 1024 : (k - 4) * 1024]
        DMF[0, k] = dot_nn(cond_low, w_k.astype(BF))

    @pl.loop(0, 16)
    def _(l):
        part = DMF[0, :, l, :]
        E3S[l] = jnp.concatenate([part[:, :512], part[:, 512:]], axis=0).astype(BF)

    E3R[s] = E3S[s]
    peers_send(2, lambda p: E3S.at[p], E3R)
    EDG[s] = msg[8:24, :]
    peers_send(7, lambda p: msg.at[8:24, :], EDG)
    pump(2)

    peers_wait(7, lambda p: msg.at[8:24, :], EDG)
    for q in range(8):
        even, odd = EDG[2 * q], EDG[2 * q + 1]
        WPT[:, q * 128 : q * 128 + 128] = jnp.concatenate([even[:, :64], odd[:, :64]], axis=1)
        WLT[:, q * 128 : q * 128 + 128] = jnp.concatenate([even[:, 64:], odd[:, 64:]], axis=1)
    for n in range(4):
        cols = slice(n * 256, n * 256 + 256)
        X0[:, cols] = dot_nn(pt[0].astype(BF), WPT[:, cols].astype(BF))

    @pl.loop(0, 16)
    def _(i):
        X0[rows_at(i, 16), 0:512] += pos[...]
        X0[rows_at(i, 16), 512:1024] += jnp.broadcast_to(pos[pl.ds(i, 1), :], (16, 512))

    DACC[...] = jnp.zeros_like(DACC)
    pump(3)
    peers_wait(2, lambda p: E3S.at[p], E3R)
    parts = E3R[0].astype(F32)
    for i in range(1, 16):
        parts += E3R[i].astype(F32)
    MODS[...] = jnp.concatenate([parts[0:8], parts[8:16]], axis=1)

    def mod_row(k):
        return MODS[k : k + 1, :]

    def modulated(src, dst, shift, scale):
        @pl.loop(0, TOK // 32)
        def _(i):
            r = rows_at(i, 32)
            hat, _ = normed(src[r, :])
            dst[c, r, :] = (hat * (1.0 + mod_row(scale)) + mod_row(shift)).astype(BF)

    modulated(X0, ATI, 0, 1)
    twin_copy(0, ATI.at[c], ATI.at[c]).start()
    pump(4)
    twin_copy(0, ATI.at[o], ATI.at[o]).wait_recv()

    def w_cols(k, n):
        return W[k, :, :, :, :, rows_at(n, 256)].reshape(1024, 256)

    for j in range(3):
        need(j)

        @pl.loop(0, 4)
        def _(t):
            lat, n = t // 2, t % 2
            QKV[j, lat, :, rows_at(n, 256)] = dot_nn(ATI[lat], w_cols(j, n)).astype(BF)

        pump(5 + j)

    lane = lax.broadcasted_iota(jnp.int32, (1, LANES), 1)
    first = lane < 64
    masks = (first.astype(F32).astype(BF), 1.0 - first.astype(F32).astype(BF))

    def probs_of(q, k):
        score = dot_nt(q, k) * 0.125
        e = jnp.exp(score - jnp.max(score, axis=-1, keepdims=True))
        return e / jnp.sum(e, axis=-1, keepdims=True)

    @pl.loop(0, 8)
    def _(t):
        lat, cols = t // 4, rows_at(t % 4, 128)
        q, k, v = QKV[0, lat, :, cols], QKV[1, lat, :, cols], QKV[2, lat, :, cols]
        outs = [dot_nn(probs_of(q * m, k).astype(BF), v) for m in masks]
        MIX[c, lat, :, cols] = jnp.where(first, outs[0], outs[1]).astype(BF)

    twin_copy(1, MIX.at[c], MIX.at[c]).start()
    need(3)
    twin_copy(2, W.at[3], WP).start()
    pump(8)
    twin_copy(1, MIX.at[o], MIX.at[o]).wait_recv()
    twin_copy(2, W.at[3], WP).wait_recv()

    def proj(own):
        def cols(n):
            return pl.ds(pl.multiple_of((c if own else o) * 512 + n * 256, 256), 256)

        @pl.loop(0, 2)
        def _(n):
            ref = W.at[3] if own else WP
            total = 0.0
            for hh in range(2):
                w_half = ref[2 * hh : 2 * hh + 2, :, :, :, rows_at(n, 256)].reshape(512, 256)
                total += dot_nn(MIX[hh, c], w_half)
            AO[:, cols(n)] = total

    proj(True)
    proj(False)

    @pl.loop(0, TOK // 32)
    def _(i):
        r = rows_at(i, 32)
        RSD[r, :] = X0[r, :] + mod_row(2) * AO[r, :]

    modulated(RSD, MLI, 3, 4)
    twin_copy(3, MLI.at[c], MLI.at[c]).start()
    pump(9)
    twin_copy(3, MLI.at[o], MLI.at[o]).wait_recv()
    for j in range(4):
        need(4 + j)

        @pl.loop(0, 4)
        def _(t):
            lat, n = t // 2, t % 2
            hidden = dot_nn(MLI[lat], w_cols(4 + j, n))
            cols = pl.ds(pl.multiple_of(j * 512 + n * 256, 256), 256)
            square = hidden * hidden
            t_in = 0.7978845608028654 * hidden * (1.0 + 0.044715 * square)
            t_out = jnp.tanh(t_in)
            half = 0.5 * (1.0 + t_out)
            ACT[lat, :, cols] = (hidden * half).astype(BF)
            slope = half + 0.5 * hidden * (1.0 - t_out * t_out) * (
                0.7978845608028654 * (1.0 + 3.0 * 0.044715 * square)
            )
            GD[lat, :, cols] = slope.astype(BF)

        if j < 3:
            pump(10 + j)

    for ch in range(2):
        need(8 + 2 * ch)
        need(9 + 2 * ch)

        def mlp_tile(lat, n):
            total = 0.0
            for rh in range(2):
                total += dot_nn(ACT[lat, :, rh * 1024 : rh * 1024 + 1024], w_cols(8 + 2 * ch + rh, n))
            return total

        @pl.loop(0, 2)
        def _(n):
            SND[ch, :, rows_at(n, 256)] = mlp_tile(o, n)

        twin_copy(4 + ch, SND.at[ch], RCV.at[ch]).start()

        @pl.loop(0, 2)
        def _(n):
            MO[:, pl.ds(pl.multiple_of(ch * 512 + n * 256, 256), 256)] = mlp_tile(c, n)

    def received(i):
        for ch in range(2):
            twin_copy(i + ch, SND.at[ch], RCV.at[ch]).wait_recv()

    def both_parts(r):
        return MO[r, :] + jnp.concatenate([RCV[0, r, :], RCV[1, r, :]], axis=1)

    received(4)
    LOSS[...] = jnp.zeros_like(LOSS)
    GLP[...] = jnp.zeros_like(GLP)

    @pl.loop(0, TOK // 32)
    def _(i):
        r = rows_at(i, 32)
        mlp_out = both_parts(r)
        x1 = RSD[r, :] + mod_row(5) * mlp_out
        hat, inv = normed(x1)
        scale = 1.0 + mod_row(7)
        final_in = (hat * scale + mod_row(6)).astype(BF)
        w_lin = WLT[...].astype(BF)
        error = dot_nt(final_in, w_lin) - pt[1, r, :]
        LOSS[...] += fold(error * error)
        d_pred = (2.0 * error / (TOK * PDIM)).astype(BF)
        GLP[16:32, :] += dot_tn(d_pred, final_in)
        d_final = dot_nn(d_pred, w_lin)
        DACC[6] += fold(d_final)
        DACC[7] += fold(d_final * hat)
        d_x = normed_back(d_final * scale, hat, inv)
        X1[r, :] = d_x
        DACC[5] += fold(d_x * mlp_out)
        DMO[c, r, :] = (d_x * mod_row(5)).astype(BF)

    twin_copy(6, DMO.at[c], DMO.at[c]).start()

    def r1_of(k, b):
        return R1.at[k - 8, b] if k >= 8 else W.at[8 + k // 2, :, k % 2, b]

    def r2_of(k):
        return R2.at[k - 8] if k >= 8 else W.at[4 + k // 4, :, (k // 2) % 2, k % 2]

    def r3_of(k):
        return R3.at[k - 8] if k >= 8 else W.at[6 + k // 4, :, (k // 2) % 2, k % 2]

    def s1_copy(k, b):
        yy, xx = yx(1 - a_me, b)
        return remote(G.at[k, :, yy, xx], r1_of(k, b), s1s.at[k * 2 + b], s1r.at[k * 2 + b], nb_a)

    def s2_copy(k):
        yy, xx = yx(a_me, 1 - b_me)
        return remote(G.at[k, :, yy, xx], r2_of(k), s2s.at[k], s2r.at[k], nb_b)

    def s2_single(k):
        yy, xx = yx(a_me, 1 - b_me)
        return remote(G.at[k, z, yy, xx], r2_of(k).at[z], s2s.at[k], s2r.at[k], nb_b)

    def s3_copy(k, dz, far=0):
        zt = (z + dz) % 4
        yy, xx = yx(a_me, 1 - b_me if far else b_me)
        dst = (r2_of(k) if far else r3_of(k)).at[z]
        i = k * 8 + far * 4
        return remote(G.at[k, zt, yy, xx], dst, s3s.at[i + dz], s3r.at[i + z], dev(c, chip_of(zt, y, x)))

    def s3_wait(k, dz, far=0):
        frm = (z + dz) % 4
        dst = (r2_of(k) if far else r3_of(k)).at[frm]
        i = k * 8 + far * 4
        remote(G.at[k, frm, y, x], dst, s3s.at[i + dz], s3r.at[i + frm], dev(c, chip_of(frm, y, x))).wait_recv()

    def s1(k):
        for b in range(2):
            s1_copy(k, b).start()

    def sum_a(k, zz, far):
        b = 1 - b_me if far else b_me
        yy, xx = yx(a_me, b)
        return G[k, zz, yy, xx].astype(F32) + r1_of(k, b)[zz].astype(F32)

    def store(k, zz, far, value):
        yy, xx = yx(a_me, 1 - b_me if far else b_me)
        G[k, zz, yy, xx] = value.astype(BF)

    def s2(k):
        for b in range(2):
            s1_copy(k, b).wait_recv()
        if k in VIA_Z:
            for dz in range(1, 4):
                for far in range(2):
                    store(k, (z + dz) % 4, far, sum_a(k, (z + dz) % 4, far))
                    s3_copy(k, dz, far).start()
        else:
            @pl.loop(0, 4)
            def _(zz):
                store(k, zz, 1, sum_a(k, zz, 1))

            s2_copy(k).start()

    def s3(k):
        if k in VIA_Z:
            for far in (1, 0):
                total = sum_a(k, z, far)
                for dz in range(1, 4):
                    s3_wait(k, dz, far)
                    total += (r2_of(k) if far else r3_of(k))[(z + dz) % 4].astype(F32)
                if far:
                    store(k, z, 1, total)
                    s2_single(k).start()
                else:
                    FIN[k] = total
        else:
            s2_copy(k).wait_recv()
            for dz in range(1, 4):
                zt = (z + dz) % 4
                store(k, zt, 0, sum_a(k, zt, 0) + r2_of(k)[zt].astype(F32))
                s3_copy(k, dz).start()
            FIN[k] = sum_a(k, z, 0) + r2_of(k)[z].astype(F32)

    def s4(k):
        total = FIN[k]
        if k in VIA_Z:
            s2_single(k).wait_recv()
            total += r2_of(k)[z].astype(F32)
        else:
            for dz in range(1, 4):
                s3_wait(k, dz)
                total += r3_of(k)[(z + dz) % 4].astype(F32)
        FIN[k] = total
        SQ[...] += fold(total * total)

    def sums_done(k):
        for b in range(2):
            s1_copy(k, b).wait_send()
        (s2_single if k in VIA_Z else s2_copy)(k).wait_send()
        for dz in range(1, 4):
            s3_copy(k, dz).wait_send()
            if k in VIA_Z:
                s3_copy(k, dz, 1).wait_send()

    def result_copies(i):
        if i < 4:
            k = 8 + i
            src = FIN.at[k]
            dst = g_out.at[
                pl.ds(pl.multiple_of(c * 128 + (i % 2) * 64, 64), 64), pl.ds((i // 2) * 512, 512)
            ]
        elif i < 20:
            j = i - 4
            src = FIN.at[4 + j // 8 + 2 * (j % 2), :, pl.ds(((j % 8) // 2) * 128, 128)]
            dst = g_in.at[:, pl.ds(pl.multiple_of(10240 + 256 * j + c * 128, 128), 128)]
        else:
            j = i - 20
            src = FIN.at[j]
            dst = g_in.at[:, pl.ds(pl.multiple_of(6144 + 1024 * j + c * 512, 512), 512)]
        return pltpu.make_async_copy(src, dst, f_l.at[i]), remote(src, dst, f_s.at[i], f_r.at[i], twin)

    def send_result(k):
        if k >= 8:
            span = (k - 8,)
        elif k == 7:
            for half in range(2):
                for q in range(4):
                    cols = slice(q * 128, q * 128 + 128)
                    low, high = FIN[4 + half, :, cols], FIN[6 + half, :, cols]
                    FIN[4 + half, :, cols] = jnp.concatenate([low[:, 0:64], high[:, 0:64]], axis=1)
                    FIN[6 + half, :, cols] = jnp.concatenate([low[:, 64:128], high[:, 64:128]], axis=1)
            span = range(4, 20)
        elif k >= 4:
            span = ()
        else:
            span = (20 + k,)
        for i in span:
            for copy in result_copies(i):
                copy.start()

    def step(t):
        if t + LEAD < CHUNKS:
            if t + LEAD == 4:
                pl.semaphore_wait(cred_a, 1)
            s1(ORDER[t + LEAD])
        if t == 4:
            pl.semaphore_wait(cred_b, 1)
            pl.semaphore_wait(cred_z, 3)
        if t < CHUNKS:
            s2(ORDER[t])
        if 0 <= t - LAG3 < CHUNKS:
            s3(ORDER[t - LAG3])
        if 0 <= t - LAG4 < CHUNKS:
            s4(ORDER[t - LAG4])
            send_result(ORDER[t - LAG4])

    def grad_tiles(k, left, right):
        @pl.loop(0, 4)
        def _(r):
            G[k, r] = dot_tn(left(r), right).astype(BF).reshape(2, 2, 64, 512)

    SQ[...] = jnp.zeros_like(SQ)
    twin_copy(6, DMO.at[o], DMO.at[o]).wait_recv()
    for ch in range(2):
        for rh in range(2):
            k = 8 + 2 * ch + rh
            grad_tiles(
                k,
                lambda r: ACT[:, :, pl.ds(pl.multiple_of(rh * 1024 + r * 256, 256), 256)].reshape(512, 256),
                DMO[:, :, ch * 512 : ch * 512 + 512].reshape(512, 512),
            )
            if 2 * ch + rh < LEAD:
                s1(k)

    for k in range(CHUNKS):
        sends_done(k)

    @pl.loop(0, 16)
    def _(t):
        lat, rh, r = t // 8, (t // 4) % 2, t % 4
        total = 0.0
        for ch in range(2):
            total += dot_nt(DMO[lat, :, ch * 512 : ch * 512 + 512], W[8 + 2 * ch + rh, r].reshape(256, 512))
        cols = pl.ds(pl.multiple_of(rh * 1024 + r * 256, 256), 256)
        GD[lat, :, cols] = (total * GD[lat, :, cols].astype(F32)).astype(BF)

    pl.semaphore_signal(cred_a, 1, device_id=nb_a, device_id_type=MESH)

    def data_back(first_k, count, left, i):
        for ch in range(2):
            @pl.loop(0, 2)
            def _(n):
                total = 0.0
                for j in range(count):
                    total += dot_nt(left(j, o), W[first_k + j, 2 * ch + n].reshape(256, 512))
                SND[ch, :, rows_at(n, 256)] = total

            twin_copy(i + ch, SND.at[ch], RCV.at[ch]).start()

        @pl.loop(0, 4)
        def _(r):
            total = 0.0
            for j in range(count):
                total += dot_nt(left(j, c), W[first_k + j, r].reshape(256, 512))
            MO[:, rows_at(r, 256)] = total

    for ch in range(2):
        twin_copy(4 + ch, SND.at[ch], RCV.at[ch]).wait_send()
    data_back(4, 4, lambda j, lat: GD[lat, :, j * 512 : j * 512 + 512], 7)
    pl.semaphore_signal(cred_b, 1, device_id=nb_b, device_id_type=MESH)
    for dz in range(1, 4):
        pl.semaphore_signal(cred_z, 1, device_id=dev(c, chip_of((z + dz) % 4, y, x)), device_id_type=MESH)

    step(0)
    for j in range(4):
        grad_tiles(
            4 + j,
            lambda r: MLI[:, :, rows_at(r, 256)].reshape(512, 256),
            GD[:, :, j * 512 : j * 512 + 512].reshape(512, 512),
        )
    received(7)

    @pl.loop(0, TOK // 32)
    def _(i):
        r = rows_at(i, 32)
        d_in = both_parts(r)
        hat, inv = normed(RSD[r, :])
        DACC[3] += fold(d_in)
        DACC[4] += fold(d_in * hat)
        d_x = normed_back(d_in * (1.0 + mod_row(4)), hat, inv) + X1[r, :]
        X1[r, :] = d_x
        DACC[2] += fold(d_x * AO[r, :])
        DAO[c, r, :] = (d_x * mod_row(2)).astype(BF)

    dao_other = pl.ds(pl.multiple_of(o * 512, 512), 512)
    dao_mine = pl.ds(pl.multiple_of(c * 512, 512), 512)
    twin_copy(9, DAO.at[c, :, dao_other], DAO.at[c, :, dao_other]).start()

    def mixed_back(hh, n):
        w_mine = W[3, 2 * hh + n].reshape(256, 512)
        w_other = WP[2 * hh + n].reshape(256, 512)
        return (dot_nt(DAO[c, :, dao_mine], w_mine) + dot_nt(DAO[c, :, dao_other], w_other)).astype(BF)

    @pl.loop(0, 2)
    def _(n):
        DMS[:, rows_at(n, 256)] = mixed_back(o, n)

    twin_copy(10, DMS, DMX.at[c]).start()

    @pl.loop(0, 2)
    def _(n):
        DMX[c, :, rows_at(n, 256)] = mixed_back(c, n)

    step(1)
    twin_copy(9, DAO.at[o, :, dao_mine], DAO.at[o, :, dao_mine]).wait_recv()

    @pl.loop(0, 4)
    def _(r):
        left = MIX[r // 2, :, :, rows_at(r % 2, 256)].reshape(512, 256)
        G[3, r] = dot_tn(left, DAO[:, :, dao_mine].reshape(512, 512)).astype(BF).reshape(2, 2, 64, 512)

    twin_copy(10, DMS, DMX.at[o]).wait_recv()

    def attention_back(t):
        lat, cols = t // 4, rows_at(t % 4, 128)
        q, k, v = QKV[0, lat, :, cols], QKV[1, lat, :, cols], QKV[2, lat, :, cols]
        dm = DMX[lat, :, cols]
        res = []
        for m in masks:
            probs = probs_of(q * m, k)
            d_probs = dot_nt(dm * m, v)
            d_v = dot_tn(probs.astype(BF), dm)
            d_s = probs * (d_probs - jnp.sum(d_probs * probs, axis=-1, keepdims=True))
            d_s = (d_s * 0.125).astype(BF)
            res.append((dot_nn(d_s, k), dot_tn(d_s, q), d_v))
        for j in range(3):
            QKV[j, lat, :, cols] = jnp.where(first, res[0][j], res[1][j]).astype(BF)

    for half in range(2):
        pl.loop(4 * half, 4 * half + 4)(attention_back)
        step(2 + half)
    for ch in range(2):
        twin_copy(7 + ch, SND.at[ch], RCV.at[ch]).wait_send()
    data_back(0, 3, lambda j, lat: QKV[j, lat], 11)
    for j in range(3):
        grad_tiles(
            j,
            lambda r: ATI[:, :, rows_at(r, 256)].reshape(512, 256),
            QKV[j].reshape(512, 512),
        )
    received(11)

    @pl.loop(0, TOK // 32)
    def _(i):
        r = rows_at(i, 32)
        d_in = both_parts(r)
        hat, inv = normed(X0[r, :])
        DACC[0] += fold(d_in)
        DACC[1] += fold(d_in * hat)
        d_x = normed_back(d_in * (1.0 + mod_row(1)), hat, inv) + X1[r, :]
        GLP[0:16, :] += dot_tn(pt[0, r, :].astype(BF), d_x.astype(BF))

    for k in range(8):
        MODS[k : k + 1, :] = jnp.sum(DACC[k], axis=0, keepdims=True)
    d_mods = MODS[...]
    DMB[c, s] = jnp.concatenate([d_mods[:, :512], d_mods[:, 512:]], axis=0).astype(BF)
    peers_send(3, lambda p: DMB.at[c, s], DMB.at[c])
    for q in range(8):
        B3S[q] = GLP[:, q * 128 : q * 128 + 128]
    B3R[s] = B3S[s // 2]
    peers_send(4, lambda p: B3S.at[p // 2], B3R)
    step(4)
    peers_wait(3, lambda p: DMB.at[c, s], DMB.at[c])
    twin_copy(13, DMB.at[c], DMB.at[c]).start()

    def unpack(g):
        @pl.loop(0, 16)
        def _(l):
            both = DMB[g, l].astype(F32)
            DMF[g, :, l, 0:512] = both[0:8]
            DMF[g, :, l, 512:1024] = both[8:16]

    unpack(c)
    d_cond_low = 0.0
    for k in range(8):
        w_k = WMOD[:, k * 1024 : k * 1024 + 1024] if k < 6 else EX[:, (k - 5) * 1024 : (k - 4) * 1024]
        d_cond_low += dot_nt(DMF[c, k].astype(BF), w_k.astype(BF))
    d_cond = d_cond_low * silu_slope(CND[1])
    CP[c, 2, :, 0:64] = d_cond
    d_temb = d_cond.astype(BF).astype(F32)
    B2S[...] = jnp.concatenate([d_temb, d_temb], axis=1)
    B2R[s] = B2S[...]
    peers_send(5, lambda p: B2S, B2R)
    step(5)
    peers_wait(4, lambda p: B3S.at[p // 2], B3R)
    B3D[c] = jnp.sum(B3R[...], axis=0)
    twin_copy(14, B3D.at[c], B3D.at[c]).start()
    peers_wait(5, lambda p: B2S, B2R)
    for q in range(8):
        DTA[c, :, q * 128 : q * 128 + 128] = jnp.concatenate(
            [B2R[2 * q, :, 0:64], B2R[2 * q + 1, :, 0:64]], axis=1
        )
    d_tact = dot_nt(DTA[c].astype(BF), EX[:, 0:1024].astype(BF))
    CP[c, 3, :, 0:64] = (d_tact * silu_slope(CND[0])).astype(BF).astype(F32)
    twin_copy(15, DTA.at[c], DTA.at[c]).start()
    twin_copy(16, CP.at[c], CP.at[c]).start()
    twin_copy(17, E1.at[c], E1.at[c]).start()
    step(6)
    twin_copy(13, DMB.at[o], DMB.at[o]).wait_recv()
    unpack(o)
    twin_copy(14, B3D.at[o], B3D.at[o]).wait_recv()
    twin_copy(15, DTA.at[o], DTA.at[o]).wait_recv()
    twin_copy(16, CP.at[o], CP.at[o]).wait_recv()
    twin_copy(17, E1.at[o], E1.at[o]).wait_recv()

    def packed(i):
        return jnp.concatenate([CP[0, i, :, 0:64], CP[1, i, :, 0:64]], axis=0)

    def square_half(value):
        part = 0.5 * value * value
        return jnp.sum(jnp.sum(part, axis=0, keepdims=True), axis=1, keepdims=True)

    cond_both = packed(0).astype(BF)
    small = jnp.zeros((1, 1), F32)
    for k in range(8):
        grad = dot_tn(cond_both, jnp.concatenate([DMF[0, k], DMF[1, k]], axis=0).astype(BF))
        small += square_half(grad)
        if k < 6:
            WMOD[:, k * 1024 : k * 1024 + 1024] = grad
        else:
            EX[:, (k - 5) * 1024 : (k - 4) * 1024] = grad
    mod_out = pltpu.make_async_copy(WMOD, g_in.at[:, pl.ds(0, 6144)], st_sem.at[26])
    mod_out.start()
    step(7)
    grad = dot_tn(packed(1).astype(BF), jnp.concatenate([DTA[0], DTA[1]], axis=0).astype(BF))
    small += square_half(grad)
    EX[:, 0:1024] = grad
    sums = B3D[0] + B3D[1]
    sums = jnp.where(x == 0, sums[:, 0:64], sums[:, 64:128])
    small += square_half(sums[16:32])
    wide = jnp.concatenate(
        [jnp.concatenate([sums[16:32], jnp.zeros((16, 64), F32)], axis=1), jnp.zeros((112, 128), F32)], axis=0
    )
    EX[:, 3072:3088] = wide.T[0:64, 0:16]
    def both(value):
        return jnp.concatenate([value(0), value(1)], axis=0)

    index = lax.broadcasted_iota(jnp.int32, (32, ENTRIES), 1)
    hot = (both(lambda g: E1[g, :, 2, 0:1]).astype(jnp.int32) + PDIM == index).astype(F32)
    grad = dot_tn_exact(packed(2), hot)
    spot = lax.broadcasted_iota(jnp.int32, (16, ENTRIES), 0) == index[0:16]
    grad += dot_tn_exact(sums[0:16], spot.astype(F32))
    ENT[...] = grad
    femb = both(lambda g: jnp.concatenate([E1[g, :, 0, :], E1[g, :, 1, :]], axis=1)).astype(BF)
    ENT[:, PDIM + NCLS :] = dot_tn(packed(3).astype(BF), femb)
    small += square_half(ENT[...])

    for t in range(8, CHUNKS + LAG4):
        step(t)

    def total_of(value):
        return jnp.sum(jnp.sum(value, axis=0, keepdims=True), axis=1, keepdims=True)

    NSS[0:1, :] = jnp.broadcast_to(total_of(SQ[...]) + small, (1, 128))
    NSS[1:2, :] = jnp.broadcast_to(total_of(LOSS[...]) / (TOK * PDIM), (1, 128))
    NSS[2:8, :] = jnp.zeros((6, 128), F32)
    NSR[s] = NSS[...]
    peers_send(6, lambda p: NSS, NSR)
    peers_wait(6, lambda p: NSS, NSR)
    NSD[c] = jnp.sum(NSR[...], axis=0)
    twin_copy(18, NSD.at[c], NSD.at[c]).start()
    twin_copy(18, NSD.at[o], NSD.at[o]).wait_recv()
    stats[...] = NSD[0] + NSD[1]

    mod_out.wait()
    for i in range(24):
        for copy in result_copies(i):
            copy.wait()
    for k in range(CHUNKS):
        sums_done(k)
    twin_copy(0, ATI.at[c], ATI.at[c]).wait_send()
    twin_copy(1, MIX.at[c], MIX.at[c]).wait_send()
    twin_copy(2, W.at[3], WP).wait_send()
    twin_copy(3, MLI.at[c], MLI.at[c]).wait_send()
    twin_copy(6, DMO.at[c], DMO.at[c]).wait_send()
    twin_copy(9, DAO.at[c, :, dao_other], DAO.at[c, :, dao_other]).wait_send()
    twin_copy(10, DMS, DMX.at[c]).wait_send()
    for ch in range(2):
        twin_copy(11 + ch, SND.at[ch], RCV.at[ch]).wait_send()
    twin_copy(13, DMB.at[c], DMB.at[c]).wait_send()
    twin_copy(14, B3D.at[c], B3D.at[c]).wait_send()
    twin_copy(15, DTA.at[c], DTA.at[c]).wait_send()
    twin_copy(16, CP.at[c], CP.at[c]).wait_send()
    twin_copy(17, E1.at[c], E1.at[c]).wait_send()
    twin_copy(18, NSD.at[c], NSD.at[c]).wait_send()


def fused_step(msg, pt, pos, block_in, block_out, entry, exit_):
    vm = pltpu.VMEM
    dma = pltpu.SemaphoreType.DMA
    scratch = [
        vm((12, 4, 2, 2, 64, 512), BF), vm((4, 2, 2, 64, 512), BF), vm((12, 4, 2, 2, 64, 512), BF),
        vm((4, 2, 4, 64, 512), BF), vm((4, 4, 64, 512), BF), vm((4, 4, 64, 512), BF), vm((12, 64, 512), F32),
        vm((2, TOK, 1024), BF), vm((3, 2, TOK, 512), BF), vm((2, 2, TOK, 512), BF), vm((2, TOK, 1024), BF),
        vm((2, TOK, 2048), BF), vm((2, TOK, 2048), BF), vm((2, TOK, 1024), BF), vm((2, TOK, 1024), BF),
        vm((2, TOK, 512), BF), vm((TOK, 512), BF),
        *[vm((TOK, 1024), F32)] * 5, vm((2, TOK, 512), F32), vm((2, TOK, 512), F32),
        vm((64, 6144), F32), vm((2, 16, 8, 128), F32), vm((16, 16, 128), F32), vm((8, 16, 128), F32), vm((16, 16, 128), F32),
        vm((16, 16, 512), BF), vm((16, 16, 512), BF), vm((2, 16, 16, 512), BF), vm((2, 8, 16, 1024), F32),
        vm((16, 128), F32), vm((16, 16, 128), F32), vm((2, 16, 1024), F32), vm((2, 4, 16, 128), F32), vm((2, 16, 64), F32),
        vm((8, 32, 128), F32), vm((16, 32, 128), F32), vm((2, 32, 128), F32),
        vm((8, 128), F32), vm((16, 8, 128), F32), vm((2, 8, 128), F32),
        vm((8, 1024), F32), vm((8, 8, 1024), F32), vm((16, 1024), F32), vm((16, 1024), F32), vm((32, 1024), F32),
        vm((8, 512), F32), vm((8, 16), F32),
        dma((27,)), dma((8, 16)), dma((8, 16)), dma((96,)), dma((96,)), dma((48,)), dma((48,)), dma((96,)), dma((96,)),
        dma((24,)), dma((24,)), dma((12,)), dma((12,)), dma((96,)), dma((96,)), dma((19,)), dma((19,)),
        dma((24,)), dma((24,)), dma((24,)),
        pltpu.SemaphoreType.REGULAR, pltpu.SemaphoreType.REGULAR, pltpu.SemaphoreType.REGULAR,
    ]
    any_ = pl.BlockSpec(memory_space=pl.ANY)
    vmem = pl.BlockSpec(memory_space=pltpu.VMEM)
    shape = jax.ShapeDtypeStruct
    return pl.pallas_call(
        step_kernel,
        out_shape=(
            shape(block_in.shape, F32), shape(block_out.shape, F32), shape(entry.shape, F32),
            shape(exit_.shape, F32), shape((8, 128), F32),
        ),
        in_specs=[vmem, vmem, vmem, any_, any_, any_, any_],
        out_specs=(any_, any_, vmem, vmem, vmem),
        scratch_shapes=scratch,
        compiler_params=pltpu.CompilerParams(
            collective_id=0, has_side_effects=True, vmem_limit_bytes=62 * 2**20
        ),
        cost_estimate=pl.CostEstimate(flops=21 * 10**9, bytes_accessed=20 * 10**6, transcendentals=4 * 10**6),
    )(msg, pt, pos, block_in, block_out, entry, exit_)


def local_fused(
    noisy, timesteps, labels, noise,
    block_in, block_in_first, block_in_second,
    block_out, block_out_first, block_out_second,
    entry_table, entry_first, entry_second,
    exit_proj, exit_first, exit_second,
):
    index = lax.axis_index("rep") * 16 + lax.axis_index("shard")
    femb = lowered(time_features(timesteps, FREQ)).astype(F32).reshape(2, LANES)
    label = labels.astype(F32)[0]
    lane = jnp.arange(LANES)[None, :]
    head = jnp.concatenate(
        [femb, jnp.full((1, LANES), label), jnp.where(lane == index, label, 0.0), jnp.zeros((4, LANES), F32)], axis=0
    )
    edge = jnp.concatenate([entry_table[:PDIM], exit_proj[:, 3 * D :].T], axis=1)
    msg = jnp.concatenate([head, edge], axis=0)
    pt = patchify(jnp.concatenate([noisy, noise], axis=0), PATCH)
    grid = noisy.shape[-1] // PATCH
    pos = position_table(grid, D)[:grid, : D // 2]
    g_in, g_out, g_entry, g_exit, stats = fused_step(
        msg, pt, pos, block_in[0], block_out[0], entry_table.T, exit_proj
    )
    loss = stats[1, 0]
    grad_norm = jnp.sqrt(stats[0, 0])
    factor = clip_limit / jnp.maximum(grad_norm, clip_limit)
    outs = [loss, grad_norm]
    for weight, first, second, grad, rate in (
        (block_in, block_in_first, block_in_second, g_in[None], rate_main),
        (block_out, block_out_first, block_out_second, g_out[None], rate_main),
        (entry_table, entry_first, entry_second, g_entry.T, rate_edge),
        (exit_proj, exit_first, exit_second, g_exit, rate_main),
    ):
        outs.extend(adam_step(weight, first, second, grad, factor, rate))
    return tuple(outs)


def solution(mesh):
    step = local_fused if dict(mesh.shape) == {"rep": 2, "shard": 16} else local
    in_specs = (
        P(("rep", "shard"), None, None, None),
        P(("rep", "shard")),
        P(("rep", "shard")),
        P(("rep", "shard"), None, None, None),
        P(None, "shard", None),
        P(None, "shard", None),
        P(None, "shard", None),
        P(None, "shard", None),
        P(None, "shard", None),
        P(None, "shard", None),
        P(None, "shard"),
        P(None, "shard"),
        P(None, "shard"),
        P("shard", None),
        P("shard", None),
        P("shard", None),
    )
    out_specs = (
        P(),
        P(),
        P(None, "shard", None),
        P(None, "shard", None),
        P(None, "shard", None),
        P(None, "shard", None),
        P(None, "shard", None),
        P(None, "shard", None),
        P(None, "shard", None),
        P(None, "shard", None),
        P(None, "shard"),
        P(None, "shard"),
        P(None, "shard"),
        P(None, "shard"),
        P("shard", None),
        P("shard", None),
        P("shard", None),
        P("shard", None),
    )
    return jax.shard_map(step, mesh=mesh, in_specs=in_specs, out_specs=out_specs, check_vma=False)
```

```python
import jax
import jax.numpy as jnp
from jax import lax
from jax.experimental import pallas as pl
from jax.experimental.pallas import tpu as pltpu
from jax.sharding import PartitionSpec as P

D = 1024
HEADS = 16
PATCH = 2
NCLS = 1000
FREQ = 256
STEP = 10
PDIM = 16
ENTRIES = PDIM + NCLS + FREQ


clip_limit = 0.5
rate_main = 0.02
rate_edge = 0.1
decay_rate = 0.01
adam_eps = 1e-08
highest = lax.Precision.HIGHEST


def lowered(value):
    return value.astype(jnp.bfloat16)


def product(left, right):
    return jnp.dot(left, right, preferred_element_type=jnp.float32)


def product_tn(left, right):
    return lax.dot_general(
        left, right, (((0,), (0,)), ((), ())), preferred_element_type=jnp.float32
    )


def product_nt(left, right):
    return lax.dot_general(
        left, right, (((1,), (1,)), ((), ())), preferred_element_type=jnp.float32
    )


def patchify(image, patch):
    batch, chans, height, width = image.shape
    grid = height // patch
    parts = image.reshape(batch, chans, grid, patch, grid, patch)
    parts = parts.transpose(0, 2, 4, 3, 5, 1)
    return parts.reshape(batch, grid * grid, patch * patch * chans)


def position_table(grid, width):
    quarter = width // 4
    omega = 1.0 / 10000.0 ** (jnp.arange(quarter, dtype=jnp.float32) / quarter)
    index = jnp.arange(grid * grid)
    row_pos = (index // grid).astype(jnp.float32)[:, None] * omega[None, :]
    col_pos = (index % grid).astype(jnp.float32)[:, None] * omega[None, :]
    return jnp.concatenate(
        [jnp.sin(col_pos), jnp.cos(col_pos), jnp.sin(row_pos), jnp.cos(row_pos)], axis=1
    )


def time_features(steps, size):
    half = size // 2
    freqs = jnp.exp(-jnp.log(10000.0) * jnp.arange(half, dtype=jnp.float32) / half)
    angles = steps.astype(jnp.float32)[:, None] * freqs[None, :]
    return jnp.concatenate([jnp.cos(angles), jnp.sin(angles)], axis=1)


def modulate(x, shift, scale):
    centered = x - jnp.mean(x, axis=-1, keepdims=True)
    var = jnp.mean(centered * centered, axis=-1, keepdims=True)
    normed = centered * lax.rsqrt(var + 1e-06)
    return normed * (1.0 + scale[:, None, :]) + shift[:, None, :]


def gelu_tanh(value):
    return jax.nn.gelu(value, approximate=True)


def adam_step(weight, first, second, grad, factor, rate):
    clipped = grad * factor
    first_new = 0.5 * first + 0.5 * clipped
    second_new = 0.5 * second + 0.5 * clipped * clipped
    corr = 1.0 - 0.5**STEP
    update = first_new / corr / (jnp.sqrt(second_new / corr) + adam_eps) + decay_rate * weight
    weight_new = weight - rate * update
    return (weight_new, first_new, second_new, weight_new.astype(jnp.bfloat16))


def layer_parts(x, cond_low, w_in, w_out):
    width = x.shape[-1]
    batch, seq = (x.shape[0], x.shape[1])
    size = width // HEADS
    mod = product(cond_low, w_in[:, : 6 * width])
    shift_a, scale_a, gate_a, shift_b, scale_b, gate_b = jnp.split(mod, 6, axis=-1)
    attn_in = lowered(modulate(x, shift_a, scale_a))
    qkv = lowered(
        jnp.einsum(
            "bsd,de->bse",
            attn_in,
            w_in[:, 6 * width : 9 * width],
            preferred_element_type=jnp.float32,
        )
    )
    query = qkv[..., :width].reshape(batch, seq, HEADS, size)
    keys = qkv[..., width : 2 * width].reshape(batch, seq, HEADS, size)
    values = qkv[..., 2 * width :].reshape(batch, seq, HEADS, size)
    scores = jnp.einsum(
        "bqhd,bkhd->bhqk", query, keys, preferred_element_type=jnp.float32
    ) * size ** (-0.5)
    weights = jax.nn.softmax(scores, axis=-1)
    weights_low = lowered(weights)
    mixed = lowered(
        jnp.einsum("bhqk,bkhd->bqhd", weights_low, values, preferred_element_type=jnp.float32)
    ).reshape(batch, seq, width)
    attn_out = jnp.einsum(
        "bsd,de->bse", mixed, w_in[:, 9 * width : 10 * width], preferred_element_type=jnp.float32
    )
    resid = x + gate_a[:, None, :] * attn_out
    mlp_in = lowered(modulate(resid, shift_b, scale_b))
    hidden = jnp.einsum(
        "bsd,df->bsf", mlp_in, w_in[:, 10 * width :], preferred_element_type=jnp.float32
    )
    active = lowered(gelu_tanh(hidden))
    mlp_out = jnp.einsum("bsf,fd->bsd", active, w_out, preferred_element_type=jnp.float32)
    result = resid + gate_b[:, None, :] * mlp_out
    return dict(
        mods=(shift_a, scale_a, gate_a, shift_b, scale_b, gate_b),
        attn_in=attn_in,
        query=query,
        keys=keys,
        values=values,
        weights=weights,
        weights_low=weights_low,
        mixed=mixed,
        attn_out=attn_out,
        resid=resid,
        mlp_in=mlp_in,
        hidden=hidden,
        active=active,
        mlp_out=mlp_out,
        result=result,
    )


def layer_back(x, cond_low, w_in, w_out, parts, grad_out, grad_cond):
    width = x.shape[-1]
    batch, seq = (x.shape[0], x.shape[1])
    size = width // HEADS
    shift_a, scale_a, gate_a, shift_b, scale_b, gate_b = parts["mods"]
    d_gate_b = jnp.sum(grad_out * parts["mlp_out"], axis=1)
    d_mlp_out = lowered(grad_out * gate_b[:, None, :])
    g_fc2 = jnp.einsum(
        "bsf,bsd->fd", parts["active"], d_mlp_out, preferred_element_type=jnp.float32
    )
    d_active = jnp.einsum("bsd,fd->bsf", d_mlp_out, w_out, preferred_element_type=jnp.float32)
    _, gelu_pull = jax.vjp(gelu_tanh, parts["hidden"])
    d_hidden = lowered(gelu_pull(d_active)[0])
    g_fc1 = jnp.einsum("bsd,bsf->df", parts["mlp_in"], d_hidden, preferred_element_type=jnp.float32)
    d_mlp_in = jnp.einsum(
        "bsf,df->bsd", d_hidden, w_in[:, 10 * width :], preferred_element_type=jnp.float32
    )
    _, norm_pull = jax.vjp(modulate, parts["resid"], shift_b, scale_b)
    d_resid, d_shift_b, d_scale_b = norm_pull(d_mlp_in)
    d_resid = d_resid + grad_out
    d_gate_a = jnp.sum(d_resid * parts["attn_out"], axis=1)
    d_attn_out = lowered(d_resid * gate_a[:, None, :])
    g_proj = jnp.einsum(
        "bsd,bse->de", parts["mixed"], d_attn_out, preferred_element_type=jnp.float32
    )
    d_mixed = lowered(
        jnp.einsum(
            "bse,de->bsd",
            d_attn_out,
            w_in[:, 9 * width : 10 * width],
            preferred_element_type=jnp.float32,
        )
    ).reshape(batch, seq, HEADS, size)
    d_probs = jnp.einsum(
        "bqhd,bkhd->bhqk", d_mixed, parts["values"], preferred_element_type=jnp.float32
    )
    d_values = jnp.einsum(
        "bhqk,bqhd->bkhd", parts["weights_low"], d_mixed, preferred_element_type=jnp.float32
    )
    weights = parts["weights"]
    d_scores = weights * (d_probs - jnp.sum(d_probs * weights, axis=-1, keepdims=True))
    d_scaled = lowered(d_scores * size ** (-0.5))
    d_query = jnp.einsum(
        "bhqk,bkhd->bqhd", d_scaled, parts["keys"], preferred_element_type=jnp.float32
    )
    d_keys = jnp.einsum(
        "bhqk,bqhd->bkhd", d_scaled, parts["query"], preferred_element_type=jnp.float32
    )
    d_qkv = lowered(
        jnp.concatenate(
            [
                d_query.reshape(batch, seq, width),
                d_keys.reshape(batch, seq, width),
                d_values.reshape(batch, seq, width),
            ],
            axis=-1,
        )
    )
    g_qkv = jnp.einsum("bsd,bse->de", parts["attn_in"], d_qkv, preferred_element_type=jnp.float32)
    d_attn_in = jnp.einsum(
        "bse,de->bsd", d_qkv, w_in[:, 6 * width : 9 * width], preferred_element_type=jnp.float32
    )
    _, first_pull = jax.vjp(modulate, x, shift_a, scale_a)
    d_x, d_shift_a, d_scale_a = first_pull(d_attn_in)
    d_x = d_x + d_resid
    d_mod = lowered(
        jnp.concatenate([d_shift_a, d_scale_a, d_gate_a, d_shift_b, d_scale_b, d_gate_b], axis=-1)
    )
    g_mod = product_tn(cond_low, d_mod)
    grad_cond = grad_cond + product_nt(d_mod, w_in[:, : 6 * width])
    g_in = jnp.concatenate([g_mod, g_qkv, g_proj, g_fc1], axis=1)
    return (d_x, grad_cond, g_in, g_fc2)


def local(
    noisy,
    timesteps,
    labels,
    noise,
    block_in,
    block_in_first,
    block_in_second,
    block_out,
    block_out_first,
    block_out_second,
    entry_table,
    entry_first,
    entry_second,
    exit_proj,
    exit_first,
    exit_second,
):
    layers = block_in.shape[0]
    entry_all, exit_all = (
        lax.all_gather(lowered(entry_table), "shard", axis=1, tiled=True),
        lax.all_gather(lowered(exit_proj), "shard", axis=0, tiled=True),
    )
    w_patch = entry_all[:PDIM]
    w_label = entry_all[PDIM : PDIM + NCLS]
    w_time = entry_all[PDIM + NCLS :]
    w_time2 = exit_all[:, :D]
    w_final = exit_all[:, D : 3 * D]
    w_output = exit_all[:, 3 * D :]
    patches = lowered(patchify(noisy, PATCH))
    target = patchify(noise, PATCH)
    seq = patches.shape[1]
    x = (
        jnp.einsum("bsp,pd->bsd", patches, w_patch, preferred_element_type=jnp.float32)
        + position_table(noisy.shape[-1] // PATCH, D)[None]
    )
    femb = lowered(time_features(timesteps, FREQ))
    t_hidden = product(femb, w_time)
    t_act = lowered(jax.nn.silu(t_hidden))
    temb = product(t_act, w_time2)
    onehot = (labels[:, None] == jnp.arange(NCLS)[None, :]).astype(jnp.float32)
    cond = temb + jnp.dot(onehot, w_label.astype(jnp.float32), precision=highest)
    cond_low = lowered(jax.nn.silu(cond))
    layer = 0
    w_in_all = lax.all_gather(lowered(block_in[layer]), "shard", axis=0, tiled=True)
    w_out_all = lax.all_gather(lowered(block_out[layer]), "shard", axis=0, tiled=True)
    inputs = [x]
    parts = layer_parts(x, cond_low, w_in_all, w_out_all)
    saved = [parts]
    x = parts["result"]
    final_mod = product(cond_low, w_final)
    shift_f, scale_f = jnp.split(final_mod, 2, axis=-1)
    final_in = lowered(modulate(x, shift_f, scale_f))
    pred = jnp.einsum("bsd,dp->bsp", final_in, w_output, preferred_element_type=jnp.float32)
    error = pred - target
    loss_part = jnp.sum(error * error) / (seq * PDIM)
    d_pred = lowered(2.0 * error / (seq * PDIM))
    g_output = jnp.einsum("bsd,bsp->dp", final_in, d_pred, preferred_element_type=jnp.float32)
    d_final_in = jnp.einsum("bsp,dp->bsd", d_pred, w_output, preferred_element_type=jnp.float32)
    _, final_pull = jax.vjp(modulate, x, shift_f, scale_f)
    d_x, d_shift_f, d_scale_f = final_pull(d_final_in)
    d_fmod = lowered(jnp.concatenate([d_shift_f, d_scale_f], axis=-1))
    g_final = product_tn(cond_low, d_fmod)
    grad_cond = product_nt(d_fmod, w_final)
    shards_in = [None] * layers
    shards_out = [None] * layers
    for layer in reversed(range(layers)):
        w_in_all, w_out_all = (
            lax.all_gather(lowered(block_in[layer]), "shard", axis=0, tiled=True),
            lax.all_gather(lowered(block_out[layer]), "shard", axis=0, tiled=True),
        )
        d_x, grad_cond, g_in, g_fc2 = layer_back(
            inputs[layer], cond_low, w_in_all, w_out_all, saved[layer], d_x, grad_cond
        )
        shards_in[layer], shards_out[layer] = (
            lax.psum_scatter(g_in, "shard", scatter_dimension=0, tiled=True),
            lax.psum_scatter(g_fc2, "shard", scatter_dimension=0, tiled=True),
        )
    _, silu_pull = jax.vjp(jax.nn.silu, cond)
    d_cond = silu_pull(grad_cond)[0]
    g_label = jnp.dot(onehot.T, d_cond, precision=highest)
    d_temb = lowered(d_cond)
    g_time2 = product_tn(t_act, d_temb)
    d_tact = product_nt(d_temb, w_time2)
    _, time_pull = jax.vjp(jax.nn.silu, t_hidden)
    d_thidden = lowered(time_pull(d_tact)[0])
    g_time = product_tn(femb, d_thidden)
    g_patch = jnp.einsum("bsp,bsd->pd", patches, lowered(d_x), preferred_element_type=jnp.float32)
    g_entry = jnp.concatenate([g_patch, g_label, g_time], axis=0)
    g_exit = jnp.concatenate([g_time2, g_final, g_output], axis=1)
    share_entry, share_exit = (
        lax.psum_scatter(g_entry, "shard", scatter_dimension=1, tiled=True),
        lax.psum_scatter(g_exit, "shard", scatter_dimension=0, tiled=True),
    )
    grads = (
        lax.psum(jnp.stack(shards_in).astype(jnp.bfloat16), "rep").astype(jnp.float32),
        lax.psum(jnp.stack(shards_out).astype(jnp.bfloat16), "rep").astype(jnp.float32),
        lax.psum(share_entry.astype(jnp.bfloat16), "rep").astype(jnp.float32),
        lax.psum(share_exit.astype(jnp.bfloat16), "rep").astype(jnp.float32),
    )
    squares = (
        jnp.sum(grads[0] * grads[0])
        + jnp.sum(grads[1] * grads[1])
        + jnp.sum(grads[2] * grads[2])
        + jnp.sum(grads[3] * grads[3])
    )
    loss = lax.psum(loss_part, ("rep", "shard"))
    norm_sq = lax.psum(squares, "shard")
    grad_norm = jnp.sqrt(norm_sq)
    factor = clip_limit / jnp.maximum(grad_norm, clip_limit)
    bi_w, bi_m, bi_v, bi_l = adam_step(
        block_in, block_in_first, block_in_second, grads[0], factor, rate_main
    )
    bo_w, bo_m, bo_v, bo_l = adam_step(
        block_out, block_out_first, block_out_second, grads[1], factor, rate_main
    )
    en_w, en_m, en_v, en_l = adam_step(
        entry_table, entry_first, entry_second, grads[2], factor, rate_edge
    )
    ex_w, ex_m, ex_v, ex_l = adam_step(
        exit_proj, exit_first, exit_second, grads[3], factor, rate_main
    )
    return (
        loss,
        grad_norm,
        bi_w,
        bi_m,
        bi_v,
        bi_l,
        bo_w,
        bo_m,
        bo_v,
        bo_l,
        en_w,
        en_m,
        en_v,
        en_l,
        ex_w,
        ex_m,
        ex_v,
        ex_l,
    )


BF = jnp.bfloat16
F32 = jnp.float32
MESH = pl.DeviceIdType.MESH
TOK = 256
TILE = 128
LANES = 128
CHUNKS = 12
START = (4, 2)
OWN_AT = ((), (4,), (5, 6), (7, 8), (9, 10), (11,))
Z_AT = ((2,), (3,), (4,), (5,), (6, 7), (8,), (9,), (10,), (11,))
VIA_Z = (1, 3, 5, 7, 9, 11)
SUM_VIA_Z = (0, 3, 6)
LEAD = 3
LAGS = (0, 1, 2, 3)
LAG_A = 1
UNITS = tuple((k, 0, 64) for k in (8, 9, 10, 11, 4, 5, 6, 7, 3, 0, 1)) + tuple((2, 16 * i, 16) for i in range(4))
NU = len(UNITS)
SMALL = 11


def dot_nn(left, right):
    return lax.dot_general(left, right, (((1,), (0,)), ((), ())), preferred_element_type=F32)


def dot_nt(left, right):
    return lax.dot_general(left, right, (((1,), (1,)), ((), ())), preferred_element_type=F32)


def dot_tn(left, right):
    return lax.dot_general(left, right, (((0,), (0,)), ((), ())), preferred_element_type=F32)


def dot_tn_exact(left, right):
    return lax.dot_general(
        left, right, (((0,), (0,)), ((), ())), preferred_element_type=F32, precision=highest
    )


def to_tile(value):
    return jnp.concatenate([value[0:8], value[8:16]], axis=1)


def from_tile(value):
    return jnp.concatenate([value[:, 0:64], value[:, 64:128]], axis=0)


def sigmoid(value):
    return 1.0 / (1.0 + jnp.exp(-value))


def silu_slope(value):
    gate = sigmoid(value)
    return gate * (1.0 + value * (1.0 - gate))


def normed(x):
    centered = x - jnp.mean(x, axis=-1, keepdims=True)
    var = jnp.mean(centered * centered, axis=-1, keepdims=True)
    inv = lax.rsqrt(var + 1e-06)
    return centered * inv, inv


def normed_back(d_normed, x_normed, inv):
    mean_d = jnp.mean(d_normed, axis=-1, keepdims=True)
    mean_dx = jnp.mean(d_normed * x_normed, axis=-1, keepdims=True)
    return inv * (d_normed - mean_d - x_normed * mean_dx)


def fold(value):
    rows, cols = value.shape
    return jnp.sum(value.reshape(rows // 8, 8, cols), axis=0)


def rows_at(i, size):
    return pl.ds(pl.multiple_of(i * size, size), size)


def step_kernel(
    msg, edge, pt, pos, bi, bo, ent_in, ex_in,
    g_in, g_out, ENT, EX, stats,
    W, WP, G, R1, R2, R3, PF, FIN,
    ATI, QKV, MIX, MLI, ACT, GD, DMO, DAO, DMX, DMS,
    X0, AO, RSD, MO, X1, SND, RCV,
    WMOD, E1, EDG, E2S, E2R, E3S, E3R, DMB, DMF, B2S, B2R, DTA, CP, CND,
    B3S, B3R, B3D, NSS, NSR, MODS, DACC, WPT, WLT, GLP, SQ, LOSS,
    st_sem, peer_s, peer_r, zs, zr, bs, br, as_, ar,
    s1s, s1r, s2s, s2r, szs, szr, pss, psr, d_s, d_r, f_l, f_s, f_r,
    far_s, far_r, cred_a, cred_b, cred_z,
):
    c = lax.axis_index("rep")
    s = lax.axis_index("shard")
    o = 1 - c
    x = s % 2
    y = (s // 2) % 2
    z = s // 4
    a_me = y * o + x * c
    b_me = x * o + y * c

    def yx(a, b):
        return a * o + b * c, b * o + a * c

    def dev(core, chip):
        return {"rep": core, "shard": chip}

    def chip_of(zz, yy, xx):
        return zz * 4 + yy * 2 + xx

    nb_a = dev(c, chip_of(z, *yx(1 - a_me, b_me)))
    nb_b = dev(c, chip_of(z, *yx(a_me, 1 - b_me)))
    twin = dev(o, s)

    def remote(src, dst, ss, rs, to):
        return pltpu.make_async_remote_copy(
            src_ref=src, dst_ref=dst, send_sem=ss, recv_sem=rs, device_id=to, device_id_type=MESH
        )

    pieces = []
    for j in range(4):
        pieces.append((bi.at[:, pl.ds(pl.multiple_of(6144 + 1024 * j + c * 512, 512), 512)], FIN.at[j]))
    for j in range(16):
        pieces.append((
            bi.at[:, pl.ds(pl.multiple_of(10240 + 256 * j + c * 128, 128), 128)],
            FIN.at[4 + j // 4, :, pl.ds((j % 4) * 128, 128)],
        ))
    for ch in range(2):
        for rh in range(2):
            pieces.append((
                bo.at[pl.ds(pl.multiple_of(c * 128 + rh * 64, 64), 64), pl.ds(ch * 512, 512)],
                FIN.at[8 + 2 * ch + rh],
            ))
    pieces.append((ent_in, ENT))
    pieces.append((ex_in, EX))
    pieces.append((bi.at[:, pl.ds(0, 6144)], WMOD))
    local = [pltpu.make_async_copy(p, q, st_sem.at[i]) for i, (p, q) in enumerate(pieces)]
    for i in (24, 25, 0, 1, 2, 3, *range(4, 24), 26):
        local[i].start()

    barrier = pltpu.get_barrier_semaphore()

    @pl.loop(1, 16)
    def _(k):
        pl.semaphore_signal(barrier, 1, device_id=dev(c, (s + k) % 16), device_id_type=MESH)

    @pl.loop(0, 16)
    def _(k):
        pl.semaphore_signal(barrier, 1, device_id=dev(o, k), device_id_type=MESH)

    pl.semaphore_wait(barrier, 31)

    def peers_copy(e, k, src_of, dst):
        peer = (s + k) % 16
        return remote(src_of(peer), dst.at[s], peer_s.at[e, k], peer_r.at[e, s], dev(c, peer))

    def peers_send(e, src_of, dst):
        @pl.loop(1, 16)
        def _(k):
            peers_copy(e, k, src_of, dst).start()

    def peers_wait(e, src_of, dst):
        @pl.loop(1, 16)
        def _(k):
            frm = (s + k) % 16
            remote(src_of(frm), dst.at[frm], peer_s.at[e, k], peer_r.at[e, frm], dev(c, frm)).wait_recv()

        @pl.loop(1, 16)
        def _(k):
            peers_copy(e, k, src_of, dst).wait_send()

    def twin_copy(i, src, dst):
        return remote(src, dst, d_s.at[i], d_r.at[i], twin)

    def block(k, zz, far):
        yy, xx = yx(a_me, 1 - b_me if far else b_me)
        return W.at[k, zz, yy, xx]

    def z_copy(k, dz, far=0):
        at = block(k, z, far)
        i = k * 8 + far * 4
        return remote(at, at, zs.at[i + dz], zr.at[i + z], dev(c, chip_of((z + dz) % 4, y, x)))

    def z_wait(k, dz, far=0):
        frm = (z + dz) % 4
        at = block(k, frm, far)
        i = k * 8 + far * 4
        remote(at, at, zs.at[i + dz], zr.at[i + frm], dev(c, chip_of(frm, y, x))).wait_recv()

    inner = jnp.logical_or(z == 1, z == 2)

    def z_pass(k, far=0):
        at = block(k, (z + 2) % 4, far)
        i = k * 8 + far * 4
        return remote(at, at, zs.at[i], zr.at[i + (z + 2) % 4], dev(c, chip_of(3 * (z - 1), y, x)))

    def z_start(k, far=0):
        z_copy(k, 2, far).start()
        pl.when(z != 3)(lambda: z_copy(k, 1, far).start())
        pl.when(z != 0)(lambda: z_copy(k, 3, far).start())

    def z_arrived(k, dz, far=0):
        z_wait(k, dz, far)
        if dz == 2:
            pl.when(inner)(lambda: z_pass(k, far).start())

    def z_sent(k, far=0):
        z_copy(k, 2, far).wait_send()
        pl.when(z != 3)(lambda: z_copy(k, 1, far).wait_send())
        pl.when(z != 0)(lambda: z_copy(k, 3, far).wait_send())
        pl.when(inner)(lambda: z_pass(k, far).wait_send())

    def b_copy(k, zz):
        at = block(k, zz, 0)
        return remote(at, at, bs.at[k * 4 + zz], br.at[k * 4 + zz], nb_b)

    def a_copy(k, zz, far=0):
        at = block(k, zz, far)
        i = k * 8 + far * 4 + zz
        return remote(at, at, as_.at[i], ar.at[i], nb_a)

    def own(k):
        cast(k)
        b_copy(k, z).start()
        a_copy(k, z).start()

    def far_start(k):
        b_copy(k, z).wait_recv()
        z_start(k, 1)
        a_copy(k, z, 1).start()

    def pump_b(k):
        for dz in (2, 1, 3):
            frm = (z + dz) % 4
            z_arrived(k, dz)
            if k not in VIA_Z:
                b_copy(k, frm).start()
            a_copy(k, frm).start()

    def pump_a(k):
        if k in VIA_Z:
            for dz in (2, 1, 3):
                z_arrived(k, dz, 1)
                a_copy(k, (z + dz) % 4, 1).start()
        else:
            for dz in range(4):
                b_copy(k, (z + dz) % 4).wait_recv()
                a_copy(k, (z + dz) % 4, 1).start()

    def sends_done(k):
        z_sent(k)
        if k in VIA_Z:
            z_sent(k, 1)
        else:
            for dz in range(1, 4):
                b_copy(k, (z + dz) % 4).wait_send()
        b_copy(k, z).wait_send()
        for far in range(2):
            for zz in range(4):
                a_copy(k, zz, far).wait_send()

    def pump(k):
        for i in OWN_AT[k] if k < len(OWN_AT) else ():
            own(i)
        for i in Z_AT[k] if k < len(Z_AT) else ():
            z_start(i)
        if k + 1 in VIA_Z:
            far_start(k + 1)
        if k < CHUNKS:
            pump_b(k)
        if 0 <= k - LAG_A < CHUNKS:
            pump_a(k - LAG_A)

    def need(k):
        for far in range(2):
            for dz in range(4):
                a_copy(k, (z + dz) % 4, far).wait_recv()

    def cast(k):
        if k < 4:
            local[k].wait()
            W[k, z, y, x] = FIN[k].astype(BF)
        elif k < 8:
            if k == 4:
                for i in range(4, 20):
                    local[i].wait()
            rh, half = (k - 4) // 2, (k - 4) % 2
            for q in range(4):
                j = half * 8 + 2 * q
                pair = FIN[4 + j // 4, :, (j % 4) * 128 : (j % 4) * 128 + 256]
                piece = jnp.concatenate(
                    [pair[:, rh * 64 : rh * 64 + 64], pair[:, 128 + rh * 64 : 128 + rh * 64 + 64]], axis=1
                )
                W[k, z, y, x, :, q * 128 : q * 128 + 128] = piece.astype(BF)
        else:
            local[20 + k - 8].wait()
            W[k, z, y, x] = FIN[k].astype(BF)

    E1[c, s] = msg[...]
    peers_send(0, lambda p: msg, E1.at[c])
    for k in range(START[0]):
        own(k)
        if k < START[1]:
            z_start(k)

    local[24].wait()
    local[25].wait()
    peers_wait(0, lambda p: msg, E1.at[c])
    t_hidden = dot_nt(E1[c, :, 0, :].astype(BF), ENT[:, 1016:1144].astype(BF)) + dot_nt(
        E1[c, :, 1, :].astype(BF), ENT[:, 1144:1272].astype(BF)
    )
    CND[0] = t_hidden
    t_act = (t_hidden * sigmoid(t_hidden)).astype(BF)
    CP[c, 1, :, 0:64] = t_act.astype(F32)
    for q in range(8):
        part = dot_nn(t_act, EX[:, q * 128 : q * 128 + 128].astype(BF))
        for h in range(2):
            E2S[2 * q + h] = to_tile(part[:, 64 * h : 64 * h + 64])
    E2R[s] = E2S[s]
    peers_send(1, lambda p: E2S.at[p], E2R)
    pump(0)
    hot = (
        E1[c, :, 2, 0:1].astype(jnp.int32) + PDIM == lax.broadcasted_iota(jnp.int32, (16, ENTRIES), 1)
    ).astype(F32).astype(BF)
    w_class = dot_nt(hot, ENT[...].astype(BF))
    pump(1)
    local[26].wait()
    peers_wait(1, lambda p: E2S.at[p], E2R)
    cond = from_tile(jnp.sum(E2R[...], axis=0)) + w_class
    CND[1] = cond
    cond_low = (cond * sigmoid(cond)).astype(BF)
    CP[c, 0, :, 0:64] = cond_low.astype(F32)
    for k in range(8):
        w_k = WMOD[:, k * 1024 : k * 1024 + 1024] if k < 6 else EX[:, (k - 5) * 1024 : (k - 4) * 1024]
        DMF[0, k] = dot_nn(cond_low, w_k.astype(BF))

    @pl.loop(0, 16)
    def _(l):
        part = DMF[0, :, l, :]
        E3S[l] = jnp.concatenate([part[:, :512], part[:, 512:]], axis=0).astype(BF)

    E3R[s] = E3S[s]
    peers_send(2, lambda p: E3S.at[p], E3R)
    EDG[s] = edge[...]
    peers_send(7, lambda p: edge, EDG)
    pump(2)

    peers_wait(7, lambda p: edge, EDG)
    for q in range(8):
        even, odd = EDG[2 * q], EDG[2 * q + 1]
        WPT[:, q * 128 : q * 128 + 128] = jnp.concatenate([even[:, :64], odd[:, :64]], axis=1)
        WLT[:, q * 128 : q * 128 + 128] = jnp.concatenate([even[:, 64:], odd[:, 64:]], axis=1)
    for n in range(4):
        cols = slice(n * 256, n * 256 + 256)
        X0[:, cols] = dot_nn(pt[0].astype(BF), WPT[:, cols])

    @pl.loop(0, 16)
    def _(i):
        X0[rows_at(i, 16), 0:512] += pos[...]
        X0[rows_at(i, 16), 512:1024] += jnp.broadcast_to(pos[pl.ds(i, 1), :], (16, 512))

    DACC[...] = jnp.zeros_like(DACC)
    pump(3)
    peers_wait(2, lambda p: E3S.at[p], E3R)
    parts = E3R[0].astype(F32)
    for i in range(1, 16):
        parts += E3R[i].astype(F32)
    MODS[...] = jnp.concatenate([parts[0:8], parts[8:16]], axis=1)

    def mod_row(k):
        return MODS[k : k + 1, :]

    def modulated(src, dst, shift, scale):
        @pl.loop(0, TOK // TILE)
        def _(i):
            r = rows_at(i, TILE)
            hat, _ = normed(src[r, :])
            dst[c, r, :] = (hat * (1.0 + mod_row(scale)) + mod_row(shift)).astype(BF)

    modulated(X0, ATI, 0, 1)
    twin_copy(0, ATI.at[c], ATI.at[c]).start()
    pump(4)
    twin_copy(0, ATI.at[o], ATI.at[o]).wait_recv()

    def w_cols(k, n):
        return W[k, :, :, :, :, rows_at(n, 256)].reshape(1024, 256)

    for j in range(3):
        need(j)

        @pl.loop(0, 4)
        def _(t):
            lat, n = t // 2, t % 2
            QKV[j, lat, :, rows_at(n, 256)] = dot_nn(ATI[lat], w_cols(j, n)).astype(BF)

        pump(5 + j)

    lane = lax.broadcasted_iota(jnp.int32, (1, LANES), 1)
    first = lane < 64
    masks = (first.astype(F32).astype(BF), 1.0 - first.astype(F32).astype(BF))

    def probs_of(q, k):
        score = dot_nt(q, k) * 0.125
        e = jnp.exp(score - jnp.max(score, axis=-1, keepdims=True))
        return e / jnp.sum(e, axis=-1, keepdims=True)

    def attention(t):
        lat, cols = t // 4, rows_at(t % 4, 128)
        q, k, v = QKV[0, lat, :, cols], QKV[1, lat, :, cols], QKV[2, lat, :, cols]
        outs = [dot_nn(probs_of(q * m, k).astype(BF), v) for m in masks]
        MIX[c, lat, :, cols] = jnp.where(first, outs[0], outs[1]).astype(BF)

    pl.loop(0, 4)(attention)
    pump(8)
    pl.loop(4, 8)(attention)

    twin_copy(1, MIX.at[c], MIX.at[c]).start()
    need(3)
    twin_copy(2, W.at[3], WP).start()
    pump(9)
    twin_copy(1, MIX.at[o], MIX.at[o]).wait_recv()
    twin_copy(2, W.at[3], WP).wait_recv()

    def proj(own):
        def cols(n):
            return pl.ds(pl.multiple_of((c if own else o) * 512 + n * 256, 256), 256)

        @pl.loop(0, 2)
        def _(n):
            ref = W.at[3] if own else WP
            total = 0.0
            for hh in range(2):
                w_half = ref[2 * hh : 2 * hh + 2, :, :, :, rows_at(n, 256)].reshape(512, 256)
                total += dot_nn(MIX[hh, c], w_half)
            AO[:, cols(n)] = total

    proj(True)
    proj(False)

    @pl.loop(0, TOK // TILE)
    def _(i):
        r = rows_at(i, TILE)
        RSD[r, :] = X0[r, :] + mod_row(2) * AO[r, :]

    modulated(RSD, MLI, 3, 4)
    twin_copy(3, MLI.at[c], MLI.at[c]).start()
    pump(10)
    twin_copy(3, MLI.at[o], MLI.at[o]).wait_recv()
    for j in range(4):
        need(4 + j)

        @pl.loop(0, 4)
        def _(t):
            lat, n = t // 2, t % 2
            hidden = dot_nn(MLI[lat], w_cols(4 + j, n))
            cols = pl.ds(pl.multiple_of(j * 512 + n * 256, 256), 256)
            square = hidden * hidden
            t_in = 0.7978845608028654 * hidden * (1.0 + 0.044715 * square)
            t_out = jnp.tanh(t_in)
            half = 0.5 * (1.0 + t_out)
            ACT[lat, :, cols] = (hidden * half).astype(BF)
            slope = half + 0.5 * hidden * (1.0 - t_out * t_out) * (
                0.7978845608028654 * (1.0 + 3.0 * 0.044715 * square)
            )
            GD[lat, :, cols] = slope.astype(BF)

        if j < 2:
            pump(11 + j)

    for ch in range(2):
        need(8 + 2 * ch)
        need(9 + 2 * ch)

        def mlp_tile(lat, n):
            total = 0.0
            for rh in range(2):
                total += dot_nn(ACT[lat, :, rh * 1024 : rh * 1024 + 1024], w_cols(8 + 2 * ch + rh, n))
            return total

        @pl.loop(0, 2)
        def _(n):
            SND[ch, :, rows_at(n, 256)] = mlp_tile(o, n)

        twin_copy(4 + ch, SND.at[ch], RCV.at[ch]).start()

        @pl.loop(0, 2)
        def _(n):
            MO[:, pl.ds(pl.multiple_of(ch * 512 + n * 256, 256), 256)] = mlp_tile(c, n)

    def received(i):
        for ch in range(2):
            twin_copy(i + ch, SND.at[ch], RCV.at[ch]).wait_recv()

    def both_parts(r):
        return MO[r, :] + jnp.concatenate([RCV[0, r, :], RCV[1, r, :]], axis=1)

    received(4)
    LOSS[...] = jnp.zeros_like(LOSS)
    GLP[...] = jnp.zeros_like(GLP)

    @pl.loop(0, TOK // TILE)
    def _(i):
        r = rows_at(i, TILE)
        mlp_out = both_parts(r)
        x1 = RSD[r, :] + mod_row(5) * mlp_out
        hat, inv = normed(x1)
        scale = 1.0 + mod_row(7)
        final_in = (hat * scale + mod_row(6)).astype(BF)
        w_lin = WLT[...]
        error = dot_nt(final_in, w_lin) - pt[1, r, :]
        LOSS[...] += fold(error * error)
        d_pred = (2.0 * error / (TOK * PDIM)).astype(BF)
        GLP[16:32, :] += dot_tn(d_pred, final_in)
        d_final = dot_nn(d_pred, w_lin)
        DACC[6] += fold(d_final)
        DACC[7] += fold(d_final * hat)
        d_x = normed_back(d_final * scale, hat, inv)
        X1[r, :] = d_x
        DACC[5] += fold(d_x * mlp_out)
        DMO[c, r, :] = (d_x * mod_row(5)).astype(BF)

    twin_copy(6, DMO.at[c], DMO.at[c]).start()

    def r1_of(k, b):
        return R1.at[k - 8, b] if k >= 8 else W.at[8 + k // 2, :, k % 2, b]

    def r2_of(k):
        return R2.at[k - 8] if k >= 8 else W.at[4 + k // 4, :, (k // 2) % 2, k % 2]

    def r3_of(k):
        return R3.at[k - 8] if k >= 8 else W.at[6 + k // 4, :, (k // 2) % 2, k % 2]

    def rows_of(u):
        return pl.ds(UNITS[u][1], UNITS[u][2])

    def g_at(u, zz, a, b):
        yy, xx = yx(a, b)
        return G.at[UNITS[u][0], zz, yy, xx, rows_of(u)]

    def b_of(far):
        return 1 - b_me if far else b_me

    def z_slot(u, i, far):
        return (r2_of if far else r3_of)(UNITS[u][0]).at[i, rows_of(u)]

    def pass_slot(u, i, far):
        return PF.at[SUM_VIA_Z.index(u)] if far else z_slot(u, i, 0)

    def s1_copy(u, b):
        k, r = UNITS[u][0], rows_of(u)
        yy, xx = yx(1 - a_me, b)
        return remote(G.at[k, :, yy, xx, r], r1_of(k, b).at[:, r], s1s.at[u * 2 + b], s1r.at[u * 2 + b], nb_a)

    def s2_copy(u):
        if u in SUM_VIA_Z:
            return remote(g_at(u, z, a_me, 1 - b_me), z_slot(u, z, 1), s2s.at[u], s2r.at[u], nb_b)
        k, r = UNITS[u][0], rows_of(u)
        yy, xx = yx(a_me, 1 - b_me)
        return remote(G.at[k, :, yy, xx, r], r2_of(k).at[:, r], s2s.at[u], s2r.at[u], nb_b)

    def line(zz):
        return dev(c, chip_of(zz, y, x))

    def sz_copy(u, dz, far):
        zt = (z + dz) % 4
        i = u * 8 + far * 4
        return remote(g_at(u, zt, a_me, b_of(far)), z_slot(u, z, far), szs.at[i + dz], szr.at[i + z], line(zt))

    def sz_wait(u, dz, far):
        frm = (z + dz) % 4
        i = u * 8 + far * 4
        remote(g_at(u, frm, a_me, b_of(far)), z_slot(u, frm, far), szs.at[i + dz], szr.at[i + frm], line(frm)).wait_recv()

    near_end = jnp.where(z < 2, 1, 2)

    def pass_copy(u, far):
        i = u * 2 + far
        return remote(g_at(u, 3 - z, a_me, b_of(far)), pass_slot(u, near_end, far), pss.at[i], psr.at[i], line(near_end))

    def sum_a(u, zz, far):
        k, r = UNITS[u][0], rows_of(u)
        b = b_of(far)
        yy, xx = yx(a_me, b)
        return G[k, zz, yy, xx, r].astype(F32) + r1_of(k, b)[zz, r].astype(F32)

    def store(u, zz, far, value):
        g_at(u, zz, a_me, b_of(far))[...] = value.astype(BF)

    def sz_start(u, far):
        for dz in (1, 3):
            alone = z != (3 if dz == 1 else 0)
            if u >= SMALL:
                sz_copy(u, dz, far).start()
            else:
                pl.when(alone)(lambda: sz_copy(u, dz, far).start())
                pl.when(jnp.logical_not(alone))(lambda: pass_copy(u, far).start())
        if u >= SMALL:
            sz_copy(u, 2, far).start()
        else:
            pl.when(jnp.logical_not(inner))(lambda: sz_copy(u, 2, far).start())

    def sz_pass(u, far):
        @pl.when(inner)
        def _():
            i = u * 2 + far
            slot = pass_slot(u, z, far)
            remote(g_at(u, z, a_me, b_of(far)), slot, pss.at[i], psr.at[i], line(z)).wait_recv()
            zt = (z + 2) % 4
            store(u, zt, far, g_at(u, zt, a_me, b_of(far))[...].astype(F32) + slot[...].astype(F32))
            sz_copy(u, 2, far).start()

    def sz_sum(u, far):
        into = FIN.at[UNITS[u][0], rows_of(u)]

        def add(dz):
            sz_wait(u, dz, far)
            into[...] += z_slot(u, (z + dz) % 4, far)[...].astype(F32)

        for dz in (1, 3, 2):
            if u >= SMALL or dz == 2:
                add(dz)
            else:
                pl.when(z != (3 if dz == 1 else 0))(lambda: add(dz))

    def s1(u):
        for b in range(2):
            s1_copy(u, b).start()

    def stage_1(u):
        for b in range(2):
            s1_copy(u, b).wait_recv()
        if u in SUM_VIA_Z:
            for far in (1, 0):
                for dz in (1, 3, 2):
                    store(u, (z + dz) % 4, far, sum_a(u, (z + dz) % 4, far))
                sz_start(u, far)
        else:
            @pl.loop(0, 4)
            def _(zz):
                store(u, zz, 1, sum_a(u, zz, 1))

            s2_copy(u).start()

    def stage_2(u):
        if u in SUM_VIA_Z:
            for far in (1, 0):
                sz_pass(u, far)
        else:
            k, r = UNITS[u][0], rows_of(u)
            s2_copy(u).wait_recv()
            for dz in (1, 3, 2):
                zt = (z + dz) % 4
                store(u, zt, 0, sum_a(u, zt, 0) + r2_of(k)[zt, r].astype(F32))
            sz_start(u, 0)
            FIN[k, r] = sum_a(u, z, 0) + r2_of(k)[z, r].astype(F32)

    def stage_3(u):
        k, r = UNITS[u][0], rows_of(u)
        if u in SUM_VIA_Z:
            FIN[k, r] = sum_a(u, z, 1)
            sz_sum(u, 1)
            store(u, z, 1, FIN[k, r])
            s2_copy(u).start()
            FIN[k, r] = sum_a(u, z, 0)
            sz_sum(u, 0)
        elif u < SMALL:
            sz_pass(u, 0)

    def stage_4(u):
        k, r = UNITS[u][0], rows_of(u)
        if u in SUM_VIA_Z:
            s2_copy(u).wait_recv()
            FIN[k, r] += z_slot(u, z, 1)[...].astype(F32)
        else:
            sz_sum(u, 0)
        total = FIN[k, r]
        SQ[...] += fold(total * total)

    def sums_done(u):
        for b in range(2):
            s1_copy(u, b).wait_send()
        s2_copy(u).wait_send()
        for far in range(2 if u in SUM_VIA_Z else 1):
            sz_copy(u, 2, far).wait_send()
            for dz in (1, 3):
                if u >= SMALL:
                    sz_copy(u, dz, far).wait_send()
                else:
                    alone = z != (3 if dz == 1 else 0)
                    pl.when(alone)(lambda: sz_copy(u, dz, far).wait_send())
                    pl.when(jnp.logical_not(alone))(lambda: pass_copy(u, far).wait_send())

    def result_copies(i):
        if i < 4:
            k = 8 + i
            src = FIN.at[k]
            dst = g_out.at[
                pl.ds(pl.multiple_of(c * 128 + (i % 2) * 64, 64), 64), pl.ds((i // 2) * 512, 512)
            ]
        elif i < 20:
            j = i - 4
            src = FIN.at[4 + j // 8 + 2 * (j % 2), :, pl.ds(((j % 8) // 2) * 128, 128)]
            dst = g_in.at[:, pl.ds(pl.multiple_of(10240 + 256 * j + c * 128, 128), 128)]
        else:
            k, r0, size = ((3, 0, 64), *UNITS[9:])[i - 20]
            src = FIN.at[k, pl.ds(r0, size)]
            dst = g_in.at[pl.ds(r0, size), pl.ds(pl.multiple_of(6144 + 1024 * k + c * 512, 512), 512)]
        return pltpu.make_async_copy(src, dst, f_l.at[i]), remote(src, dst, f_s.at[i], f_r.at[i], twin)

    def send_result(u):
        k = UNITS[u][0]
        if k >= 8:
            span = (k - 8,)
        elif k == 7:
            for half in range(2):
                for q in range(4):
                    cols = slice(q * 128, q * 128 + 128)
                    low, high = FIN[4 + half, :, cols], FIN[6 + half, :, cols]
                    FIN[4 + half, :, cols] = jnp.concatenate([low[:, 0:64], high[:, 0:64]], axis=1)
                    FIN[6 + half, :, cols] = jnp.concatenate([low[:, 64:128], high[:, 64:128]], axis=1)
            span = range(4, 20)
        elif k >= 4:
            span = ()
        else:
            span = (20 + u - 8,)
        for i in span:
            for copy in result_copies(i):
                copy.start()

    def step(t):
        for u in range(t + LEAD, NU):
            if u == t + LEAD and u <= 11 or t + LEAD == 11:
                if u == 4:
                    pl.semaphore_wait(cred_a, 1)
                s1(u)
        if t == 4:
            pl.semaphore_wait(cred_b, 1)
            pl.semaphore_wait(cred_z, 3)
        for stage, lag in zip((stage_1, stage_2, stage_3, stage_4), LAGS):
            if 0 <= t - lag < NU:
                stage(t - lag)
                if stage is stage_4:
                    send_result(t - lag)

    def grad_tiles(k, left, right):
        @pl.loop(0, 4)
        def _(r):
            G[k, r] = dot_tn(left(r), right).astype(BF).reshape(2, 2, 64, 512)

    SQ[...] = jnp.zeros_like(SQ)
    twin_copy(6, DMO.at[o], DMO.at[o]).wait_recv()
    for ch in range(2):
        for rh in range(2):
            k = 8 + 2 * ch + rh
            grad_tiles(
                k,
                lambda r: ACT[:, :, pl.ds(pl.multiple_of(rh * 1024 + r * 256, 256), 256)].reshape(512, 256),
                DMO[:, :, ch * 512 : ch * 512 + 512].reshape(512, 512),
            )
            if 2 * ch + rh < LEAD:
                s1(2 * ch + rh)

    for k in range(CHUNKS):
        sends_done(k)

    @pl.loop(0, 16)
    def _(t):
        lat, rh, r = t // 8, (t // 4) % 2, t % 4
        total = 0.0
        for ch in range(2):
            total += dot_nt(DMO[lat, :, ch * 512 : ch * 512 + 512], W[8 + 2 * ch + rh, r].reshape(256, 512))
        cols = pl.ds(pl.multiple_of(rh * 1024 + r * 256, 256), 256)
        GD[lat, :, cols] = (total * GD[lat, :, cols].astype(F32)).astype(BF)

    pl.semaphore_signal(cred_a, 1, device_id=nb_a, device_id_type=MESH)

    def data_back(first_k, count, left, i):
        for ch in range(2):
            @pl.loop(0, 2)
            def _(n):
                total = 0.0
                for j in range(count):
                    total += dot_nt(left(j, o), W[first_k + j, 2 * ch + n].reshape(256, 512))
                SND[ch, :, rows_at(n, 256)] = total

            twin_copy(i + ch, SND.at[ch], RCV.at[ch]).start()

        @pl.loop(0, 4)
        def _(r):
            total = 0.0
            for j in range(count):
                total += dot_nt(left(j, c), W[first_k + j, r].reshape(256, 512))
            MO[:, rows_at(r, 256)] = total

    for ch in range(2):
        twin_copy(4 + ch, SND.at[ch], RCV.at[ch]).wait_send()
    data_back(4, 4, lambda j, lat: GD[lat, :, j * 512 : j * 512 + 512], 7)
    pl.semaphore_signal(cred_b, 1, device_id=nb_b, device_id_type=MESH)
    for dz in range(1, 4):
        pl.semaphore_signal(cred_z, 1, device_id=dev(c, chip_of((z + dz) % 4, y, x)), device_id_type=MESH)

    step(0)
    for j in range(4):
        grad_tiles(
            4 + j,
            lambda r: MLI[:, :, rows_at(r, 256)].reshape(512, 256),
            GD[:, :, j * 512 : j * 512 + 512].reshape(512, 512),
        )
    received(7)

    @pl.loop(0, TOK // TILE)
    def _(i):
        r = rows_at(i, TILE)
        d_in = both_parts(r)
        hat, inv = normed(RSD[r, :])
        DACC[3] += fold(d_in)
        DACC[4] += fold(d_in * hat)
        d_x = normed_back(d_in * (1.0 + mod_row(4)), hat, inv) + X1[r, :]
        X1[r, :] = d_x
        DACC[2] += fold(d_x * AO[r, :])
        DAO[c, r, :] = (d_x * mod_row(2)).astype(BF)

    dao_other = pl.ds(pl.multiple_of(o * 512, 512), 512)
    dao_mine = pl.ds(pl.multiple_of(c * 512, 512), 512)
    twin_copy(9, DAO.at[c, :, dao_other], DAO.at[c, :, dao_other]).start()

    def mixed_back(hh, n):
        w_mine = W[3, 2 * hh + n].reshape(256, 512)
        w_other = WP[2 * hh + n].reshape(256, 512)
        return (dot_nt(DAO[c, :, dao_mine], w_mine) + dot_nt(DAO[c, :, dao_other], w_other)).astype(BF)

    @pl.loop(0, 2)
    def _(n):
        DMS[:, rows_at(n, 256)] = mixed_back(o, n)

    twin_copy(10, DMS, DMX.at[c]).start()

    @pl.loop(0, 2)
    def _(n):
        DMX[c, :, rows_at(n, 256)] = mixed_back(c, n)

    step(1)
    twin_copy(9, DAO.at[o, :, dao_mine], DAO.at[o, :, dao_mine]).wait_recv()

    @pl.loop(0, 4)
    def _(r):
        left = MIX[r // 2, :, :, rows_at(r % 2, 256)].reshape(512, 256)
        G[3, r] = dot_tn(left, DAO[:, :, dao_mine].reshape(512, 512)).astype(BF).reshape(2, 2, 64, 512)

    twin_copy(10, DMS, DMX.at[o]).wait_recv()

    def attention_back(t):
        lat, cols = t // 4, rows_at(t % 4, 128)
        q, k, v = QKV[0, lat, :, cols], QKV[1, lat, :, cols], QKV[2, lat, :, cols]
        dm = DMX[lat, :, cols]
        res = []
        for m in masks:
            probs = probs_of(q * m, k)
            d_probs = dot_nt(dm * m, v)
            d_v = dot_tn(probs.astype(BF), dm)
            d_s = probs * (d_probs - jnp.sum(d_probs * probs, axis=-1, keepdims=True))
            d_s = (d_s * 0.125).astype(BF)
            res.append((dot_nn(d_s, k), dot_tn(d_s, q), d_v))
        for j in range(3):
            QKV[j, lat, :, cols] = jnp.where(first, res[0][j], res[1][j]).astype(BF)

    for half in range(2):
        pl.loop(4 * half, 4 * half + 4)(attention_back)
        step(2 + half)
    for ch in range(2):
        twin_copy(7 + ch, SND.at[ch], RCV.at[ch]).wait_send()
    data_back(0, 3, lambda j, lat: QKV[j, lat], 11)
    for j in range(3):
        grad_tiles(
            j,
            lambda r: ATI[:, :, rows_at(r, 256)].reshape(512, 256),
            QKV[j].reshape(512, 512),
        )
    received(11)

    @pl.loop(0, TOK // TILE)
    def _(i):
        r = rows_at(i, TILE)
        d_in = both_parts(r)
        hat, inv = normed(X0[r, :])
        DACC[0] += fold(d_in)
        DACC[1] += fold(d_in * hat)
        d_x = normed_back(d_in * (1.0 + mod_row(1)), hat, inv) + X1[r, :]
        GLP[0:16, :] += dot_tn(pt[0, r, :].astype(BF), d_x.astype(BF))

    for k in range(8):
        MODS[k : k + 1, :] = jnp.sum(DACC[k], axis=0, keepdims=True)
    d_mods = MODS[...]
    DMB[c, s] = jnp.concatenate([d_mods[:, :512], d_mods[:, 512:]], axis=0).astype(BF)
    peers_send(3, lambda p: DMB.at[c, s], DMB.at[c])
    for q in range(16):
        cols = slice(q * 64, q * 64 + 64)
        B3S[q] = jnp.concatenate([GLP[0:16, cols], GLP[16:32, cols]], axis=1).astype(BF)
    B3R[s] = B3S[s]
    peers_send(4, lambda p: B3S.at[p], B3R)
    step(4)
    step(5)
    step(6)
    peers_wait(3, lambda p: DMB.at[c, s], DMB.at[c])
    twin_copy(13, DMB.at[c], DMB.at[c]).start()

    def unpack(g):
        @pl.loop(0, 16)
        def _(l):
            both = DMB[g, l].astype(F32)
            DMF[g, :, l, 0:512] = both[0:8]
            DMF[g, :, l, 512:1024] = both[8:16]

    unpack(c)
    d_cond_low = 0.0
    for k in range(8):
        w_k = WMOD[:, k * 1024 : k * 1024 + 1024] if k < 6 else EX[:, (k - 5) * 1024 : (k - 4) * 1024]
        d_cond_low += dot_nt(DMF[c, k].astype(BF), w_k.astype(BF))
    d_cond = d_cond_low * silu_slope(CND[1])
    CP[c, 2, :, 0:64] = d_cond
    d_temb = d_cond.astype(BF).astype(F32)
    B2S[...] = to_tile(d_temb)
    B2R[s] = B2S[...]
    peers_send(5, lambda p: B2S, B2R)
    step(7)
    peers_wait(4, lambda p: B3S.at[p], B3R)
    sums = B3R[0].astype(F32)
    for i in range(1, 16):
        sums += B3R[i].astype(F32)
    B3D[c] = sums
    twin_copy(14, B3D.at[c], B3D.at[c]).start()
    peers_wait(5, lambda p: B2S, B2R)
    for q in range(8):
        DTA[c, :, q * 128 : q * 128 + 128] = jnp.concatenate(
            [from_tile(B2R[2 * q]), from_tile(B2R[2 * q + 1])], axis=1
        )
    d_tact = dot_nt(DTA[c].astype(BF), EX[:, 0:1024].astype(BF))
    CP[c, 3, :, 0:64] = (d_tact * silu_slope(CND[0])).astype(BF).astype(F32)
    twin_copy(15, DTA.at[c], DTA.at[c]).start()
    twin_copy(16, CP.at[c], CP.at[c]).start()
    twin_copy(17, E1.at[c], E1.at[c]).start()
    step(8)
    twin_copy(13, DMB.at[o], DMB.at[o]).wait_recv()
    unpack(o)
    twin_copy(14, B3D.at[o], B3D.at[o]).wait_recv()
    twin_copy(15, DTA.at[o], DTA.at[o]).wait_recv()
    twin_copy(16, CP.at[o], CP.at[o]).wait_recv()
    twin_copy(17, E1.at[o], E1.at[o]).wait_recv()

    def packed(i):
        return jnp.concatenate([CP[0, i, :, 0:64], CP[1, i, :, 0:64]], axis=0)

    def square_half(value):
        part = 0.5 * value * value
        return jnp.sum(jnp.sum(part, axis=0, keepdims=True), axis=1, keepdims=True)

    cond_both = packed(0).astype(BF)
    small = jnp.zeros((1, 1), F32)
    for k in range(8):
        grad = dot_tn(cond_both, jnp.concatenate([DMF[0, k], DMF[1, k]], axis=0).astype(BF))
        small += square_half(grad)
        if k < 6:
            WMOD[:, k * 1024 : k * 1024 + 1024] = grad
        else:
            EX[:, (k - 5) * 1024 : (k - 4) * 1024] = grad
    mod_out = pltpu.make_async_copy(WMOD, g_in.at[:, pl.ds(0, 6144)], st_sem.at[26])
    mod_out.start()
    step(9)
    grad = dot_tn(packed(1).astype(BF), jnp.concatenate([DTA[0], DTA[1]], axis=0).astype(BF))
    small += square_half(grad)
    EX[:, 0:1024] = grad
    sums = B3D[0] + B3D[1]
    small += square_half(sums[:, 64:128])
    wide = jnp.concatenate(
        [sums, jnp.zeros((112, 128), F32)], axis=0
    )
    EX[:, 3072:3088] = wide.T[64:128, 0:16]
    def both(value):
        return jnp.concatenate([value(0), value(1)], axis=0)

    index = lax.broadcasted_iota(jnp.int32, (32, ENTRIES), 1)
    hot = (both(lambda g: E1[g, :, 2, 0:1]).astype(jnp.int32) + PDIM == index).astype(F32)
    grad = dot_tn_exact(packed(2), hot)
    spot = lax.broadcasted_iota(jnp.int32, (16, ENTRIES), 0) == index[0:16]
    grad += dot_tn_exact(sums[:, 0:64], spot.astype(F32))
    ENT[...] = grad
    femb = both(lambda g: jnp.concatenate([E1[g, :, 0, :], E1[g, :, 1, :]], axis=1)).astype(BF)
    ENT[:, PDIM + NCLS :] = dot_tn(packed(3).astype(BF), femb)
    small += square_half(ENT[...])

    for t in range(10, NU + LAGS[3]):
        step(t)

    def total_of(value):
        return jnp.sum(jnp.sum(value, axis=0, keepdims=True), axis=1, keepdims=True)

    NSS[0:1, :] = jnp.broadcast_to(total_of(SQ[...]) + small, (1, 128))
    NSS[1:2, :] = jnp.broadcast_to(total_of(LOSS[...]) / (TOK * PDIM), (1, 128))
    NSS[2:8, :] = jnp.zeros((6, 128), F32)
    NSR[c * 16 + s] = NSS[...]

    def far_copy(k, frm):
        return remote(NSS, NSR.at[frm], far_s.at[k], far_r.at[frm % 16], dev(o, k))

    @pl.loop(0, 16)
    def _(k):
        far_copy(k, c * 16 + s).start()

    mine = NSR.at[pl.ds(c * 16, 16)]
    peers_send(6, lambda p: NSS, mine)
    peers_wait(6, lambda p: NSS, mine)

    @pl.loop(0, 16)
    def _(k):
        far_copy(k, o * 16 + k).wait()

    stats[...] = jnp.sum(NSR[...], axis=0)

    mod_out.wait()
    for i in range(27):
        for copy in result_copies(i):
            copy.wait()
    for u in range(NU):
        sums_done(u)
    twin_copy(0, ATI.at[c], ATI.at[c]).wait_send()
    twin_copy(1, MIX.at[c], MIX.at[c]).wait_send()
    twin_copy(2, W.at[3], WP).wait_send()
    twin_copy(3, MLI.at[c], MLI.at[c]).wait_send()
    twin_copy(6, DMO.at[c], DMO.at[c]).wait_send()
    twin_copy(9, DAO.at[c, :, dao_other], DAO.at[c, :, dao_other]).wait_send()
    twin_copy(10, DMS, DMX.at[c]).wait_send()
    for ch in range(2):
        twin_copy(11 + ch, SND.at[ch], RCV.at[ch]).wait_send()
    twin_copy(13, DMB.at[c], DMB.at[c]).wait_send()
    twin_copy(14, B3D.at[c], B3D.at[c]).wait_send()
    twin_copy(15, DTA.at[c], DTA.at[c]).wait_send()
    twin_copy(16, CP.at[c], CP.at[c]).wait_send()
    twin_copy(17, E1.at[c], E1.at[c]).wait_send()


def fused_step(msg, edge, pt, pos, block_in, block_out, entry, exit_):
    vm = pltpu.VMEM
    dma = pltpu.SemaphoreType.DMA
    scratch = [
        vm((12, 4, 2, 2, 64, 512), BF), vm((4, 2, 2, 64, 512), BF), vm((12, 4, 2, 2, 64, 512), BF),
        vm((4, 2, 4, 64, 512), BF), vm((4, 4, 64, 512), BF), vm((4, 4, 64, 512), BF),
        vm((len(SUM_VIA_Z), 64, 512), BF), vm((12, 64, 512), F32),
        vm((2, TOK, 1024), BF), vm((3, 2, TOK, 512), BF), vm((2, 2, TOK, 512), BF), vm((2, TOK, 1024), BF),
        vm((2, TOK, 2048), BF), vm((2, TOK, 2048), BF), vm((2, TOK, 1024), BF), vm((2, TOK, 1024), BF),
        vm((2, TOK, 512), BF), vm((TOK, 512), BF),
        *[vm((TOK, 1024), F32)] * 5, vm((2, TOK, 512), F32), vm((2, TOK, 512), F32),
        vm((64, 6144), F32), vm((2, 16, 8, 128), F32), vm((16, 16, 128), BF), vm((16, 8, 128), F32), vm((16, 8, 128), F32),
        vm((16, 16, 512), BF), vm((16, 16, 512), BF), vm((2, 16, 16, 512), BF), vm((2, 8, 16, 1024), F32),
        vm((8, 128), F32), vm((16, 8, 128), F32), vm((2, 16, 1024), F32), vm((2, 4, 16, 128), F32), vm((2, 16, 64), F32),
        vm((16, 16, 128), BF), vm((16, 16, 128), BF), vm((2, 16, 128), F32),
        vm((8, 128), F32), vm((32, 8, 128), F32),
        vm((8, 1024), F32), vm((8, 8, 1024), F32), vm((16, 1024), BF), vm((16, 1024), BF), vm((32, 1024), F32),
        vm((8, 512), F32), vm((8, 16), F32),
        dma((27,)), dma((8, 16)), dma((8, 16)), dma((96,)), dma((96,)), dma((48,)), dma((48,)), dma((96,)), dma((96,)),
        dma((30,)), dma((30,)), dma((15,)), dma((15,)), dma((120,)), dma((120,)), dma((30,)), dma((30,)), dma((19,)), dma((19,)),
        dma((27,)), dma((27,)), dma((27,)), dma((16,)), dma((16,)),
        pltpu.SemaphoreType.REGULAR, pltpu.SemaphoreType.REGULAR, pltpu.SemaphoreType.REGULAR,
    ]
    any_ = pl.BlockSpec(memory_space=pl.ANY)
    vmem = pl.BlockSpec(memory_space=pltpu.VMEM)
    shape = jax.ShapeDtypeStruct
    return pl.pallas_call(
        step_kernel,
        out_shape=(
            shape(block_in.shape, F32), shape(block_out.shape, F32), shape(entry.shape, F32),
            shape(exit_.shape, F32), shape((8, 128), F32),
        ),
        in_specs=[vmem, vmem, vmem, vmem, any_, any_, any_, any_],
        out_specs=(any_, any_, vmem, vmem, vmem),
        scratch_shapes=scratch,
        compiler_params=pltpu.CompilerParams(
            collective_id=0, has_side_effects=True, vmem_limit_bytes=62 * 2**20
        ),
        cost_estimate=pl.CostEstimate(flops=21 * 10**9, bytes_accessed=20 * 10**6, transcendentals=4 * 10**6),
    )(msg, edge, pt, pos, block_in, block_out, entry, exit_)


def local_fused(
    noisy, timesteps, labels, noise,
    block_in, block_in_first, block_in_second,
    block_out, block_out_first, block_out_second,
    entry_table, entry_first, entry_second,
    exit_proj, exit_first, exit_second,
):
    index = lax.axis_index("rep") * 16 + lax.axis_index("shard")
    femb = lowered(time_features(timesteps, FREQ)).astype(F32).reshape(2, LANES)
    label = labels.astype(F32)[0]
    lane = jnp.arange(LANES)[None, :]
    head = jnp.concatenate(
        [femb, jnp.full((1, LANES), label), jnp.where(lane == index, label, 0.0), jnp.zeros((4, LANES), F32)], axis=0
    )
    edge = jnp.concatenate([entry_table[:PDIM], exit_proj[:, 3 * D :].T], axis=1)
    pt = patchify(jnp.concatenate([noisy, noise], axis=0), PATCH)
    grid = noisy.shape[-1] // PATCH
    pos = position_table(grid, D)[:grid, : D // 2]
    g_in, g_out, g_entry, g_exit, stats = fused_step(
        head, lowered(edge), pt, pos, block_in[0], block_out[0], entry_table.T, exit_proj
    )
    loss = stats[1, 0]
    grad_norm = jnp.sqrt(stats[0, 0])
    factor = clip_limit / jnp.maximum(grad_norm, clip_limit)
    outs = [loss, grad_norm]
    for weight, first, second, grad, rate in (
        (block_in, block_in_first, block_in_second, g_in[None], rate_main),
        (block_out, block_out_first, block_out_second, g_out[None], rate_main),
        (entry_table, entry_first, entry_second, g_entry.T, rate_edge),
        (exit_proj, exit_first, exit_second, g_exit, rate_main),
    ):
        outs.extend(adam_step(weight, first, second, grad, factor, rate))
    return tuple(outs)


def solution(mesh):
    step = local_fused if dict(mesh.shape) == {"rep": 2, "shard": 16} else local
    in_specs = (
        P(("rep", "shard"), None, None, None),
        P(("rep", "shard")),
        P(("rep", "shard")),
        P(("rep", "shard"), None, None, None),
        P(None, "shard", None),
        P(None, "shard", None),
        P(None, "shard", None),
        P(None, "shard", None),
        P(None, "shard", None),
        P(None, "shard", None),
        P(None, "shard"),
        P(None, "shard"),
        P(None, "shard"),
        P("shard", None),
        P("shard", None),
        P("shard", None),
    )
    out_specs = (
        P(),
        P(),
        P(None, "shard", None),
        P(None, "shard", None),
        P(None, "shard", None),
        P(None, "shard", None),
        P(None, "shard", None),
        P(None, "shard", None),
        P(None, "shard", None),
        P(None, "shard", None),
        P(None, "shard"),
        P(None, "shard"),
        P(None, "shard"),
        P(None, "shard"),
        P("shard", None),
        P("shard", None),
        P("shard", None),
        P("shard", None),
    )
    return jax.shard_map(step, mesh=mesh, in_specs=in_specs, out_specs=out_specs, check_vma=False)
```

```python
import jax
import jax.numpy as jnp
import numpy as np
from jax import lax
from jax.experimental import pallas as pl
from jax.experimental.pallas import tpu as pltpu
from jax.sharding import PartitionSpec as P

D = 1024
HEADS = 16
PATCH = 2
NCLS = 1000
FREQ = 256
STEP = 10
PDIM = 16
ENTRIES = PDIM + NCLS + FREQ


clip_limit = 0.5
rate_main = 0.02
rate_edge = 0.1
decay_rate = 0.01
adam_eps = 1e-08
highest = lax.Precision.HIGHEST


def lowered(value):
    return value.astype(jnp.bfloat16)


def product(left, right):
    return jnp.dot(left, right, preferred_element_type=jnp.float32)


def product_tn(left, right):
    return lax.dot_general(
        left, right, (((0,), (0,)), ((), ())), preferred_element_type=jnp.float32
    )


def product_nt(left, right):
    return lax.dot_general(
        left, right, (((1,), (1,)), ((), ())), preferred_element_type=jnp.float32
    )


def patchify(image, patch):
    batch, chans, height, width = image.shape
    grid = height // patch
    parts = image.reshape(batch, chans, grid, patch, grid, patch)
    parts = parts.transpose(0, 2, 4, 3, 5, 1)
    return parts.reshape(batch, grid * grid, patch * patch * chans)


def position_table(grid, width):
    quarter = width // 4
    omega = 1.0 / 10000.0 ** (jnp.arange(quarter, dtype=jnp.float32) / quarter)
    index = jnp.arange(grid * grid)
    row_pos = (index // grid).astype(jnp.float32)[:, None] * omega[None, :]
    col_pos = (index % grid).astype(jnp.float32)[:, None] * omega[None, :]
    return jnp.concatenate(
        [jnp.sin(col_pos), jnp.cos(col_pos), jnp.sin(row_pos), jnp.cos(row_pos)], axis=1
    )


def time_features(steps, size):
    half = size // 2
    freqs = jnp.exp(-jnp.log(10000.0) * jnp.arange(half, dtype=jnp.float32) / half)
    angles = steps.astype(jnp.float32)[:, None] * freqs[None, :]
    return jnp.concatenate([jnp.cos(angles), jnp.sin(angles)], axis=1)


def modulate(x, shift, scale):
    centered = x - jnp.mean(x, axis=-1, keepdims=True)
    var = jnp.mean(centered * centered, axis=-1, keepdims=True)
    normed = centered * lax.rsqrt(var + 1e-06)
    return normed * (1.0 + scale[:, None, :]) + shift[:, None, :]


def gelu_tanh(value):
    return jax.nn.gelu(value, approximate=True)


def adam_step(weight, first, second, grad, factor, rate):
    clipped = grad * factor
    first_new = 0.5 * first + 0.5 * clipped
    second_new = 0.5 * second + 0.5 * clipped * clipped
    corr = 1.0 - 0.5**STEP
    update = first_new / corr / (jnp.sqrt(second_new / corr) + adam_eps) + decay_rate * weight
    weight_new = weight - rate * update
    return (weight_new, first_new, second_new, weight_new.astype(jnp.bfloat16))


def layer_parts(x, cond_low, w_in, w_out):
    width = x.shape[-1]
    batch, seq = (x.shape[0], x.shape[1])
    size = width // HEADS
    mod = product(cond_low, w_in[:, : 6 * width])
    shift_a, scale_a, gate_a, shift_b, scale_b, gate_b = jnp.split(mod, 6, axis=-1)
    attn_in = lowered(modulate(x, shift_a, scale_a))
    qkv = lowered(
        jnp.einsum(
            "bsd,de->bse",
            attn_in,
            w_in[:, 6 * width : 9 * width],
            preferred_element_type=jnp.float32,
        )
    )
    query = qkv[..., :width].reshape(batch, seq, HEADS, size)
    keys = qkv[..., width : 2 * width].reshape(batch, seq, HEADS, size)
    values = qkv[..., 2 * width :].reshape(batch, seq, HEADS, size)
    scores = jnp.einsum(
        "bqhd,bkhd->bhqk", query, keys, preferred_element_type=jnp.float32
    ) * size ** (-0.5)
    weights = jax.nn.softmax(scores, axis=-1)
    weights_low = lowered(weights)
    mixed = lowered(
        jnp.einsum("bhqk,bkhd->bqhd", weights_low, values, preferred_element_type=jnp.float32)
    ).reshape(batch, seq, width)
    attn_out = jnp.einsum(
        "bsd,de->bse", mixed, w_in[:, 9 * width : 10 * width], preferred_element_type=jnp.float32
    )
    resid = x + gate_a[:, None, :] * attn_out
    mlp_in = lowered(modulate(resid, shift_b, scale_b))
    hidden = jnp.einsum(
        "bsd,df->bsf", mlp_in, w_in[:, 10 * width :], preferred_element_type=jnp.float32
    )
    active = lowered(gelu_tanh(hidden))
    mlp_out = jnp.einsum("bsf,fd->bsd", active, w_out, preferred_element_type=jnp.float32)
    result = resid + gate_b[:, None, :] * mlp_out
    return dict(
        mods=(shift_a, scale_a, gate_a, shift_b, scale_b, gate_b),
        attn_in=attn_in,
        query=query,
        keys=keys,
        values=values,
        weights=weights,
        weights_low=weights_low,
        mixed=mixed,
        attn_out=attn_out,
        resid=resid,
        mlp_in=mlp_in,
        hidden=hidden,
        active=active,
        mlp_out=mlp_out,
        result=result,
    )


def layer_back(x, cond_low, w_in, w_out, parts, grad_out, grad_cond):
    width = x.shape[-1]
    batch, seq = (x.shape[0], x.shape[1])
    size = width // HEADS
    shift_a, scale_a, gate_a, shift_b, scale_b, gate_b = parts["mods"]
    d_gate_b = jnp.sum(grad_out * parts["mlp_out"], axis=1)
    d_mlp_out = lowered(grad_out * gate_b[:, None, :])
    g_fc2 = jnp.einsum(
        "bsf,bsd->fd", parts["active"], d_mlp_out, preferred_element_type=jnp.float32
    )
    d_active = jnp.einsum("bsd,fd->bsf", d_mlp_out, w_out, preferred_element_type=jnp.float32)
    _, gelu_pull = jax.vjp(gelu_tanh, parts["hidden"])
    d_hidden = lowered(gelu_pull(d_active)[0])
    g_fc1 = jnp.einsum("bsd,bsf->df", parts["mlp_in"], d_hidden, preferred_element_type=jnp.float32)
    d_mlp_in = jnp.einsum(
        "bsf,df->bsd", d_hidden, w_in[:, 10 * width :], preferred_element_type=jnp.float32
    )
    _, norm_pull = jax.vjp(modulate, parts["resid"], shift_b, scale_b)
    d_resid, d_shift_b, d_scale_b = norm_pull(d_mlp_in)
    d_resid = d_resid + grad_out
    d_gate_a = jnp.sum(d_resid * parts["attn_out"], axis=1)
    d_attn_out = lowered(d_resid * gate_a[:, None, :])
    g_proj = jnp.einsum(
        "bsd,bse->de", parts["mixed"], d_attn_out, preferred_element_type=jnp.float32
    )
    d_mixed = lowered(
        jnp.einsum(
            "bse,de->bsd",
            d_attn_out,
            w_in[:, 9 * width : 10 * width],
            preferred_element_type=jnp.float32,
        )
    ).reshape(batch, seq, HEADS, size)
    d_probs = jnp.einsum(
        "bqhd,bkhd->bhqk", d_mixed, parts["values"], preferred_element_type=jnp.float32
    )
    d_values = jnp.einsum(
        "bhqk,bqhd->bkhd", parts["weights_low"], d_mixed, preferred_element_type=jnp.float32
    )
    weights = parts["weights"]
    d_scores = weights * (d_probs - jnp.sum(d_probs * weights, axis=-1, keepdims=True))
    d_scaled = lowered(d_scores * size ** (-0.5))
    d_query = jnp.einsum(
        "bhqk,bkhd->bqhd", d_scaled, parts["keys"], preferred_element_type=jnp.float32
    )
    d_keys = jnp.einsum(
        "bhqk,bqhd->bkhd", d_scaled, parts["query"], preferred_element_type=jnp.float32
    )
    d_qkv = lowered(
        jnp.concatenate(
            [
                d_query.reshape(batch, seq, width),
                d_keys.reshape(batch, seq, width),
                d_values.reshape(batch, seq, width),
            ],
            axis=-1,
        )
    )
    g_qkv = jnp.einsum("bsd,bse->de", parts["attn_in"], d_qkv, preferred_element_type=jnp.float32)
    d_attn_in = jnp.einsum(
        "bse,de->bsd", d_qkv, w_in[:, 6 * width : 9 * width], preferred_element_type=jnp.float32
    )
    _, first_pull = jax.vjp(modulate, x, shift_a, scale_a)
    d_x, d_shift_a, d_scale_a = first_pull(d_attn_in)
    d_x = d_x + d_resid
    d_mod = lowered(
        jnp.concatenate([d_shift_a, d_scale_a, d_gate_a, d_shift_b, d_scale_b, d_gate_b], axis=-1)
    )
    g_mod = product_tn(cond_low, d_mod)
    grad_cond = grad_cond + product_nt(d_mod, w_in[:, : 6 * width])
    g_in = jnp.concatenate([g_mod, g_qkv, g_proj, g_fc1], axis=1)
    return (d_x, grad_cond, g_in, g_fc2)


def local(
    noisy,
    timesteps,
    labels,
    noise,
    block_in,
    block_in_first,
    block_in_second,
    block_out,
    block_out_first,
    block_out_second,
    entry_table,
    entry_first,
    entry_second,
    exit_proj,
    exit_first,
    exit_second,
):
    layers = block_in.shape[0]
    entry_all, exit_all = (
        lax.all_gather(lowered(entry_table), "shard", axis=1, tiled=True),
        lax.all_gather(lowered(exit_proj), "shard", axis=0, tiled=True),
    )
    w_patch = entry_all[:PDIM]
    w_label = entry_all[PDIM : PDIM + NCLS]
    w_time = entry_all[PDIM + NCLS :]
    w_time2 = exit_all[:, :D]
    w_final = exit_all[:, D : 3 * D]
    w_output = exit_all[:, 3 * D :]
    patches = lowered(patchify(noisy, PATCH))
    target = patchify(noise, PATCH)
    seq = patches.shape[1]
    x = (
        jnp.einsum("bsp,pd->bsd", patches, w_patch, preferred_element_type=jnp.float32)
        + position_table(noisy.shape[-1] // PATCH, D)[None]
    )
    femb = lowered(time_features(timesteps, FREQ))
    t_hidden = product(femb, w_time)
    t_act = lowered(jax.nn.silu(t_hidden))
    temb = product(t_act, w_time2)
    onehot = (labels[:, None] == jnp.arange(NCLS)[None, :]).astype(jnp.float32)
    cond = temb + jnp.dot(onehot, w_label.astype(jnp.float32), precision=highest)
    cond_low = lowered(jax.nn.silu(cond))
    layer = 0
    w_in_all = lax.all_gather(lowered(block_in[layer]), "shard", axis=0, tiled=True)
    w_out_all = lax.all_gather(lowered(block_out[layer]), "shard", axis=0, tiled=True)
    inputs = [x]
    parts = layer_parts(x, cond_low, w_in_all, w_out_all)
    saved = [parts]
    x = parts["result"]
    final_mod = product(cond_low, w_final)
    shift_f, scale_f = jnp.split(final_mod, 2, axis=-1)
    final_in = lowered(modulate(x, shift_f, scale_f))
    pred = jnp.einsum("bsd,dp->bsp", final_in, w_output, preferred_element_type=jnp.float32)
    error = pred - target
    loss_part = jnp.sum(error * error) / (seq * PDIM)
    d_pred = lowered(2.0 * error / (seq * PDIM))
    g_output = jnp.einsum("bsd,bsp->dp", final_in, d_pred, preferred_element_type=jnp.float32)
    d_final_in = jnp.einsum("bsp,dp->bsd", d_pred, w_output, preferred_element_type=jnp.float32)
    _, final_pull = jax.vjp(modulate, x, shift_f, scale_f)
    d_x, d_shift_f, d_scale_f = final_pull(d_final_in)
    d_fmod = lowered(jnp.concatenate([d_shift_f, d_scale_f], axis=-1))
    g_final = product_tn(cond_low, d_fmod)
    grad_cond = product_nt(d_fmod, w_final)
    shards_in = [None] * layers
    shards_out = [None] * layers
    for layer in reversed(range(layers)):
        w_in_all, w_out_all = (
            lax.all_gather(lowered(block_in[layer]), "shard", axis=0, tiled=True),
            lax.all_gather(lowered(block_out[layer]), "shard", axis=0, tiled=True),
        )
        d_x, grad_cond, g_in, g_fc2 = layer_back(
            inputs[layer], cond_low, w_in_all, w_out_all, saved[layer], d_x, grad_cond
        )
        shards_in[layer], shards_out[layer] = (
            lax.psum_scatter(g_in, "shard", scatter_dimension=0, tiled=True),
            lax.psum_scatter(g_fc2, "shard", scatter_dimension=0, tiled=True),
        )
    _, silu_pull = jax.vjp(jax.nn.silu, cond)
    d_cond = silu_pull(grad_cond)[0]
    g_label = jnp.dot(onehot.T, d_cond, precision=highest)
    d_temb = lowered(d_cond)
    g_time2 = product_tn(t_act, d_temb)
    d_tact = product_nt(d_temb, w_time2)
    _, time_pull = jax.vjp(jax.nn.silu, t_hidden)
    d_thidden = lowered(time_pull(d_tact)[0])
    g_time = product_tn(femb, d_thidden)
    g_patch = jnp.einsum("bsp,bsd->pd", patches, lowered(d_x), preferred_element_type=jnp.float32)
    g_entry = jnp.concatenate([g_patch, g_label, g_time], axis=0)
    g_exit = jnp.concatenate([g_time2, g_final, g_output], axis=1)
    share_entry, share_exit = (
        lax.psum_scatter(g_entry, "shard", scatter_dimension=1, tiled=True),
        lax.psum_scatter(g_exit, "shard", scatter_dimension=0, tiled=True),
    )
    grads = (
        lax.psum(jnp.stack(shards_in).astype(jnp.bfloat16), "rep").astype(jnp.float32),
        lax.psum(jnp.stack(shards_out).astype(jnp.bfloat16), "rep").astype(jnp.float32),
        lax.psum(share_entry.astype(jnp.bfloat16), "rep").astype(jnp.float32),
        lax.psum(share_exit.astype(jnp.bfloat16), "rep").astype(jnp.float32),
    )
    squares = (
        jnp.sum(grads[0] * grads[0])
        + jnp.sum(grads[1] * grads[1])
        + jnp.sum(grads[2] * grads[2])
        + jnp.sum(grads[3] * grads[3])
    )
    loss = lax.psum(loss_part, ("rep", "shard"))
    norm_sq = lax.psum(squares, "shard")
    grad_norm = jnp.sqrt(norm_sq)
    factor = clip_limit / jnp.maximum(grad_norm, clip_limit)
    bi_w, bi_m, bi_v, bi_l = adam_step(
        block_in, block_in_first, block_in_second, grads[0], factor, rate_main
    )
    bo_w, bo_m, bo_v, bo_l = adam_step(
        block_out, block_out_first, block_out_second, grads[1], factor, rate_main
    )
    en_w, en_m, en_v, en_l = adam_step(
        entry_table, entry_first, entry_second, grads[2], factor, rate_edge
    )
    ex_w, ex_m, ex_v, ex_l = adam_step(
        exit_proj, exit_first, exit_second, grads[3], factor, rate_main
    )
    return (
        loss,
        grad_norm,
        bi_w,
        bi_m,
        bi_v,
        bi_l,
        bo_w,
        bo_m,
        bo_v,
        bo_l,
        en_w,
        en_m,
        en_v,
        en_l,
        ex_w,
        ex_m,
        ex_v,
        ex_l,
    )


BF = jnp.bfloat16
F32 = jnp.float32
MESH = pl.DeviceIdType.MESH
TOK = 256
TILE = 128
LANES = 128
CHUNKS = 12
START = (4, 2)
OWN_AT = ((), (4,), (5, 6), (7, 8), (9, 10), (11,))
Z_AT = ((2,), (3,), (4,), (5,), (6, 7), (8,), (9,), (10,), (11,))
VIA_Z = (1, 3, 5, 7, 9, 11)
SUM_VIA_Z = (0, 2, 4, 6, 8)
LEAD = 3
LAGS = (0, 2, 3, 4)
LAG_A = 1
UNITS = tuple((k, 0, 64) for k in (8, 9, 10, 11, 4, 5, 6, 7, 3, 0, 1)) + tuple((2, 16 * i, 16) for i in range(4))
NU = len(UNITS)
SMALL = 11


def dot_nn(left, right):
    return lax.dot_general(left, right, (((1,), (0,)), ((), ())), preferred_element_type=F32)


def dot_nt(left, right):
    return lax.dot_general(left, right, (((1,), (1,)), ((), ())), preferred_element_type=F32)


def dot_tn(left, right):
    return lax.dot_general(left, right, (((0,), (0,)), ((), ())), preferred_element_type=F32)


def dot_tn_exact(left, right):
    return lax.dot_general(
        left, right, (((0,), (0,)), ((), ())), preferred_element_type=F32, precision=highest
    )


def patches_of(image):
    how = highest if image.dtype == F32 else None

    def product_of(left, right, dims):
        return lax.dot_general(
            left.astype(image.dtype), right.astype(image.dtype), (dims, ((), ())),
            preferred_element_type=F32, precision=how,
        )

    def iota(shape, dim):
        return lax.broadcasted_iota(jnp.int32, shape, dim)

    total = 0.0
    mine = iota((TOK, 128), 0) >> 4 == (iota((TOK, 128), 1) & 31) >> 1
    for pc in range(2):
        pick = (2 * iota((16, 32), 0) + pc == iota((16, 32), 1)).astype(F32)
        cols = product_of(pick, image, ((1,), (1,)))
        spread = jnp.where(mine, jnp.concatenate([cols] * 16, axis=0), 0.0)
        row = iota((128, PDIM), 0)
        place = (row & 1) * 8 + pc * 4 + (row >> 5) == iota((128, PDIM), 1)
        total += product_of(spread, place.astype(F32), ((1,), (0,)))
    return total


def to_tile(value):
    return jnp.concatenate([value[0:8], value[8:16]], axis=1)


def from_tile(value):
    return jnp.concatenate([value[:, 0:64], value[:, 64:128]], axis=0)


def sigmoid(value):
    return 1.0 / (1.0 + jnp.exp(-value))


def silu_slope(value):
    gate = sigmoid(value)
    return gate * (1.0 + value * (1.0 - gate))


def normed(x):
    centered = x - jnp.mean(x, axis=-1, keepdims=True)
    var = jnp.mean(centered * centered, axis=-1, keepdims=True)
    inv = lax.rsqrt(var + 1e-06)
    return centered * inv, inv


def normed_back(d_normed, x_normed, inv):
    mean_d = jnp.mean(d_normed, axis=-1, keepdims=True)
    mean_dx = jnp.mean(d_normed * x_normed, axis=-1, keepdims=True)
    return inv * (d_normed - mean_d - x_normed * mean_dx)


def fold(value):
    rows, cols = value.shape
    return jnp.sum(value.reshape(rows // 8, 8, cols), axis=0)


def rows_at(i, size):
    return pl.ds(pl.multiple_of(i * size, size), size)


def step_kernel(
    msg, noisy, noise, pos, bi, bo, ent_in, ex_in,
    g_in, g_out, ENT, EX, stats,
    W, WP, G, R1, R2, R3, PF, FIN,
    ATI, QKV, MIX, MLI, ACT, GD, DMO, DAO, DMX, DMS,
    X0, AO, RSD, MO, X1, SND, RCV,
    WMOD, PAT, TGT, EDS, E1, EDG, E2S, E2R, E3S, E3R, DMB, DMF, B2S, B2R, DTA, CP, CND,
    B3S, B3R, B3D, NSS, NSR, MODS, DACC, WPT, WLT, GLP, SQ, LOSS,
    st_sem, peer_s, peer_r, zs, zr, bs, br, as_, ar,
    s1s, s1r, s2s, s2r, szs, szr, pss, psr, d_s, d_r, f_l, f_s, f_r,
    far_s, far_r, cred_a, cred_b, cred_z,
):
    c = lax.axis_index("rep")
    s = lax.axis_index("shard")
    o = 1 - c
    x = s % 2
    y = (s // 2) % 2
    z = s // 4
    a_me = y * o + x * c
    b_me = x * o + y * c

    def yx(a, b):
        return a * o + b * c, b * o + a * c

    def dev(core, chip):
        return {"rep": core, "shard": chip}

    def chip_of(zz, yy, xx):
        return zz * 4 + yy * 2 + xx

    nb_a = dev(c, chip_of(z, *yx(1 - a_me, b_me)))
    nb_b = dev(c, chip_of(z, *yx(a_me, 1 - b_me)))
    twin = dev(o, s)

    def remote(src, dst, ss, rs, to):
        return pltpu.make_async_remote_copy(
            src_ref=src, dst_ref=dst, send_sem=ss, recv_sem=rs, device_id=to, device_id_type=MESH
        )

    pieces = []
    for j in range(4):
        pieces.append((bi.at[:, pl.ds(pl.multiple_of(6144 + 1024 * j + c * 512, 512), 512)], FIN.at[j]))
    for j in range(16):
        pieces.append((
            bi.at[:, pl.ds(pl.multiple_of(10240 + 256 * j + c * 128, 128), 128)],
            FIN.at[4 + j // 4, :, pl.ds((j % 4) * 128, 128)],
        ))
    for ch in range(2):
        for rh in range(2):
            pieces.append((
                bo.at[pl.ds(pl.multiple_of(c * 128 + rh * 64, 64), 64), pl.ds(ch * 512, 512)],
                FIN.at[8 + 2 * ch + rh],
            ))
    pieces.append((ent_in, ENT))
    pieces.append((ex_in, EX))
    pieces.append((bi.at[:, pl.ds(0, 6144)], WMOD))
    local = [pltpu.make_async_copy(p, q, st_sem.at[i]) for i, (p, q) in enumerate(pieces)]
    for i in (24, 25, 0, 1, 2, 3, *range(4, 24), 26):
        local[i].start()

    barrier = pltpu.get_barrier_semaphore()

    @pl.loop(1, 16)
    def _(k):
        pl.semaphore_signal(barrier, 1, device_id=dev(c, (s + k) % 16), device_id_type=MESH)

    @pl.loop(0, 16)
    def _(k):
        pl.semaphore_signal(barrier, 1, device_id=dev(o, k), device_id_type=MESH)

    pl.semaphore_wait(barrier, 31)

    def peers_copy(e, k, src_of, dst):
        peer = (s + k) % 16
        return remote(src_of(peer), dst.at[s], peer_s.at[e, k], peer_r.at[e, s], dev(c, peer))

    def peers_send(e, src_of, dst):
        @pl.loop(1, 16)
        def _(k):
            peers_copy(e, k, src_of, dst).start()

    def peers_wait(e, src_of, dst):
        @pl.loop(1, 16)
        def _(k):
            frm = (s + k) % 16
            remote(src_of(frm), dst.at[frm], peer_s.at[e, k], peer_r.at[e, frm], dev(c, frm)).wait_recv()

        @pl.loop(1, 16)
        def _(k):
            peers_copy(e, k, src_of, dst).wait_send()

    def twin_copy(i, src, dst):
        return remote(src, dst, d_s.at[i], d_r.at[i], twin)

    def block(k, zz, far):
        yy, xx = yx(a_me, 1 - b_me if far else b_me)
        return W.at[k, zz, yy, xx]

    def z_copy(k, dz, far=0):
        at = block(k, z, far)
        i = k * 8 + far * 4
        return remote(at, at, zs.at[i + dz], zr.at[i + z], dev(c, chip_of((z + dz) % 4, y, x)))

    def z_wait(k, dz, far=0):
        frm = (z + dz) % 4
        at = block(k, frm, far)
        i = k * 8 + far * 4
        remote(at, at, zs.at[i + dz], zr.at[i + frm], dev(c, chip_of(frm, y, x))).wait_recv()

    inner = jnp.logical_or(z == 1, z == 2)

    def z_pass(k, far=0):
        at = block(k, (z + 2) % 4, far)
        i = k * 8 + far * 4
        return remote(at, at, zs.at[i], zr.at[i + (z + 2) % 4], dev(c, chip_of(3 * (z - 1), y, x)))

    def z_start(k, far=0):
        z_copy(k, 2, far).start()
        pl.when(z != 3)(lambda: z_copy(k, 1, far).start())
        pl.when(z != 0)(lambda: z_copy(k, 3, far).start())

    def z_arrived(k, dz, far=0):
        z_wait(k, dz, far)
        if dz == 2:
            pl.when(inner)(lambda: z_pass(k, far).start())

    def z_sent(k, far=0):
        z_copy(k, 2, far).wait_send()
        pl.when(z != 3)(lambda: z_copy(k, 1, far).wait_send())
        pl.when(z != 0)(lambda: z_copy(k, 3, far).wait_send())
        pl.when(inner)(lambda: z_pass(k, far).wait_send())

    def b_copy(k, zz):
        at = block(k, zz, 0)
        return remote(at, at, bs.at[k * 4 + zz], br.at[k * 4 + zz], nb_b)

    def a_copy(k, zz, far=0):
        at = block(k, zz, far)
        i = k * 8 + far * 4 + zz
        return remote(at, at, as_.at[i], ar.at[i], nb_a)

    def own(k):
        cast(k)
        b_copy(k, z).start()
        a_copy(k, z).start()

    def far_start(k):
        b_copy(k, z).wait_recv()
        z_start(k, 1)
        a_copy(k, z, 1).start()

    def pump_b(k):
        for dz in (2, 1, 3):
            frm = (z + dz) % 4
            z_arrived(k, dz)
            if k not in VIA_Z:
                b_copy(k, frm).start()
            a_copy(k, frm).start()

    def pump_a(k):
        if k in VIA_Z:
            for dz in (2, 1, 3):
                z_arrived(k, dz, 1)
                a_copy(k, (z + dz) % 4, 1).start()
        else:
            for dz in range(4):
                b_copy(k, (z + dz) % 4).wait_recv()
                a_copy(k, (z + dz) % 4, 1).start()

    def sends_done(k):
        z_sent(k)
        if k in VIA_Z:
            z_sent(k, 1)
        else:
            for dz in range(1, 4):
                b_copy(k, (z + dz) % 4).wait_send()
        b_copy(k, z).wait_send()
        for far in range(2):
            for zz in range(4):
                a_copy(k, zz, far).wait_send()

    def pump(k):
        for i in OWN_AT[k] if k < len(OWN_AT) else ():
            own(i)
        for i in Z_AT[k] if k < len(Z_AT) else ():
            z_start(i)
        if k + 1 in VIA_Z:
            far_start(k + 1)
        if k < CHUNKS:
            pump_b(k)
        if 0 <= k - LAG_A < CHUNKS:
            pump_a(k - LAG_A)

    def need(k):
        for far in range(2):
            for dz in range(4):
                a_copy(k, (z + dz) % 4, far).wait_recv()

    def cast(k):
        if k < 4:
            local[k].wait()
            W[k, z, y, x] = FIN[k].astype(BF)
        elif k < 8:
            if k == 4:
                for i in range(4, 20):
                    local[i].wait()
            rh, half = (k - 4) // 2, (k - 4) % 2
            for q in range(4):
                j = half * 8 + 2 * q
                pair = FIN[4 + j // 4, :, (j % 4) * 128 : (j % 4) * 128 + 256]
                piece = jnp.concatenate(
                    [pair[:, rh * 64 : rh * 64 + 64], pair[:, 128 + rh * 64 : 128 + rh * 64 + 64]], axis=1
                )
                W[k, z, y, x, :, q * 128 : q * 128 + 128] = piece.astype(BF)
        else:
            local[20 + k - 8].wait()
            W[k, z, y, x] = FIN[k].astype(BF)

    E1[c, s] = msg[...]
    peers_send(0, lambda p: msg, E1.at[c])
    for k in range(START[0]):
        own(k)
        if k < START[1]:
            z_start(k)

    local[24].wait()
    local[25].wait()
    peers_wait(0, lambda p: msg, E1.at[c])
    t_hidden = dot_nt(E1[c, :, 0, :].astype(BF), ENT[:, 1016:1144].astype(BF)) + dot_nt(
        E1[c, :, 1, :].astype(BF), ENT[:, 1144:1272].astype(BF)
    )
    CND[0] = t_hidden
    t_act = (t_hidden * sigmoid(t_hidden)).astype(BF)
    CP[c, 1, :, 0:64] = t_act.astype(F32)
    for q in range(8):
        part = dot_nn(t_act, EX[:, q * 128 : q * 128 + 128].astype(BF))
        for h in range(2):
            E2S[2 * q + h] = to_tile(part[:, 64 * h : 64 * h + 64])
    E2R[s] = E2S[s]
    peers_send(1, lambda p: E2S.at[p], E2R)
    pump(0)
    hot = (
        E1[c, :, 2, 0:1].astype(jnp.int32) + PDIM == lax.broadcasted_iota(jnp.int32, (16, ENTRIES), 1)
    ).astype(F32).astype(BF)
    w_class = dot_nt(hot, ENT[...].astype(BF))
    pump(1)
    local[26].wait()
    peers_wait(1, lambda p: E2S.at[p], E2R)
    cond = from_tile(jnp.sum(E2R[...], axis=0)) + w_class
    CND[1] = cond
    cond_low = (cond * sigmoid(cond)).astype(BF)
    CP[c, 0, :, 0:64] = cond_low.astype(F32)
    for k in range(8):
        w_k = WMOD[:, k * 1024 : k * 1024 + 1024] if k < 6 else EX[:, (k - 5) * 1024 : (k - 4) * 1024]
        DMF[0, k] = dot_nn(cond_low, w_k.astype(BF))

    @pl.loop(0, 16)
    def _(l):
        part = DMF[0, :, l, :]
        E3S[l] = jnp.concatenate([part[:, :512], part[:, 512:]], axis=0).astype(BF)

    E3R[s] = E3S[s]
    peers_send(2, lambda p: E3S.at[p], E3R)
    edges = jnp.concatenate(
        [ENT[:, 0:128], jnp.concatenate([EX[:, 3072:3088], jnp.zeros((64, 112), F32)], axis=1)], axis=0
    )
    edges = edges.T[0:16].astype(BF)
    EDS[...] = edges
    EDG[s] = edges
    peers_send(7, lambda p: EDS, EDG)
    pump(2)

    PAT[...] = patches_of(noisy[...].astype(BF)).astype(BF)
    TGT[...] = patches_of(noise[...])
    peers_wait(7, lambda p: EDS, EDG)
    for q in range(8):
        even, odd = EDG[2 * q], EDG[2 * q + 1]
        WPT[:, q * 128 : q * 128 + 128] = jnp.concatenate([even[:, :64], odd[:, :64]], axis=1)
        WLT[:, q * 128 : q * 128 + 128] = jnp.concatenate([even[:, 64:], odd[:, 64:]], axis=1)
    for n in range(4):
        cols = slice(n * 256, n * 256 + 256)
        X0[:, cols] = dot_nn(PAT[...], WPT[:, cols])

    @pl.loop(0, 16)
    def _(i):
        X0[rows_at(i, 16), 0:512] += pos[...]
        X0[rows_at(i, 16), 512:1024] += jnp.broadcast_to(pos[pl.ds(i, 1), :], (16, 512))

    DACC[...] = jnp.zeros_like(DACC)
    pump(3)
    peers_wait(2, lambda p: E3S.at[p], E3R)
    parts = E3R[0].astype(F32)
    for i in range(1, 16):
        parts += E3R[i].astype(F32)
    MODS[...] = jnp.concatenate([parts[0:8], parts[8:16]], axis=1)

    def mod_row(k):
        return MODS[k : k + 1, :]

    def modulated(src, dst, shift, scale):
        @pl.loop(0, TOK // TILE)
        def _(i):
            r = rows_at(i, TILE)
            hat, _ = normed(src[r, :])
            dst[c, r, :] = (hat * (1.0 + mod_row(scale)) + mod_row(shift)).astype(BF)

    modulated(X0, ATI, 0, 1)
    twin_copy(0, ATI.at[c], ATI.at[c]).start()
    pump(4)
    twin_copy(0, ATI.at[o], ATI.at[o]).wait_recv()

    def w_cols(k, n):
        return W[k, :, :, :, :, rows_at(n, 256)].reshape(1024, 256)

    for j in range(3):
        need(j)

        @pl.loop(0, 4)
        def _(t):
            lat, n = t // 2, t % 2
            QKV[j, lat, :, rows_at(n, 256)] = dot_nn(ATI[lat], w_cols(j, n)).astype(BF)

        pump(5 + j)

    lane = lax.broadcasted_iota(jnp.int32, (1, LANES), 1)
    first = lane < 64
    masks = (first.astype(F32).astype(BF), 1.0 - first.astype(F32).astype(BF))

    def probs_of(q, k):
        score = dot_nt(q, k) * 0.125
        e = jnp.exp(score - jnp.max(score, axis=-1, keepdims=True))
        return e / jnp.sum(e, axis=-1, keepdims=True)

    def attention(t):
        lat, cols = t // 4, rows_at(t % 4, 128)
        q, k, v = QKV[0, lat, :, cols], QKV[1, lat, :, cols], QKV[2, lat, :, cols]
        outs = [dot_nn(probs_of(q * m, k).astype(BF), v) for m in masks]
        MIX[c, lat, :, cols] = jnp.where(first, outs[0], outs[1]).astype(BF)

    pl.loop(0, 4)(attention)
    pump(8)
    pl.loop(4, 8)(attention)

    twin_copy(1, MIX.at[c], MIX.at[c]).start()
    need(3)
    twin_copy(2, W.at[3], WP).start()
    pump(9)
    twin_copy(1, MIX.at[o], MIX.at[o]).wait_recv()
    twin_copy(2, W.at[3], WP).wait_recv()

    def proj(own):
        def cols(n):
            return pl.ds(pl.multiple_of((c if own else o) * 512 + n * 256, 256), 256)

        @pl.loop(0, 2)
        def _(n):
            ref = W.at[3] if own else WP
            total = 0.0
            for hh in range(2):
                w_half = ref[2 * hh : 2 * hh + 2, :, :, :, rows_at(n, 256)].reshape(512, 256)
                total += dot_nn(MIX[hh, c], w_half)
            AO[:, cols(n)] = total

    proj(True)
    proj(False)

    @pl.loop(0, TOK // TILE)
    def _(i):
        r = rows_at(i, TILE)
        RSD[r, :] = X0[r, :] + mod_row(2) * AO[r, :]

    modulated(RSD, MLI, 3, 4)
    twin_copy(3, MLI.at[c], MLI.at[c]).start()
    pump(10)
    twin_copy(3, MLI.at[o], MLI.at[o]).wait_recv()
    for j in range(4):
        need(4 + j)

        @pl.loop(0, 4)
        def _(t):
            lat, n = t // 2, t % 2
            hidden = dot_nn(MLI[lat], w_cols(4 + j, n))
            cols = pl.ds(pl.multiple_of(j * 512 + n * 256, 256), 256)
            square = hidden * hidden
            t_in = 0.7978845608028654 * hidden * (1.0 + 0.044715 * square)
            t_out = jnp.tanh(t_in)
            half = 0.5 * (1.0 + t_out)
            ACT[lat, :, cols] = (hidden * half).astype(BF)
            slope = half + 0.5 * hidden * (1.0 - t_out * t_out) * (
                0.7978845608028654 * (1.0 + 3.0 * 0.044715 * square)
            )
            GD[lat, :, cols] = slope.astype(BF)

        if j < 2:
            pump(11 + j)

    for ch in range(2):
        need(8 + 2 * ch)
        need(9 + 2 * ch)

        def mlp_tile(lat, n):
            total = 0.0
            for rh in range(2):
                total += dot_nn(ACT[lat, :, rh * 1024 : rh * 1024 + 1024], w_cols(8 + 2 * ch + rh, n))
            return total

        @pl.loop(0, 2)
        def _(n):
            SND[ch, :, rows_at(n, 256)] = mlp_tile(o, n)

        twin_copy(4 + ch, SND.at[ch], RCV.at[ch]).start()

        @pl.loop(0, 2)
        def _(n):
            MO[:, pl.ds(pl.multiple_of(ch * 512 + n * 256, 256), 256)] = mlp_tile(c, n)

    def received(i):
        for ch in range(2):
            twin_copy(i + ch, SND.at[ch], RCV.at[ch]).wait_recv()

    def both_parts(r):
        return MO[r, :] + jnp.concatenate([RCV[0, r, :], RCV[1, r, :]], axis=1)

    received(4)
    LOSS[...] = jnp.zeros_like(LOSS)
    GLP[...] = jnp.zeros_like(GLP)

    @pl.loop(0, TOK // TILE)
    def _(i):
        r = rows_at(i, TILE)
        mlp_out = both_parts(r)
        x1 = RSD[r, :] + mod_row(5) * mlp_out
        hat, inv = normed(x1)
        scale = 1.0 + mod_row(7)
        final_in = (hat * scale + mod_row(6)).astype(BF)
        w_lin = WLT[...]
        error = dot_nt(final_in, w_lin) - TGT[r, :]
        LOSS[...] += fold(error * error)
        d_pred = (2.0 * error / (TOK * PDIM)).astype(BF)
        GLP[16:32, :] += dot_tn(d_pred, final_in)
        d_final = dot_nn(d_pred, w_lin)
        DACC[6] += fold(d_final)
        DACC[7] += fold(d_final * hat)
        d_x = normed_back(d_final * scale, hat, inv)
        X1[r, :] = d_x
        DACC[5] += fold(d_x * mlp_out)
        DMO[c, r, :] = (d_x * mod_row(5)).astype(BF)

    twin_copy(6, DMO.at[c], DMO.at[c]).start()

    def r1_of(k, b):
        return R1.at[k - 8, b] if k >= 8 else W.at[8 + k // 2, :, k % 2, b]

    def r2_of(k):
        return R2.at[k - 8] if k >= 8 else W.at[4 + k // 4, :, (k // 2) % 2, k % 2]

    def r3_of(k):
        return R3.at[k - 8] if k >= 8 else W.at[6 + k // 4, :, (k // 2) % 2, k % 2]

    def rows_of(u):
        return pl.ds(UNITS[u][1], UNITS[u][2])

    def g_at(u, zz, a, b):
        yy, xx = yx(a, b)
        return G.at[UNITS[u][0], zz, yy, xx, rows_of(u)]

    def b_of(far):
        return 1 - b_me if far else b_me

    def z_slot(u, i, far):
        return (r2_of if far else r3_of)(UNITS[u][0]).at[i, rows_of(u)]

    def pass_slot(u, i, far):
        return PF.at[SUM_VIA_Z.index(u)] if far else z_slot(u, i, 0)

    def s1_copy(u, b):
        k, r = UNITS[u][0], rows_of(u)
        yy, xx = yx(1 - a_me, b)
        return remote(G.at[k, :, yy, xx, r], r1_of(k, b).at[:, r], s1s.at[u * 2 + b], s1r.at[u * 2 + b], nb_a)

    def s2_copy(u):
        if u in SUM_VIA_Z:
            return remote(g_at(u, z, a_me, 1 - b_me), z_slot(u, z, 1), s2s.at[u], s2r.at[u], nb_b)
        k, r = UNITS[u][0], rows_of(u)
        yy, xx = yx(a_me, 1 - b_me)
        return remote(G.at[k, :, yy, xx, r], r2_of(k).at[:, r], s2s.at[u], s2r.at[u], nb_b)

    def line(zz):
        return dev(c, chip_of(zz, y, x))

    def sz_copy(u, dz, far):
        zt = (z + dz) % 4
        i = u * 8 + far * 4
        return remote(g_at(u, zt, a_me, b_of(far)), z_slot(u, z, far), szs.at[i + dz], szr.at[i + z], line(zt))

    def sz_wait(u, dz, far):
        frm = (z + dz) % 4
        i = u * 8 + far * 4
        remote(g_at(u, frm, a_me, b_of(far)), z_slot(u, frm, far), szs.at[i + dz], szr.at[i + frm], line(frm)).wait_recv()

    near_end = jnp.where(z < 2, 1, 2)

    def pass_copy(u, far):
        i = u * 2 + far
        return remote(g_at(u, 3 - z, a_me, b_of(far)), pass_slot(u, near_end, far), pss.at[i], psr.at[i], line(near_end))

    def sum_a(u, zz, far):
        k, r = UNITS[u][0], rows_of(u)
        b = b_of(far)
        yy, xx = yx(a_me, b)
        return G[k, zz, yy, xx, r].astype(F32) + r1_of(k, b)[zz, r].astype(F32)

    def store(u, zz, far, value):
        g_at(u, zz, a_me, b_of(far))[...] = value.astype(BF)

    def sz_start(u, far):
        for dz in (1, 3):
            alone = z != (3 if dz == 1 else 0)
            if u >= SMALL:
                sz_copy(u, dz, far).start()
            else:
                pl.when(alone)(lambda: sz_copy(u, dz, far).start())
                pl.when(jnp.logical_not(alone))(lambda: pass_copy(u, far).start())
        if u >= SMALL:
            sz_copy(u, 2, far).start()
        else:
            pl.when(jnp.logical_not(inner))(lambda: sz_copy(u, 2, far).start())

    def sz_pass(u, far):
        @pl.when(inner)
        def _():
            i = u * 2 + far
            slot = pass_slot(u, z, far)
            remote(g_at(u, z, a_me, b_of(far)), slot, pss.at[i], psr.at[i], line(z)).wait_recv()
            zt = (z + 2) % 4
            store(u, zt, far, g_at(u, zt, a_me, b_of(far))[...].astype(F32) + slot[...].astype(F32))
            sz_copy(u, 2, far).start()

    def sz_sum(u, far):
        into = FIN.at[UNITS[u][0], rows_of(u)]

        def add(dz):
            sz_wait(u, dz, far)
            into[...] += z_slot(u, (z + dz) % 4, far)[...].astype(F32)

        for dz in (1, 3, 2):
            if u >= SMALL or dz == 2:
                add(dz)
            else:
                pl.when(z != (3 if dz == 1 else 0))(lambda: add(dz))

    def s1(u):
        for b in range(2):
            s1_copy(u, b).start()

    def stage_1(u):
        for b in range(2):
            s1_copy(u, b).wait_recv()
        if u in SUM_VIA_Z:
            for far in (1, 0):
                for dz in (1, 3, 2):
                    store(u, (z + dz) % 4, far, sum_a(u, (z + dz) % 4, far))
                sz_start(u, far)
        else:
            @pl.loop(0, 4)
            def _(zz):
                store(u, zz, 1, sum_a(u, zz, 1))

            s2_copy(u).start()

    def stage_2(u):
        if u in SUM_VIA_Z:
            for far in (1, 0):
                sz_pass(u, far)
        else:
            k, r = UNITS[u][0], rows_of(u)
            s2_copy(u).wait_recv()
            for dz in (1, 3, 2):
                zt = (z + dz) % 4
                store(u, zt, 0, sum_a(u, zt, 0) + r2_of(k)[zt, r].astype(F32))
            sz_start(u, 0)
            FIN[k, r] = sum_a(u, z, 0) + r2_of(k)[z, r].astype(F32)

    def stage_3(u):
        k, r = UNITS[u][0], rows_of(u)
        if u in SUM_VIA_Z:
            FIN[k, r] = sum_a(u, z, 1)
            sz_sum(u, 1)
            store(u, z, 1, FIN[k, r])
            s2_copy(u).start()
            FIN[k, r] = sum_a(u, z, 0)
            sz_sum(u, 0)
        elif u < SMALL:
            sz_pass(u, 0)

    def stage_4(u):
        k, r = UNITS[u][0], rows_of(u)
        if u in SUM_VIA_Z:
            s2_copy(u).wait_recv()
            FIN[k, r] += z_slot(u, z, 1)[...].astype(F32)
        else:
            sz_sum(u, 0)
        total = FIN[k, r]
        SQ[...] += fold(total * total)

    def sums_done(u):
        for b in range(2):
            s1_copy(u, b).wait_send()
        s2_copy(u).wait_send()
        for far in range(2 if u in SUM_VIA_Z else 1):
            sz_copy(u, 2, far).wait_send()
            for dz in (1, 3):
                if u >= SMALL:
                    sz_copy(u, dz, far).wait_send()
                else:
                    alone = z != (3 if dz == 1 else 0)
                    pl.when(alone)(lambda: sz_copy(u, dz, far).wait_send())
                    pl.when(jnp.logical_not(alone))(lambda: pass_copy(u, far).wait_send())

    def result_copies(i):
        if i < 4:
            k = 8 + i
            src = FIN.at[k]
            dst = g_out.at[
                pl.ds(pl.multiple_of(c * 128 + (i % 2) * 64, 64), 64), pl.ds((i // 2) * 512, 512)
            ]
        elif i < 20:
            j = i - 4
            src = FIN.at[4 + j // 8 + 2 * (j % 2), :, pl.ds(((j % 8) // 2) * 128, 128)]
            dst = g_in.at[:, pl.ds(pl.multiple_of(10240 + 256 * j + c * 128, 128), 128)]
        else:
            k, r0, size = ((3, 0, 64), *UNITS[9:])[i - 20]
            src = FIN.at[k, pl.ds(r0, size)]
            dst = g_in.at[pl.ds(r0, size), pl.ds(pl.multiple_of(6144 + 1024 * k + c * 512, 512), 512)]
        return pltpu.make_async_copy(src, dst, f_l.at[i]), remote(src, dst, f_s.at[i], f_r.at[i], twin)

    def send_result(u):
        k = UNITS[u][0]
        if k >= 8:
            span = (k - 8,)
        elif k == 7:
            for half in range(2):
                for q in range(4):
                    cols = slice(q * 128, q * 128 + 128)
                    low, high = FIN[4 + half, :, cols], FIN[6 + half, :, cols]
                    FIN[4 + half, :, cols] = jnp.concatenate([low[:, 0:64], high[:, 0:64]], axis=1)
                    FIN[6 + half, :, cols] = jnp.concatenate([low[:, 64:128], high[:, 64:128]], axis=1)
            span = range(4, 20)
        elif k >= 4:
            span = ()
        else:
            span = (20 + u - 8,)
        for i in span:
            for copy in result_copies(i):
                copy.start()

    def step(t):
        for u in range(t + LEAD, NU):
            if u == t + LEAD and u <= 11 or t + LEAD == 11:
                if u == 4:
                    pl.semaphore_wait(cred_a, 1)
                s1(u)
        if t == 4:
            pl.semaphore_wait(cred_b, 1)
            pl.semaphore_wait(cred_z, 3)
        for stage, lag in zip((stage_1, stage_2, stage_3, stage_4), LAGS):
            if 0 <= t - lag < NU:
                stage(t - lag)
                if stage is stage_4:
                    send_result(t - lag)

    def grad_tiles(k, left, right):
        @pl.loop(0, 4)
        def _(r):
            G[k, r] = dot_tn(left(r), right).astype(BF).reshape(2, 2, 64, 512)

    SQ[...] = jnp.zeros_like(SQ)
    twin_copy(6, DMO.at[o], DMO.at[o]).wait_recv()
    for ch in range(2):
        for rh in range(2):
            k = 8 + 2 * ch + rh
            grad_tiles(
                k,
                lambda r: ACT[:, :, pl.ds(pl.multiple_of(rh * 1024 + r * 256, 256), 256)].reshape(512, 256),
                DMO[:, :, ch * 512 : ch * 512 + 512].reshape(512, 512),
            )
            if 2 * ch + rh < LEAD:
                s1(2 * ch + rh)

    for k in range(CHUNKS):
        sends_done(k)

    @pl.loop(0, 16)
    def _(t):
        lat, rh, r = t // 8, (t // 4) % 2, t % 4
        total = 0.0
        for ch in range(2):
            total += dot_nt(DMO[lat, :, ch * 512 : ch * 512 + 512], W[8 + 2 * ch + rh, r].reshape(256, 512))
        cols = pl.ds(pl.multiple_of(rh * 1024 + r * 256, 256), 256)
        GD[lat, :, cols] = (total * GD[lat, :, cols].astype(F32)).astype(BF)

    pl.semaphore_signal(cred_a, 1, device_id=nb_a, device_id_type=MESH)

    def data_back(first_k, count, left, i):
        for ch in range(2):
            @pl.loop(0, 2)
            def _(n):
                total = 0.0
                for j in range(count):
                    total += dot_nt(left(j, o), W[first_k + j, 2 * ch + n].reshape(256, 512))
                SND[ch, :, rows_at(n, 256)] = total

            twin_copy(i + ch, SND.at[ch], RCV.at[ch]).start()

        @pl.loop(0, 4)
        def _(r):
            total = 0.0
            for j in range(count):
                total += dot_nt(left(j, c), W[first_k + j, r].reshape(256, 512))
            MO[:, rows_at(r, 256)] = total

    for ch in range(2):
        twin_copy(4 + ch, SND.at[ch], RCV.at[ch]).wait_send()
    data_back(4, 4, lambda j, lat: GD[lat, :, j * 512 : j * 512 + 512], 7)
    pl.semaphore_signal(cred_b, 1, device_id=nb_b, device_id_type=MESH)
    for dz in range(1, 4):
        pl.semaphore_signal(cred_z, 1, device_id=dev(c, chip_of((z + dz) % 4, y, x)), device_id_type=MESH)

    step(0)
    for j in range(4):
        grad_tiles(
            4 + j,
            lambda r: MLI[:, :, rows_at(r, 256)].reshape(512, 256),
            GD[:, :, j * 512 : j * 512 + 512].reshape(512, 512),
        )
    received(7)

    @pl.loop(0, TOK // TILE)
    def _(i):
        r = rows_at(i, TILE)
        d_in = both_parts(r)
        hat, inv = normed(RSD[r, :])
        DACC[3] += fold(d_in)
        DACC[4] += fold(d_in * hat)
        d_x = normed_back(d_in * (1.0 + mod_row(4)), hat, inv) + X1[r, :]
        X1[r, :] = d_x
        DACC[2] += fold(d_x * AO[r, :])
        DAO[c, r, :] = (d_x * mod_row(2)).astype(BF)

    dao_other = pl.ds(pl.multiple_of(o * 512, 512), 512)
    dao_mine = pl.ds(pl.multiple_of(c * 512, 512), 512)
    twin_copy(9, DAO.at[c, :, dao_other], DAO.at[c, :, dao_other]).start()

    def mixed_back(hh, n):
        w_mine = W[3, 2 * hh + n].reshape(256, 512)
        w_other = WP[2 * hh + n].reshape(256, 512)
        return (dot_nt(DAO[c, :, dao_mine], w_mine) + dot_nt(DAO[c, :, dao_other], w_other)).astype(BF)

    @pl.loop(0, 2)
    def _(n):
        DMS[:, rows_at(n, 256)] = mixed_back(o, n)

    twin_copy(10, DMS, DMX.at[c]).start()

    @pl.loop(0, 2)
    def _(n):
        DMX[c, :, rows_at(n, 256)] = mixed_back(c, n)

    step(1)
    twin_copy(9, DAO.at[o, :, dao_mine], DAO.at[o, :, dao_mine]).wait_recv()

    @pl.loop(0, 4)
    def _(r):
        left = MIX[r // 2, :, :, rows_at(r % 2, 256)].reshape(512, 256)
        G[3, r] = dot_tn(left, DAO[:, :, dao_mine].reshape(512, 512)).astype(BF).reshape(2, 2, 64, 512)

    twin_copy(10, DMS, DMX.at[o]).wait_recv()

    def attention_back(t):
        lat, cols = t // 4, rows_at(t % 4, 128)
        q, k, v = QKV[0, lat, :, cols], QKV[1, lat, :, cols], QKV[2, lat, :, cols]
        dm = DMX[lat, :, cols]
        res = []
        for m in masks:
            probs = probs_of(q * m, k)
            d_probs = dot_nt(dm * m, v)
            d_v = dot_tn(probs.astype(BF), dm)
            d_s = probs * (d_probs - jnp.sum(d_probs * probs, axis=-1, keepdims=True))
            d_s = (d_s * 0.125).astype(BF)
            res.append((dot_nn(d_s, k), dot_tn(d_s, q), d_v))
        for j in range(3):
            QKV[j, lat, :, cols] = jnp.where(first, res[0][j], res[1][j]).astype(BF)

    for half in range(2):
        pl.loop(4 * half, 4 * half + 4)(attention_back)
        step(2 + half)
    for ch in range(2):
        twin_copy(7 + ch, SND.at[ch], RCV.at[ch]).wait_send()
    data_back(0, 3, lambda j, lat: QKV[j, lat], 11)
    for j in range(3):
        grad_tiles(
            j,
            lambda r: ATI[:, :, rows_at(r, 256)].reshape(512, 256),
            QKV[j].reshape(512, 512),
        )
    received(11)

    @pl.loop(0, TOK // TILE)
    def _(i):
        r = rows_at(i, TILE)
        d_in = both_parts(r)
        hat, inv = normed(X0[r, :])
        DACC[0] += fold(d_in)
        DACC[1] += fold(d_in * hat)
        d_x = normed_back(d_in * (1.0 + mod_row(1)), hat, inv) + X1[r, :]
        GLP[0:16, :] += dot_tn(PAT[r, :], d_x.astype(BF))

    for k in range(8):
        MODS[k : k + 1, :] = jnp.sum(DACC[k], axis=0, keepdims=True)
    d_mods = MODS[...]
    DMB[c, s] = jnp.concatenate([d_mods[:, :512], d_mods[:, 512:]], axis=0).astype(BF)
    peers_send(3, lambda p: DMB.at[c, s], DMB.at[c])
    for q in range(16):
        cols = slice(q * 64, q * 64 + 64)
        B3S[q] = jnp.concatenate([GLP[0:16, cols], GLP[16:32, cols]], axis=1).astype(BF)
    B3R[s] = B3S[s]
    peers_send(4, lambda p: B3S.at[p], B3R)
    step(4)
    step(5)
    step(6)
    peers_wait(3, lambda p: DMB.at[c, s], DMB.at[c])
    twin_copy(13, DMB.at[c], DMB.at[c]).start()

    def unpack(g):
        @pl.loop(0, 16)
        def _(l):
            both = DMB[g, l].astype(F32)
            DMF[g, :, l, 0:512] = both[0:8]
            DMF[g, :, l, 512:1024] = both[8:16]

    unpack(c)
    d_cond_low = 0.0
    for k in range(8):
        w_k = WMOD[:, k * 1024 : k * 1024 + 1024] if k < 6 else EX[:, (k - 5) * 1024 : (k - 4) * 1024]
        d_cond_low += dot_nt(DMF[c, k].astype(BF), w_k.astype(BF))
    d_cond = d_cond_low * silu_slope(CND[1])
    CP[c, 2, :, 0:64] = d_cond
    d_temb = d_cond.astype(BF).astype(F32)
    B2S[...] = to_tile(d_temb)
    B2R[s] = B2S[...]
    peers_send(5, lambda p: B2S, B2R)
    step(7)
    peers_wait(4, lambda p: B3S.at[p], B3R)
    sums = B3R[0].astype(F32)
    for i in range(1, 16):
        sums += B3R[i].astype(F32)
    B3D[c] = sums
    twin_copy(14, B3D.at[c], B3D.at[c]).start()
    peers_wait(5, lambda p: B2S, B2R)
    for q in range(8):
        DTA[c, :, q * 128 : q * 128 + 128] = jnp.concatenate(
            [from_tile(B2R[2 * q]), from_tile(B2R[2 * q + 1])], axis=1
        )
    d_tact = dot_nt(DTA[c].astype(BF), EX[:, 0:1024].astype(BF))
    CP[c, 3, :, 0:64] = (d_tact * silu_slope(CND[0])).astype(BF).astype(F32)
    twin_copy(15, DTA.at[c], DTA.at[c]).start()
    twin_copy(16, CP.at[c], CP.at[c]).start()
    twin_copy(17, E1.at[c], E1.at[c]).start()
    step(8)
    twin_copy(13, DMB.at[o], DMB.at[o]).wait_recv()
    unpack(o)
    twin_copy(14, B3D.at[o], B3D.at[o]).wait_recv()
    twin_copy(15, DTA.at[o], DTA.at[o]).wait_recv()
    twin_copy(16, CP.at[o], CP.at[o]).wait_recv()
    twin_copy(17, E1.at[o], E1.at[o]).wait_recv()

    def packed(i):
        return jnp.concatenate([CP[0, i, :, 0:64], CP[1, i, :, 0:64]], axis=0)

    def square_half(value):
        part = 0.5 * value * value
        return jnp.sum(jnp.sum(part, axis=0, keepdims=True), axis=1, keepdims=True)

    cond_both = packed(0).astype(BF)
    small = jnp.zeros((1, 1), F32)
    for k in range(8):
        grad = dot_tn(cond_both, jnp.concatenate([DMF[0, k], DMF[1, k]], axis=0).astype(BF))
        small += square_half(grad)
        if k < 6:
            WMOD[:, k * 1024 : k * 1024 + 1024] = grad
        else:
            EX[:, (k - 5) * 1024 : (k - 4) * 1024] = grad
    mod_out = pltpu.make_async_copy(WMOD, g_in.at[:, pl.ds(0, 6144)], st_sem.at[26])
    mod_out.start()
    step(9)
    grad = dot_tn(packed(1).astype(BF), jnp.concatenate([DTA[0], DTA[1]], axis=0).astype(BF))
    small += square_half(grad)
    EX[:, 0:1024] = grad
    sums = B3D[0] + B3D[1]
    small += square_half(sums[:, 64:128])
    wide = jnp.concatenate(
        [sums, jnp.zeros((112, 128), F32)], axis=0
    )
    EX[:, 3072:3088] = wide.T[64:128, 0:16]
    def both(value):
        return jnp.concatenate([value(0), value(1)], axis=0)

    index = lax.broadcasted_iota(jnp.int32, (32, ENTRIES), 1)
    hot = (both(lambda g: E1[g, :, 2, 0:1]).astype(jnp.int32) + PDIM == index).astype(F32)
    grad = dot_tn_exact(packed(2), hot)
    spot = lax.broadcasted_iota(jnp.int32, (16, ENTRIES), 0) == index[0:16]
    grad += dot_tn_exact(sums[:, 0:64], spot.astype(F32))
    ENT[...] = grad
    femb = both(lambda g: jnp.concatenate([E1[g, :, 0, :], E1[g, :, 1, :]], axis=1)).astype(BF)
    ENT[:, PDIM + NCLS :] = dot_tn(packed(3).astype(BF), femb)
    small += square_half(ENT[...])

    for t in range(10, NU + LAGS[3]):
        step(t)

    def total_of(value):
        return jnp.sum(jnp.sum(value, axis=0, keepdims=True), axis=1, keepdims=True)

    NSS[0:1, :] = jnp.broadcast_to(total_of(SQ[...]) + small, (1, 128))
    NSS[1:2, :] = jnp.broadcast_to(total_of(LOSS[...]) / (TOK * PDIM), (1, 128))
    NSS[2:8, :] = jnp.zeros((6, 128), F32)
    NSR[c * 16 + s] = NSS[...]

    def far_copy(k, frm):
        return remote(NSS, NSR.at[frm], far_s.at[k], far_r.at[frm % 16], dev(o, k))

    @pl.loop(0, 16)
    def _(k):
        far_copy(k, c * 16 + s).start()

    mine = NSR.at[pl.ds(c * 16, 16)]
    peers_send(6, lambda p: NSS, mine)
    peers_wait(6, lambda p: NSS, mine)

    @pl.loop(0, 16)
    def _(k):
        far_copy(k, o * 16 + k).wait()

    totals = jnp.sum(NSR[...], axis=0)
    norm = jnp.sqrt(totals[0:1])
    stats[...] = totals
    stats[0:1, :] = norm
    stats[2:3, :] = clip_limit / jnp.maximum(norm, clip_limit)

    mod_out.wait()
    for i in range(27):
        for copy in result_copies(i):
            copy.wait()
    for u in range(NU):
        sums_done(u)
    twin_copy(0, ATI.at[c], ATI.at[c]).wait_send()
    twin_copy(1, MIX.at[c], MIX.at[c]).wait_send()
    twin_copy(2, W.at[3], WP).wait_send()
    twin_copy(3, MLI.at[c], MLI.at[c]).wait_send()
    twin_copy(6, DMO.at[c], DMO.at[c]).wait_send()
    twin_copy(9, DAO.at[c, :, dao_other], DAO.at[c, :, dao_other]).wait_send()
    twin_copy(10, DMS, DMX.at[c]).wait_send()
    for ch in range(2):
        twin_copy(11 + ch, SND.at[ch], RCV.at[ch]).wait_send()
    twin_copy(13, DMB.at[c], DMB.at[c]).wait_send()
    twin_copy(14, B3D.at[c], B3D.at[c]).wait_send()
    twin_copy(15, DTA.at[c], DTA.at[c]).wait_send()
    twin_copy(16, CP.at[c], CP.at[c]).wait_send()
    twin_copy(17, E1.at[c], E1.at[c]).wait_send()


def fused_step(msg, noisy, noise, pos, block_in, block_out, entry, exit_):
    vm = pltpu.VMEM
    dma = pltpu.SemaphoreType.DMA
    scratch = [
        vm((12, 4, 2, 2, 64, 512), BF), vm((4, 2, 2, 64, 512), BF), vm((12, 4, 2, 2, 64, 512), BF),
        vm((4, 2, 4, 64, 512), BF), vm((4, 4, 64, 512), BF), vm((4, 4, 64, 512), BF),
        vm((len(SUM_VIA_Z), 64, 512), BF), vm((12, 64, 512), F32),
        vm((2, TOK, 1024), BF), vm((3, 2, TOK, 512), BF), vm((2, 2, TOK, 512), BF), vm((2, TOK, 1024), BF),
        vm((2, TOK, 2048), BF), vm((2, TOK, 2048), BF), vm((2, TOK, 1024), BF), vm((2, TOK, 1024), BF),
        vm((2, TOK, 512), BF), vm((TOK, 512), BF),
        *[vm((TOK, 1024), F32)] * 5, vm((2, TOK, 512), F32), vm((2, TOK, 512), F32),
        vm((64, 6144), F32), vm((TOK, PDIM), BF), vm((TOK, PDIM), F32), vm((16, 128), BF), vm((2, 16, 8, 128), F32), vm((16, 16, 128), BF), vm((16, 8, 128), F32), vm((16, 8, 128), F32),
        vm((16, 16, 512), BF), vm((16, 16, 512), BF), vm((2, 16, 16, 512), BF), vm((2, 8, 16, 1024), F32),
        vm((8, 128), F32), vm((16, 8, 128), F32), vm((2, 16, 1024), F32), vm((2, 4, 16, 128), F32), vm((2, 16, 64), F32),
        vm((16, 16, 128), BF), vm((16, 16, 128), BF), vm((2, 16, 128), F32),
        vm((8, 128), F32), vm((32, 8, 128), F32),
        vm((8, 1024), F32), vm((8, 8, 1024), F32), vm((16, 1024), BF), vm((16, 1024), BF), vm((32, 1024), F32),
        vm((8, 512), F32), vm((8, 16), F32),
        dma((27,)), dma((8, 16)), dma((8, 16)), dma((96,)), dma((96,)), dma((48,)), dma((48,)), dma((96,)), dma((96,)),
        dma((30,)), dma((30,)), dma((15,)), dma((15,)), dma((120,)), dma((120,)), dma((30,)), dma((30,)), dma((19,)), dma((19,)),
        dma((27,)), dma((27,)), dma((27,)), dma((16,)), dma((16,)),
        pltpu.SemaphoreType.REGULAR, pltpu.SemaphoreType.REGULAR, pltpu.SemaphoreType.REGULAR,
    ]
    any_ = pl.BlockSpec(memory_space=pl.ANY)
    vmem = pl.BlockSpec(memory_space=pltpu.VMEM)
    shape = jax.ShapeDtypeStruct
    return pl.pallas_call(
        step_kernel,
        out_shape=(
            shape(block_in.shape, F32), shape(block_out.shape, F32), shape(entry.shape, F32),
            shape(exit_.shape, F32), shape((8, 128), F32),
        ),
        in_specs=[vmem, vmem, vmem, vmem, any_, any_, any_, any_],
        out_specs=(any_, any_, vmem, vmem, vmem),
        scratch_shapes=scratch,
        compiler_params=pltpu.CompilerParams(
            collective_id=0, has_side_effects=True, vmem_limit_bytes=62 * 2**20
        ),
        cost_estimate=pl.CostEstimate(flops=21 * 10**9, bytes_accessed=20 * 10**6, transcendentals=4 * 10**6),
    )(msg, noisy, noise, pos, block_in, block_out, entry, exit_)


def local_fused(
    noisy, timesteps, labels, noise,
    block_in, block_in_first, block_in_second,
    block_out, block_out_first, block_out_second,
    entry_table, entry_first, entry_second,
    exit_proj, exit_first, exit_second,
):
    index = lax.axis_index("rep") * 16 + lax.axis_index("shard")
    femb = lowered(time_features(timesteps, FREQ)).astype(F32).reshape(2, LANES)
    label = labels.astype(F32)[0]
    lane = jnp.arange(LANES)[None, :]
    head = jnp.concatenate(
        [femb, jnp.full((1, LANES), label), jnp.where(lane == index, label, 0.0), jnp.zeros((4, LANES), F32)], axis=0
    )
    side = noisy.shape[-1]
    grid, quarter = side // PATCH, D // 4
    angle = np.arange(grid)[:, None] / 10000.0 ** (np.arange(quarter)[None, :] / quarter)
    pos = jnp.asarray(np.concatenate([np.sin(angle), np.cos(angle)], axis=1), F32)
    g_in, g_out, g_entry, g_exit, stats = fused_step(
        head, noisy.reshape(-1, side), noise.reshape(-1, side), pos, block_in[0], block_out[0], entry_table.T, exit_proj
    )
    loss = stats[1, 0]
    grad_norm, factor = stats[0, 0], stats[2, 0]
    outs = [loss, grad_norm]
    for weight, first, second, grad, rate in (
        (block_in, block_in_first, block_in_second, g_in[None], rate_main),
        (block_out, block_out_first, block_out_second, g_out[None], rate_main),
        (entry_table, entry_first, entry_second, g_entry.T, rate_edge),
        (exit_proj, exit_first, exit_second, g_exit, rate_main),
    ):
        outs.extend(adam_step(weight, first, second, grad, factor, rate))
    return tuple(outs)


def solution(mesh):
    step = local_fused if dict(mesh.shape) == {"rep": 2, "shard": 16} else local
    in_specs = (
        P(("rep", "shard"), None, None, None),
        P(("rep", "shard")),
        P(("rep", "shard")),
        P(("rep", "shard"), None, None, None),
        P(None, "shard", None),
        P(None, "shard", None),
        P(None, "shard", None),
        P(None, "shard", None),
        P(None, "shard", None),
        P(None, "shard", None),
        P(None, "shard"),
        P(None, "shard"),
        P(None, "shard"),
        P("shard", None),
        P("shard", None),
        P("shard", None),
    )
    out_specs = (
        P(),
        P(),
        P(None, "shard", None),
        P(None, "shard", None),
        P(None, "shard", None),
        P(None, "shard", None),
        P(None, "shard", None),
        P(None, "shard", None),
        P(None, "shard", None),
        P(None, "shard", None),
        P(None, "shard"),
        P(None, "shard"),
        P(None, "shard"),
        P(None, "shard"),
        P("shard", None),
        P("shard", None),
        P("shard", None),
        P("shard", None),
    )
    return jax.shard_map(step, mesh=mesh, in_specs=in_specs, out_specs=out_specs, check_vma=False)
```

```python
import jax
import jax.numpy as jnp
import numpy as np
from jax import lax
from jax.experimental import pallas as pl
from jax.experimental.pallas import tpu as pltpu
from jax.sharding import PartitionSpec as P

D = 1024
HEADS = 16
PATCH = 2
NCLS = 1000
FREQ = 256
STEP = 10
PDIM = 16
ENTRIES = PDIM + NCLS + FREQ


clip_limit = 0.5
rate_main = 0.02
rate_edge = 0.1
decay_rate = 0.01
adam_eps = 1e-08
highest = lax.Precision.HIGHEST


def lowered(value):
    return value.astype(jnp.bfloat16)


def product(left, right):
    return jnp.dot(left, right, preferred_element_type=jnp.float32)


def product_tn(left, right):
    return lax.dot_general(
        left, right, (((0,), (0,)), ((), ())), preferred_element_type=jnp.float32
    )


def product_nt(left, right):
    return lax.dot_general(
        left, right, (((1,), (1,)), ((), ())), preferred_element_type=jnp.float32
    )


def patchify(image, patch):
    batch, chans, height, width = image.shape
    grid = height // patch
    parts = image.reshape(batch, chans, grid, patch, grid, patch)
    parts = parts.transpose(0, 2, 4, 3, 5, 1)
    return parts.reshape(batch, grid * grid, patch * patch * chans)


def position_table(grid, width):
    quarter = width // 4
    omega = 1.0 / 10000.0 ** (jnp.arange(quarter, dtype=jnp.float32) / quarter)
    index = jnp.arange(grid * grid)
    row_pos = (index // grid).astype(jnp.float32)[:, None] * omega[None, :]
    col_pos = (index % grid).astype(jnp.float32)[:, None] * omega[None, :]
    return jnp.concatenate(
        [jnp.sin(col_pos), jnp.cos(col_pos), jnp.sin(row_pos), jnp.cos(row_pos)], axis=1
    )


def time_features(steps, size):
    half = size // 2
    freqs = jnp.exp(-jnp.log(10000.0) * jnp.arange(half, dtype=jnp.float32) / half)
    angles = steps.astype(jnp.float32)[:, None] * freqs[None, :]
    return jnp.concatenate([jnp.cos(angles), jnp.sin(angles)], axis=1)


def modulate(x, shift, scale):
    centered = x - jnp.mean(x, axis=-1, keepdims=True)
    var = jnp.mean(centered * centered, axis=-1, keepdims=True)
    normed = centered * lax.rsqrt(var + 1e-06)
    return normed * (1.0 + scale[:, None, :]) + shift[:, None, :]


def gelu_tanh(value):
    return jax.nn.gelu(value, approximate=True)


def adam_step(weight, first, second, grad, factor, rate):
    clipped = grad * factor
    first_new = 0.5 * first + 0.5 * clipped
    second_new = 0.5 * second + 0.5 * clipped * clipped
    corr = 1.0 - 0.5**STEP
    update = first_new / corr / (jnp.sqrt(second_new / corr) + adam_eps) + decay_rate * weight
    weight_new = weight - rate * update
    return (weight_new, first_new, second_new, weight_new.astype(jnp.bfloat16))


def layer_parts(x, cond_low, w_in, w_out):
    width = x.shape[-1]
    batch, seq = (x.shape[0], x.shape[1])
    size = width // HEADS
    mod = product(cond_low, w_in[:, : 6 * width])
    shift_a, scale_a, gate_a, shift_b, scale_b, gate_b = jnp.split(mod, 6, axis=-1)
    attn_in = lowered(modulate(x, shift_a, scale_a))
    qkv = lowered(
        jnp.einsum(
            "bsd,de->bse",
            attn_in,
            w_in[:, 6 * width : 9 * width],
            preferred_element_type=jnp.float32,
        )
    )
    query = qkv[..., :width].reshape(batch, seq, HEADS, size)
    keys = qkv[..., width : 2 * width].reshape(batch, seq, HEADS, size)
    values = qkv[..., 2 * width :].reshape(batch, seq, HEADS, size)
    scores = jnp.einsum(
        "bqhd,bkhd->bhqk", query, keys, preferred_element_type=jnp.float32
    ) * size ** (-0.5)
    weights = jax.nn.softmax(scores, axis=-1)
    weights_low = lowered(weights)
    mixed = lowered(
        jnp.einsum("bhqk,bkhd->bqhd", weights_low, values, preferred_element_type=jnp.float32)
    ).reshape(batch, seq, width)
    attn_out = jnp.einsum(
        "bsd,de->bse", mixed, w_in[:, 9 * width : 10 * width], preferred_element_type=jnp.float32
    )
    resid = x + gate_a[:, None, :] * attn_out
    mlp_in = lowered(modulate(resid, shift_b, scale_b))
    hidden = jnp.einsum(
        "bsd,df->bsf", mlp_in, w_in[:, 10 * width :], preferred_element_type=jnp.float32
    )
    active = lowered(gelu_tanh(hidden))
    mlp_out = jnp.einsum("bsf,fd->bsd", active, w_out, preferred_element_type=jnp.float32)
    result = resid + gate_b[:, None, :] * mlp_out
    return dict(
        mods=(shift_a, scale_a, gate_a, shift_b, scale_b, gate_b),
        attn_in=attn_in,
        query=query,
        keys=keys,
        values=values,
        weights=weights,
        weights_low=weights_low,
        mixed=mixed,
        attn_out=attn_out,
        resid=resid,
        mlp_in=mlp_in,
        hidden=hidden,
        active=active,
        mlp_out=mlp_out,
        result=result,
    )


def layer_back(x, cond_low, w_in, w_out, parts, grad_out, grad_cond):
    width = x.shape[-1]
    batch, seq = (x.shape[0], x.shape[1])
    size = width // HEADS
    shift_a, scale_a, gate_a, shift_b, scale_b, gate_b = parts["mods"]
    d_gate_b = jnp.sum(grad_out * parts["mlp_out"], axis=1)
    d_mlp_out = lowered(grad_out * gate_b[:, None, :])
    g_fc2 = jnp.einsum(
        "bsf,bsd->fd", parts["active"], d_mlp_out, preferred_element_type=jnp.float32
    )
    d_active = jnp.einsum("bsd,fd->bsf", d_mlp_out, w_out, preferred_element_type=jnp.float32)
    _, gelu_pull = jax.vjp(gelu_tanh, parts["hidden"])
    d_hidden = lowered(gelu_pull(d_active)[0])
    g_fc1 = jnp.einsum("bsd,bsf->df", parts["mlp_in"], d_hidden, preferred_element_type=jnp.float32)
    d_mlp_in = jnp.einsum(
        "bsf,df->bsd", d_hidden, w_in[:, 10 * width :], preferred_element_type=jnp.float32
    )
    _, norm_pull = jax.vjp(modulate, parts["resid"], shift_b, scale_b)
    d_resid, d_shift_b, d_scale_b = norm_pull(d_mlp_in)
    d_resid = d_resid + grad_out
    d_gate_a = jnp.sum(d_resid * parts["attn_out"], axis=1)
    d_attn_out = lowered(d_resid * gate_a[:, None, :])
    g_proj = jnp.einsum(
        "bsd,bse->de", parts["mixed"], d_attn_out, preferred_element_type=jnp.float32
    )
    d_mixed = lowered(
        jnp.einsum(
            "bse,de->bsd",
            d_attn_out,
            w_in[:, 9 * width : 10 * width],
            preferred_element_type=jnp.float32,
        )
    ).reshape(batch, seq, HEADS, size)
    d_probs = jnp.einsum(
        "bqhd,bkhd->bhqk", d_mixed, parts["values"], preferred_element_type=jnp.float32
    )
    d_values = jnp.einsum(
        "bhqk,bqhd->bkhd", parts["weights_low"], d_mixed, preferred_element_type=jnp.float32
    )
    weights = parts["weights"]
    d_scores = weights * (d_probs - jnp.sum(d_probs * weights, axis=-1, keepdims=True))
    d_scaled = lowered(d_scores * size ** (-0.5))
    d_query = jnp.einsum(
        "bhqk,bkhd->bqhd", d_scaled, parts["keys"], preferred_element_type=jnp.float32
    )
    d_keys = jnp.einsum(
        "bhqk,bqhd->bkhd", d_scaled, parts["query"], preferred_element_type=jnp.float32
    )
    d_qkv = lowered(
        jnp.concatenate(
            [
                d_query.reshape(batch, seq, width),
                d_keys.reshape(batch, seq, width),
                d_values.reshape(batch, seq, width),
            ],
            axis=-1,
        )
    )
    g_qkv = jnp.einsum("bsd,bse->de", parts["attn_in"], d_qkv, preferred_element_type=jnp.float32)
    d_attn_in = jnp.einsum(
        "bse,de->bsd", d_qkv, w_in[:, 6 * width : 9 * width], preferred_element_type=jnp.float32
    )
    _, first_pull = jax.vjp(modulate, x, shift_a, scale_a)
    d_x, d_shift_a, d_scale_a = first_pull(d_attn_in)
    d_x = d_x + d_resid
    d_mod = lowered(
        jnp.concatenate([d_shift_a, d_scale_a, d_gate_a, d_shift_b, d_scale_b, d_gate_b], axis=-1)
    )
    g_mod = product_tn(cond_low, d_mod)
    grad_cond = grad_cond + product_nt(d_mod, w_in[:, : 6 * width])
    g_in = jnp.concatenate([g_mod, g_qkv, g_proj, g_fc1], axis=1)
    return (d_x, grad_cond, g_in, g_fc2)


def local(
    noisy,
    timesteps,
    labels,
    noise,
    block_in,
    block_in_first,
    block_in_second,
    block_out,
    block_out_first,
    block_out_second,
    entry_table,
    entry_first,
    entry_second,
    exit_proj,
    exit_first,
    exit_second,
):
    layers = block_in.shape[0]
    entry_all, exit_all = (
        lax.all_gather(lowered(entry_table), "shard", axis=1, tiled=True),
        lax.all_gather(lowered(exit_proj), "shard", axis=0, tiled=True),
    )
    w_patch = entry_all[:PDIM]
    w_label = entry_all[PDIM : PDIM + NCLS]
    w_time = entry_all[PDIM + NCLS :]
    w_time2 = exit_all[:, :D]
    w_final = exit_all[:, D : 3 * D]
    w_output = exit_all[:, 3 * D :]
    patches = lowered(patchify(noisy, PATCH))
    target = patchify(noise, PATCH)
    seq = patches.shape[1]
    x = (
        jnp.einsum("bsp,pd->bsd", patches, w_patch, preferred_element_type=jnp.float32)
        + position_table(noisy.shape[-1] // PATCH, D)[None]
    )
    femb = lowered(time_features(timesteps, FREQ))
    t_hidden = product(femb, w_time)
    t_act = lowered(jax.nn.silu(t_hidden))
    temb = product(t_act, w_time2)
    onehot = (labels[:, None] == jnp.arange(NCLS)[None, :]).astype(jnp.float32)
    cond = temb + jnp.dot(onehot, w_label.astype(jnp.float32), precision=highest)
    cond_low = lowered(jax.nn.silu(cond))
    layer = 0
    w_in_all = lax.all_gather(lowered(block_in[layer]), "shard", axis=0, tiled=True)
    w_out_all = lax.all_gather(lowered(block_out[layer]), "shard", axis=0, tiled=True)
    inputs = [x]
    parts = layer_parts(x, cond_low, w_in_all, w_out_all)
    saved = [parts]
    x = parts["result"]
    final_mod = product(cond_low, w_final)
    shift_f, scale_f = jnp.split(final_mod, 2, axis=-1)
    final_in = lowered(modulate(x, shift_f, scale_f))
    pred = jnp.einsum("bsd,dp->bsp", final_in, w_output, preferred_element_type=jnp.float32)
    error = pred - target
    loss_part = jnp.sum(error * error) / (seq * PDIM)
    d_pred = lowered(2.0 * error / (seq * PDIM))
    g_output = jnp.einsum("bsd,bsp->dp", final_in, d_pred, preferred_element_type=jnp.float32)
    d_final_in = jnp.einsum("bsp,dp->bsd", d_pred, w_output, preferred_element_type=jnp.float32)
    _, final_pull = jax.vjp(modulate, x, shift_f, scale_f)
    d_x, d_shift_f, d_scale_f = final_pull(d_final_in)
    d_fmod = lowered(jnp.concatenate([d_shift_f, d_scale_f], axis=-1))
    g_final = product_tn(cond_low, d_fmod)
    grad_cond = product_nt(d_fmod, w_final)
    shards_in = [None] * layers
    shards_out = [None] * layers
    for layer in reversed(range(layers)):
        w_in_all, w_out_all = (
            lax.all_gather(lowered(block_in[layer]), "shard", axis=0, tiled=True),
            lax.all_gather(lowered(block_out[layer]), "shard", axis=0, tiled=True),
        )
        d_x, grad_cond, g_in, g_fc2 = layer_back(
            inputs[layer], cond_low, w_in_all, w_out_all, saved[layer], d_x, grad_cond
        )
        shards_in[layer], shards_out[layer] = (
            lax.psum_scatter(g_in, "shard", scatter_dimension=0, tiled=True),
            lax.psum_scatter(g_fc2, "shard", scatter_dimension=0, tiled=True),
        )
    _, silu_pull = jax.vjp(jax.nn.silu, cond)
    d_cond = silu_pull(grad_cond)[0]
    g_label = jnp.dot(onehot.T, d_cond, precision=highest)
    d_temb = lowered(d_cond)
    g_time2 = product_tn(t_act, d_temb)
    d_tact = product_nt(d_temb, w_time2)
    _, time_pull = jax.vjp(jax.nn.silu, t_hidden)
    d_thidden = lowered(time_pull(d_tact)[0])
    g_time = product_tn(femb, d_thidden)
    g_patch = jnp.einsum("bsp,bsd->pd", patches, lowered(d_x), preferred_element_type=jnp.float32)
    g_entry = jnp.concatenate([g_patch, g_label, g_time], axis=0)
    g_exit = jnp.concatenate([g_time2, g_final, g_output], axis=1)
    share_entry, share_exit = (
        lax.psum_scatter(g_entry, "shard", scatter_dimension=1, tiled=True),
        lax.psum_scatter(g_exit, "shard", scatter_dimension=0, tiled=True),
    )
    grads = (
        lax.psum(jnp.stack(shards_in).astype(jnp.bfloat16), "rep").astype(jnp.float32),
        lax.psum(jnp.stack(shards_out).astype(jnp.bfloat16), "rep").astype(jnp.float32),
        lax.psum(share_entry.astype(jnp.bfloat16), "rep").astype(jnp.float32),
        lax.psum(share_exit.astype(jnp.bfloat16), "rep").astype(jnp.float32),
    )
    squares = (
        jnp.sum(grads[0] * grads[0])
        + jnp.sum(grads[1] * grads[1])
        + jnp.sum(grads[2] * grads[2])
        + jnp.sum(grads[3] * grads[3])
    )
    loss = lax.psum(loss_part, ("rep", "shard"))
    norm_sq = lax.psum(squares, "shard")
    grad_norm = jnp.sqrt(norm_sq)
    factor = clip_limit / jnp.maximum(grad_norm, clip_limit)
    bi_w, bi_m, bi_v, bi_l = adam_step(
        block_in, block_in_first, block_in_second, grads[0], factor, rate_main
    )
    bo_w, bo_m, bo_v, bo_l = adam_step(
        block_out, block_out_first, block_out_second, grads[1], factor, rate_main
    )
    en_w, en_m, en_v, en_l = adam_step(
        entry_table, entry_first, entry_second, grads[2], factor, rate_edge
    )
    ex_w, ex_m, ex_v, ex_l = adam_step(
        exit_proj, exit_first, exit_second, grads[3], factor, rate_main
    )
    return (
        loss,
        grad_norm,
        bi_w,
        bi_m,
        bi_v,
        bi_l,
        bo_w,
        bo_m,
        bo_v,
        bo_l,
        en_w,
        en_m,
        en_v,
        en_l,
        ex_w,
        ex_m,
        ex_v,
        ex_l,
    )


BF = jnp.bfloat16
F32 = jnp.float32
MESH = pl.DeviceIdType.MESH
TOK = 256
TILE = 128
LANES = 128
CHUNKS = 12
START = (4, 2)
OWN_AT = ((), (4,), (5, 6), (7, 8), (9, 10), (11,))
Z_AT = ((2,), (3,), (4,), (5,), (6, 7), (8,), (9,), (10,), (11,))
VIA_Z = (1, 3, 5, 7, 9, 11)
SUM_VIA_Z = (0, 2, 4, 6, 8)
LEAD = 3
LAGS = (0, 2, 3, 4)
LAG_A = 1
UNITS = tuple((k, 0, 64) for k in (8, 9, 10, 11, 4, 5, 6, 7, 3, 0, 1)) + tuple((2, 16 * i, 16) for i in range(4))
NU = len(UNITS)
SMALL = 11


def dot_nn(left, right):
    return lax.dot_general(left, right, (((1,), (0,)), ((), ())), preferred_element_type=F32)


def dot_nt(left, right):
    return lax.dot_general(left, right, (((1,), (1,)), ((), ())), preferred_element_type=F32)


def dot_tn(left, right):
    return lax.dot_general(left, right, (((0,), (0,)), ((), ())), preferred_element_type=F32)


def dot_tn_exact(left, right):
    return lax.dot_general(
        left, right, (((0,), (0,)), ((), ())), preferred_element_type=F32, precision=highest
    )


def patches_of(image):
    how = highest if image.dtype == F32 else None

    def product_of(left, right, dims):
        return lax.dot_general(
            left.astype(image.dtype), right.astype(image.dtype), (dims, ((), ())),
            preferred_element_type=F32, precision=how,
        )

    def iota(shape, dim):
        return lax.broadcasted_iota(jnp.int32, shape, dim)

    total = 0.0
    mine = iota((TOK, 128), 0) >> 4 == (iota((TOK, 128), 1) & 31) >> 1
    for pc in range(2):
        pick = (2 * iota((16, 32), 0) + pc == iota((16, 32), 1)).astype(F32)
        cols = product_of(pick, image, ((1,), (1,)))
        spread = jnp.where(mine, jnp.concatenate([cols] * 16, axis=0), 0.0)
        row = iota((128, PDIM), 0)
        place = (row & 1) * 8 + pc * 4 + (row >> 5) == iota((128, PDIM), 1)
        total += product_of(spread, place.astype(F32), ((1,), (0,)))
    return total


def to_tile(value):
    return jnp.concatenate([value[0:8], value[8:16]], axis=1)


def from_tile(value):
    return jnp.concatenate([value[:, 0:64], value[:, 64:128]], axis=0)


def sigmoid(value):
    return 1.0 / (1.0 + jnp.exp(-value))


def silu_slope(value):
    gate = sigmoid(value)
    return gate * (1.0 + value * (1.0 - gate))


def normed(x):
    centered = x - jnp.mean(x, axis=-1, keepdims=True)
    var = jnp.mean(centered * centered, axis=-1, keepdims=True)
    inv = lax.rsqrt(var + 1e-06)
    return centered * inv, inv


def normed_back(d_normed, x_normed, inv):
    mean_d = jnp.mean(d_normed, axis=-1, keepdims=True)
    mean_dx = jnp.mean(d_normed * x_normed, axis=-1, keepdims=True)
    return inv * (d_normed - mean_d - x_normed * mean_dx)


def fold(value):
    rows, cols = value.shape
    return jnp.sum(value.reshape(rows // 8, 8, cols), axis=0)


def rows_at(i, size):
    return pl.ds(pl.multiple_of(i * size, size), size)


def step_kernel(
    msg, noisy, noise, pos, bi, bo, ent_in, ex_in,
    g_in, g_out, ENT, EX, stats,
    W, WP, G, R1, R2, R3, PF, FIN,
    ATI, QKV, MIX, MLI, ACT, GD, DMO, DAO, DMX, DMS,
    X0, AO, RSD, MO, X1, SND, RCV,
    WMOD, PAT, TGT, EDS, E1, EDG, E2S, E2R, E3S, E3R, DMB, DMF, B2S, B2R, DTA, CP, CND,
    B3S, B3R, B3D, NSS, NSR, MODS, DACC, WPT, WLT, GLP, SQ, LOSS,
    st_sem, peer_s, peer_r, zs, zr, bs, br, as_, ar,
    s1s, s1r, s2s, s2r, szs, szr, pss, psr, d_s, d_r, f_l, f_s, f_r,
    far_s, far_r, cred_a, cred_b, cred_z,
):
    c = lax.axis_index("rep")
    s = lax.axis_index("shard")
    o = 1 - c
    x = s % 2
    y = (s // 2) % 2
    z = s // 4
    a_me = y * o + x * c
    b_me = x * o + y * c

    def yx(a, b):
        return a * o + b * c, b * o + a * c

    def dev(core, chip):
        return {"rep": core, "shard": chip}

    def chip_of(zz, yy, xx):
        return zz * 4 + yy * 2 + xx

    nb_a = dev(c, chip_of(z, *yx(1 - a_me, b_me)))
    nb_b = dev(c, chip_of(z, *yx(a_me, 1 - b_me)))
    twin = dev(o, s)

    def remote(src, dst, ss, rs, to):
        return pltpu.make_async_remote_copy(
            src_ref=src, dst_ref=dst, send_sem=ss, recv_sem=rs, device_id=to, device_id_type=MESH
        )

    pieces = []
    for j in range(4):
        pieces.append((bi.at[:, pl.ds(pl.multiple_of(6144 + 1024 * j + c * 512, 512), 512)], FIN.at[j]))
    for j in range(16):
        pieces.append((
            bi.at[:, pl.ds(pl.multiple_of(10240 + 256 * j + c * 128, 128), 128)],
            FIN.at[4 + j // 4, :, pl.ds((j % 4) * 128, 128)],
        ))
    for ch in range(2):
        for rh in range(2):
            pieces.append((
                bo.at[pl.ds(pl.multiple_of(c * 128 + rh * 64, 64), 64), pl.ds(ch * 512, 512)],
                FIN.at[8 + 2 * ch + rh],
            ))
    pieces.append((ent_in, ENT))
    pieces.append((ex_in, EX))
    pieces.append((bi.at[:, pl.ds(0, 6144)], WMOD))
    local = [pltpu.make_async_copy(p, q, st_sem.at[i]) for i, (p, q) in enumerate(pieces)]
    for i in (24, 25, 0, 1, 2, 3, *range(4, 24), 26):
        local[i].start()

    barrier = pltpu.get_barrier_semaphore()

    @pl.loop(1, 16)
    def _(k):
        pl.semaphore_signal(barrier, 1, device_id=dev(c, (s + k) % 16), device_id_type=MESH)

    @pl.loop(0, 16)
    def _(k):
        pl.semaphore_signal(barrier, 1, device_id=dev(o, k), device_id_type=MESH)

    pl.semaphore_wait(barrier, 31)

    def peers_copy(e, k, src_of, dst):
        peer = (s + k) % 16
        return remote(src_of(peer), dst.at[s], peer_s.at[e, k], peer_r.at[e, s], dev(c, peer))

    def peers_send(e, src_of, dst):
        @pl.loop(1, 16)
        def _(k):
            peers_copy(e, k, src_of, dst).start()

    def peers_wait(e, src_of, dst):
        @pl.loop(1, 16)
        def _(k):
            frm = (s + k) % 16
            remote(src_of(frm), dst.at[frm], peer_s.at[e, k], peer_r.at[e, frm], dev(c, frm)).wait_recv()

        @pl.loop(1, 16)
        def _(k):
            peers_copy(e, k, src_of, dst).wait_send()

    def twin_copy(i, src, dst):
        return remote(src, dst, d_s.at[i], d_r.at[i], twin)

    def block(k, zz, far):
        yy, xx = yx(a_me, 1 - b_me if far else b_me)
        return W.at[k, zz, yy, xx]

    def z_copy(k, dz, far=0):
        at = block(k, z, far)
        i = k * 8 + far * 4
        return remote(at, at, zs.at[i + dz], zr.at[i + z], dev(c, chip_of((z + dz) % 4, y, x)))

    def z_wait(k, dz, far=0):
        frm = (z + dz) % 4
        at = block(k, frm, far)
        i = k * 8 + far * 4
        remote(at, at, zs.at[i + dz], zr.at[i + frm], dev(c, chip_of(frm, y, x))).wait_recv()

    inner = jnp.logical_or(z == 1, z == 2)

    def z_pass(k, far=0):
        at = block(k, (z + 2) % 4, far)
        i = k * 8 + far * 4
        return remote(at, at, zs.at[i], zr.at[i + (z + 2) % 4], dev(c, chip_of(3 * (z - 1), y, x)))

    def z_start(k, far=0):
        z_copy(k, 2, far).start()
        pl.when(z != 3)(lambda: z_copy(k, 1, far).start())
        pl.when(z != 0)(lambda: z_copy(k, 3, far).start())

    def z_arrived(k, dz, far=0):
        z_wait(k, dz, far)
        if dz == 2:
            pl.when(inner)(lambda: z_pass(k, far).start())

    def z_sent(k, far=0):
        z_copy(k, 2, far).wait_send()
        pl.when(z != 3)(lambda: z_copy(k, 1, far).wait_send())
        pl.when(z != 0)(lambda: z_copy(k, 3, far).wait_send())
        pl.when(inner)(lambda: z_pass(k, far).wait_send())

    def b_copy(k, zz):
        at = block(k, zz, 0)
        return remote(at, at, bs.at[k * 4 + zz], br.at[k * 4 + zz], nb_b)

    def a_copy(k, zz, far=0):
        at = block(k, zz, far)
        i = k * 8 + far * 4 + zz
        return remote(at, at, as_.at[i], ar.at[i], nb_a)

    def own(k):
        cast(k)
        b_copy(k, z).start()
        a_copy(k, z).start()

    def far_start(k):
        b_copy(k, z).wait_recv()
        z_start(k, 1)
        a_copy(k, z, 1).start()

    def pump_b(k):
        for dz in (2, 1, 3):
            frm = (z + dz) % 4
            z_arrived(k, dz)
            if k not in VIA_Z:
                b_copy(k, frm).start()
            a_copy(k, frm).start()

    def pump_a(k):
        if k in VIA_Z:
            for dz in (2, 1, 3):
                z_arrived(k, dz, 1)
                a_copy(k, (z + dz) % 4, 1).start()
        else:
            for dz in range(4):
                b_copy(k, (z + dz) % 4).wait_recv()
                a_copy(k, (z + dz) % 4, 1).start()

    def sends_done(k):
        z_sent(k)
        if k in VIA_Z:
            z_sent(k, 1)
        else:
            for dz in range(1, 4):
                b_copy(k, (z + dz) % 4).wait_send()
        b_copy(k, z).wait_send()
        for far in range(2):
            for zz in range(4):
                a_copy(k, zz, far).wait_send()

    def pump(k):
        for i in OWN_AT[k] if k < len(OWN_AT) else ():
            own(i)
        for i in Z_AT[k] if k < len(Z_AT) else ():
            z_start(i)
        if k + 1 in VIA_Z:
            far_start(k + 1)
        if k < CHUNKS:
            pump_b(k)
        if 0 <= k - LAG_A < CHUNKS:
            pump_a(k - LAG_A)

    def need(k):
        for far in range(2):
            for dz in range(4):
                a_copy(k, (z + dz) % 4, far).wait_recv()

    def cast(k):
        if k < 4:
            local[k].wait()
            W[k, z, y, x] = FIN[k].astype(BF)
        elif k < 8:
            if k == 4:
                for i in range(4, 20):
                    local[i].wait()
            rh, half = (k - 4) // 2, (k - 4) % 2
            for q in range(4):
                j = half * 8 + 2 * q
                pair = FIN[4 + j // 4, :, (j % 4) * 128 : (j % 4) * 128 + 256]
                piece = jnp.concatenate(
                    [pair[:, rh * 64 : rh * 64 + 64], pair[:, 128 + rh * 64 : 128 + rh * 64 + 64]], axis=1
                )
                W[k, z, y, x, :, q * 128 : q * 128 + 128] = piece.astype(BF)
        else:
            local[20 + k - 8].wait()
            W[k, z, y, x] = FIN[k].astype(BF)

    E1[c, s] = msg[...]
    peers_send(0, lambda p: msg, E1.at[c])
    for k in range(START[0]):
        own(k)
        if k < START[1]:
            z_start(k)

    local[24].wait()
    local[25].wait()
    peers_wait(0, lambda p: msg, E1.at[c])
    t_hidden = dot_nt(E1[c, :, 0, :].astype(BF), ENT[:, 1016:1144].astype(BF)) + dot_nt(
        E1[c, :, 1, :].astype(BF), ENT[:, 1144:1272].astype(BF)
    )
    CND[0] = t_hidden
    t_act = (t_hidden * sigmoid(t_hidden)).astype(BF)
    CP[c, 1, :, 0:64] = t_act.astype(F32)
    for q in range(8):
        part = dot_nn(t_act, EX[:, q * 128 : q * 128 + 128].astype(BF))
        for h in range(2):
            E2S[2 * q + h] = to_tile(part[:, 64 * h : 64 * h + 64])
    E2R[s] = E2S[s]
    peers_send(1, lambda p: E2S.at[p], E2R)
    pump(0)
    hot = (
        E1[c, :, 2, 0:1].astype(jnp.int32) + PDIM == lax.broadcasted_iota(jnp.int32, (16, ENTRIES), 1)
    ).astype(F32).astype(BF)
    w_class = dot_nt(hot, ENT[...].astype(BF))
    pump(1)
    local[26].wait()
    peers_wait(1, lambda p: E2S.at[p], E2R)
    cond = from_tile(jnp.sum(E2R[...], axis=0)) + w_class
    CND[1] = cond
    cond_low = (cond * sigmoid(cond)).astype(BF)
    CP[c, 0, :, 0:64] = cond_low.astype(F32)
    for k in range(8):
        w_k = WMOD[:, k * 1024 : k * 1024 + 1024] if k < 6 else EX[:, (k - 5) * 1024 : (k - 4) * 1024]
        DMF[0, k] = dot_nn(cond_low, w_k.astype(BF))

    @pl.loop(0, 16)
    def _(l):
        part = DMF[0, :, l, :]
        E3S[l] = jnp.concatenate([part[:, :512], part[:, 512:]], axis=0).astype(BF)

    E3R[s] = E3S[s]
    peers_send(2, lambda p: E3S.at[p], E3R)
    edges = jnp.concatenate(
        [ENT[:, 0:128], jnp.concatenate([EX[:, 3072:3088], jnp.zeros((64, 112), F32)], axis=1)], axis=0
    )
    edges = edges.T[0:16].astype(BF)
    EDS[...] = edges
    EDG[s] = edges
    peers_send(7, lambda p: EDS, EDG)
    pump(2)

    PAT[...] = patches_of(noisy[...].astype(BF)).astype(BF)
    TGT[...] = patches_of(noise[...])
    peers_wait(7, lambda p: EDS, EDG)
    for q in range(8):
        even, odd = EDG[2 * q], EDG[2 * q + 1]
        WPT[:, q * 128 : q * 128 + 128] = jnp.concatenate([even[:, :64], odd[:, :64]], axis=1)
        WLT[:, q * 128 : q * 128 + 128] = jnp.concatenate([even[:, 64:], odd[:, 64:]], axis=1)
    for n in range(4):
        cols = slice(n * 256, n * 256 + 256)
        X0[:, cols] = dot_nn(PAT[...], WPT[:, cols])

    @pl.loop(0, 16)
    def _(i):
        X0[rows_at(i, 16), 0:512] += pos[...]
        X0[rows_at(i, 16), 512:1024] += jnp.broadcast_to(pos[pl.ds(i, 1), :], (16, 512))

    DACC[...] = jnp.zeros_like(DACC)
    pump(3)
    peers_wait(2, lambda p: E3S.at[p], E3R)
    parts = E3R[0].astype(F32)
    for i in range(1, 16):
        parts += E3R[i].astype(F32)
    MODS[...] = jnp.concatenate([parts[0:8], parts[8:16]], axis=1)

    def mod_row(k):
        return MODS[k : k + 1, :]

    def modulated(src, dst, shift, scale):
        @pl.loop(0, TOK // TILE)
        def _(i):
            r = rows_at(i, TILE)
            hat, _ = normed(src[r, :])
            dst[c, r, :] = (hat * (1.0 + mod_row(scale)) + mod_row(shift)).astype(BF)

    modulated(X0, ATI, 0, 1)
    twin_copy(0, ATI.at[c], ATI.at[c]).start()
    pump(4)
    twin_copy(0, ATI.at[o], ATI.at[o]).wait_recv()

    def w_cols(k, n):
        return W[k, :, :, :, :, rows_at(n, 256)].reshape(1024, 256)

    for j in range(3):
        need(j)

        @pl.loop(0, 4)
        def _(t):
            lat, n = t // 2, t % 2
            QKV[j, lat, :, rows_at(n, 256)] = dot_nn(ATI[lat], w_cols(j, n)).astype(BF)

        pump(5 + j)

    lane = lax.broadcasted_iota(jnp.int32, (1, LANES), 1)
    first = lane < 64
    masks = (first.astype(F32).astype(BF), 1.0 - first.astype(F32).astype(BF))

    def probs_of(q, k):
        score = dot_nt(q, k) * 0.125
        e = jnp.exp(score - jnp.max(score, axis=-1, keepdims=True))
        return e / jnp.sum(e, axis=-1, keepdims=True)

    def attention(t):
        lat, cols = t // 4, rows_at(t % 4, 128)
        q, k, v = QKV[0, lat, :, cols], QKV[1, lat, :, cols], QKV[2, lat, :, cols]
        outs = [dot_nn(probs_of(q * m, k).astype(BF), v) for m in masks]
        MIX[c, lat, :, cols] = jnp.where(first, outs[0], outs[1]).astype(BF)

    pl.loop(0, 4)(attention)
    pump(8)
    pl.loop(4, 8)(attention)

    twin_copy(1, MIX.at[c], MIX.at[c]).start()
    need(3)
    twin_copy(2, W.at[3], WP).start()
    pump(9)
    twin_copy(1, MIX.at[o], MIX.at[o]).wait_recv()
    twin_copy(2, W.at[3], WP).wait_recv()

    def proj(own):
        def cols(n):
            return pl.ds(pl.multiple_of((c if own else o) * 512 + n * 256, 256), 256)

        @pl.loop(0, 2)
        def _(n):
            ref = W.at[3] if own else WP
            total = 0.0
            for hh in range(2):
                w_half = ref[2 * hh : 2 * hh + 2, :, :, :, rows_at(n, 256)].reshape(512, 256)
                total += dot_nn(MIX[hh, c], w_half)
            AO[:, cols(n)] = total

    proj(True)
    proj(False)

    @pl.loop(0, TOK // TILE)
    def _(i):
        r = rows_at(i, TILE)
        RSD[r, :] = X0[r, :] + mod_row(2) * AO[r, :]

    modulated(RSD, MLI, 3, 4)
    twin_copy(3, MLI.at[c], MLI.at[c]).start()
    pump(10)
    twin_copy(3, MLI.at[o], MLI.at[o]).wait_recv()
    for j in range(4):
        need(4 + j)

        @pl.loop(0, 4)
        def _(t):
            lat, n = t // 2, t % 2
            hidden = dot_nn(MLI[lat], w_cols(4 + j, n))
            cols = pl.ds(pl.multiple_of(j * 512 + n * 256, 256), 256)
            square = hidden * hidden
            t_in = 0.7978845608028654 * hidden * (1.0 + 0.044715 * square)
            t_out = jnp.tanh(t_in)
            half = 0.5 * (1.0 + t_out)
            ACT[lat, :, cols] = (hidden * half).astype(BF)
            slope = half + 0.5 * hidden * (1.0 - t_out * t_out) * (
                0.7978845608028654 * (1.0 + 3.0 * 0.044715 * square)
            )
            GD[lat, :, cols] = slope.astype(BF)

        if j < 2:
            pump(11 + j)

    for k in range(8):
        sends_done(k)
    for ch in range(2):
        need(8 + 2 * ch)
        need(9 + 2 * ch)

        def mlp_tile(lat, n):
            total = 0.0
            for rh in range(2):
                total += dot_nn(ACT[lat, :, rh * 1024 : rh * 1024 + 1024], w_cols(8 + 2 * ch + rh, n))
            return total

        @pl.loop(0, 2)
        def _(n):
            SND[ch, :, rows_at(n, 256)] = mlp_tile(o, n)

        twin_copy(4 + ch, SND.at[ch], RCV.at[ch]).start()

        @pl.loop(0, 2)
        def _(n):
            MO[:, pl.ds(pl.multiple_of(ch * 512 + n * 256, 256), 256)] = mlp_tile(c, n)

    def received(i):
        for ch in range(2):
            twin_copy(i + ch, SND.at[ch], RCV.at[ch]).wait_recv()

    def both_parts(r):
        return MO[r, :] + jnp.concatenate([RCV[0, r, :], RCV[1, r, :]], axis=1)

    received(4)
    LOSS[...] = jnp.zeros_like(LOSS)
    GLP[...] = jnp.zeros_like(GLP)

    @pl.loop(0, TOK // TILE)
    def _(i):
        r = rows_at(i, TILE)
        mlp_out = both_parts(r)
        x1 = RSD[r, :] + mod_row(5) * mlp_out
        hat, inv = normed(x1)
        scale = 1.0 + mod_row(7)
        final_in = (hat * scale + mod_row(6)).astype(BF)
        w_lin = WLT[...]
        error = dot_nt(final_in, w_lin) - TGT[r, :]
        LOSS[...] += fold(error * error)
        d_pred = (2.0 * error / (TOK * PDIM)).astype(BF)
        GLP[16:32, :] += dot_tn(d_pred, final_in)
        d_final = dot_nn(d_pred, w_lin)
        DACC[6] += fold(d_final)
        DACC[7] += fold(d_final * hat)
        d_x = normed_back(d_final * scale, hat, inv)
        X1[r, :] = d_x
        DACC[5] += fold(d_x * mlp_out)
        DMO[c, r, :] = (d_x * mod_row(5)).astype(BF)

    twin_copy(6, DMO.at[c], DMO.at[c]).start()

    def r1_of(k, b):
        return R1.at[k - 8, b] if k >= 8 else W.at[8 + k // 2, :, k % 2, b]

    def r2_of(k):
        return R2.at[k - 8] if k >= 8 else W.at[4 + k // 4, :, (k // 2) % 2, k % 2]

    def r3_of(k):
        return R3.at[k - 8] if k >= 8 else W.at[6 + k // 4, :, (k // 2) % 2, k % 2]

    def rows_of(u):
        return pl.ds(UNITS[u][1], UNITS[u][2])

    def g_at(u, zz, a, b):
        yy, xx = yx(a, b)
        return G.at[UNITS[u][0], zz, yy, xx, rows_of(u)]

    def b_of(far):
        return 1 - b_me if far else b_me

    def z_slot(u, i, far):
        return (r2_of if far else r3_of)(UNITS[u][0]).at[i, rows_of(u)]

    def pass_slot(u, i, far):
        return PF.at[SUM_VIA_Z.index(u)] if far else z_slot(u, i, 0)

    def s1_copy(u, b):
        k, r = UNITS[u][0], rows_of(u)
        yy, xx = yx(1 - a_me, b)
        return remote(G.at[k, :, yy, xx, r], r1_of(k, b).at[:, r], s1s.at[u * 2 + b], s1r.at[u * 2 + b], nb_a)

    def s2_copy(u):
        if u in SUM_VIA_Z:
            return remote(g_at(u, z, a_me, 1 - b_me), z_slot(u, z, 1), s2s.at[u], s2r.at[u], nb_b)
        k, r = UNITS[u][0], rows_of(u)
        yy, xx = yx(a_me, 1 - b_me)
        return remote(G.at[k, :, yy, xx, r], r2_of(k).at[:, r], s2s.at[u], s2r.at[u], nb_b)

    def line(zz):
        return dev(c, chip_of(zz, y, x))

    def sz_copy(u, dz, far):
        zt = (z + dz) % 4
        i = u * 8 + far * 4
        return remote(g_at(u, zt, a_me, b_of(far)), z_slot(u, z, far), szs.at[i + dz], szr.at[i + z], line(zt))

    def sz_wait(u, dz, far):
        frm = (z + dz) % 4
        i = u * 8 + far * 4
        remote(g_at(u, frm, a_me, b_of(far)), z_slot(u, frm, far), szs.at[i + dz], szr.at[i + frm], line(frm)).wait_recv()

    near_end = jnp.where(z < 2, 1, 2)

    def pass_copy(u, far):
        i = u * 2 + far
        return remote(g_at(u, 3 - z, a_me, b_of(far)), pass_slot(u, near_end, far), pss.at[i], psr.at[i], line(near_end))

    def sum_a(u, zz, far):
        k, r = UNITS[u][0], rows_of(u)
        b = b_of(far)
        yy, xx = yx(a_me, b)
        return G[k, zz, yy, xx, r].astype(F32) + r1_of(k, b)[zz, r].astype(F32)

    def store(u, zz, far, value):
        g_at(u, zz, a_me, b_of(far))[...] = value.astype(BF)

    def sz_start(u, far):
        for dz in (1, 3):
            alone = z != (3 if dz == 1 else 0)
            if u >= SMALL:
                sz_copy(u, dz, far).start()
            else:
                pl.when(alone)(lambda: sz_copy(u, dz, far).start())
                pl.when(jnp.logical_not(alone))(lambda: pass_copy(u, far).start())
        if u >= SMALL:
            sz_copy(u, 2, far).start()
        else:
            pl.when(jnp.logical_not(inner))(lambda: sz_copy(u, 2, far).start())

    def sz_pass(u, far):
        @pl.when(inner)
        def _():
            i = u * 2 + far
            slot = pass_slot(u, z, far)
            remote(g_at(u, z, a_me, b_of(far)), slot, pss.at[i], psr.at[i], line(z)).wait_recv()
            zt = (z + 2) % 4
            store(u, zt, far, g_at(u, zt, a_me, b_of(far))[...].astype(F32) + slot[...].astype(F32))
            sz_copy(u, 2, far).start()

    def sz_sum(u, far):
        into = FIN.at[UNITS[u][0], rows_of(u)]

        def add(dz):
            sz_wait(u, dz, far)
            into[...] += z_slot(u, (z + dz) % 4, far)[...].astype(F32)

        for dz in (1, 3, 2):
            if u >= SMALL or dz == 2:
                add(dz)
            else:
                pl.when(z != (3 if dz == 1 else 0))(lambda: add(dz))

    def s1(u):
        for b in range(2):
            s1_copy(u, b).start()

    def stage_1(u):
        for b in range(2):
            s1_copy(u, b).wait_recv()
        if u in SUM_VIA_Z:
            for far in (1, 0):
                for dz in (1, 3, 2):
                    store(u, (z + dz) % 4, far, sum_a(u, (z + dz) % 4, far))
                sz_start(u, far)
        else:
            @pl.loop(0, 4)
            def _(zz):
                store(u, zz, 1, sum_a(u, zz, 1))

            s2_copy(u).start()

    def stage_2(u):
        if u in SUM_VIA_Z:
            for far in (1, 0):
                sz_pass(u, far)
        else:
            k, r = UNITS[u][0], rows_of(u)
            s2_copy(u).wait_recv()
            for dz in (1, 3, 2):
                zt = (z + dz) % 4
                store(u, zt, 0, sum_a(u, zt, 0) + r2_of(k)[zt, r].astype(F32))
            sz_start(u, 0)
            FIN[k, r] = sum_a(u, z, 0) + r2_of(k)[z, r].astype(F32)

    def stage_3(u):
        k, r = UNITS[u][0], rows_of(u)
        if u in SUM_VIA_Z:
            FIN[k, r] = sum_a(u, z, 1)
            sz_sum(u, 1)
            store(u, z, 1, FIN[k, r])
            s2_copy(u).start()
            FIN[k, r] = sum_a(u, z, 0)
            sz_sum(u, 0)
        elif u < SMALL:
            sz_pass(u, 0)

    def stage_4(u):
        k, r = UNITS[u][0], rows_of(u)
        if u in SUM_VIA_Z:
            s2_copy(u).wait_recv()
            FIN[k, r] += z_slot(u, z, 1)[...].astype(F32)
        else:
            sz_sum(u, 0)
        total = FIN[k, r]
        SQ[...] += fold(total * total)

    def sums_done(u):
        for b in range(2):
            s1_copy(u, b).wait_send()
        s2_copy(u).wait_send()
        for far in range(2 if u in SUM_VIA_Z else 1):
            sz_copy(u, 2, far).wait_send()
            for dz in (1, 3):
                if u >= SMALL:
                    sz_copy(u, dz, far).wait_send()
                else:
                    alone = z != (3 if dz == 1 else 0)
                    pl.when(alone)(lambda: sz_copy(u, dz, far).wait_send())
                    pl.when(jnp.logical_not(alone))(lambda: pass_copy(u, far).wait_send())

    def result_copies(i):
        if i < 4:
            k = 8 + i
            src = FIN.at[k]
            dst = g_out.at[
                pl.ds(pl.multiple_of(c * 128 + (i % 2) * 64, 64), 64), pl.ds((i // 2) * 512, 512)
            ]
        elif i < 20:
            j = i - 4
            src = FIN.at[4 + j // 8 + 2 * (j % 2), :, pl.ds(((j % 8) // 2) * 128, 128)]
            dst = g_in.at[:, pl.ds(pl.multiple_of(10240 + 256 * j + c * 128, 128), 128)]
        else:
            k, r0, size = ((3, 0, 64), *UNITS[9:])[i - 20]
            src = FIN.at[k, pl.ds(r0, size)]
            dst = g_in.at[pl.ds(r0, size), pl.ds(pl.multiple_of(6144 + 1024 * k + c * 512, 512), 512)]
        return pltpu.make_async_copy(src, dst, f_l.at[i]), remote(src, dst, f_s.at[i], f_r.at[i], twin)

    def send_result(u):
        k = UNITS[u][0]
        if k >= 8:
            span = (k - 8,)
        elif k == 7:
            for half in range(2):
                for q in range(4):
                    cols = slice(q * 128, q * 128 + 128)
                    low, high = FIN[4 + half, :, cols], FIN[6 + half, :, cols]
                    FIN[4 + half, :, cols] = jnp.concatenate([low[:, 0:64], high[:, 0:64]], axis=1)
                    FIN[6 + half, :, cols] = jnp.concatenate([low[:, 64:128], high[:, 64:128]], axis=1)
            span = range(4, 20)
        elif k >= 4:
            span = ()
        else:
            span = (20 + u - 8,)
        for i in span:
            for copy in result_copies(i):
                copy.start()

    def step(t):
        for u in range(t + LEAD, NU):
            if u == t + LEAD and u <= 11 or t + LEAD == 11:
                if u == 4:
                    pl.semaphore_wait(cred_a, 1)
                s1(u)
        if t == 4:
            pl.semaphore_wait(cred_b, 1)
            pl.semaphore_wait(cred_z, 3)
        for stage, lag in zip((stage_1, stage_2, stage_3, stage_4), LAGS):
            if 0 <= t - lag < NU:
                stage(t - lag)
                if stage is stage_4:
                    send_result(t - lag)
                    if 2 <= t - lag < 11:
                        sums_done(t - lag - 2)

    def grad_tiles(k, left, right):
        @pl.loop(0, 4)
        def _(r):
            G[k, r] = dot_tn(left(r), right).astype(BF).reshape(2, 2, 64, 512)

    SQ[...] = jnp.zeros_like(SQ)
    twin_copy(6, DMO.at[o], DMO.at[o]).wait_recv()
    for ch in range(2):
        for rh in range(2):
            k = 8 + 2 * ch + rh
            grad_tiles(
                k,
                lambda r: ACT[:, :, pl.ds(pl.multiple_of(rh * 1024 + r * 256, 256), 256)].reshape(512, 256),
                DMO[:, :, ch * 512 : ch * 512 + 512].reshape(512, 512),
            )
            if 2 * ch + rh < LEAD:
                s1(2 * ch + rh)

    for k in range(8, CHUNKS):
        sends_done(k)

    @pl.loop(0, 16)
    def _(t):
        lat, rh, r = t // 8, (t // 4) % 2, t % 4
        total = 0.0
        for ch in range(2):
            total += dot_nt(DMO[lat, :, ch * 512 : ch * 512 + 512], W[8 + 2 * ch + rh, r].reshape(256, 512))
        cols = pl.ds(pl.multiple_of(rh * 1024 + r * 256, 256), 256)
        GD[lat, :, cols] = (total * GD[lat, :, cols].astype(F32)).astype(BF)

    pl.semaphore_signal(cred_a, 1, device_id=nb_a, device_id_type=MESH)

    def data_back(first_k, count, left, i):
        for ch in range(2):
            @pl.loop(0, 2)
            def _(n):
                total = 0.0
                for j in range(count):
                    total += dot_nt(left(j, o), W[first_k + j, 2 * ch + n].reshape(256, 512))
                SND[ch, :, rows_at(n, 256)] = total

            twin_copy(i + ch, SND.at[ch], RCV.at[ch]).start()

        @pl.loop(0, 4)
        def _(r):
            total = 0.0
            for j in range(count):
                total += dot_nt(left(j, c), W[first_k + j, r].reshape(256, 512))
            MO[:, rows_at(r, 256)] = total

    for ch in range(2):
        twin_copy(4 + ch, SND.at[ch], RCV.at[ch]).wait_send()
    data_back(4, 4, lambda j, lat: GD[lat, :, j * 512 : j * 512 + 512], 7)
    pl.semaphore_signal(cred_b, 1, device_id=nb_b, device_id_type=MESH)
    for dz in range(1, 4):
        pl.semaphore_signal(cred_z, 1, device_id=dev(c, chip_of((z + dz) % 4, y, x)), device_id_type=MESH)

    step(0)
    for j in range(4):
        grad_tiles(
            4 + j,
            lambda r: MLI[:, :, rows_at(r, 256)].reshape(512, 256),
            GD[:, :, j * 512 : j * 512 + 512].reshape(512, 512),
        )
    received(7)

    @pl.loop(0, TOK // TILE)
    def _(i):
        r = rows_at(i, TILE)
        d_in = both_parts(r)
        hat, inv = normed(RSD[r, :])
        DACC[3] += fold(d_in)
        DACC[4] += fold(d_in * hat)
        d_x = normed_back(d_in * (1.0 + mod_row(4)), hat, inv) + X1[r, :]
        X1[r, :] = d_x
        DACC[2] += fold(d_x * AO[r, :])
        DAO[c, r, :] = (d_x * mod_row(2)).astype(BF)

    dao_other = pl.ds(pl.multiple_of(o * 512, 512), 512)
    dao_mine = pl.ds(pl.multiple_of(c * 512, 512), 512)
    twin_copy(9, DAO.at[c, :, dao_other], DAO.at[c, :, dao_other]).start()

    def mixed_back(hh, n):
        w_mine = W[3, 2 * hh + n].reshape(256, 512)
        w_other = WP[2 * hh + n].reshape(256, 512)
        return (dot_nt(DAO[c, :, dao_mine], w_mine) + dot_nt(DAO[c, :, dao_other], w_other)).astype(BF)

    @pl.loop(0, 2)
    def _(n):
        DMS[:, rows_at(n, 256)] = mixed_back(o, n)

    twin_copy(10, DMS, DMX.at[c]).start()

    @pl.loop(0, 2)
    def _(n):
        DMX[c, :, rows_at(n, 256)] = mixed_back(c, n)

    step(1)
    twin_copy(9, DAO.at[o, :, dao_mine], DAO.at[o, :, dao_mine]).wait_recv()

    @pl.loop(0, 4)
    def _(r):
        left = MIX[r // 2, :, :, rows_at(r % 2, 256)].reshape(512, 256)
        G[3, r] = dot_tn(left, DAO[:, :, dao_mine].reshape(512, 512)).astype(BF).reshape(2, 2, 64, 512)

    twin_copy(10, DMS, DMX.at[o]).wait_recv()

    def attention_back(t):
        lat, cols = t // 4, rows_at(t % 4, 128)
        q, k, v = QKV[0, lat, :, cols], QKV[1, lat, :, cols], QKV[2, lat, :, cols]
        dm = DMX[lat, :, cols]
        res = []
        for m in masks:
            probs = probs_of(q * m, k)
            d_probs = dot_nt(dm * m, v)
            d_v = dot_tn(probs.astype(BF), dm)
            d_s = probs * (d_probs - jnp.sum(d_probs * probs, axis=-1, keepdims=True))
            d_s = (d_s * 0.125).astype(BF)
            res.append((dot_nn(d_s, k), dot_tn(d_s, q), d_v))
        for j in range(3):
            QKV[j, lat, :, cols] = jnp.where(first, res[0][j], res[1][j]).astype(BF)

    for half in range(2):
        pl.loop(4 * half, 4 * half + 4)(attention_back)
        step(2 + half)
    for ch in range(2):
        twin_copy(7 + ch, SND.at[ch], RCV.at[ch]).wait_send()
    data_back(0, 3, lambda j, lat: QKV[j, lat], 11)
    for j in range(3):
        grad_tiles(
            j,
            lambda r: ATI[:, :, rows_at(r, 256)].reshape(512, 256),
            QKV[j].reshape(512, 512),
        )
    received(11)

    @pl.loop(0, TOK // TILE)
    def _(i):
        r = rows_at(i, TILE)
        d_in = both_parts(r)
        hat, inv = normed(X0[r, :])
        DACC[0] += fold(d_in)
        DACC[1] += fold(d_in * hat)
        d_x = normed_back(d_in * (1.0 + mod_row(1)), hat, inv) + X1[r, :]
        GLP[0:16, :] += dot_tn(PAT[r, :], d_x.astype(BF))

    for k in range(8):
        MODS[k : k + 1, :] = jnp.sum(DACC[k], axis=0, keepdims=True)
    d_mods = MODS[...]
    DMB[c, s] = jnp.concatenate([d_mods[:, :512], d_mods[:, 512:]], axis=0).astype(BF)
    peers_send(3, lambda p: DMB.at[c, s], DMB.at[c])
    for q in range(16):
        cols = slice(q * 64, q * 64 + 64)
        B3S[q] = jnp.concatenate([GLP[0:16, cols], GLP[16:32, cols]], axis=1).astype(BF)
    B3R[s] = B3S[s]
    peers_send(4, lambda p: B3S.at[p], B3R)
    step(4)
    step(5)
    step(6)
    peers_wait(3, lambda p: DMB.at[c, s], DMB.at[c])
    twin_copy(13, DMB.at[c], DMB.at[c]).start()

    def unpack(g):
        @pl.loop(0, 16)
        def _(l):
            both = DMB[g, l].astype(F32)
            DMF[g, :, l, 0:512] = both[0:8]
            DMF[g, :, l, 512:1024] = both[8:16]

    unpack(c)
    d_cond_low = 0.0
    for k in range(8):
        w_k = WMOD[:, k * 1024 : k * 1024 + 1024] if k < 6 else EX[:, (k - 5) * 1024 : (k - 4) * 1024]
        d_cond_low += dot_nt(DMF[c, k].astype(BF), w_k.astype(BF))
    d_cond = d_cond_low * silu_slope(CND[1])
    CP[c, 2, :, 0:64] = d_cond
    d_temb = d_cond.astype(BF).astype(F32)
    B2S[...] = to_tile(d_temb)
    B2R[s] = B2S[...]
    peers_send(5, lambda p: B2S, B2R)
    step(7)
    peers_wait(4, lambda p: B3S.at[p], B3R)
    sums = B3R[0].astype(F32)
    for i in range(1, 16):
        sums += B3R[i].astype(F32)
    B3D[c] = sums
    twin_copy(14, B3D.at[c], B3D.at[c]).start()
    peers_wait(5, lambda p: B2S, B2R)
    for q in range(8):
        DTA[c, :, q * 128 : q * 128 + 128] = jnp.concatenate(
            [from_tile(B2R[2 * q]), from_tile(B2R[2 * q + 1])], axis=1
        )
    d_tact = dot_nt(DTA[c].astype(BF), EX[:, 0:1024].astype(BF))
    CP[c, 3, :, 0:64] = (d_tact * silu_slope(CND[0])).astype(BF).astype(F32)
    twin_copy(15, DTA.at[c], DTA.at[c]).start()
    twin_copy(16, CP.at[c], CP.at[c]).start()
    twin_copy(17, E1.at[c], E1.at[c]).start()
    step(8)
    twin_copy(13, DMB.at[o], DMB.at[o]).wait_recv()
    unpack(o)
    twin_copy(14, B3D.at[o], B3D.at[o]).wait_recv()
    twin_copy(15, DTA.at[o], DTA.at[o]).wait_recv()
    twin_copy(16, CP.at[o], CP.at[o]).wait_recv()
    twin_copy(17, E1.at[o], E1.at[o]).wait_recv()

    def packed(i):
        return jnp.concatenate([CP[0, i, :, 0:64], CP[1, i, :, 0:64]], axis=0)

    def square_half(value):
        part = 0.5 * value * value
        return jnp.sum(jnp.sum(part, axis=0, keepdims=True), axis=1, keepdims=True)

    cond_both = packed(0).astype(BF)
    small = jnp.zeros((1, 1), F32)
    for k in range(8):
        grad = dot_tn(cond_both, jnp.concatenate([DMF[0, k], DMF[1, k]], axis=0).astype(BF))
        small += square_half(grad)
        if k < 6:
            WMOD[:, k * 1024 : k * 1024 + 1024] = grad
        else:
            EX[:, (k - 5) * 1024 : (k - 4) * 1024] = grad
    mod_out = pltpu.make_async_copy(WMOD, g_in.at[:, pl.ds(0, 6144)], st_sem.at[26])
    mod_out.start()
    step(9)
    grad = dot_tn(packed(1).astype(BF), jnp.concatenate([DTA[0], DTA[1]], axis=0).astype(BF))
    small += square_half(grad)
    EX[:, 0:1024] = grad
    sums = B3D[0] + B3D[1]
    small += square_half(sums[:, 64:128])
    wide = jnp.concatenate(
        [sums, jnp.zeros((112, 128), F32)], axis=0
    )
    EX[:, 3072:3088] = wide.T[64:128, 0:16]
    def both(value):
        return jnp.concatenate([value(0), value(1)], axis=0)

    index = lax.broadcasted_iota(jnp.int32, (32, ENTRIES), 1)
    hot = (both(lambda g: E1[g, :, 2, 0:1]).astype(jnp.int32) + PDIM == index).astype(F32)
    grad = dot_tn_exact(packed(2), hot)
    spot = lax.broadcasted_iota(jnp.int32, (16, ENTRIES), 0) == index[0:16]
    grad += dot_tn_exact(sums[:, 0:64], spot.astype(F32))
    ENT[...] = grad
    femb = both(lambda g: jnp.concatenate([E1[g, :, 0, :], E1[g, :, 1, :]], axis=1)).astype(BF)
    ENT[:, PDIM + NCLS :] = dot_tn(packed(3).astype(BF), femb)
    small += square_half(ENT[...])

    for t in range(10, NU + LAGS[3]):
        step(t)

    def total_of(value):
        return jnp.sum(jnp.sum(value, axis=0, keepdims=True), axis=1, keepdims=True)

    NSS[0:1, :] = jnp.broadcast_to(total_of(SQ[...]) + small, (1, 128))
    NSS[1:2, :] = jnp.broadcast_to(total_of(LOSS[...]) / (TOK * PDIM), (1, 128))
    NSS[2:8, :] = jnp.zeros((6, 128), F32)
    NSR[c * 16 + s] = NSS[...]

    def far_copy(k, frm):
        return remote(NSS, NSR.at[frm], far_s.at[k], far_r.at[frm % 16], dev(o, k))

    @pl.loop(0, 16)
    def _(k):
        far_copy(k, c * 16 + s).start()

    mine = NSR.at[pl.ds(c * 16, 16)]
    peers_send(6, lambda p: NSS, mine)
    mod_out.wait()
    for i in range(27):
        for copy in result_copies(i):
            copy.wait()
    for u in range(9, NU):
        sums_done(u)
    twin_copy(0, ATI.at[c], ATI.at[c]).wait_send()
    twin_copy(1, MIX.at[c], MIX.at[c]).wait_send()
    twin_copy(2, W.at[3], WP).wait_send()
    twin_copy(3, MLI.at[c], MLI.at[c]).wait_send()
    twin_copy(6, DMO.at[c], DMO.at[c]).wait_send()
    twin_copy(9, DAO.at[c, :, dao_other], DAO.at[c, :, dao_other]).wait_send()
    twin_copy(10, DMS, DMX.at[c]).wait_send()
    for ch in range(2):
        twin_copy(11 + ch, SND.at[ch], RCV.at[ch]).wait_send()
    twin_copy(13, DMB.at[c], DMB.at[c]).wait_send()
    twin_copy(14, B3D.at[c], B3D.at[c]).wait_send()
    twin_copy(15, DTA.at[c], DTA.at[c]).wait_send()
    twin_copy(16, CP.at[c], CP.at[c]).wait_send()
    twin_copy(17, E1.at[c], E1.at[c]).wait_send()

    peers_wait(6, lambda p: NSS, mine)

    @pl.loop(0, 16)
    def _(k):
        far_copy(k, o * 16 + k).wait()

    totals = jnp.sum(NSR[...], axis=0)
    norm = jnp.sqrt(totals[0:1])
    stats[...] = totals
    stats[0:1, :] = norm
    stats[2:3, :] = clip_limit / jnp.maximum(norm, clip_limit)


def fused_step(msg, noisy, noise, pos, block_in, block_out, entry, exit_):
    vm = pltpu.VMEM
    dma = pltpu.SemaphoreType.DMA
    scratch = [
        vm((12, 4, 2, 2, 64, 512), BF), vm((4, 2, 2, 64, 512), BF), vm((12, 4, 2, 2, 64, 512), BF),
        vm((4, 2, 4, 64, 512), BF), vm((4, 4, 64, 512), BF), vm((4, 4, 64, 512), BF),
        vm((len(SUM_VIA_Z), 64, 512), BF), vm((12, 64, 512), F32),
        vm((2, TOK, 1024), BF), vm((3, 2, TOK, 512), BF), vm((2, 2, TOK, 512), BF), vm((2, TOK, 1024), BF),
        vm((2, TOK, 2048), BF), vm((2, TOK, 2048), BF), vm((2, TOK, 1024), BF), vm((2, TOK, 1024), BF),
        vm((2, TOK, 512), BF), vm((TOK, 512), BF),
        *[vm((TOK, 1024), F32)] * 5, vm((2, TOK, 512), F32), vm((2, TOK, 512), F32),
        vm((64, 6144), F32), vm((TOK, PDIM), BF), vm((TOK, PDIM), F32), vm((16, 128), BF), vm((2, 16, 8, 128), F32), vm((16, 16, 128), BF), vm((16, 8, 128), F32), vm((16, 8, 128), F32),
        vm((16, 16, 512), BF), vm((16, 16, 512), BF), vm((2, 16, 16, 512), BF), vm((2, 8, 16, 1024), F32),
        vm((8, 128), F32), vm((16, 8, 128), F32), vm((2, 16, 1024), F32), vm((2, 4, 16, 128), F32), vm((2, 16, 64), F32),
        vm((16, 16, 128), BF), vm((16, 16, 128), BF), vm((2, 16, 128), F32),
        vm((8, 128), F32), vm((32, 8, 128), F32),
        vm((8, 1024), F32), vm((8, 8, 1024), F32), vm((16, 1024), BF), vm((16, 1024), BF), vm((32, 1024), F32),
        vm((8, 512), F32), vm((8, 16), F32),
        dma((27,)), dma((8, 16)), dma((8, 16)), dma((96,)), dma((96,)), dma((48,)), dma((48,)), dma((96,)), dma((96,)),
        dma((30,)), dma((30,)), dma((15,)), dma((15,)), dma((120,)), dma((120,)), dma((30,)), dma((30,)), dma((19,)), dma((19,)),
        dma((27,)), dma((27,)), dma((27,)), dma((16,)), dma((16,)),
        pltpu.SemaphoreType.REGULAR, pltpu.SemaphoreType.REGULAR, pltpu.SemaphoreType.REGULAR,
    ]
    any_ = pl.BlockSpec(memory_space=pl.ANY)
    vmem = pl.BlockSpec(memory_space=pltpu.VMEM)
    shape = jax.ShapeDtypeStruct
    return pl.pallas_call(
        step_kernel,
        out_shape=(
            shape(block_in.shape, F32), shape(block_out.shape, F32), shape(entry.shape, F32),
            shape(exit_.shape, F32), shape((8, 128), F32),
        ),
        in_specs=[vmem, vmem, vmem, vmem, any_, any_, any_, any_],
        out_specs=(any_, any_, vmem, vmem, vmem),
        scratch_shapes=scratch,
        compiler_params=pltpu.CompilerParams(
            collective_id=0, has_side_effects=True, vmem_limit_bytes=62 * 2**20
        ),
        cost_estimate=pl.CostEstimate(flops=21 * 10**9, bytes_accessed=20 * 10**6, transcendentals=4 * 10**6),
    )(msg, noisy, noise, pos, block_in, block_out, entry, exit_)


def adam_kernel(stats, *refs):
    ins, (loss, grad_norm), outs = refs[:16], refs[16:18], refs[18:]
    factor = stats[2, 0]
    loss[0, 0] = stats[1, 0]
    grad_norm[0, 0] = stats[0, 0]
    corr = 1.0 - 0.5**STEP

    def update(i, rate):
        weight, first, second, grad = (r[...] for r in ins[4 * i : 4 * i + 4])
        clipped = grad * factor
        first_new = 0.5 * first + 0.5 * clipped
        second_new = 0.5 * second + 0.5 * clipped * clipped
        change = first_new * (1.0 / corr) / (jnp.sqrt(second_new * (1.0 / corr)) + adam_eps)
        weight_new = weight - rate * (change + decay_rate * weight)
        for ref, value in zip(outs[4 * i : 4 * i + 4], (weight_new, first_new, second_new, weight_new)):
            ref[...] = value.astype(ref.dtype)

    update(0, rate_main)
    update(1, rate_main)
    update(2, rate_edge)
    update(3, rate_main)


def adam_all(stats, *groups):
    steps = 4
    specs = []
    for i, group in enumerate(groups):
        rows, cols = group[0].shape
        if i == 0:
            specs.append(pl.BlockSpec((rows, cols // steps), lambda t: (0, t)))
        elif i == 1:
            specs.append(pl.BlockSpec((rows // steps, cols), lambda t: (t, 0)))
        else:
            specs.append(pl.BlockSpec((rows // steps, cols), lambda t: (t, 0)))
    scalar = pl.BlockSpec(memory_space=pltpu.SMEM)
    shape = jax.ShapeDtypeStruct
    count = sum(group[0].size for group in groups)
    return pl.pallas_call(
        adam_kernel,
        grid=(steps,),
        out_shape=(
            shape((1, 1), F32), shape((1, 1), F32),
            *(shape(group[0].shape, d) for group in groups for d in (F32, F32, F32, BF)),
        ),
        in_specs=[scalar, *(spec for spec in specs for _ in range(4))],
        out_specs=(scalar, scalar, *(spec for spec in specs for _ in range(4))),
        compiler_params=pltpu.CompilerParams(vmem_limit_bytes=62 * 2**20),
        cost_estimate=pl.CostEstimate(flops=20 * count, bytes_accessed=30 * count, transcendentals=2 * count),
    )(stats, *(a for group in groups for a in group))


def local_fused(
    noisy, timesteps, labels, noise,
    block_in, block_in_first, block_in_second,
    block_out, block_out_first, block_out_second,
    entry_table, entry_first, entry_second,
    exit_proj, exit_first, exit_second,
):
    index = lax.axis_index("rep") * 16 + lax.axis_index("shard")
    femb = lowered(time_features(timesteps, FREQ)).astype(F32).reshape(2, LANES)
    label = labels.astype(F32)[0]
    lane = jnp.arange(LANES)[None, :]
    head = jnp.concatenate(
        [femb, jnp.full((1, LANES), label), jnp.where(lane == index, label, 0.0), jnp.zeros((4, LANES), F32)], axis=0
    )
    side = noisy.shape[-1]
    grid, quarter = side // PATCH, D // 4
    angle = np.arange(grid)[:, None] / 10000.0 ** (np.arange(quarter)[None, :] / quarter)
    pos = jnp.asarray(np.concatenate([np.sin(angle), np.cos(angle)], axis=1), F32)
    g_in, g_out, g_entry, g_exit, stats = fused_step(
        head, noisy.reshape(-1, side), noise.reshape(-1, side), pos, block_in[0], block_out[0], entry_table.T, exit_proj
    )
    loss, grad_norm, *new = adam_all(
        stats,
        (block_in[0], block_in_first[0], block_in_second[0], g_in),
        (block_out[0], block_out_first[0], block_out_second[0], g_out),
        (entry_table.T, entry_first.T, entry_second.T, g_entry),
        (exit_proj, exit_first, exit_second, g_exit),
    )
    return (
        loss[0, 0], grad_norm[0, 0], *(a[None] for a in new[:8]), *(a.T for a in new[8:12]), *new[12:]
    )


def solution(mesh):
    step = local_fused if dict(mesh.shape) == {"rep": 2, "shard": 16} else local
    in_specs = (
        P(("rep", "shard"), None, None, None),
        P(("rep", "shard")),
        P(("rep", "shard")),
        P(("rep", "shard"), None, None, None),
        P(None, "shard", None),
        P(None, "shard", None),
        P(None, "shard", None),
        P(None, "shard", None),
        P(None, "shard", None),
        P(None, "shard", None),
        P(None, "shard"),
        P(None, "shard"),
        P(None, "shard"),
        P("shard", None),
        P("shard", None),
        P("shard", None),
    )
    out_specs = (
        P(),
        P(),
        P(None, "shard", None),
        P(None, "shard", None),
        P(None, "shard", None),
        P(None, "shard", None),
        P(None, "shard", None),
        P(None, "shard", None),
        P(None, "shard", None),
        P(None, "shard", None),
        P(None, "shard"),
        P(None, "shard"),
        P(None, "shard"),
        P(None, "shard"),
        P("shard", None),
        P("shard", None),
        P("shard", None),
        P("shard", None),
    )
    return jax.shard_map(step, mesh=mesh, in_specs=in_specs, out_specs=out_specs, check_vma=False)
```

```python
import jax
import jax.numpy as jnp
import numpy as np
from jax import lax
from jax.experimental import pallas as pl
from jax.experimental.pallas import tpu as pltpu
from jax.sharding import PartitionSpec as P

D = 1024
HEADS = 16
PATCH = 2
NCLS = 1000
FREQ = 256
STEP = 10
PDIM = 16
ENTRIES = PDIM + NCLS + FREQ


clip_limit = 0.5
rate_main = 0.02
rate_edge = 0.1
decay_rate = 0.01
adam_eps = 1e-08
highest = lax.Precision.HIGHEST


def lowered(value):
    return value.astype(jnp.bfloat16)


def product(left, right):
    return jnp.dot(left, right, preferred_element_type=jnp.float32)


def product_tn(left, right):
    return lax.dot_general(
        left, right, (((0,), (0,)), ((), ())), preferred_element_type=jnp.float32
    )


def product_nt(left, right):
    return lax.dot_general(
        left, right, (((1,), (1,)), ((), ())), preferred_element_type=jnp.float32
    )


def patchify(image, patch):
    batch, chans, height, width = image.shape
    grid = height // patch
    parts = image.reshape(batch, chans, grid, patch, grid, patch)
    parts = parts.transpose(0, 2, 4, 3, 5, 1)
    return parts.reshape(batch, grid * grid, patch * patch * chans)


def position_table(grid, width):
    quarter = width // 4
    omega = 1.0 / 10000.0 ** (jnp.arange(quarter, dtype=jnp.float32) / quarter)
    index = jnp.arange(grid * grid)
    row_pos = (index // grid).astype(jnp.float32)[:, None] * omega[None, :]
    col_pos = (index % grid).astype(jnp.float32)[:, None] * omega[None, :]
    return jnp.concatenate(
        [jnp.sin(col_pos), jnp.cos(col_pos), jnp.sin(row_pos), jnp.cos(row_pos)], axis=1
    )


def time_features(steps, size):
    half = size // 2
    freqs = jnp.exp(-jnp.log(10000.0) * jnp.arange(half, dtype=jnp.float32) / half)
    angles = steps.astype(jnp.float32)[:, None] * freqs[None, :]
    return jnp.concatenate([jnp.cos(angles), jnp.sin(angles)], axis=1)


def modulate(x, shift, scale):
    centered = x - jnp.mean(x, axis=-1, keepdims=True)
    var = jnp.mean(centered * centered, axis=-1, keepdims=True)
    normed = centered * lax.rsqrt(var + 1e-06)
    return normed * (1.0 + scale[:, None, :]) + shift[:, None, :]


def gelu_tanh(value):
    return jax.nn.gelu(value, approximate=True)


def adam_step(weight, first, second, grad, factor, rate):
    clipped = grad * factor
    first_new = 0.5 * first + 0.5 * clipped
    second_new = 0.5 * second + 0.5 * clipped * clipped
    corr = 1.0 - 0.5**STEP
    update = first_new / corr / (jnp.sqrt(second_new / corr) + adam_eps) + decay_rate * weight
    weight_new = weight - rate * update
    return (weight_new, first_new, second_new, weight_new.astype(jnp.bfloat16))


def layer_parts(x, cond_low, w_in, w_out):
    width = x.shape[-1]
    batch, seq = (x.shape[0], x.shape[1])
    size = width // HEADS
    mod = product(cond_low, w_in[:, : 6 * width])
    shift_a, scale_a, gate_a, shift_b, scale_b, gate_b = jnp.split(mod, 6, axis=-1)
    attn_in = lowered(modulate(x, shift_a, scale_a))
    qkv = lowered(
        jnp.einsum(
            "bsd,de->bse",
            attn_in,
            w_in[:, 6 * width : 9 * width],
            preferred_element_type=jnp.float32,
        )
    )
    query = qkv[..., :width].reshape(batch, seq, HEADS, size)
    keys = qkv[..., width : 2 * width].reshape(batch, seq, HEADS, size)
    values = qkv[..., 2 * width :].reshape(batch, seq, HEADS, size)
    scores = jnp.einsum(
        "bqhd,bkhd->bhqk", query, keys, preferred_element_type=jnp.float32
    ) * size ** (-0.5)
    weights = jax.nn.softmax(scores, axis=-1)
    weights_low = lowered(weights)
    mixed = lowered(
        jnp.einsum("bhqk,bkhd->bqhd", weights_low, values, preferred_element_type=jnp.float32)
    ).reshape(batch, seq, width)
    attn_out = jnp.einsum(
        "bsd,de->bse", mixed, w_in[:, 9 * width : 10 * width], preferred_element_type=jnp.float32
    )
    resid = x + gate_a[:, None, :] * attn_out
    mlp_in = lowered(modulate(resid, shift_b, scale_b))
    hidden = jnp.einsum(
        "bsd,df->bsf", mlp_in, w_in[:, 10 * width :], preferred_element_type=jnp.float32
    )
    active = lowered(gelu_tanh(hidden))
    mlp_out = jnp.einsum("bsf,fd->bsd", active, w_out, preferred_element_type=jnp.float32)
    result = resid + gate_b[:, None, :] * mlp_out
    return dict(
        mods=(shift_a, scale_a, gate_a, shift_b, scale_b, gate_b),
        attn_in=attn_in,
        query=query,
        keys=keys,
        values=values,
        weights=weights,
        weights_low=weights_low,
        mixed=mixed,
        attn_out=attn_out,
        resid=resid,
        mlp_in=mlp_in,
        hidden=hidden,
        active=active,
        mlp_out=mlp_out,
        result=result,
    )


def layer_back(x, cond_low, w_in, w_out, parts, grad_out, grad_cond):
    width = x.shape[-1]
    batch, seq = (x.shape[0], x.shape[1])
    size = width // HEADS
    shift_a, scale_a, gate_a, shift_b, scale_b, gate_b = parts["mods"]
    d_gate_b = jnp.sum(grad_out * parts["mlp_out"], axis=1)
    d_mlp_out = lowered(grad_out * gate_b[:, None, :])
    g_fc2 = jnp.einsum(
        "bsf,bsd->fd", parts["active"], d_mlp_out, preferred_element_type=jnp.float32
    )
    d_active = jnp.einsum("bsd,fd->bsf", d_mlp_out, w_out, preferred_element_type=jnp.float32)
    _, gelu_pull = jax.vjp(gelu_tanh, parts["hidden"])
    d_hidden = lowered(gelu_pull(d_active)[0])
    g_fc1 = jnp.einsum("bsd,bsf->df", parts["mlp_in"], d_hidden, preferred_element_type=jnp.float32)
    d_mlp_in = jnp.einsum(
        "bsf,df->bsd", d_hidden, w_in[:, 10 * width :], preferred_element_type=jnp.float32
    )
    _, norm_pull = jax.vjp(modulate, parts["resid"], shift_b, scale_b)
    d_resid, d_shift_b, d_scale_b = norm_pull(d_mlp_in)
    d_resid = d_resid + grad_out
    d_gate_a = jnp.sum(d_resid * parts["attn_out"], axis=1)
    d_attn_out = lowered(d_resid * gate_a[:, None, :])
    g_proj = jnp.einsum(
        "bsd,bse->de", parts["mixed"], d_attn_out, preferred_element_type=jnp.float32
    )
    d_mixed = lowered(
        jnp.einsum(
            "bse,de->bsd",
            d_attn_out,
            w_in[:, 9 * width : 10 * width],
            preferred_element_type=jnp.float32,
        )
    ).reshape(batch, seq, HEADS, size)
    d_probs = jnp.einsum(
        "bqhd,bkhd->bhqk", d_mixed, parts["values"], preferred_element_type=jnp.float32
    )
    d_values = jnp.einsum(
        "bhqk,bqhd->bkhd", parts["weights_low"], d_mixed, preferred_element_type=jnp.float32
    )
    weights = parts["weights"]
    d_scores = weights * (d_probs - jnp.sum(d_probs * weights, axis=-1, keepdims=True))
    d_scaled = lowered(d_scores * size ** (-0.5))
    d_query = jnp.einsum(
        "bhqk,bkhd->bqhd", d_scaled, parts["keys"], preferred_element_type=jnp.float32
    )
    d_keys = jnp.einsum(
        "bhqk,bqhd->bkhd", d_scaled, parts["query"], preferred_element_type=jnp.float32
    )
    d_qkv = lowered(
        jnp.concatenate(
            [
                d_query.reshape(batch, seq, width),
                d_keys.reshape(batch, seq, width),
                d_values.reshape(batch, seq, width),
            ],
            axis=-1,
        )
    )
    g_qkv = jnp.einsum("bsd,bse->de", parts["attn_in"], d_qkv, preferred_element_type=jnp.float32)
    d_attn_in = jnp.einsum(
        "bse,de->bsd", d_qkv, w_in[:, 6 * width : 9 * width], preferred_element_type=jnp.float32
    )
    _, first_pull = jax.vjp(modulate, x, shift_a, scale_a)
    d_x, d_shift_a, d_scale_a = first_pull(d_attn_in)
    d_x = d_x + d_resid
    d_mod = lowered(
        jnp.concatenate([d_shift_a, d_scale_a, d_gate_a, d_shift_b, d_scale_b, d_gate_b], axis=-1)
    )
    g_mod = product_tn(cond_low, d_mod)
    grad_cond = grad_cond + product_nt(d_mod, w_in[:, : 6 * width])
    g_in = jnp.concatenate([g_mod, g_qkv, g_proj, g_fc1], axis=1)
    return (d_x, grad_cond, g_in, g_fc2)


def local(
    noisy,
    timesteps,
    labels,
    noise,
    block_in,
    block_in_first,
    block_in_second,
    block_out,
    block_out_first,
    block_out_second,
    entry_table,
    entry_first,
    entry_second,
    exit_proj,
    exit_first,
    exit_second,
):
    layers = block_in.shape[0]
    entry_all, exit_all = (
        lax.all_gather(lowered(entry_table), "shard", axis=1, tiled=True),
        lax.all_gather(lowered(exit_proj), "shard", axis=0, tiled=True),
    )
    w_patch = entry_all[:PDIM]
    w_label = entry_all[PDIM : PDIM + NCLS]
    w_time = entry_all[PDIM + NCLS :]
    w_time2 = exit_all[:, :D]
    w_final = exit_all[:, D : 3 * D]
    w_output = exit_all[:, 3 * D :]
    patches = lowered(patchify(noisy, PATCH))
    target = patchify(noise, PATCH)
    seq = patches.shape[1]
    x = (
        jnp.einsum("bsp,pd->bsd", patches, w_patch, preferred_element_type=jnp.float32)
        + position_table(noisy.shape[-1] // PATCH, D)[None]
    )
    femb = lowered(time_features(timesteps, FREQ))
    t_hidden = product(femb, w_time)
    t_act = lowered(jax.nn.silu(t_hidden))
    temb = product(t_act, w_time2)
    onehot = (labels[:, None] == jnp.arange(NCLS)[None, :]).astype(jnp.float32)
    cond = temb + jnp.dot(onehot, w_label.astype(jnp.float32), precision=highest)
    cond_low = lowered(jax.nn.silu(cond))
    layer = 0
    w_in_all = lax.all_gather(lowered(block_in[layer]), "shard", axis=0, tiled=True)
    w_out_all = lax.all_gather(lowered(block_out[layer]), "shard", axis=0, tiled=True)
    inputs = [x]
    parts = layer_parts(x, cond_low, w_in_all, w_out_all)
    saved = [parts]
    x = parts["result"]
    final_mod = product(cond_low, w_final)
    shift_f, scale_f = jnp.split(final_mod, 2, axis=-1)
    final_in = lowered(modulate(x, shift_f, scale_f))
    pred = jnp.einsum("bsd,dp->bsp", final_in, w_output, preferred_element_type=jnp.float32)
    error = pred - target
    loss_part = jnp.sum(error * error) / (seq * PDIM)
    d_pred = lowered(2.0 * error / (seq * PDIM))
    g_output = jnp.einsum("bsd,bsp->dp", final_in, d_pred, preferred_element_type=jnp.float32)
    d_final_in = jnp.einsum("bsp,dp->bsd", d_pred, w_output, preferred_element_type=jnp.float32)
    _, final_pull = jax.vjp(modulate, x, shift_f, scale_f)
    d_x, d_shift_f, d_scale_f = final_pull(d_final_in)
    d_fmod = lowered(jnp.concatenate([d_shift_f, d_scale_f], axis=-1))
    g_final = product_tn(cond_low, d_fmod)
    grad_cond = product_nt(d_fmod, w_final)
    shards_in = [None] * layers
    shards_out = [None] * layers
    for layer in reversed(range(layers)):
        w_in_all, w_out_all = (
            lax.all_gather(lowered(block_in[layer]), "shard", axis=0, tiled=True),
            lax.all_gather(lowered(block_out[layer]), "shard", axis=0, tiled=True),
        )
        d_x, grad_cond, g_in, g_fc2 = layer_back(
            inputs[layer], cond_low, w_in_all, w_out_all, saved[layer], d_x, grad_cond
        )
        shards_in[layer], shards_out[layer] = (
            lax.psum_scatter(g_in, "shard", scatter_dimension=0, tiled=True),
            lax.psum_scatter(g_fc2, "shard", scatter_dimension=0, tiled=True),
        )
    _, silu_pull = jax.vjp(jax.nn.silu, cond)
    d_cond = silu_pull(grad_cond)[0]
    g_label = jnp.dot(onehot.T, d_cond, precision=highest)
    d_temb = lowered(d_cond)
    g_time2 = product_tn(t_act, d_temb)
    d_tact = product_nt(d_temb, w_time2)
    _, time_pull = jax.vjp(jax.nn.silu, t_hidden)
    d_thidden = lowered(time_pull(d_tact)[0])
    g_time = product_tn(femb, d_thidden)
    g_patch = jnp.einsum("bsp,bsd->pd", patches, lowered(d_x), preferred_element_type=jnp.float32)
    g_entry = jnp.concatenate([g_patch, g_label, g_time], axis=0)
    g_exit = jnp.concatenate([g_time2, g_final, g_output], axis=1)
    share_entry, share_exit = (
        lax.psum_scatter(g_entry, "shard", scatter_dimension=1, tiled=True),
        lax.psum_scatter(g_exit, "shard", scatter_dimension=0, tiled=True),
    )
    grads = (
        lax.psum(jnp.stack(shards_in).astype(jnp.bfloat16), "rep").astype(jnp.float32),
        lax.psum(jnp.stack(shards_out).astype(jnp.bfloat16), "rep").astype(jnp.float32),
        lax.psum(share_entry.astype(jnp.bfloat16), "rep").astype(jnp.float32),
        lax.psum(share_exit.astype(jnp.bfloat16), "rep").astype(jnp.float32),
    )
    squares = (
        jnp.sum(grads[0] * grads[0])
        + jnp.sum(grads[1] * grads[1])
        + jnp.sum(grads[2] * grads[2])
        + jnp.sum(grads[3] * grads[3])
    )
    loss = lax.psum(loss_part, ("rep", "shard"))
    norm_sq = lax.psum(squares, "shard")
    grad_norm = jnp.sqrt(norm_sq)
    factor = clip_limit / jnp.maximum(grad_norm, clip_limit)
    bi_w, bi_m, bi_v, bi_l = adam_step(
        block_in, block_in_first, block_in_second, grads[0], factor, rate_main
    )
    bo_w, bo_m, bo_v, bo_l = adam_step(
        block_out, block_out_first, block_out_second, grads[1], factor, rate_main
    )
    en_w, en_m, en_v, en_l = adam_step(
        entry_table, entry_first, entry_second, grads[2], factor, rate_edge
    )
    ex_w, ex_m, ex_v, ex_l = adam_step(
        exit_proj, exit_first, exit_second, grads[3], factor, rate_main
    )
    return (
        loss,
        grad_norm,
        bi_w,
        bi_m,
        bi_v,
        bi_l,
        bo_w,
        bo_m,
        bo_v,
        bo_l,
        en_w,
        en_m,
        en_v,
        en_l,
        ex_w,
        ex_m,
        ex_v,
        ex_l,
    )


BF = jnp.bfloat16
F32 = jnp.float32
MESH = pl.DeviceIdType.MESH
TOK = 256
TILE = 256
LANES = 128
CHUNKS = 12
START = (4, 2)
OWN_AT = ((), (4,), (5, 6), (7, 8), (9, 10), (11,))
Z_AT = ((2,), (3,), (4,), (5,), (6, 7), (8,), (9,), (10,), (11,))
VIA_Z = (1, 3, 5, 7, 9, 11)
SUM_VIA_Z = (0, 2, 4, 6, 8)
LEAD = 3
LAGS = (0, 2, 4, 5)
LAG_A = 1
UNITS = tuple((k, 0, 64) for k in (8, 9, 10, 11, 4, 5, 6, 7, 3, 0, 1)) + tuple((2, 16 * i, 16) for i in range(4))
NU = len(UNITS)
SMALL = 11


def dot_nn(left, right):
    return lax.dot_general(left, right, (((1,), (0,)), ((), ())), preferred_element_type=F32)


def dot_nt(left, right):
    return lax.dot_general(left, right, (((1,), (1,)), ((), ())), preferred_element_type=F32)


def dot_tn(left, right):
    return lax.dot_general(left, right, (((0,), (0,)), ((), ())), preferred_element_type=F32)


def dot_tn_exact(left, right):
    return lax.dot_general(
        left, right, (((0,), (0,)), ((), ())), preferred_element_type=F32, precision=highest
    )


def patches_of(image):
    how = highest if image.dtype == F32 else None

    def product_of(left, right, dims):
        return lax.dot_general(
            left.astype(image.dtype), right.astype(image.dtype), (dims, ((), ())),
            preferred_element_type=F32, precision=how,
        )

    def iota(shape, dim):
        return lax.broadcasted_iota(jnp.int32, shape, dim)

    total = 0.0
    mine = iota((TOK, 128), 0) >> 4 == (iota((TOK, 128), 1) & 31) >> 1
    for pc in range(2):
        pick = (2 * iota((16, 32), 0) + pc == iota((16, 32), 1)).astype(F32)
        cols = product_of(pick, image, ((1,), (1,)))
        spread = jnp.where(mine, jnp.concatenate([cols] * 16, axis=0), 0.0)
        row = iota((128, PDIM), 0)
        place = (row & 1) * 8 + pc * 4 + (row >> 5) == iota((128, PDIM), 1)
        total += product_of(spread, place.astype(F32), ((1,), (0,)))
    return total


def to_tile(value):
    return jnp.concatenate([value[0:8], value[8:16]], axis=1)


def from_tile(value):
    return jnp.concatenate([value[:, 0:64], value[:, 64:128]], axis=0)


def sigmoid(value):
    return 1.0 / (1.0 + jnp.exp(-value))


def silu_slope(value):
    gate = sigmoid(value)
    return gate * (1.0 + value * (1.0 - gate))


def normed(x):
    centered = x - jnp.mean(x, axis=-1, keepdims=True)
    var = jnp.mean(centered * centered, axis=-1, keepdims=True)
    inv = lax.rsqrt(var + 1e-06)
    return centered * inv, inv


def normed_back(d_normed, x_normed, inv):
    mean_d = jnp.mean(d_normed, axis=-1, keepdims=True)
    mean_dx = jnp.mean(d_normed * x_normed, axis=-1, keepdims=True)
    return inv * (d_normed - mean_d - x_normed * mean_dx)


def fold(value):
    rows, cols = value.shape
    return jnp.sum(value.reshape(rows // 8, 8, cols), axis=0)


def rows_at(i, size):
    return pl.ds(pl.multiple_of(i * size, size), size)


def step_kernel(
    msg, noisy, noise, pos, bi, bo, ent_in, ex_in,
    g_in, g_out, ENT, EX, stats,
    W, WP, G, R1, R2, R3, PF, FIN,
    ATI, QKV, MIX, MLI, ACT, GD, DMO, DAO, DMX, DMS,
    X0, AO, RSD, MO, X1, SND, RCV,
    WMOD, PAT, TGT, EDS, E1, EDG, E2S, E2R, E3S, E3R, DMB, DMF, B2S, B2R, DTA, CP, CND,
    B3S, B3R, B3D, NSS, NSR, MODS, DACC, WPT, WLT, GLP, SQ, LOSS,
    st_sem, peer_s, peer_r, zs, zr, bs, br, as_, ar,
    s1s, s1r, s2s, s2r, szs, szr, pss, psr, d_s, d_r, f_l, f_s, f_r,
    far_s, far_r, cred_a, cred_b, cred_z,
):
    c = lax.axis_index("rep")
    s = lax.axis_index("shard")
    o = 1 - c
    x = s % 2
    y = (s // 2) % 2
    z = s // 4
    a_me = y * o + x * c
    b_me = x * o + y * c

    def yx(a, b):
        return a * o + b * c, b * o + a * c

    def dev(core, chip):
        return {"rep": core, "shard": chip}

    def chip_of(zz, yy, xx):
        return zz * 4 + yy * 2 + xx

    nb_a = dev(c, chip_of(z, *yx(1 - a_me, b_me)))
    nb_b = dev(c, chip_of(z, *yx(a_me, 1 - b_me)))
    twin = dev(o, s)

    def remote(src, dst, ss, rs, to):
        return pltpu.make_async_remote_copy(
            src_ref=src, dst_ref=dst, send_sem=ss, recv_sem=rs, device_id=to, device_id_type=MESH
        )

    pieces = []
    for j in range(4):
        pieces.append((bi.at[:, pl.ds(pl.multiple_of(6144 + 1024 * j + c * 512, 512), 512)], FIN.at[j]))
    for j in range(16):
        pieces.append((
            bi.at[:, pl.ds(pl.multiple_of(10240 + 256 * j + c * 128, 128), 128)],
            FIN.at[4 + j // 4, :, pl.ds((j % 4) * 128, 128)],
        ))
    for ch in range(2):
        for rh in range(2):
            pieces.append((
                bo.at[pl.ds(pl.multiple_of(c * 128 + rh * 64, 64), 64), pl.ds(ch * 512, 512)],
                FIN.at[8 + 2 * ch + rh],
            ))
    pieces.append((ent_in, ENT))
    pieces.append((ex_in, EX))
    pieces.append((bi.at[:, pl.ds(0, 6144)], WMOD))
    local = [pltpu.make_async_copy(p, q, st_sem.at[i]) for i, (p, q) in enumerate(pieces)]
    for i in (0, 1, 2, 3, 24, 25, *range(4, 24), 26):
        local[i].start()

    barrier = pltpu.get_barrier_semaphore()

    @pl.loop(1, 16)
    def _(k):
        pl.semaphore_signal(barrier, 1, device_id=dev(c, (s + k) % 16), device_id_type=MESH)

    @pl.loop(0, 16)
    def _(k):
        pl.semaphore_signal(barrier, 1, device_id=dev(o, k), device_id_type=MESH)

    for k in range(START[0]):
        local[k].wait()
        W[k, z, y, x] = FIN[k].astype(BF)

    pl.semaphore_wait(barrier, 31)

    def peers_copy(e, k, src_of, dst):
        peer = (s + k) % 16
        return remote(src_of(peer), dst.at[s], peer_s.at[e, k], peer_r.at[e, s], dev(c, peer))

    def peers_send(e, src_of, dst):
        @pl.loop(1, 16)
        def _(k):
            peers_copy(e, k, src_of, dst).start()

    def peers_wait(e, src_of, dst):
        @pl.loop(1, 16)
        def _(k):
            frm = (s + k) % 16
            remote(src_of(frm), dst.at[frm], peer_s.at[e, k], peer_r.at[e, frm], dev(c, frm)).wait_recv()

        @pl.loop(1, 16)
        def _(k):
            peers_copy(e, k, src_of, dst).wait_send()

    def twin_copy(i, src, dst):
        return remote(src, dst, d_s.at[i], d_r.at[i], twin)

    def block(k, zz, far):
        yy, xx = yx(a_me, 1 - b_me if far else b_me)
        return W.at[k, zz, yy, xx]

    def z_copy(k, dz, far=0):
        at = block(k, z, far)
        i = k * 8 + far * 4
        return remote(at, at, zs.at[i + dz], zr.at[i + z], dev(c, chip_of((z + dz) % 4, y, x)))

    def z_wait(k, dz, far=0):
        frm = (z + dz) % 4
        at = block(k, frm, far)
        i = k * 8 + far * 4
        remote(at, at, zs.at[i + dz], zr.at[i + frm], dev(c, chip_of(frm, y, x))).wait_recv()

    inner = jnp.logical_or(z == 1, z == 2)

    def z_pass(k, far=0):
        at = block(k, (z + 2) % 4, far)
        i = k * 8 + far * 4
        return remote(at, at, zs.at[i], zr.at[i + (z + 2) % 4], dev(c, chip_of(3 * (z - 1), y, x)))

    def z_start(k, far=0):
        z_copy(k, 2, far).start()
        pl.when(z != 3)(lambda: z_copy(k, 1, far).start())
        pl.when(z != 0)(lambda: z_copy(k, 3, far).start())

    def z_arrived(k, dz, far=0):
        z_wait(k, dz, far)
        if dz == 2:
            pl.when(inner)(lambda: z_pass(k, far).start())

    def z_sent(k, far=0):
        z_copy(k, 2, far).wait_send()
        pl.when(z != 3)(lambda: z_copy(k, 1, far).wait_send())
        pl.when(z != 0)(lambda: z_copy(k, 3, far).wait_send())
        pl.when(inner)(lambda: z_pass(k, far).wait_send())

    def b_copy(k, zz):
        at = block(k, zz, 0)
        return remote(at, at, bs.at[k * 4 + zz], br.at[k * 4 + zz], nb_b)

    def a_copy(k, zz, far=0):
        at = block(k, zz, far)
        i = k * 8 + far * 4 + zz
        return remote(at, at, as_.at[i], ar.at[i], nb_a)

    def own(k):
        cast(k)
        b_copy(k, z).start()
        a_copy(k, z).start()

    def far_start(k):
        b_copy(k, z).wait_recv()
        z_start(k, 1)
        a_copy(k, z, 1).start()

    def pump_b(k):
        for dz in (2, 1, 3):
            frm = (z + dz) % 4
            z_arrived(k, dz)
            if k not in VIA_Z:
                b_copy(k, frm).start()
            a_copy(k, frm).start()

    def pump_a(k):
        if k in VIA_Z:
            for dz in (2, 1, 3):
                z_arrived(k, dz, 1)
                a_copy(k, (z + dz) % 4, 1).start()
        else:
            for dz in range(4):
                b_copy(k, (z + dz) % 4).wait_recv()
                a_copy(k, (z + dz) % 4, 1).start()

    def sends_done(k):
        z_sent(k)
        if k in VIA_Z:
            z_sent(k, 1)
        else:
            for dz in range(1, 4):
                b_copy(k, (z + dz) % 4).wait_send()
        b_copy(k, z).wait_send()
        for far in range(2):
            for zz in range(4):
                a_copy(k, zz, far).wait_send()

    def pump(k):
        for i in OWN_AT[k] if k < len(OWN_AT) else ():
            own(i)
        for i in Z_AT[k] if k < len(Z_AT) else ():
            z_start(i)
        if k + 1 in VIA_Z:
            far_start(k + 1)
        if k < CHUNKS:
            pump_b(k)
        if 0 <= k - LAG_A < CHUNKS:
            pump_a(k - LAG_A)

    def need(k):
        for far in range(2):
            for dz in range(4):
                a_copy(k, (z + dz) % 4, far).wait_recv()

    def cast(k):
        if k < START[0]:
            return
        if k < 8:
            if k == 4:
                for i in range(4, 20):
                    local[i].wait()
            rh, half = (k - 4) // 2, (k - 4) % 2
            for q in range(4):
                j = half * 8 + 2 * q
                pair = FIN[4 + j // 4, :, (j % 4) * 128 : (j % 4) * 128 + 256]
                piece = jnp.concatenate(
                    [pair[:, rh * 64 : rh * 64 + 64], pair[:, 128 + rh * 64 : 128 + rh * 64 + 64]], axis=1
                )
                W[k, z, y, x, :, q * 128 : q * 128 + 128] = piece.astype(BF)
        else:
            local[20 + k - 8].wait()
            W[k, z, y, x] = FIN[k].astype(BF)

    E1[c, s] = msg[...]
    peers_send(0, lambda p: msg, E1.at[c])
    for k in range(START[0]):
        own(k)
        if k < START[1]:
            z_start(k)

    local[24].wait()
    local[25].wait()
    peers_wait(0, lambda p: msg, E1.at[c])
    t_hidden = dot_nt(E1[c, :, 0, :].astype(BF), ENT[:, 1016:1144].astype(BF)) + dot_nt(
        E1[c, :, 1, :].astype(BF), ENT[:, 1144:1272].astype(BF)
    )
    CND[0] = t_hidden
    t_act = (t_hidden * sigmoid(t_hidden)).astype(BF)
    CP[c, 1, :, 0:64] = t_act.astype(F32)
    for q in range(8):
        part = dot_nn(t_act, EX[:, q * 128 : q * 128 + 128].astype(BF))
        for h in range(2):
            E2S[2 * q + h] = to_tile(part[:, 64 * h : 64 * h + 64])
    E2R[s] = E2S[s]
    peers_send(1, lambda p: E2S.at[p], E2R)
    pump(0)
    hot = (
        E1[c, :, 2, 0:1].astype(jnp.int32) + PDIM == lax.broadcasted_iota(jnp.int32, (16, ENTRIES), 1)
    ).astype(F32).astype(BF)
    w_class = dot_nt(hot, ENT[...].astype(BF))
    pump(1)
    local[26].wait()
    peers_wait(1, lambda p: E2S.at[p], E2R)
    cond = from_tile(jnp.sum(E2R[...], axis=0)) + w_class
    CND[1] = cond
    cond_low = (cond * sigmoid(cond)).astype(BF)
    CP[c, 0, :, 0:64] = cond_low.astype(F32)
    for k in range(8):
        w_k = WMOD[:, k * 1024 : k * 1024 + 1024] if k < 6 else EX[:, (k - 5) * 1024 : (k - 4) * 1024]
        DMF[0, k] = dot_nn(cond_low, w_k.astype(BF))

    @pl.loop(0, 16)
    def _(l):
        part = DMF[0, :, l, :]
        E3S[l] = jnp.concatenate([part[:, :512], part[:, 512:]], axis=0).astype(BF)

    E3R[s] = E3S[s]
    peers_send(2, lambda p: E3S.at[p], E3R)
    edges = jnp.concatenate(
        [ENT[:, 0:128], jnp.concatenate([EX[:, 3072:3088], jnp.zeros((64, 112), F32)], axis=1)], axis=0
    )
    edges = edges.T[0:16].astype(BF)
    EDS[...] = edges
    EDG[s] = edges
    peers_send(7, lambda p: EDS, EDG)
    pump(2)

    PAT[...] = patches_of(noisy[...].astype(BF)).astype(BF)
    TGT[...] = patches_of(noise[...])
    peers_wait(7, lambda p: EDS, EDG)
    for q in range(8):
        even, odd = EDG[2 * q], EDG[2 * q + 1]
        WPT[:, q * 128 : q * 128 + 128] = jnp.concatenate([even[:, :64], odd[:, :64]], axis=1)
        WLT[:, q * 128 : q * 128 + 128] = jnp.concatenate([even[:, 64:], odd[:, 64:]], axis=1)
    for n in range(4):
        cols = slice(n * 256, n * 256 + 256)
        X0[:, cols] = dot_nn(PAT[...], WPT[:, cols])

    @pl.loop(0, 16)
    def _(i):
        X0[rows_at(i, 16), 0:512] += pos[...]
        X0[rows_at(i, 16), 512:1024] += jnp.broadcast_to(pos[pl.ds(i, 1), :], (16, 512))

    DACC[...] = jnp.zeros_like(DACC)
    pump(3)
    peers_wait(2, lambda p: E3S.at[p], E3R)
    parts = E3R[0].astype(F32)
    for i in range(1, 16):
        parts += E3R[i].astype(F32)
    MODS[...] = jnp.concatenate([parts[0:8], parts[8:16]], axis=1)

    def mod_row(k):
        return MODS[k : k + 1, :]

    def modulated(src, dst, shift, scale):
        @pl.loop(0, TOK // TILE)
        def _(i):
            r = rows_at(i, TILE)
            hat, _ = normed(src[r, :])
            dst[c, r, :] = (hat * (1.0 + mod_row(scale)) + mod_row(shift)).astype(BF)

    modulated(X0, ATI, 0, 1)
    twin_copy(0, ATI.at[c], ATI.at[c]).start()
    pump(4)
    twin_copy(0, ATI.at[o], ATI.at[o]).wait_recv()

    def w_cols(k, n):
        return W[k, :, :, :, :, rows_at(n, 256)].reshape(1024, 256)

    for j in range(3):
        need(j)

        @pl.loop(0, 4)
        def _(t):
            lat, n = t // 2, t % 2
            QKV[j, lat, :, rows_at(n, 256)] = dot_nn(ATI[lat], w_cols(j, n)).astype(BF)

        pump(5 + j)

    lane = lax.broadcasted_iota(jnp.int32, (1, LANES), 1)
    first = lane < 64
    masks = (first.astype(F32).astype(BF), 1.0 - first.astype(F32).astype(BF))

    def probs_of(q, k):
        score = dot_nt(q, k) * 0.125
        e = jnp.exp(score - jnp.max(score, axis=-1, keepdims=True))
        return e / jnp.sum(e, axis=-1, keepdims=True)

    def attention(t):
        lat, cols = t // 4, rows_at(t % 4, 128)
        q, k, v = QKV[0, lat, :, cols], QKV[1, lat, :, cols], QKV[2, lat, :, cols]
        outs = [dot_nn(probs_of(q * m, k).astype(BF), v) for m in masks]
        MIX[c, lat, :, cols] = jnp.where(first, outs[0], outs[1]).astype(BF)

    pl.loop(0, 4)(attention)
    pump(8)
    pl.loop(4, 8)(attention)

    twin_copy(1, MIX.at[c], MIX.at[c]).start()
    need(3)
    twin_copy(2, W.at[3], WP).start()
    pump(9)
    twin_copy(1, MIX.at[o], MIX.at[o]).wait_recv()
    twin_copy(2, W.at[3], WP).wait_recv()

    def proj(own):
        def cols(n):
            return pl.ds(pl.multiple_of((c if own else o) * 512 + n * 256, 256), 256)

        @pl.loop(0, 2)
        def _(n):
            ref = W.at[3] if own else WP
            total = 0.0
            for hh in range(2):
                w_half = ref[2 * hh : 2 * hh + 2, :, :, :, rows_at(n, 256)].reshape(512, 256)
                total += dot_nn(MIX[hh, c], w_half)
            AO[:, cols(n)] = total

    proj(True)
    proj(False)

    @pl.loop(0, TOK // TILE)
    def _(i):
        r = rows_at(i, TILE)
        RSD[r, :] = X0[r, :] + mod_row(2) * AO[r, :]

    modulated(RSD, MLI, 3, 4)
    twin_copy(3, MLI.at[c], MLI.at[c]).start()
    pump(10)
    twin_copy(3, MLI.at[o], MLI.at[o]).wait_recv()
    for j in range(4):
        need(4 + j)

        @pl.loop(0, 4)
        def _(t):
            lat, n = t // 2, t % 2
            hidden = dot_nn(MLI[lat], w_cols(4 + j, n))
            cols = pl.ds(pl.multiple_of(j * 512 + n * 256, 256), 256)
            square = hidden * hidden
            t_in = 0.7978845608028654 * hidden * (1.0 + 0.044715 * square)
            t_out = jnp.tanh(t_in)
            half = 0.5 * (1.0 + t_out)
            ACT[lat, :, cols] = (hidden * half).astype(BF)
            slope = half + 0.5 * hidden * (1.0 - t_out * t_out) * (
                0.7978845608028654 * (1.0 + 3.0 * 0.044715 * square)
            )
            GD[lat, :, cols] = slope.astype(BF)

        if j < 2:
            pump(11 + j)

    for k in range(8):
        sends_done(k)
    for ch in range(2):
        need(8 + 2 * ch)
        need(9 + 2 * ch)

        def mlp_tile(lat, n):
            total = 0.0
            for rh in range(2):
                total += dot_nn(ACT[lat, :, rh * 1024 : rh * 1024 + 1024], w_cols(8 + 2 * ch + rh, n))
            return total

        @pl.loop(0, 2)
        def _(n):
            SND[ch, :, rows_at(n, 256)] = mlp_tile(o, n)

        twin_copy(4 + ch, SND.at[ch], RCV.at[ch]).start()

        @pl.loop(0, 2)
        def _(n):
            MO[:, pl.ds(pl.multiple_of(ch * 512 + n * 256, 256), 256)] = mlp_tile(c, n)

    def received(i):
        for ch in range(2):
            twin_copy(i + ch, SND.at[ch], RCV.at[ch]).wait_recv()

    def both_parts(r):
        return MO[r, :] + jnp.concatenate([RCV[0, r, :], RCV[1, r, :]], axis=1)

    received(4)
    LOSS[...] = jnp.zeros_like(LOSS)
    GLP[...] = jnp.zeros_like(GLP)

    @pl.loop(0, TOK // TILE)
    def _(i):
        r = rows_at(i, TILE)
        mlp_out = both_parts(r)
        x1 = RSD[r, :] + mod_row(5) * mlp_out
        hat, inv = normed(x1)
        scale = 1.0 + mod_row(7)
        final_in = (hat * scale + mod_row(6)).astype(BF)
        w_lin = WLT[...]
        error = dot_nt(final_in, w_lin) - TGT[r, :]
        LOSS[...] += fold(error * error)
        d_pred = (2.0 * error / (TOK * PDIM)).astype(BF)
        GLP[16:32, :] += dot_tn(d_pred, final_in)
        d_final = dot_nn(d_pred, w_lin)
        DACC[6] += fold(d_final)
        DACC[7] += fold(d_final * hat)
        d_x = normed_back(d_final * scale, hat, inv)
        X1[r, :] = d_x
        DACC[5] += fold(d_x * mlp_out)
        DMO[c, r, :] = (d_x * mod_row(5)).astype(BF)

    twin_copy(6, DMO.at[c], DMO.at[c]).start()

    def r1_of(k, b):
        return R1.at[k - 8, b] if k >= 8 else W.at[8 + k // 2, :, k % 2, b]

    def r2_of(k):
        return R2.at[k - 8] if k >= 8 else W.at[4 + k // 4, :, (k // 2) % 2, k % 2]

    def r3_of(k):
        return R3.at[k - 8] if k >= 8 else W.at[6 + k // 4, :, (k // 2) % 2, k % 2]

    def rows_of(u):
        return pl.ds(UNITS[u][1], UNITS[u][2])

    def g_at(u, zz, a, b):
        yy, xx = yx(a, b)
        return G.at[UNITS[u][0], zz, yy, xx, rows_of(u)]

    def b_of(far):
        return 1 - b_me if far else b_me

    def z_slot(u, i, far):
        return (r2_of if far else r3_of)(UNITS[u][0]).at[i, rows_of(u)]

    def pass_slot(u, i, far):
        return PF.at[SUM_VIA_Z.index(u)] if far else z_slot(u, i, 0)

    def s1_copy(u, b):
        k, r = UNITS[u][0], rows_of(u)
        yy, xx = yx(1 - a_me, b)
        return remote(G.at[k, :, yy, xx, r], r1_of(k, b).at[:, r], s1s.at[u * 2 + b], s1r.at[u * 2 + b], nb_a)

    def s2_copy(u):
        if u in SUM_VIA_Z:
            return remote(g_at(u, z, a_me, 1 - b_me), z_slot(u, z, 1), s2s.at[u], s2r.at[u], nb_b)
        k, r = UNITS[u][0], rows_of(u)
        yy, xx = yx(a_me, 1 - b_me)
        return remote(G.at[k, :, yy, xx, r], r2_of(k).at[:, r], s2s.at[u], s2r.at[u], nb_b)

    def line(zz):
        return dev(c, chip_of(zz, y, x))

    def sz_copy(u, dz, far):
        zt = (z + dz) % 4
        i = u * 8 + far * 4
        return remote(g_at(u, zt, a_me, b_of(far)), z_slot(u, z, far), szs.at[i + dz], szr.at[i + z], line(zt))

    def sz_wait(u, dz, far):
        frm = (z + dz) % 4
        i = u * 8 + far * 4
        remote(g_at(u, frm, a_me, b_of(far)), z_slot(u, frm, far), szs.at[i + dz], szr.at[i + frm], line(frm)).wait_recv()

    near_end = jnp.where(z < 2, 1, 2)

    def pass_copy(u, far):
        i = u * 2 + far
        return remote(g_at(u, 3 - z, a_me, b_of(far)), pass_slot(u, near_end, far), pss.at[i], psr.at[i], line(near_end))

    def sum_a(u, zz, far):
        k, r = UNITS[u][0], rows_of(u)
        b = b_of(far)
        yy, xx = yx(a_me, b)
        return G[k, zz, yy, xx, r].astype(F32) + r1_of(k, b)[zz, r].astype(F32)

    def store(u, zz, far, value):
        g_at(u, zz, a_me, b_of(far))[...] = value.astype(BF)

    def sz_start(u, far):
        for dz in (1, 3):
            alone = z != (3 if dz == 1 else 0)
            if u >= SMALL:
                sz_copy(u, dz, far).start()
            else:
                pl.when(alone)(lambda: sz_copy(u, dz, far).start())
                pl.when(jnp.logical_not(alone))(lambda: pass_copy(u, far).start())
        if u >= SMALL:
            sz_copy(u, 2, far).start()
        else:
            pl.when(jnp.logical_not(inner))(lambda: sz_copy(u, 2, far).start())

    def sz_pass(u, far):
        @pl.when(inner)
        def _():
            i = u * 2 + far
            slot = pass_slot(u, z, far)
            remote(g_at(u, z, a_me, b_of(far)), slot, pss.at[i], psr.at[i], line(z)).wait_recv()
            zt = (z + 2) % 4
            store(u, zt, far, g_at(u, zt, a_me, b_of(far))[...].astype(F32) + slot[...].astype(F32))
            sz_copy(u, 2, far).start()

    def sz_sum(u, far):
        into = FIN.at[UNITS[u][0], rows_of(u)]

        def add(dz):
            sz_wait(u, dz, far)
            into[...] += z_slot(u, (z + dz) % 4, far)[...].astype(F32)

        for dz in (1, 3, 2):
            if u >= SMALL or dz == 2:
                add(dz)
            else:
                pl.when(z != (3 if dz == 1 else 0))(lambda: add(dz))

    def s1(u):
        for b in range(2):
            s1_copy(u, b).start()

    def stage_1(u):
        for b in range(2):
            s1_copy(u, b).wait_recv()
        if u in SUM_VIA_Z:
            for far in (1, 0):
                for dz in (1, 3, 2):
                    store(u, (z + dz) % 4, far, sum_a(u, (z + dz) % 4, far))
                sz_start(u, far)
        else:
            @pl.loop(0, 4)
            def _(zz):
                store(u, zz, 1, sum_a(u, zz, 1))

            s2_copy(u).start()

    def stage_2(u):
        if u in SUM_VIA_Z:
            for far in (1, 0):
                sz_pass(u, far)
        else:
            k, r = UNITS[u][0], rows_of(u)
            s2_copy(u).wait_recv()
            for dz in (1, 3, 2):
                zt = (z + dz) % 4
                store(u, zt, 0, sum_a(u, zt, 0) + r2_of(k)[zt, r].astype(F32))
            sz_start(u, 0)
            FIN[k, r] = sum_a(u, z, 0) + r2_of(k)[z, r].astype(F32)

    def stage_3(u):
        k, r = UNITS[u][0], rows_of(u)
        if u in SUM_VIA_Z:
            FIN[k, r] = sum_a(u, z, 1)
            sz_sum(u, 1)
            store(u, z, 1, FIN[k, r])
            s2_copy(u).start()
            FIN[k, r] = sum_a(u, z, 0)
            sz_sum(u, 0)
        elif u < SMALL:
            sz_pass(u, 0)

    def stage_4(u):
        k, r = UNITS[u][0], rows_of(u)
        if u in SUM_VIA_Z:
            s2_copy(u).wait_recv()
            FIN[k, r] += z_slot(u, z, 1)[...].astype(F32)
        else:
            sz_sum(u, 0)
        total = FIN[k, r]
        SQ[...] += fold(total * total)

    def sums_done(u):
        for b in range(2):
            s1_copy(u, b).wait_send()
        s2_copy(u).wait_send()
        for far in range(2 if u in SUM_VIA_Z else 1):
            sz_copy(u, 2, far).wait_send()
            for dz in (1, 3):
                if u >= SMALL:
                    sz_copy(u, dz, far).wait_send()
                else:
                    alone = z != (3 if dz == 1 else 0)
                    pl.when(alone)(lambda: sz_copy(u, dz, far).wait_send())
                    pl.when(jnp.logical_not(alone))(lambda: pass_copy(u, far).wait_send())

    def result_copies(i):
        if i < 4:
            k = 8 + i
            src = FIN.at[k]
            dst = g_out.at[
                pl.ds(pl.multiple_of(c * 128 + (i % 2) * 64, 64), 64), pl.ds((i // 2) * 512, 512)
            ]
        elif i < 20:
            j = i - 4
            src = FIN.at[4 + j // 8 + 2 * (j % 2), :, pl.ds(((j % 8) // 2) * 128, 128)]
            dst = g_in.at[:, pl.ds(pl.multiple_of(10240 + 256 * j + c * 128, 128), 128)]
        else:
            k, r0, size = ((3, 0, 64), *UNITS[9:])[i - 20]
            src = FIN.at[k, pl.ds(r0, size)]
            dst = g_in.at[pl.ds(r0, size), pl.ds(pl.multiple_of(6144 + 1024 * k + c * 512, 512), 512)]
        return pltpu.make_async_copy(src, dst, f_l.at[i]), remote(src, dst, f_s.at[i], f_r.at[i], twin)

    def send_result(u):
        k = UNITS[u][0]
        if k >= 8:
            span = (k - 8,)
        elif k == 7:
            for half in range(2):
                for q in range(4):
                    cols = slice(q * 128, q * 128 + 128)
                    low, high = FIN[4 + half, :, cols], FIN[6 + half, :, cols]
                    FIN[4 + half, :, cols] = jnp.concatenate([low[:, 0:64], high[:, 0:64]], axis=1)
                    FIN[6 + half, :, cols] = jnp.concatenate([low[:, 64:128], high[:, 64:128]], axis=1)
            span = range(4, 20)
        elif k >= 4:
            span = ()
        else:
            span = (20 + u - 8,)
        for i in span:
            for copy in result_copies(i):
                copy.start()

    def step(t):
        for u in range(t + LEAD, NU):
            if u == t + LEAD and u <= 11 or t + LEAD == 11:
                if u == 4:
                    pl.semaphore_wait(cred_a, 1)
                s1(u)
        if t == 4:
            pl.semaphore_wait(cred_b, 1)
            pl.semaphore_wait(cred_z, 3)
        for stage, lag in zip((stage_1, stage_2, stage_3, stage_4), LAGS):
            if 0 <= t - lag < NU:
                stage(t - lag)
                if stage is stage_4:
                    send_result(t - lag)
                    if 2 <= t - lag < 11:
                        sums_done(t - lag - 2)

    def grad_tiles(k, left, right):
        @pl.loop(0, 4)
        def _(r):
            G[k, r] = dot_tn(left(r), right).astype(BF).reshape(2, 2, 64, 512)

    SQ[...] = jnp.zeros_like(SQ)
    twin_copy(6, DMO.at[o], DMO.at[o]).wait_recv()
    for ch in range(2):
        for rh in range(2):
            k = 8 + 2 * ch + rh
            grad_tiles(
                k,
                lambda r: ACT[:, :, pl.ds(pl.multiple_of(rh * 1024 + r * 256, 256), 256)].reshape(512, 256),
                DMO[:, :, ch * 512 : ch * 512 + 512].reshape(512, 512),
            )
            if 2 * ch + rh < LEAD:
                s1(2 * ch + rh)

    for k in range(8, CHUNKS):
        sends_done(k)

    @pl.loop(0, 16)
    def _(t):
        lat, rh, r = t // 8, (t // 4) % 2, t % 4
        total = 0.0
        for ch in range(2):
            total += dot_nt(DMO[lat, :, ch * 512 : ch * 512 + 512], W[8 + 2 * ch + rh, r].reshape(256, 512))
        cols = pl.ds(pl.multiple_of(rh * 1024 + r * 256, 256), 256)
        GD[lat, :, cols] = (total * GD[lat, :, cols].astype(F32)).astype(BF)

    pl.semaphore_signal(cred_a, 1, device_id=nb_a, device_id_type=MESH)
    step(0)

    def data_back(first_k, count, left, i):
        for ch in range(2):
            @pl.loop(0, 2)
            def _(n):
                total = 0.0
                for j in range(count):
                    total += dot_nt(left(j, o), W[first_k + j, 2 * ch + n].reshape(256, 512))
                SND[ch, :, rows_at(n, 256)] = total

            twin_copy(i + ch, SND.at[ch], RCV.at[ch]).start()

        @pl.loop(0, 4)
        def _(r):
            total = 0.0
            for j in range(count):
                total += dot_nt(left(j, c), W[first_k + j, r].reshape(256, 512))
            MO[:, rows_at(r, 256)] = total

    for ch in range(2):
        twin_copy(4 + ch, SND.at[ch], RCV.at[ch]).wait_send()
    data_back(4, 4, lambda j, lat: GD[lat, :, j * 512 : j * 512 + 512], 7)
    pl.semaphore_signal(cred_b, 1, device_id=nb_b, device_id_type=MESH)
    for dz in range(1, 4):
        pl.semaphore_signal(cred_z, 1, device_id=dev(c, chip_of((z + dz) % 4, y, x)), device_id_type=MESH)

    for j in range(4):
        grad_tiles(
            4 + j,
            lambda r: MLI[:, :, rows_at(r, 256)].reshape(512, 256),
            GD[:, :, j * 512 : j * 512 + 512].reshape(512, 512),
        )
    step(1)
    received(7)

    @pl.loop(0, TOK // TILE)
    def _(i):
        r = rows_at(i, TILE)
        d_in = both_parts(r)
        hat, inv = normed(RSD[r, :])
        DACC[3] += fold(d_in)
        DACC[4] += fold(d_in * hat)
        d_x = normed_back(d_in * (1.0 + mod_row(4)), hat, inv) + X1[r, :]
        X1[r, :] = d_x
        DACC[2] += fold(d_x * AO[r, :])
        DAO[c, r, :] = (d_x * mod_row(2)).astype(BF)

    dao_other = pl.ds(pl.multiple_of(o * 512, 512), 512)
    dao_mine = pl.ds(pl.multiple_of(c * 512, 512), 512)
    twin_copy(9, DAO.at[c, :, dao_other], DAO.at[c, :, dao_other]).start()

    def mixed_back(hh, n):
        w_mine = W[3, 2 * hh + n].reshape(256, 512)
        w_other = WP[2 * hh + n].reshape(256, 512)
        return (dot_nt(DAO[c, :, dao_mine], w_mine) + dot_nt(DAO[c, :, dao_other], w_other)).astype(BF)

    @pl.loop(0, 2)
    def _(n):
        DMS[:, rows_at(n, 256)] = mixed_back(o, n)

    twin_copy(10, DMS, DMX.at[c]).start()

    @pl.loop(0, 2)
    def _(n):
        DMX[c, :, rows_at(n, 256)] = mixed_back(c, n)

    step(2)
    twin_copy(9, DAO.at[o, :, dao_mine], DAO.at[o, :, dao_mine]).wait_recv()

    @pl.loop(0, 4)
    def _(r):
        left = MIX[r // 2, :, :, rows_at(r % 2, 256)].reshape(512, 256)
        G[3, r] = dot_tn(left, DAO[:, :, dao_mine].reshape(512, 512)).astype(BF).reshape(2, 2, 64, 512)

    twin_copy(10, DMS, DMX.at[o]).wait_recv()

    def attention_back(t):
        lat, cols = t // 4, rows_at(t % 4, 128)
        q, k, v = QKV[0, lat, :, cols], QKV[1, lat, :, cols], QKV[2, lat, :, cols]
        dm = DMX[lat, :, cols]
        res = []
        for m in masks:
            probs = probs_of(q * m, k)
            d_probs = dot_nt(dm * m, v)
            d_v = dot_tn(probs.astype(BF), dm)
            d_s = probs * (d_probs - jnp.sum(d_probs * probs, axis=-1, keepdims=True))
            d_s = (d_s * 0.125).astype(BF)
            res.append((dot_nn(d_s, k), dot_tn(d_s, q), d_v))
        for j in range(3):
            QKV[j, lat, :, cols] = jnp.where(first, res[0][j], res[1][j]).astype(BF)

    for half in range(2):
        pl.loop(4 * half, 4 * half + 4)(attention_back)
        step(3 + half)
    for ch in range(2):
        twin_copy(7 + ch, SND.at[ch], RCV.at[ch]).wait_send()
    data_back(0, 3, lambda j, lat: QKV[j, lat], 11)
    for j in range(3):
        grad_tiles(
            j,
            lambda r: ATI[:, :, rows_at(r, 256)].reshape(512, 256),
            QKV[j].reshape(512, 512),
        )
    received(11)

    @pl.loop(0, TOK // TILE)
    def _(i):
        r = rows_at(i, TILE)
        d_in = both_parts(r)
        hat, inv = normed(X0[r, :])
        DACC[0] += fold(d_in)
        DACC[1] += fold(d_in * hat)
        d_x = normed_back(d_in * (1.0 + mod_row(1)), hat, inv) + X1[r, :]
        GLP[0:16, :] += dot_tn(PAT[r, :], d_x.astype(BF))

    for k in range(8):
        MODS[k : k + 1, :] = jnp.sum(DACC[k], axis=0, keepdims=True)
    d_mods = MODS[...]
    DMB[c, s] = jnp.concatenate([d_mods[:, :512], d_mods[:, 512:]], axis=0).astype(BF)
    peers_send(3, lambda p: DMB.at[c, s], DMB.at[c])
    for q in range(16):
        cols = slice(q * 64, q * 64 + 64)
        B3S[q] = jnp.concatenate([GLP[0:16, cols], GLP[16:32, cols]], axis=1).astype(BF)
    B3R[s] = B3S[s]
    peers_send(4, lambda p: B3S.at[p], B3R)
    step(5)
    step(6)
    peers_wait(3, lambda p: DMB.at[c, s], DMB.at[c])
    twin_copy(13, DMB.at[c], DMB.at[c]).start()

    def unpack(g):
        @pl.loop(0, 16)
        def _(l):
            both = DMB[g, l].astype(F32)
            DMF[g, :, l, 0:512] = both[0:8]
            DMF[g, :, l, 512:1024] = both[8:16]

    unpack(c)
    d_cond_low = 0.0
    for k in range(8):
        w_k = WMOD[:, k * 1024 : k * 1024 + 1024] if k < 6 else EX[:, (k - 5) * 1024 : (k - 4) * 1024]
        d_cond_low += dot_nt(DMF[c, k].astype(BF), w_k.astype(BF))
    d_cond = d_cond_low * silu_slope(CND[1])
    CP[c, 2, :, 0:64] = d_cond
    d_temb = d_cond.astype(BF).astype(F32)
    B2S[...] = to_tile(d_temb)
    B2R[s] = B2S[...]
    peers_send(5, lambda p: B2S, B2R)
    step(7)
    peers_wait(4, lambda p: B3S.at[p], B3R)
    sums = B3R[0].astype(F32)
    for i in range(1, 16):
        sums += B3R[i].astype(F32)
    B3D[c] = sums
    twin_copy(14, B3D.at[c], B3D.at[c]).start()
    peers_wait(5, lambda p: B2S, B2R)
    for q in range(8):
        DTA[c, :, q * 128 : q * 128 + 128] = jnp.concatenate(
            [from_tile(B2R[2 * q]), from_tile(B2R[2 * q + 1])], axis=1
        )
    d_tact = dot_nt(DTA[c].astype(BF), EX[:, 0:1024].astype(BF))
    CP[c, 3, :, 0:64] = (d_tact * silu_slope(CND[0])).astype(BF).astype(F32)
    twin_copy(15, DTA.at[c], DTA.at[c]).start()
    twin_copy(16, CP.at[c], CP.at[c]).start()
    twin_copy(17, E1.at[c], E1.at[c]).start()
    step(8)
    twin_copy(13, DMB.at[o], DMB.at[o]).wait_recv()
    unpack(o)
    twin_copy(14, B3D.at[o], B3D.at[o]).wait_recv()
    twin_copy(15, DTA.at[o], DTA.at[o]).wait_recv()
    twin_copy(16, CP.at[o], CP.at[o]).wait_recv()
    twin_copy(17, E1.at[o], E1.at[o]).wait_recv()

    def packed(i):
        return jnp.concatenate([CP[0, i, :, 0:64], CP[1, i, :, 0:64]], axis=0)

    def square_half(value):
        part = 0.5 * value * value
        return jnp.sum(jnp.sum(part, axis=0, keepdims=True), axis=1, keepdims=True)

    cond_both = packed(0).astype(BF)
    small = jnp.zeros((1, 1), F32)
    for k in range(8):
        grad = dot_tn(cond_both, jnp.concatenate([DMF[0, k], DMF[1, k]], axis=0).astype(BF))
        small += square_half(grad)
        if k < 6:
            WMOD[:, k * 1024 : k * 1024 + 1024] = grad
        else:
            EX[:, (k - 5) * 1024 : (k - 4) * 1024] = grad
    mod_out = pltpu.make_async_copy(WMOD, g_in.at[:, pl.ds(0, 6144)], st_sem.at[26])
    mod_out.start()
    step(9)
    grad = dot_tn(packed(1).astype(BF), jnp.concatenate([DTA[0], DTA[1]], axis=0).astype(BF))
    small += square_half(grad)
    EX[:, 0:1024] = grad
    sums = B3D[0] + B3D[1]
    small += square_half(sums[:, 64:128])
    wide = jnp.concatenate(
        [sums, jnp.zeros((112, 128), F32)], axis=0
    )
    EX[:, 3072:3088] = wide.T[64:128, 0:16]
    def both(value):
        return jnp.concatenate([value(0), value(1)], axis=0)

    index = lax.broadcasted_iota(jnp.int32, (32, ENTRIES), 1)
    hot = (both(lambda g: E1[g, :, 2, 0:1]).astype(jnp.int32) + PDIM == index).astype(F32)
    grad = dot_tn_exact(packed(2), hot)
    spot = lax.broadcasted_iota(jnp.int32, (16, ENTRIES), 0) == index[0:16]
    grad += dot_tn_exact(sums[:, 0:64], spot.astype(F32))
    ENT[...] = grad
    femb = both(lambda g: jnp.concatenate([E1[g, :, 0, :], E1[g, :, 1, :]], axis=1)).astype(BF)
    ENT[:, PDIM + NCLS :] = dot_tn(packed(3).astype(BF), femb)
    small += square_half(ENT[...])

    for t in range(10, NU + LAGS[3]):
        step(t)

    def total_of(value):
        return jnp.sum(jnp.sum(value, axis=0, keepdims=True), axis=1, keepdims=True)

    NSS[0:1, :] = jnp.broadcast_to(total_of(SQ[...]) + small, (1, 128))
    NSS[1:2, :] = jnp.broadcast_to(total_of(LOSS[...]) / (TOK * PDIM), (1, 128))
    NSS[2:8, :] = jnp.zeros((6, 128), F32)
    NSR[c * 16 + s] = NSS[...]

    def far_copy(k, frm):
        return remote(NSS, NSR.at[frm], far_s.at[k], far_r.at[frm % 16], dev(o, k))

    @pl.loop(0, 16)
    def _(k):
        far_copy(k, c * 16 + s).start()

    mine = NSR.at[pl.ds(c * 16, 16)]
    peers_send(6, lambda p: NSS, mine)
    mod_out.wait()
    for i in range(27):
        for copy in result_copies(i):
            copy.wait()
    for u in range(9, NU):
        sums_done(u)
    twin_copy(0, ATI.at[c], ATI.at[c]).wait_send()
    twin_copy(1, MIX.at[c], MIX.at[c]).wait_send()
    twin_copy(2, W.at[3], WP).wait_send()
    twin_copy(3, MLI.at[c], MLI.at[c]).wait_send()
    twin_copy(6, DMO.at[c], DMO.at[c]).wait_send()
    twin_copy(9, DAO.at[c, :, dao_other], DAO.at[c, :, dao_other]).wait_send()
    twin_copy(10, DMS, DMX.at[c]).wait_send()
    for ch in range(2):
        twin_copy(11 + ch, SND.at[ch], RCV.at[ch]).wait_send()
    twin_copy(13, DMB.at[c], DMB.at[c]).wait_send()
    twin_copy(14, B3D.at[c], B3D.at[c]).wait_send()
    twin_copy(15, DTA.at[c], DTA.at[c]).wait_send()
    twin_copy(16, CP.at[c], CP.at[c]).wait_send()
    twin_copy(17, E1.at[c], E1.at[c]).wait_send()

    peers_wait(6, lambda p: NSS, mine)

    @pl.loop(0, 16)
    def _(k):
        far_copy(k, o * 16 + k).wait()

    totals = jnp.sum(NSR[...], axis=0)
    norm = jnp.sqrt(totals[0:1])
    stats[...] = totals
    stats[0:1, :] = norm
    stats[2:3, :] = clip_limit / jnp.maximum(norm, clip_limit)


def fused_step(msg, noisy, noise, pos, block_in, block_out, entry, exit_):
    vm = pltpu.VMEM
    dma = pltpu.SemaphoreType.DMA
    scratch = [
        vm((12, 4, 2, 2, 64, 512), BF), vm((4, 2, 2, 64, 512), BF), vm((12, 4, 2, 2, 64, 512), BF),
        vm((4, 2, 4, 64, 512), BF), vm((4, 4, 64, 512), BF), vm((4, 4, 64, 512), BF),
        vm((len(SUM_VIA_Z), 64, 512), BF), vm((12, 64, 512), F32),
        vm((2, TOK, 1024), BF), vm((3, 2, TOK, 512), BF), vm((2, 2, TOK, 512), BF), vm((2, TOK, 1024), BF),
        vm((2, TOK, 2048), BF), vm((2, TOK, 2048), BF), vm((2, TOK, 1024), BF), vm((2, TOK, 1024), BF),
        vm((2, TOK, 512), BF), vm((TOK, 512), BF),
        *[vm((TOK, 1024), F32)] * 5, vm((2, TOK, 512), F32), vm((2, TOK, 512), F32),
        vm((64, 6144), F32), vm((TOK, PDIM), BF), vm((TOK, PDIM), F32), vm((16, 128), BF), vm((2, 16, 8, 128), F32), vm((16, 16, 128), BF), vm((16, 8, 128), F32), vm((16, 8, 128), F32),
        vm((16, 16, 512), BF), vm((16, 16, 512), BF), vm((2, 16, 16, 512), BF), vm((2, 8, 16, 1024), F32),
        vm((8, 128), F32), vm((16, 8, 128), F32), vm((2, 16, 1024), F32), vm((2, 4, 16, 128), F32), vm((2, 16, 64), F32),
        vm((16, 16, 128), BF), vm((16, 16, 128), BF), vm((2, 16, 128), F32),
        vm((8, 128), F32), vm((32, 8, 128), F32),
        vm((8, 1024), F32), vm((8, 8, 1024), F32), vm((16, 1024), BF), vm((16, 1024), BF), vm((32, 1024), F32),
        vm((8, 512), F32), vm((8, 16), F32),
        dma((27,)), dma((8, 16)), dma((8, 16)), dma((96,)), dma((96,)), dma((48,)), dma((48,)), dma((96,)), dma((96,)),
        dma((30,)), dma((30,)), dma((15,)), dma((15,)), dma((120,)), dma((120,)), dma((30,)), dma((30,)), dma((19,)), dma((19,)),
        dma((27,)), dma((27,)), dma((27,)), dma((16,)), dma((16,)),
        pltpu.SemaphoreType.REGULAR, pltpu.SemaphoreType.REGULAR, pltpu.SemaphoreType.REGULAR,
    ]
    any_ = pl.BlockSpec(memory_space=pl.ANY)
    vmem = pl.BlockSpec(memory_space=pltpu.VMEM)
    shape = jax.ShapeDtypeStruct
    return pl.pallas_call(
        step_kernel,
        out_shape=(
            shape(block_in.shape, F32), shape(block_out.shape, F32), shape(entry.shape, F32),
            shape(exit_.shape, F32), shape((8, 128), F32),
        ),
        in_specs=[vmem, vmem, vmem, vmem, any_, any_, any_, any_],
        out_specs=(any_, any_, vmem, vmem, vmem),
        scratch_shapes=scratch,
        compiler_params=pltpu.CompilerParams(
            collective_id=0, has_side_effects=True, vmem_limit_bytes=62 * 2**20
        ),
        cost_estimate=pl.CostEstimate(flops=21 * 10**9, bytes_accessed=20 * 10**6, transcendentals=4 * 10**6),
    )(msg, noisy, noise, pos, block_in, block_out, entry, exit_)


def adam_kernel(stats, *refs):
    ins, (loss, grad_norm), outs = refs[:16], refs[16:18], refs[18:]
    factor = stats[2, 0]
    loss[0, 0] = stats[1, 0]
    grad_norm[0, 0] = stats[0, 0]
    corr = 1.0 - 0.5**STEP

    def update(i, rate):
        weight, first, second, grad = (r[...] for r in ins[4 * i : 4 * i + 4])
        clipped = grad * factor
        first_new = 0.5 * first + 0.5 * clipped
        second_new = 0.5 * second + 0.5 * clipped * clipped
        change = first_new * (1.0 / corr) / (jnp.sqrt(second_new * (1.0 / corr)) + adam_eps)
        weight_new = weight - rate * (change + decay_rate * weight)
        for ref, value in zip(outs[4 * i : 4 * i + 4], (weight_new, first_new, second_new, weight_new)):
            ref[...] = value.astype(ref.dtype)

    update(0, rate_main)
    update(1, rate_main)
    update(2, rate_edge)
    update(3, rate_main)


def adam_all(stats, *groups):
    steps = 2
    specs = []
    for i, group in enumerate(groups):
        rows, cols = group[0].shape
        if i == 0:
            specs.append(pl.BlockSpec((rows, cols // steps), lambda t: (0, t)))
        elif i == 1:
            specs.append(pl.BlockSpec((rows // steps, cols), lambda t: (t, 0)))
        else:
            specs.append(pl.BlockSpec((rows // steps, cols), lambda t: (t, 0)))
    scalar = pl.BlockSpec(memory_space=pltpu.SMEM)
    shape = jax.ShapeDtypeStruct
    count = sum(group[0].size for group in groups)
    return pl.pallas_call(
        adam_kernel,
        grid=(steps,),
        out_shape=(
            shape((1, 1), F32), shape((1, 1), F32),
            *(shape(group[0].shape, d) for group in groups for d in (F32, F32, F32, BF)),
        ),
        in_specs=[scalar, *(spec for spec in specs for _ in range(4))],
        out_specs=(scalar, scalar, *(spec for spec in specs for _ in range(4))),
        compiler_params=pltpu.CompilerParams(vmem_limit_bytes=62 * 2**20),
        cost_estimate=pl.CostEstimate(flops=20 * count, bytes_accessed=30 * count, transcendentals=2 * count),
    )(stats, *(a for group in groups for a in group))


def local_fused(
    noisy, timesteps, labels, noise,
    block_in, block_in_first, block_in_second,
    block_out, block_out_first, block_out_second,
    entry_table, entry_first, entry_second,
    exit_proj, exit_first, exit_second,
):
    index = lax.axis_index("rep") * 16 + lax.axis_index("shard")
    femb = lowered(time_features(timesteps, FREQ)).astype(F32).reshape(2, LANES)
    label = labels.astype(F32)[0]
    lane = jnp.arange(LANES)[None, :]
    head = jnp.concatenate(
        [femb, jnp.full((1, LANES), label), jnp.where(lane == index, label, 0.0), jnp.zeros((4, LANES), F32)], axis=0
    )
    side = noisy.shape[-1]
    grid, quarter = side // PATCH, D // 4
    angle = np.arange(grid)[:, None] / 10000.0 ** (np.arange(quarter)[None, :] / quarter)
    pos = jnp.asarray(np.concatenate([np.sin(angle), np.cos(angle)], axis=1), F32)
    g_in, g_out, g_entry, g_exit, stats = fused_step(
        head, noisy.reshape(-1, side), noise.reshape(-1, side), pos, block_in[0], block_out[0], entry_table.T, exit_proj
    )
    loss, grad_norm, *new = adam_all(
        stats,
        (block_in[0], block_in_first[0], block_in_second[0], g_in),
        (block_out[0], block_out_first[0], block_out_second[0], g_out),
        (entry_table.T, entry_first.T, entry_second.T, g_entry),
        (exit_proj, exit_first, exit_second, g_exit),
    )
    return (
        loss[0, 0], grad_norm[0, 0], *(a[None] for a in new[:8]), *(a.T for a in new[8:12]), *new[12:]
    )


def solution(mesh):
    step = local_fused if dict(mesh.shape) == {"rep": 2, "shard": 16} else local
    in_specs = (
        P(("rep", "shard"), None, None, None),
        P(("rep", "shard")),
        P(("rep", "shard")),
        P(("rep", "shard"), None, None, None),
        P(None, "shard", None),
        P(None, "shard", None),
        P(None, "shard", None),
        P(None, "shard", None),
        P(None, "shard", None),
        P(None, "shard", None),
        P(None, "shard"),
        P(None, "shard"),
        P(None, "shard"),
        P("shard", None),
        P("shard", None),
        P("shard", None),
    )
    out_specs = (
        P(),
        P(),
        P(None, "shard", None),
        P(None, "shard", None),
        P(None, "shard", None),
        P(None, "shard", None),
        P(None, "shard", None),
        P(None, "shard", None),
        P(None, "shard", None),
        P(None, "shard", None),
        P(None, "shard"),
        P(None, "shard"),
        P(None, "shard"),
        P(None, "shard"),
        P("shard", None),
        P("shard", None),
        P("shard", None),
        P("shard", None),
    )
    return jax.shard_map(step, mesh=mesh, in_specs=in_specs, out_specs=out_specs, check_vma=False)
```
